32 devices in a mesh: groups: 2 (over y), coord: 16 (over z, x, core).
Axes of the slice: x: 2, y: 2, z: 4, core: 2. Of those that a mesh axis runs over, the one named last changes fastest.
Arguments:
- activations: bfloat16 [64, 128, 4096], P(('groups', 'coord')), parts along dimension 0, may hold values from -6 to 6
- out_grads: bfloat16 [64, 128, 4096], P(('groups', 'coord')), parts along dimension 0, may hold values from -6 to 6
- proj_in: bfloat16 [4096, 128], P('coord'), may hold values from -0.09375 to 0.09375
- proj_out: bfloat16 [4096, 128], P('coord'), may hold values from -0.09375 to 0.09375
- cov_in: float32 [128, 128], replicated
- cov_out: float32 [128, 128], replicated
- lengths: int32 [64], P(('groups', 'coord')), parts along dimension 0, may hold values from 1 to 128
- seq_ids: int32 [64], P(('groups', 'coord')), parts along dimension 0, may hold values from 0 to 31, each once
- bank: bfloat16 [1536, 16384], P(None, 'coord'), may hold values from -0.015625 to 0.015625
Outputs:
- scores: bfloat16 [64, 1536], P('groups', 'coord'), parts along dimension 0
The draws below stay inside these ranges and needn't reach their ends.
There are 2 independent parts, one for each index of `groups`. The reference program is written for one: setup_inputs(seed, part) draws one part's arguments, and reference() takes and returns one part's arrays. A program takes and returns all parts, laid end to end along the dimension named above; an argument that names none is the same for every part. Nothing has to cross between parts.
All inputs are finite; a program needn't handle non-finite values.
Results may differ from the reference program's by a relative error of at most 0.0064.
Values may be sent and summed in bfloat16 or wider, within the bound.
No kernel may reach another device: no remote copies, remote signals or barrier semaphores. Data moves between devices by JAX's collectives and lax.ppermute only.
A program may use at most 128 MiB of HBM per device.

```python
import math
import jax
import jax.numpy as jnp
from jax import lax

D = 4096
RANK = 128
LEN = 128
SEQS = 32
QUERIES = 1536
COORDS = 16384


def make_factor(key):
    first, second = jax.random.split(key)
    mixing = jax.random.normal(first, (RANK, RANK), jnp.float32)
    lower_end, upper_end = (0.5, 5.0)
    diagonal = jnp.exp(jax.random.uniform(second, (RANK,), jnp.float32, math.log(lower_end), math.log(upper_end)))
    factor = jnp.dot(mixing, mixing.T) / RANK + jnp.diag(diagonal)
    return 0.5 * (factor + factor.T)


def draw_cov_in(key, part):
    return make_factor(jax.random.fold_in(key, 21))


def draw_cov_out(key, part):
    return make_factor(jax.random.fold_in(key, 37))


def draw_lengths(key, part):
    values = jax.random.randint(jax.random.fold_in(key, 5), (SEQS,), 1, LEN + 1)
    return values.at[0].set(LEN).at[1].set(1).astype(jnp.int32)


def strengthened(result, key, source, target, blocks, factor):
    def block_of(axis_at):
        return (jnp.arange(result.shape[axis_at]) // (result.shape[axis_at] // blocks)).reshape((-1,) + (1,) * (result.ndim - 1 - axis_at))

    one_side = jax.random.permutation(key, blocks)[block_of(target)]
    far = (block_of(target) + blocks // 2) % blocks
    return jnp.where((block_of(source) == one_side) | (block_of(source) == far), factor * result, result)


def shard_levels(stream_key, extent, shards, smallest, largest):
    factor_of, own = 1.0, jax.random.fold_in(stream_key, 6)
    for dim, parts in shards:
        steps = jnp.exp(jax.random.uniform(jax.random.fold_in(own, dim), (parts,), jnp.float32, smallest / len(shards), largest / len(shards)))
        factor_of = factor_of * jnp.repeat(steps, extent[dim] // parts).reshape([-1 if axis == dim else 1 for axis in range(len(extent))])
    return factor_of


def scatter_about(stream_key, extent, scale, bound, cuts=(), held_as=jnp.bfloat16):
    array = jax.random.normal(stream_key, extent, jnp.float32) * scale
    if len(cuts) > 0:
        array = shard_levels(stream_key, extent, cuts, -0.22, 0.18) * array
    return jnp.clip(array, min=-bound, max=bound).astype(held_as)


def heavy_noise(own_key, shape, scale, reach, cuts, heavy, held_as=jnp.bfloat16):
    values = scale * jax.random.normal(own_key, shape, jnp.float32)
    if cuts:
        values = values * shard_levels(own_key, shape, cuts, -0.22, 0.18)
    return jnp.clip(strengthened(values, jax.random.fold_in(own_key, 3), *heavy), -reach, reach).astype(held_as)


def setup_inputs(seed: int = 0, part: int = 0) -> dict:
    seeds = jax.random.split(jax.random.key(seed), 10)
    own_keys = jax.random.split(jax.random.fold_in(seeds[9], part), 10)
    activations = scatter_about(own_keys[0], (SEQS, LEN, D), 1.0, 6.0, ((0, 16),))
    out_grads = scatter_about(own_keys[1], (SEQS, LEN, D), 1.0, 6.0, ((0, 16),))
    proj_in = scatter_about(seeds[2], (D, RANK), D ** -0.5, 0.09375, ((0, 16),))
    proj_out = scatter_about(seeds[3], (D, RANK), D ** -0.5, 0.09375, ((0, 16),))
    cov_in = draw_cov_in(jax.random.fold_in(seeds[9], 71), part)
    cov_out = draw_cov_out(jax.random.fold_in(seeds[9], 71), part)
    lengths = draw_lengths(jax.random.fold_in(jax.random.fold_in(seeds[9], part), 71), part)
    seq_ids = jax.random.permutation(own_keys[7], SEQS).astype(jnp.int32)
    bank = heavy_noise(seeds[8], (QUERIES, COORDS), (COORDS * 16) ** -0.5, 0.015625, ((1, 16),), (1, 0, 16, 2.0))
    return {"activations": activations, "out_grads": out_grads, "proj_in": proj_in, "proj_out": proj_out, "cov_in": cov_in, "cov_out": cov_out, "lengths": lengths, "seq_ids": seq_ids, "bank": bank}


def inverse_factor(cov):
    size = cov.shape[0]
    damping = 0.1 * jnp.trace(cov) / size
    eye = jnp.eye(size, dtype=jnp.float32)
    lower = jnp.linalg.cholesky(cov + damping * eye)
    return jax.scipy.linalg.cho_solve((lower, True), eye)

def reference(activations, out_grads, proj_in, proj_out, cov_in, cov_out, lengths, seq_ids, bank):
    seqs, length, width = activations.shape
    rank = proj_in.shape[1]
    x_full = jnp.dot(activations.reshape(seqs * length, width).astype(jnp.float32), proj_in.astype(jnp.float32), preferred_element_type=jnp.float32).reshape(seqs, length, rank)
    position = lax.broadcasted_iota(jnp.int32, (seqs, length), 1)
    valid = (position < lengths[:, None]).astype(jnp.float32)
    x_proj = (x_full * valid[:, :, None]).astype(jnp.bfloat16)
    d_proj = jnp.dot(out_grads.reshape(seqs * length, width).astype(jnp.float32), proj_out.astype(jnp.float32), preferred_element_type=jnp.float32).reshape(seqs, length, rank).astype(jnp.bfloat16)
    grads = jnp.einsum('sto,sti->soi', d_proj.astype(jnp.float32), x_proj.astype(jnp.float32), preferred_element_type=jnp.float32)
    k_in = inverse_factor(cov_in)
    k_out = inverse_factor(cov_out)
    left = jnp.einsum('ab,sbc->sac', k_out, grads, precision=lax.Precision.HIGHEST)
    whitened = jnp.einsum('sac,cd->sad', left, k_in, precision=lax.Precision.HIGHEST)
    whitened = whitened.astype(jnp.bfloat16).reshape(seqs, rank * rank)
    raw = lax.dot_general(whitened.astype(jnp.float32), bank.astype(jnp.float32), (((1,), (1,)), ((), ())), preferred_element_type=jnp.float32).astype(jnp.bfloat16)
    return jnp.zeros_like(raw).at[seq_ids].set(raw)
```

```python
import functools

import jax
import jax.numpy as jnp
from jax import lax
from jax.experimental import pallas as pl
from jax.experimental.pallas import tpu as pltpu
from jax.sharding import PartitionSpec as P

SUB = 8
LANES = 128
EXACT = lax.Precision.HIGHEST
VMEM = pl.BlockSpec(memory_space=pltpu.VMEM)
SMEM = pl.BlockSpec(memory_space=pltpu.SMEM)


def factors(n):
    c = 2 if n % 2 == 0 else 1
    rest = n // c
    b = max(f for f in range(1, rest + 1) if rest % f == 0 and f * f <= rest)
    return rest // b, b, c


def sources(me, n):
    a, b, c = factors(n)
    ia, ib, ic = me // (b * c), (me // c) % b, me % c
    return [
        (((ia + a - da) % a) * b + (ib + b - db) % b) * c + (ic + c - dc) % c
        for dc in range(c)
        for db in range(b)
        for da in range(a)
    ]


def gather_blocks(shard, n):
    sizes = factors(n)
    a, b, c = sizes

    def moved(value, axis, by):
        pairs = []
        for me in range(n):
            at = [me // (b * c), (me // c) % b, me % c]
            at[axis] = (at[axis] + by) % sizes[axis]
            pairs.append((me, (at[0] * b + at[1]) * c + at[2]))
        return lax.ppermute(value, "coord", pairs)

    along_a = [shard] + [moved(shard, 0, da) for da in range(1, a)]
    along_b = list(along_a)
    for db in range(1, b):
        along_b += [moved(block, 1, db) for block in along_a]
    blocks = list(along_b)
    for dc in range(1, c):
        blocks += [moved(block, 2, dc) for block in along_b]
    return blocks


def inverse_kernel(cov_in_ref, cov_out_ref, k_in_ref, k_out_ref):
    size = cov_in_ref.shape[0]
    groups = size // SUB
    lane = lax.broadcasted_iota(jnp.int32, (SUB, size), 1)
    sub = lax.broadcasted_iota(jnp.int32, (SUB, size), 0)
    head = lane < SUB

    def damped(ref):
        cov = ref[...]
        cov = 0.5 * (cov + cov.T)
        row = lax.broadcasted_iota(jnp.int32, (size, size), 0)
        col = lax.broadcasted_iota(jnp.int32, (size, size), 1)
        diagonal = row == col
        damping = 0.1 * jnp.sum(jnp.where(diagonal, cov, 0.0)) / size
        cov = jnp.where(diagonal, cov + damping, cov)
        return [cov[g * SUB : (g + 1) * SUB, :] for g in range(groups)]

    def column(block, p):
        return jnp.broadcast_to(block[:, p : p + 1], (SUB, size))

    def step(blocks):
        pivot = blocks[0]
        rows = [jnp.broadcast_to(pivot[i : i + 1, :], (SUB, size)) for i in range(SUB)]
        diag = {(i, j): column(rows[i], j) for i in range(SUB) for j in range(i, SUB)}
        rows = [jnp.where(head, (lane == i).astype(jnp.float32), rows[i]) for i in range(SUB)]
        inverse, factor = [], {}
        for p in range(SUB):
            inverse.append(1.0 / diag[p, p])
            for i in range(p + 1, SUB):
                factor[p, i] = diag[p, i] * inverse[p]
                for j in range(i, SUB):
                    diag[i, j] = diag[i, j] - factor[p, i] * diag[p, j]
                rows[i] = rows[i] - factor[p, i] * rows[p]
        rows = [rows[p] * inverse[p] for p in range(SUB)]
        for p in reversed(range(SUB)):
            for i in range(p):
                rows[i] = rows[i] - factor[i, p] * rows[p]
        done = rows[0]
        for i in range(1, SUB):
            done = jnp.where(sub == i, rows[i], done)
        out = []
        for block in blocks[1:]:
            terms = [column(block, p) * rows[p] for p in range(SUB)]
            while len(terms) > 1:
                terms = [terms[i] + terms[i + 1] for i in range(0, len(terms), 2)]
            out.append(jnp.where(head, 0.0, block) - terms[0])
        out.append(done)
        return [pltpu.roll(block, size - SUB, 1) for block in out]

    def both(_, carry):
        return tuple(step(list(blocks)) for blocks in carry)

    carry = lax.fori_loop(0, groups, both, (damped(cov_in_ref), damped(cov_out_ref)))
    for blocks, ref in zip(carry, (k_in_ref, k_out_ref)):
        for g in range(groups):
            ref[g * SUB : (g + 1) * SUB, :] = blocks[g]


def inverses(cov_in, cov_out):
    size = cov_in.shape[0]
    shape = jax.ShapeDtypeStruct((size, size), jnp.float32)
    return pl.pallas_call(
        lambda a, b, c, d: inverse_kernel(a, b, c, d),
        out_shape=(shape, shape),
        in_specs=[VMEM, VMEM],
        out_specs=(VMEM, VMEM),
        cost_estimate=pl.CostEstimate(flops=4 * size**3, bytes_accessed=24 << 20, transcendentals=0),
        name="inverses",
    )(cov_in, cov_out)


def whiten_kernel(n, me_ref, len_ref, act_ref, grad_ref, k_in_ref, k_out_ref, *rest):
    blocks, (out_ref, p_in, p_out, white) = rest[:n], rest[n:]
    seqs, rank = len_ref.shape[0], k_in_ref.shape[0]
    length = act_ref.shape[0] // seqs
    rows = blocks[0].shape[0] // 2
    for block, src in zip(blocks, sources(me_ref[0], n)):
        at = pl.ds(pl.multiple_of(src * rows, rows), rows)
        p_in[at, :] = block[:rows, :]
        p_out[at, :] = block[rows:, :]
    x_full = jnp.dot(act_ref[...], p_in[...], preferred_element_type=jnp.float32)
    d_proj = jnp.dot(grad_ref[...], p_out[...], preferred_element_type=jnp.float32).astype(jnp.bfloat16)
    token = lax.broadcasted_iota(jnp.int32, (length, rank), 0)
    share = rank // n
    for s in range(seqs):
        part = slice(s * length, (s + 1) * length)
        x_proj = jnp.where(token < len_ref[s], x_full[part], 0.0).astype(jnp.bfloat16)
        grads = lax.dot_general(
            d_proj[part], x_proj, (((0,), (0,)), ((), ())), preferred_element_type=jnp.float32
        )
        left = jnp.dot(k_out_ref[...], grads, precision=EXACT, preferred_element_type=jnp.float32)
        full = jnp.dot(left, k_in_ref[...], precision=EXACT, preferred_element_type=jnp.float32)
        for d in range(n):
            white[d, s * share : (s + 1) * share, :] = full[d * share : (d + 1) * share, :]
    out_ref[...] = white[...].astype(jnp.bfloat16)


def whitened_blocks(me, lengths, activations, out_grads, k_in, k_out, blocks):
    n = len(blocks)
    seqs, length, width = activations.shape
    rank = k_in.shape[0]
    shape = (n, seqs * (rank // n), rank)
    return pl.pallas_call(
        functools.partial(whiten_kernel, n),
        out_shape=jax.ShapeDtypeStruct(shape, jnp.bfloat16),
        in_specs=[SMEM, SMEM] + [VMEM] * (4 + n),
        out_specs=VMEM,
        scratch_shapes=[
            pltpu.VMEM((width, rank), jnp.bfloat16),
            pltpu.VMEM((width, rank), jnp.bfloat16),
            pltpu.VMEM(shape, jnp.float32),
        ],
        compiler_params=pltpu.CompilerParams(vmem_limit_bytes=32 << 20),
        cost_estimate=pl.CostEstimate(
            flops=4 * seqs * length * width * rank, bytes_accessed=6 << 20, transcendentals=0
        ),
        name="whiten",
    )(
        me,
        lengths,
        activations.reshape(seqs * length, width),
        out_grads.reshape(seqs * length, width),
        k_in,
        k_out,
        *blocks,
    )


def score_kernel(n, me_ref, ids_ref, white_ref, bank_ref, out_ref, spread):
    seqs = ids_ref.shape[0]
    chunk, rank = white_ref.shape[1:]
    share = chunk // seqs
    total = n * seqs
    spread[...] = white_ref[...].astype(jnp.float32).reshape(n * chunk, rank)
    columns = jnp.concatenate(
        [spread[pl.ds(j, total, stride=share), :].astype(jnp.bfloat16) for j in range(share)], axis=1
    )
    queries = bank_ref.shape[0] // n
    row = lax.broadcasted_iota(jnp.int32, (total, out_ref.shape[2] - queries), 0)
    tail = jnp.zeros(row.shape, jnp.float32)
    for s in range(seqs):
        tail = jnp.where(row == me_ref[0] * seqs + s, ids_ref[s].astype(jnp.float32), tail)
    partial = lax.dot_general(
        columns, bank_ref[...], (((1,), (1,)), ((), ())), preferred_element_type=jnp.float32
    )
    for d in range(n):
        out_ref[d, :, :queries] = partial[:, d * queries : (d + 1) * queries]
        out_ref[d, :, queries:] = tail


def partial_scores(me, seq_ids, white, bank):
    n = white.shape[0]
    seqs = seq_ids.shape[0]
    queries = bank.shape[0] // n
    width = (queries // LANES + 1) * LANES
    return pl.pallas_call(
        functools.partial(score_kernel, n),
        out_shape=jax.ShapeDtypeStruct((n, n * seqs, width), jnp.float32),
        in_specs=[SMEM, SMEM, VMEM, VMEM],
        out_specs=VMEM,
        scratch_shapes=[pltpu.VMEM((n * white.shape[1], white.shape[2]), jnp.float32)],
        compiler_params=pltpu.CompilerParams(vmem_limit_bytes=48 << 20),
        cost_estimate=pl.CostEstimate(
            flops=2 * n * seqs * bank.size, bytes_accessed=2 * bank.size, transcendentals=0
        ),
        name="score",
    )(me, seq_ids, white, bank)


def place_kernel(partial_ref, out_ref):
    rows, queries = out_ref.shape
    total = jnp.sum(partial_ref[...], axis=0)
    raw = total[:, :queries].astype(jnp.bfloat16)
    ids = total[:, queries : queries + 1].astype(jnp.int32)
    chosen = ids == lax.broadcasted_iota(jnp.int32, (rows, rows), 1)
    out_ref[...] = lax.dot_general(
        chosen.astype(jnp.bfloat16), raw, (((0,), (0,)), ((), ())), preferred_element_type=jnp.float32
    ).astype(jnp.bfloat16)


def place(partials, queries):
    return pl.pallas_call(
        lambda a, b: place_kernel(a, b),
        out_shape=jax.ShapeDtypeStruct((partials.shape[1], queries), jnp.bfloat16),
        in_specs=[VMEM],
        out_specs=VMEM,
        compiler_params=pltpu.CompilerParams(vmem_limit_bytes=48 << 20),
        name="place",
    )(partials)


def body(n, activations, out_grads, proj_in, proj_out, cov_in, cov_out, lengths, seq_ids, bank):
    me = lax.axis_index("coord").reshape(1)
    blocks = gather_blocks(jnp.concatenate([proj_in, proj_out], axis=0), n)
    k_in, k_out = inverses(cov_in, cov_out)
    white = whitened_blocks(me, lengths, activations, out_grads, k_in, k_out, blocks)
    white = lax.all_to_all(white, "coord", split_axis=0, concat_axis=0, tiled=True)
    partials = partial_scores(me, seq_ids, white, bank)
    partials = lax.all_to_all(partials, "coord", split_axis=0, concat_axis=0, tiled=True)
    return place(partials, bank.shape[0] // n)


def solution(mesh):
    in_specs = (
        P(("groups", "coord"), None, None),
        P(("groups", "coord"), None, None),
        P("coord", None),
        P("coord", None),
        P(),
        P(),
        P(("groups", "coord")),
        P(("groups", "coord")),
        P(None, "coord"),
    )
    out_specs = P("groups", "coord")
    return jax.shard_map(
        functools.partial(body, mesh.shape["coord"]),
        mesh=mesh,
        in_specs=in_specs,
        out_specs=out_specs,
        check_vma=False,
    )
```

```python
import functools

import jax
import jax.numpy as jnp
from jax import lax
from jax.experimental import pallas as pl
from jax.experimental.pallas import tpu as pltpu
from jax.sharding import PartitionSpec as P

SUB = 8
LANES = 128
EXACT = lax.Precision.HIGHEST
VMEM = pl.BlockSpec(memory_space=pltpu.VMEM)
HBM = pl.BlockSpec(memory_space=pltpu.HBM)
SMEM = pl.BlockSpec(memory_space=pltpu.SMEM)


def factors(n):
    c = 2 if n % 2 == 0 else 1
    rest = n // c
    b = max(f for f in range(1, rest + 1) if rest % f == 0 and f * f <= rest)
    return rest // b, b, c


def sources(me, n):
    a, b, c = factors(n)
    ia, ib, ic = me // (b * c), (me // c) % b, me % c
    return [
        (((ia + a - da) % a) * b + (ib + b - db) % b) * c + (ic + c - dc) % c
        for dc in range(c)
        for db in range(b)
        for da in range(a)
    ]


def gather_blocks(shard, n, before):
    sizes = factors(n)
    a, b, c = sizes

    def moved(value, axis, by):
        pairs = []
        for me in range(n):
            at = [me // (b * c), (me // c) % b, me % c]
            at[axis] = (at[axis] + by) % sizes[axis]
            pairs.append((me, (at[0] * b + at[1]) * c + at[2]))
        return lax.ppermute(value, "coord", pairs)

    along_a = [shard] + [lax.optimization_barrier((moved(shard, 0, da), before))[0] for da in range(1, a)]
    along_b = list(along_a)
    for db in range(1, b):
        along_b += [moved(block, 1, db) for block in along_a]
    blocks = list(along_b)
    for dc in range(1, c):
        blocks += [moved(block, 2, dc) for block in along_b]
    return blocks


def gauss_jordan(blocks):
    width = blocks[0].shape[1]
    half = width // 2
    lane = lax.broadcasted_iota(jnp.int32, (SUB, width), 1)
    sub = lax.broadcasted_iota(jnp.int32, (SUB, width), 0)
    start, within = lane // half * half, lane % half

    def column(block, at):
        return jnp.take_along_axis(block, start + at, axis=1, mode="promise_in_bounds")

    for k in range(len(blocks)):
        at = k * SUB
        head = within // SUB == k
        rows = [jnp.broadcast_to(blocks[k][i : i + 1, :], (SUB, width)) for i in range(SUB)]
        diag = {(i, j): column(rows[i], at + j) for i in range(SUB) for j in range(i, SUB)}
        rows = [jnp.where(head, (within == at + i).astype(jnp.float32), rows[i]) for i in range(SUB)]
        inverse, factor = [], {}
        for p in range(SUB):
            inverse.append(1.0 / diag[p, p])
            for i in range(p + 1, SUB):
                factor[p, i] = diag[p, i] * inverse[p]
                for j in range(i, SUB):
                    diag[i, j] = diag[i, j] - factor[p, i] * diag[p, j]
                rows[i] = rows[i] - factor[p, i] * rows[p]
        rows = [rows[p] * inverse[p] for p in range(SUB)]
        for p in reversed(range(SUB)):
            for i in range(p):
                rows[i] = rows[i] - factor[i, p] * rows[p]
        done = rows[0]
        for i in range(1, SUB):
            done = jnp.where(sub == i, rows[i], done)
        out = []
        for g, block in enumerate(blocks):
            if g == k:
                out.append(done)
                continue
            terms = [column(block, at + p) * rows[p] for p in range(SUB)]
            while len(terms) > 1:
                terms = [terms[i] + terms[i + 1] for i in range(0, len(terms), 2)]
            out.append(jnp.where(head, 0.0, block) - terms[0])
        blocks = out
    return blocks


def side_by_side_inverses(first, second):
    half = first.shape[0]
    both = jnp.concatenate([first, second], axis=1)
    blocks = gauss_jordan([both[g : g + SUB, :] for g in range(0, half, SUB)])
    both = jnp.concatenate(blocks, axis=0)
    return both[:, :half], both[:, half:]


def damped(cov):
    size = cov.shape[0]
    cov = 0.5 * (cov + cov.T)
    row = lax.broadcasted_iota(jnp.int32, (size, size), 0)
    col = lax.broadcasted_iota(jnp.int32, (size, size), 1)
    damping = 0.1 * jnp.sum(jnp.where(row == col, cov, 0.0)) / size
    return jnp.where(row == col, cov + damping, cov)


def product(left, right, dims=((1,), (0,))):
    return lax.dot_general(left, right, (dims, ((), ())), precision=EXACT, preferred_element_type=jnp.float32)


def inverse_kernel(
    len_hbm, cov_in_hbm, cov_out_hbm, act_hbm, grad_hbm, k_ref, act_ref, grad_ref, cov_in_ref, cov_out_ref, len_ref, sems
):
    pairs = (
        (cov_in_hbm, cov_in_ref),
        (cov_out_hbm, cov_out_ref),
        (len_hbm, len_ref),
        (act_hbm, act_ref),
        (grad_hbm, grad_ref),
    )
    copies = [pltpu.make_async_copy(source, target, sems.at[i]) for i, (source, target) in enumerate(pairs)]
    for copy in copies:
        copy.start()
    for copy in copies[:2]:
        copy.wait()
    size = cov_in_ref.shape[0]
    half = size // 2
    covs = [damped(cov_in_ref[...]), damped(cov_out_ref[...])]
    corner = [cov[:half, half:] for cov in covs]
    upper = side_by_side_inverses(*[cov[:half, :half] for cov in covs])
    solved = [product(u, c) for u, c in zip(upper, corner)]
    lower = side_by_side_inverses(
        *[cov[half:, half:] - product(c, t, ((0,), (0,))) for cov, c, t in zip(covs, corner, solved)]
    )
    for m, (u, t, low) in enumerate(zip(upper, solved, lower)):
        side = product(t, low)
        k_ref[m, :half, :half] = u + product(side, t, ((1,), (1,)))
        k_ref[m, :half, half:] = -side
        k_ref[m, half:, :half] = -side.T
        k_ref[m, half:, half:] = low
    for copy in copies[2:]:
        copy.wait()
    token = lax.broadcasted_iota(jnp.int32, (size, size), 0)
    lane = lax.broadcasted_iota(jnp.int32, (size, size), 1)
    mask = jnp.zeros((size, size), jnp.float32)
    for s in range(len_ref.shape[0]):
        mask = jnp.where((lane == s) & (token < len_ref[s]), 1.0, mask)
    k_ref[2] = mask


def inverses_and_inputs(lengths, cov_in, cov_out, activations, out_grads):
    size = cov_in.shape[0]
    return pl.pallas_call(
        inverse_kernel,
        out_shape=(
            jax.ShapeDtypeStruct((3, size, size), jnp.float32),
            jax.ShapeDtypeStruct(activations.shape, activations.dtype),
            jax.ShapeDtypeStruct(out_grads.shape, out_grads.dtype),
        ),
        in_specs=[HBM] * 5,
        out_specs=(VMEM, VMEM, VMEM),
        scratch_shapes=[
            pltpu.VMEM((size, size), jnp.float32),
            pltpu.VMEM((size, size), jnp.float32),
            pltpu.SMEM(lengths.shape, jnp.int32),
            pltpu.SemaphoreType.DMA((5,)),
        ],
        compiler_params=pltpu.CompilerParams(vmem_limit_bytes=24 << 20),
        cost_estimate=pl.CostEstimate(flops=4 * size**3, bytes_accessed=24 << 20, transcendentals=0),
        name="inverses",
    )(*(pltpu.with_memory_space_constraint(x, pltpu.HBM) for x in (lengths, cov_in, cov_out, activations, out_grads)))


def whiten_kernel(n, seqs, me_ref, act_ref, grad_ref, k_ref, *rest):
    blocks, (out_ref, p_in, p_out, white) = rest[:n], rest[n:]
    rank = k_ref.shape[1]
    length = act_ref.shape[0] // seqs
    rows = blocks[0].shape[0] // 2
    for block, src in zip(blocks, sources(me_ref[0], n)):
        at = pl.ds(pl.multiple_of(src * rows, rows), rows)
        p_in[at, :] = block[:rows, :]
        p_out[at, :] = block[rows:, :]
    x_full = jnp.dot(act_ref[...], p_in[...], preferred_element_type=jnp.float32)
    d_proj = jnp.dot(grad_ref[...], p_out[...], preferred_element_type=jnp.float32).astype(jnp.bfloat16)
    share = rank // n
    for s in range(seqs):
        part = slice(s * length, (s + 1) * length)
        x_proj = (x_full[part] * k_ref[2][:length, s : s + 1]).astype(jnp.bfloat16)
        grads = lax.dot_general(
            d_proj[part], x_proj, (((0,), (0,)), ((), ())), preferred_element_type=jnp.float32
        )
        full = product(product(k_ref[1], grads), k_ref[0])
        for d in range(n):
            white[d, s * share : (s + 1) * share, :] = full[d * share : (d + 1) * share, :]
    out_ref[...] = white[...].astype(jnp.bfloat16)


def whitened_blocks(me, seqs, activations, out_grads, k, blocks):
    n = len(blocks)
    tokens, width = activations.shape
    rank = k.shape[1]
    shape = (n, seqs * (rank // n), rank)
    return pl.pallas_call(
        functools.partial(whiten_kernel, n, seqs),
        out_shape=jax.ShapeDtypeStruct(shape, jnp.bfloat16),
        in_specs=[SMEM] + [VMEM] * (3 + n),
        out_specs=VMEM,
        scratch_shapes=[
            pltpu.VMEM((width, rank), jnp.bfloat16),
            pltpu.VMEM((width, rank), jnp.bfloat16),
            pltpu.VMEM(shape, jnp.float32),
        ],
        compiler_params=pltpu.CompilerParams(vmem_limit_bytes=32 << 20),
        cost_estimate=pl.CostEstimate(flops=4 * tokens * width * rank, bytes_accessed=6 << 20, transcendentals=0),
        name="whiten",
    )(me, activations, out_grads, k, *blocks)


def score_kernel(n, me_ref, ids_ref, white_ref, bank_ref, out_ref, spread):
    seqs = ids_ref.shape[0]
    chunk, rank = white_ref.shape[1:]
    share = chunk // seqs
    total = n * seqs
    spread[...] = white_ref[...].astype(jnp.float32).reshape(n * chunk, rank)
    columns = jnp.concatenate(
        [spread[pl.ds(j, total, stride=share), :].astype(jnp.bfloat16) for j in range(share)], axis=1
    )
    queries = bank_ref.shape[0] // n
    row = lax.broadcasted_iota(jnp.int32, (total, out_ref.shape[2] - queries), 0)
    tail = jnp.zeros(row.shape, jnp.float32)
    for s in range(seqs):
        tail = jnp.where(row == me_ref[0] * seqs + s, ids_ref[s].astype(jnp.float32), tail)
    partial = lax.dot_general(
        columns, bank_ref[...], (((1,), (1,)), ((), ())), preferred_element_type=jnp.float32
    )
    for d in range(n):
        out_ref[d, :, :queries] = partial[:, d * queries : (d + 1) * queries].astype(out_ref.dtype)
        out_ref[d, :, queries:] = tail.astype(out_ref.dtype)


def partial_scores(me, seq_ids, white, bank):
    n = white.shape[0]
    seqs = seq_ids.shape[0]
    queries = bank.shape[0] // n
    width = (queries // LANES + 1) * LANES
    return pl.pallas_call(
        functools.partial(score_kernel, n),
        out_shape=jax.ShapeDtypeStruct((n, n * seqs, width), jnp.bfloat16),
        in_specs=[SMEM, SMEM, VMEM, VMEM],
        out_specs=VMEM,
        scratch_shapes=[pltpu.VMEM((n * white.shape[1], white.shape[2]), jnp.float32)],
        compiler_params=pltpu.CompilerParams(vmem_limit_bytes=48 << 20),
        cost_estimate=pl.CostEstimate(
            flops=2 * n * seqs * bank.size, bytes_accessed=2 * bank.size, transcendentals=0
        ),
        name="score",
    )(me, seq_ids, white, bank)


def place_kernel(partial_ref, out_ref):
    rows, queries = out_ref.shape
    total = jnp.sum(partial_ref[...].astype(jnp.float32), axis=0)
    raw = total[:, :queries].astype(jnp.bfloat16)
    ids = total[:, queries : queries + 1].astype(jnp.int32)
    chosen = ids == lax.broadcasted_iota(jnp.int32, (rows, rows), 1)
    out_ref[...] = lax.dot_general(
        chosen.astype(jnp.bfloat16), raw, (((0,), (0,)), ((), ())), preferred_element_type=jnp.float32
    ).astype(jnp.bfloat16)


def place(partials, queries):
    return pl.pallas_call(
        lambda a, b: place_kernel(a, b),
        out_shape=jax.ShapeDtypeStruct((partials.shape[1], queries), jnp.bfloat16),
        in_specs=[VMEM],
        out_specs=VMEM,
        compiler_params=pltpu.CompilerParams(vmem_limit_bytes=48 << 20),
        name="place",
    )(partials)


def body(n, activations, out_grads, proj_in, proj_out, cov_in, cov_out, lengths, seq_ids, bank):
    me = lax.axis_index("coord").reshape(1)
    seqs, length, width = activations.shape
    k, activations, out_grads = inverses_and_inputs(
        lengths,
        cov_in,
        cov_out,
        activations.reshape(seqs * length, width),
        out_grads.reshape(seqs * length, width),
    )
    blocks = gather_blocks(jnp.concatenate([proj_in, proj_out], axis=0), n, k)
    white = whitened_blocks(me, seqs, activations, out_grads, k, blocks)
    white = lax.all_to_all(white, "coord", split_axis=0, concat_axis=0, tiled=True)
    partials = partial_scores(me, seq_ids, white, bank)
    partials = lax.all_to_all(partials, "coord", split_axis=0, concat_axis=0, tiled=True)
    return place(partials, bank.shape[0] // n)


def solution(mesh):
    in_specs = (
        P(("groups", "coord"), None, None),
        P(("groups", "coord"), None, None),
        P("coord", None),
        P("coord", None),
        P(),
        P(),
        P(("groups", "coord")),
        P(("groups", "coord")),
        P(None, "coord"),
    )
    out_specs = P("groups", "coord")
    return jax.shard_map(
        functools.partial(body, mesh.shape["coord"]),
        mesh=mesh,
        in_specs=in_specs,
        out_specs=out_specs,
        check_vma=False,
    )
```

```python
import functools

import jax
import jax.numpy as jnp
from jax import lax
from jax.experimental import pallas as pl
from jax.experimental.pallas import tpu as pltpu
from jax.sharding import PartitionSpec as P

SUB = 8
LANES = 128
EXACT = lax.Precision.HIGHEST
VMEM = pl.BlockSpec(memory_space=pltpu.VMEM)
HBM = pl.BlockSpec(memory_space=pltpu.HBM)
SMEM = pl.BlockSpec(memory_space=pltpu.SMEM)


def factors(n):
    c = 2 if n % 2 == 0 else 1
    rest = n // c
    b = max(f for f in range(1, rest + 1) if rest % f == 0 and f * f <= rest)
    return rest // b, b, c


def partner(at, by, size, towards):
    if size & (size - 1) == 0:
        return at ^ by
    return (at + (by if towards else size - by)) % size


def sources(me, n):
    a, b, c = factors(n)
    ia, ib, ic = me // (b * c), (me // c) % b, me % c
    return [
        (partner(ia, da, a, False) * b + partner(ib, db, b, False)) * c + partner(ic, dc, c, False)
        for dc in range(c)
        for db in range(b)
        for da in range(a)
    ]


def moved(value, axis, by, n):
    sizes = factors(n)
    a, b, c = sizes
    pairs = []
    for me in range(n):
        at = [me // (b * c), (me // c) % b, me % c]
        at[axis] = partner(at[axis], by, sizes[axis], True)
        pairs.append((me, (at[0] * b + at[1]) * c + at[2]))
    return lax.ppermute(value, "coord", pairs)


def pack_kernel(first_hbm, second_hbm, out_ref, sems):
    rows = first_hbm.shape[0]
    copies = [
        pltpu.make_async_copy(source, out_ref.at[pl.ds(i * rows, rows)], sems.at[i])
        for i, source in enumerate((first_hbm, second_hbm))
    ]
    for copy in copies:
        copy.start()
    for copy in copies:
        copy.wait()


def pack(first, second):
    rows, columns = first.shape
    return pl.pallas_call(
        pack_kernel,
        out_shape=jax.ShapeDtypeStruct((2 * rows, columns), first.dtype),
        in_specs=[HBM, HBM],
        out_specs=VMEM,
        scratch_shapes=[pltpu.SemaphoreType.DMA((2,))],
        compiler_params=pltpu.CompilerParams(vmem_limit_bytes=8 << 20),
        name="pack",
    )(pinned(first), pinned(second))


def pinned(value):
    return pltpu.with_memory_space_constraint(value, pltpu.HBM)


def gauss_jordan(blocks):
    width = blocks[0].shape[1]
    half = width // 2
    lane = lax.broadcasted_iota(jnp.int32, (SUB, width), 1)
    sub = lax.broadcasted_iota(jnp.int32, (SUB, width), 0)
    start, within = lane // half * half, lane % half

    def column(block, at):
        return jnp.take_along_axis(block, start + at, axis=1, mode="promise_in_bounds")

    for k in range(len(blocks)):
        at = k * SUB
        head = within // SUB == k
        rows = [jnp.broadcast_to(blocks[k][i : i + 1, :], (SUB, width)) for i in range(SUB)]
        diag = {(i, j): column(rows[i], at + j) for i in range(SUB) for j in range(i, SUB)}
        rows = [jnp.where(head, (within == at + i).astype(jnp.float32), rows[i]) for i in range(SUB)]
        inverse, factor = [], {}
        for p in range(SUB):
            inverse.append(1.0 / diag[p, p])
            for i in range(p + 1, SUB):
                factor[p, i] = diag[p, i] * inverse[p]
                for j in range(i, SUB):
                    diag[i, j] = diag[i, j] - factor[p, i] * diag[p, j]
                rows[i] = rows[i] - factor[p, i] * rows[p]
        rows = [rows[p] * inverse[p] for p in range(SUB)]
        for p in reversed(range(SUB)):
            for i in range(p):
                rows[i] = rows[i] - factor[i, p] * rows[p]
        done = rows[0]
        for i in range(1, SUB):
            done = jnp.where(sub == i, rows[i], done)
        out = []
        for g, block in enumerate(blocks):
            if g == k:
                out.append(done)
                continue
            terms = [column(block, at + p) * rows[p] for p in range(SUB)]
            while len(terms) > 1:
                terms = [terms[i] + terms[i + 1] for i in range(0, len(terms), 2)]
            out.append(jnp.where(head, 0.0, block) - terms[0])
        blocks = out
    return blocks


def side_by_side_inverses(first, second):
    half = first.shape[0]
    both = jnp.concatenate([first, second], axis=1)
    blocks = gauss_jordan([both[g : g + SUB, :] for g in range(0, half, SUB)])
    both = jnp.concatenate(blocks, axis=0)
    return both[:, :half], both[:, half:]


def damped(cov):
    size = cov.shape[0]
    cov = 0.5 * (cov + cov.T)
    row = lax.broadcasted_iota(jnp.int32, (size, size), 0)
    col = lax.broadcasted_iota(jnp.int32, (size, size), 1)
    damping = 0.1 * jnp.sum(jnp.where(row == col, cov, 0.0)) / size
    return jnp.where(row == col, cov + damping, cov)


def product(left, right, dims=((1,), (0,))):
    return lax.dot_general(left, right, (dims, ((), ())), precision=EXACT, preferred_element_type=jnp.float32)


def first_half_kernel(cov_in_hbm, cov_out_hbm, out_ref, cov_ref, sems):
    copies = [
        pltpu.make_async_copy(source, cov_ref.at[i], sems.at[i]) for i, source in enumerate((cov_in_hbm, cov_out_hbm))
    ]
    for copy in copies:
        copy.start()
    for copy in copies:
        copy.wait()
    half = cov_ref.shape[1] // 2
    covs = [damped(cov_ref[0]), damped(cov_ref[1])]
    corner = [cov[:half, half:] for cov in covs]
    upper = side_by_side_inverses(*[cov[:half, :half] for cov in covs])
    solved = [product(u, c) for u, c in zip(upper, corner)]
    schur = [cov[half:, half:] - product(c, t, ((0,), (0,))) for cov, c, t in zip(covs, corner, solved)]
    for i, pair in enumerate((upper, solved, schur)):
        out_ref[i] = jnp.concatenate(pair, axis=1)


def second_half_kernel(first_ref, len_hbm, act_hbm, grad_hbm, k_ref, act_ref, grad_ref, len_ref, sems):
    pairs = ((len_hbm, len_ref), (act_hbm, act_ref), (grad_hbm, grad_ref))
    copies = [pltpu.make_async_copy(source, target, sems.at[i]) for i, (source, target) in enumerate(pairs)]
    for copy in copies:
        copy.start()
    size = k_ref.shape[1]
    half = size // 2
    upper, solved, schur = [(first_ref[i][:, :half], first_ref[i][:, half:]) for i in range(3)]
    lower = side_by_side_inverses(*schur)
    for m, (u, t, low) in enumerate(zip(upper, solved, lower)):
        side = product(t, low)
        k_ref[m, :half, :half] = u + product(side, t, ((1,), (1,)))
        k_ref[m, :half, half:] = -side
        k_ref[m, half:, :half] = -side.T
        k_ref[m, half:, half:] = low
    copies[0].wait()
    token = lax.broadcasted_iota(jnp.int32, (size, size), 0)
    lane = lax.broadcasted_iota(jnp.int32, (size, size), 1)
    mask = jnp.zeros((size, size), jnp.float32)
    for s in range(len_ref.shape[0]):
        mask = jnp.where((lane == s) & (token < len_ref[s]), 1.0, mask)
    k_ref[2] = mask
    for copy in copies[1:]:
        copy.wait()


def first_half(cov_in, cov_out):
    size = cov_in.shape[0]
    return pl.pallas_call(
        first_half_kernel,
        out_shape=jax.ShapeDtypeStruct((3, size // 2, size), jnp.float32),
        in_specs=[HBM, HBM],
        out_specs=VMEM,
        scratch_shapes=[pltpu.VMEM((2, size, size), jnp.float32), pltpu.SemaphoreType.DMA((2,))],
        compiler_params=pltpu.CompilerParams(vmem_limit_bytes=8 << 20),
        cost_estimate=pl.CostEstimate(flops=2 * size**3, bytes_accessed=12 << 20, transcendentals=0),
        name="first_half",
    )(pinned(cov_in), pinned(cov_out))


def second_half(first, lengths, activations, out_grads):
    size = first.shape[2]
    return pl.pallas_call(
        second_half_kernel,
        out_shape=(
            jax.ShapeDtypeStruct((3, size, size), jnp.float32),
            jax.ShapeDtypeStruct(activations.shape, activations.dtype),
            jax.ShapeDtypeStruct(out_grads.shape, out_grads.dtype),
        ),
        in_specs=[VMEM, HBM, HBM, HBM],
        out_specs=(VMEM, VMEM, VMEM),
        scratch_shapes=[pltpu.SMEM(lengths.shape, jnp.int32), pltpu.SemaphoreType.DMA((3,))],
        compiler_params=pltpu.CompilerParams(vmem_limit_bytes=8 << 20),
        cost_estimate=pl.CostEstimate(flops=2 * size**3, bytes_accessed=12 << 20, transcendentals=0),
        name="second_half",
    )(first, pinned(lengths), pinned(activations), pinned(out_grads))


def whiten_kernel(n, seqs, me_ref, act_ref, grad_ref, k_ref, *rest):
    blocks, (out_ref, p_in, p_out, white) = rest[:n], rest[n:]
    rank = k_ref.shape[1]
    length = act_ref.shape[0] // seqs
    rows = blocks[0].shape[0] // 2
    for block, src in zip(blocks, sources(me_ref[0], n)):
        at = pl.ds(pl.multiple_of(src * rows, rows), rows)
        p_in[at, :] = block[:rows, :]
        p_out[at, :] = block[rows:, :]
    x_full = jnp.dot(act_ref[...], p_in[...], preferred_element_type=jnp.float32)
    d_proj = jnp.dot(grad_ref[...], p_out[...], preferred_element_type=jnp.float32).astype(jnp.bfloat16)
    share = rank // n
    for s in range(seqs):
        part = slice(s * length, (s + 1) * length)
        x_proj = (x_full[part] * k_ref[2][:length, s : s + 1]).astype(jnp.bfloat16)
        grads = lax.dot_general(
            d_proj[part], x_proj, (((0,), (0,)), ((), ())), preferred_element_type=jnp.float32
        )
        full = product(product(k_ref[1], grads), k_ref[0])
        for d in range(n):
            white[d, s * share : (s + 1) * share, :] = full[d * share : (d + 1) * share, :]
    out_ref[...] = white[...].astype(jnp.bfloat16)


def whitened_blocks(me, seqs, activations, out_grads, k, blocks):
    n = len(blocks)
    tokens, width = activations.shape
    rank = k.shape[1]
    shape = (n, seqs * (rank // n), rank)
    return pl.pallas_call(
        functools.partial(whiten_kernel, n, seqs),
        out_shape=jax.ShapeDtypeStruct(shape, jnp.bfloat16),
        in_specs=[SMEM] + [VMEM] * (3 + n),
        out_specs=VMEM,
        scratch_shapes=[
            pltpu.VMEM((width, rank), jnp.bfloat16),
            pltpu.VMEM((width, rank), jnp.bfloat16),
            pltpu.VMEM(shape, jnp.float32),
        ],
        compiler_params=pltpu.CompilerParams(vmem_limit_bytes=16 << 20),
        cost_estimate=pl.CostEstimate(flops=4 * tokens * width * rank, bytes_accessed=6 << 20, transcendentals=0),
        name="whiten",
    )(me, activations, out_grads, k, *blocks)


def score_kernel(n, me_ref, ids_ref, white_ref, bank_ref, out_ref, spread):
    seqs = ids_ref.shape[0]
    chunk, rank = white_ref.shape[1:]
    share = chunk // seqs
    total = n * seqs
    spread[...] = white_ref[...].astype(jnp.float32).reshape(n * chunk, rank)
    columns = jnp.concatenate(
        [spread[pl.ds(j, total, stride=share), :].astype(jnp.bfloat16) for j in range(share)], axis=1
    )
    queries = bank_ref.shape[0] // n
    row = lax.broadcasted_iota(jnp.int32, (total, out_ref.shape[2] - queries), 0)
    tail = jnp.zeros(row.shape, jnp.float32)
    for s in range(seqs):
        tail = jnp.where(row == me_ref[0] * seqs + s, ids_ref[s].astype(jnp.float32), tail)
    partial = lax.dot_general(
        columns, bank_ref[...], (((1,), (1,)), ((), ())), preferred_element_type=jnp.float32
    )
    for d in range(n):
        out_ref[d, :, :queries] = partial[:, d * queries : (d + 1) * queries].astype(out_ref.dtype)
        out_ref[d, :, queries:] = tail.astype(out_ref.dtype)


def partial_scores(me, seq_ids, white, bank):
    n = white.shape[0]
    seqs = seq_ids.shape[0]
    queries = bank.shape[0] // n
    width = (queries // LANES + 1) * LANES
    return pl.pallas_call(
        functools.partial(score_kernel, n),
        out_shape=jax.ShapeDtypeStruct((n, n * seqs, width), jnp.bfloat16),
        in_specs=[SMEM, SMEM, VMEM, VMEM],
        out_specs=VMEM,
        scratch_shapes=[pltpu.VMEM((n * white.shape[1], white.shape[2]), jnp.float32)],
        compiler_params=pltpu.CompilerParams(vmem_limit_bytes=16 << 20),
        cost_estimate=pl.CostEstimate(
            flops=2 * n * seqs * bank.size, bytes_accessed=2 * bank.size, transcendentals=0
        ),
        name="score",
    )(me, seq_ids, white, bank)


def place_kernel(partial_ref, out_ref):
    rows, queries = out_ref.shape
    total = jnp.sum(partial_ref[...].astype(jnp.float32), axis=0)
    raw = total[:, :queries].astype(jnp.bfloat16)
    ids = total[:, queries : queries + 1].astype(jnp.int32)
    chosen = ids == lax.broadcasted_iota(jnp.int32, (rows, rows), 1)
    out_ref[...] = lax.dot_general(
        chosen.astype(jnp.bfloat16), raw, (((0,), (0,)), ((), ())), preferred_element_type=jnp.float32
    ).astype(jnp.bfloat16)


def place(partials, queries):
    return pl.pallas_call(
        lambda a, b: place_kernel(a, b),
        out_shape=jax.ShapeDtypeStruct((partials.shape[1], queries), jnp.bfloat16),
        in_specs=[VMEM],
        out_specs=VMEM,
        compiler_params=pltpu.CompilerParams(vmem_limit_bytes=16 << 20),
        name="place",
    )(partials)


def body(n, activations, out_grads, proj_in, proj_out, cov_in, cov_out, lengths, seq_ids, bank):
    me = lax.axis_index("coord").reshape(1)
    seqs, length, width = activations.shape
    activations, out_grads = activations.reshape(seqs * length, width), out_grads.reshape(seqs * length, width)
    a, b, c = factors(n)
    packed = pack(proj_in, proj_out)
    blocks = [packed] + [moved(packed, 0, by, n) for by in range(1, a)]
    half = first_half(cov_in, cov_out)
    after = min(1, a - 1)
    blocks[after], half = lax.optimization_barrier((blocks[after], half))
    blocks += [moved(block, 1, by, n) for by in range(1, b) for block in blocks[:a]]
    after = min(a + 1, len(blocks) - 1)
    blocks[after], half = lax.optimization_barrier((blocks[after], half))
    k, activations, out_grads = second_half(half, lengths, activations, out_grads)
    blocks[-1], k = lax.optimization_barrier((blocks[-1], k))
    blocks += [moved(block, 2, by, n) for by in range(1, c) for block in blocks[: a * b]]
    white = whitened_blocks(me, seqs, activations, out_grads, k, blocks)
    white = lax.all_to_all(white, "coord", split_axis=0, concat_axis=0, tiled=True)
    partials = partial_scores(me, seq_ids, white, bank)
    partials = lax.all_to_all(partials, "coord", split_axis=0, concat_axis=0, tiled=True)
    return place(partials, bank.shape[0] // n)


def solution(mesh):
    in_specs = (
        P(("groups", "coord"), None, None),
        P(("groups", "coord"), None, None),
        P("coord", None),
        P("coord", None),
        P(),
        P(),
        P(("groups", "coord")),
        P(("groups", "coord")),
        P(None, "coord"),
    )
    out_specs = P("groups", "coord")
    return jax.shard_map(
        functools.partial(body, mesh.shape["coord"]),
        mesh=mesh,
        in_specs=in_specs,
        out_specs=out_specs,
        check_vma=False,
    )
```

```python
import functools

import jax
import jax.numpy as jnp
from jax import lax
from jax.experimental import pallas as pl
from jax.experimental.pallas import tpu as pltpu
from jax.sharding import PartitionSpec as P

SUB = 8
LANES = 128
EXACT = lax.Precision.HIGHEST
VMEM = pl.BlockSpec(memory_space=pltpu.VMEM)
HBM = pl.BlockSpec(memory_space=pltpu.HBM)
SMEM = pl.BlockSpec(memory_space=pltpu.SMEM)


def factors(n):
    c = 2 if n % 2 == 0 else 1
    rest = n // c
    b = max(f for f in range(1, rest + 1) if rest % f == 0 and f * f <= rest)
    return rest // b, b, c


def partner(at, by, size, towards):
    if size & (size - 1) == 0:
        return at ^ by
    return (at + (by if towards else size - by)) % size


def sources(me, n):
    a, b, c = factors(n)
    ia, ib, ic = me // (b * c), (me // c) % b, me % c
    return [
        (partner(ia, da, a, False) * b + partner(ib, db, b, False)) * c + partner(ic, dc, c, False)
        for dc in range(c)
        for db in range(b)
        for da in range(a)
    ]


def moved(value, axis, by, n):
    sizes = factors(n)
    a, b, c = sizes
    pairs = []
    for me in range(n):
        at = [me // (b * c), (me // c) % b, me % c]
        at[axis] = partner(at[axis], by, sizes[axis], True)
        pairs.append((me, (at[0] * b + at[1]) * c + at[2]))
    return lax.ppermute(value, "coord", pairs)


def pack_kernel(first_hbm, second_hbm, out_ref, sems):
    rows = first_hbm.shape[0]
    copies = [
        pltpu.make_async_copy(source, out_ref.at[pl.ds(i * rows, rows)], sems.at[i])
        for i, source in enumerate((first_hbm, second_hbm))
    ]
    for copy in copies:
        copy.start()
    for copy in copies:
        copy.wait()


def pack(first, second):
    rows, columns = first.shape
    return pl.pallas_call(
        pack_kernel,
        out_shape=jax.ShapeDtypeStruct((2 * rows, columns), first.dtype),
        in_specs=[HBM, HBM],
        out_specs=VMEM,
        scratch_shapes=[pltpu.SemaphoreType.DMA((2,))],
        compiler_params=pltpu.CompilerParams(vmem_limit_bytes=8 << 20),
        name="pack",
    )(pinned(first), pinned(second))


def pinned(value):
    return pltpu.with_memory_space_constraint(value, pltpu.HBM)


def gauss_jordan(blocks):
    width = blocks[0].shape[1]
    half = width // 2
    lane = lax.broadcasted_iota(jnp.int32, (SUB, width), 1)
    sub = lax.broadcasted_iota(jnp.int32, (SUB, width), 0)
    start, within = lane // half * half, lane % half

    def column(block, at):
        return jnp.take_along_axis(block, start + at, axis=1, mode="promise_in_bounds")

    for k in range(len(blocks)):
        at = k * SUB
        head = within // SUB == k
        rows = [jnp.broadcast_to(blocks[k][i : i + 1, :], (SUB, width)) for i in range(SUB)]
        diag = {(i, j): column(rows[i], at + j) for i in range(SUB) for j in range(i, SUB)}
        rows = [jnp.where(head, (within == at + i).astype(jnp.float32), rows[i]) for i in range(SUB)]
        inverse, factor = [], {}
        for p in range(SUB):
            inverse.append(1.0 / diag[p, p])
            for i in range(p + 1, SUB):
                factor[p, i] = diag[p, i] * inverse[p]
                for j in range(i, SUB):
                    diag[i, j] = diag[i, j] - factor[p, i] * diag[p, j]
                rows[i] = rows[i] - factor[p, i] * rows[p]
        rows = [rows[p] * inverse[p] for p in range(SUB)]
        for p in reversed(range(SUB)):
            for i in range(p):
                rows[i] = rows[i] - factor[i, p] * rows[p]
        done = rows[0]
        for i in range(1, SUB):
            done = jnp.where(sub == i, rows[i], done)
        out = []
        for g, block in enumerate(blocks):
            if g == k:
                out.append(done)
                continue
            terms = [column(block, at + p) * rows[p] for p in range(SUB)]
            while len(terms) > 1:
                terms = [terms[i] + terms[i + 1] for i in range(0, len(terms), 2)]
            out.append(jnp.where(head, 0.0, block) - terms[0])
        blocks = out
    return blocks


def side_by_side_inverses(first, second):
    half = first.shape[0]
    both = jnp.concatenate([first, second], axis=1)
    blocks = gauss_jordan([both[g : g + SUB, :] for g in range(0, half, SUB)])
    both = jnp.concatenate(blocks, axis=0)
    return both[:, :half], both[:, half:]


def damped(cov):
    size = cov.shape[0]
    cov = 0.5 * (cov + cov.T)
    row = lax.broadcasted_iota(jnp.int32, (size, size), 0)
    col = lax.broadcasted_iota(jnp.int32, (size, size), 1)
    damping = 0.1 * jnp.sum(jnp.where(row == col, cov, 0.0)) / size
    return jnp.where(row == col, cov + damping, cov)


def product(left, right, dims=((1,), (0,))):
    return lax.dot_general(left, right, (dims, ((), ())), precision=EXACT, preferred_element_type=jnp.float32)


def first_half_kernel(cov_in_hbm, cov_out_hbm, out_ref, cov_ref, sems):
    copies = [
        pltpu.make_async_copy(source, cov_ref.at[i], sems.at[i]) for i, source in enumerate((cov_in_hbm, cov_out_hbm))
    ]
    for copy in copies:
        copy.start()
    for copy in copies:
        copy.wait()
    half = cov_ref.shape[1] // 2
    covs = [damped(cov_ref[0]), damped(cov_ref[1])]
    corner = [cov[:half, half:] for cov in covs]
    upper = side_by_side_inverses(*[cov[:half, :half] for cov in covs])
    solved = [product(u, c) for u, c in zip(upper, corner)]
    schur = [cov[half:, half:] - product(c, t, ((0,), (0,))) for cov, c, t in zip(covs, corner, solved)]
    for i, pair in enumerate((upper, solved, schur)):
        out_ref[i] = jnp.concatenate(pair, axis=1)


def second_half_kernel(first_ref, len_hbm, k_ref, len_ref, sem):
    copy = pltpu.make_async_copy(len_hbm, len_ref, sem)
    copy.start()
    size = k_ref.shape[1]
    half = size // 2
    upper, solved, schur = [(first_ref[i][:, :half], first_ref[i][:, half:]) for i in range(3)]
    lower = side_by_side_inverses(*schur)
    for m, (u, t, low) in enumerate(zip(upper, solved, lower)):
        side = product(t, low)
        k_ref[m, :half, :half] = u + product(side, t, ((1,), (1,)))
        k_ref[m, :half, half:] = -side
        k_ref[m, half:, :half] = -side.T
        k_ref[m, half:, half:] = low
    copy.wait()
    token = lax.broadcasted_iota(jnp.int32, (size, size), 0)
    lane = lax.broadcasted_iota(jnp.int32, (size, size), 1)
    mask = jnp.zeros((size, size), jnp.float32)
    for s in range(len_ref.shape[0]):
        mask = jnp.where((lane == s) & (token < len_ref[s]), 1.0, mask)
    k_ref[2] = mask


def first_half(cov_in, cov_out):
    size = cov_in.shape[0]
    return pl.pallas_call(
        first_half_kernel,
        out_shape=jax.ShapeDtypeStruct((3, size // 2, size), jnp.float32),
        in_specs=[HBM, HBM],
        out_specs=VMEM,
        scratch_shapes=[pltpu.VMEM((2, size, size), jnp.float32), pltpu.SemaphoreType.DMA((2,))],
        compiler_params=pltpu.CompilerParams(vmem_limit_bytes=8 << 20),
        cost_estimate=pl.CostEstimate(flops=size, bytes_accessed=size, transcendentals=0),
        name="first_half",
    )(pinned(cov_in), pinned(cov_out))


def second_half(first, lengths):
    size = first.shape[2]
    return pl.pallas_call(
        second_half_kernel,
        out_shape=jax.ShapeDtypeStruct((3, size, size), jnp.float32),
        in_specs=[VMEM, HBM],
        out_specs=VMEM,
        scratch_shapes=[pltpu.SMEM(lengths.shape, jnp.int32), pltpu.SemaphoreType.DMA],
        compiler_params=pltpu.CompilerParams(vmem_limit_bytes=8 << 20),
        cost_estimate=pl.CostEstimate(flops=size, bytes_accessed=size, transcendentals=0),
        name="second_half",
    )(first, pinned(lengths))


def whiten_kernel(n, seqs, me_ref, act_hbm, grad_hbm, k_ref, *rest):
    blocks, (out_ref, held, proj, total, white, sems) = rest[:n], rest[n:]
    rank = k_ref.shape[1]
    tokens, width = act_hbm.shape
    length = tokens // seqs
    chunks = held.shape[0] // 2
    part = width // chunks
    copies = [
        pltpu.make_async_copy(source.at[:, pl.ds(i * part, part)], held.at[t * chunks + i], sems.at[t * chunks + i])
        for t, source in enumerate((act_hbm, grad_hbm))
        for i in range(chunks)
    ]
    for copy in copies:
        copy.start()
    rows = blocks[0].shape[0] // 2
    for block, src in zip(blocks, sources(me_ref[0], n)):
        at = pl.ds(pl.multiple_of(src * rows, rows), rows)
        proj[0, at, :] = block[:rows, :]
        proj[1, at, :] = block[rows:, :]
    for i, copy in enumerate(copies):
        copy.wait()
        t, at = i // chunks, i % chunks * part
        term = jnp.dot(held[i], proj[t, at : at + part, :], preferred_element_type=jnp.float32)
        total[t] = term if at == 0 else total[t] + term
    share = rank // n
    for s in range(seqs):
        token = slice(s * length, (s + 1) * length)
        x_proj = (total[0, token, :] * k_ref[2][:length, s : s + 1]).astype(jnp.bfloat16)
        d_proj = total[1, token, :].astype(jnp.bfloat16)
        grads = lax.dot_general(d_proj, x_proj, (((0,), (0,)), ((), ())), preferred_element_type=jnp.float32)
        full = product(product(k_ref[1], grads), k_ref[0])
        for d in range(n):
            white[d, s * share : (s + 1) * share, :] = full[d * share : (d + 1) * share, :]
    out_ref[...] = white[...].astype(jnp.bfloat16)


def whitened_blocks(me, activations, out_grads, k, blocks):
    n = len(blocks)
    seqs, length, width = activations.shape
    tokens = seqs * length
    rank = k.shape[1]
    chunks = 4 if width % (4 * LANES) == 0 else 1
    shape = (n, seqs * (rank // n), rank)
    return pl.pallas_call(
        functools.partial(whiten_kernel, n, seqs),
        out_shape=jax.ShapeDtypeStruct(shape, jnp.bfloat16),
        in_specs=[SMEM, HBM, HBM] + [VMEM] * (1 + n),
        out_specs=VMEM,
        scratch_shapes=[
            pltpu.VMEM((2 * chunks, tokens, width // chunks), activations.dtype),
            pltpu.VMEM((2, width, rank), jnp.bfloat16),
            pltpu.VMEM((2, tokens, rank), jnp.float32),
            pltpu.VMEM(shape, jnp.float32),
            pltpu.SemaphoreType.DMA((2 * chunks,)),
        ],
        compiler_params=pltpu.CompilerParams(vmem_limit_bytes=24 << 20),
        cost_estimate=pl.CostEstimate(flops=4 * tokens * width * rank, bytes_accessed=6 << 20, transcendentals=0),
        name="whiten",
    )(
        me,
        pinned(activations.reshape(tokens, width)),
        pinned(out_grads.reshape(tokens, width)),
        k,
        *blocks,
    )


def score_kernel(n, me_ref, ids_ref, white_ref, bank_ref, out_ref, spread):
    seqs = ids_ref.shape[0]
    chunk, rank = white_ref.shape[1:]
    share = chunk // seqs
    total = n * seqs
    spread[...] = white_ref[...].astype(jnp.float32).reshape(n * chunk, rank)
    columns = jnp.concatenate(
        [spread[pl.ds(j, total, stride=share), :].astype(jnp.bfloat16) for j in range(share)], axis=1
    )
    queries = bank_ref.shape[0] // n
    row = lax.broadcasted_iota(jnp.int32, (total, out_ref.shape[2] - queries), 0)
    tail = jnp.zeros(row.shape, jnp.float32)
    for s in range(seqs):
        tail = jnp.where(row == me_ref[0] * seqs + s, ids_ref[s].astype(jnp.float32), tail)
    partial = lax.dot_general(
        columns, bank_ref[...], (((1,), (1,)), ((), ())), preferred_element_type=jnp.float32
    )
    for d in range(n):
        out_ref[d, :, :queries] = partial[:, d * queries : (d + 1) * queries].astype(out_ref.dtype)
        out_ref[d, :, queries:] = tail.astype(out_ref.dtype)


def partial_scores(me, seq_ids, white, bank):
    n = white.shape[0]
    seqs = seq_ids.shape[0]
    queries = bank.shape[0] // n
    width = (queries // LANES + 1) * LANES
    return pl.pallas_call(
        functools.partial(score_kernel, n),
        out_shape=jax.ShapeDtypeStruct((n, n * seqs, width), jnp.bfloat16),
        in_specs=[SMEM, SMEM, VMEM, VMEM],
        out_specs=VMEM,
        scratch_shapes=[pltpu.VMEM((n * white.shape[1], white.shape[2]), jnp.float32)],
        compiler_params=pltpu.CompilerParams(vmem_limit_bytes=16 << 20),
        cost_estimate=pl.CostEstimate(
            flops=2 * n * seqs * bank.size, bytes_accessed=2 * bank.size, transcendentals=0
        ),
        name="score",
    )(me, seq_ids, white, bank)


def place_kernel(partial_ref, out_ref):
    rows, queries = out_ref.shape
    total = jnp.sum(partial_ref[...].astype(jnp.float32), axis=0)
    raw = total[:, :queries].astype(jnp.bfloat16)
    ids = total[:, queries : queries + 1].astype(jnp.int32)
    chosen = ids == lax.broadcasted_iota(jnp.int32, (rows, rows), 1)
    out_ref[...] = lax.dot_general(
        chosen.astype(jnp.bfloat16), raw, (((0,), (0,)), ((), ())), preferred_element_type=jnp.float32
    ).astype(jnp.bfloat16)


def place(partials, queries):
    return pl.pallas_call(
        lambda a, b: place_kernel(a, b),
        out_shape=jax.ShapeDtypeStruct((partials.shape[1], queries), jnp.bfloat16),
        in_specs=[VMEM],
        out_specs=VMEM,
        compiler_params=pltpu.CompilerParams(vmem_limit_bytes=16 << 20),
        name="place",
    )(partials)


def body(n, activations, out_grads, proj_in, proj_out, cov_in, cov_out, lengths, seq_ids, bank):
    me = lax.axis_index("coord").reshape(1)
    a, b, c = factors(n)
    packed = pack(proj_in, proj_out)
    half = first_half(cov_in, cov_out)
    held = {(0, 0): packed}
    for by in range(1, min(a, 3)):
        held[by, 0] = moved(packed, 0, by, n)
    for by in range(1, b):
        held[0, by] = moved(packed, 1, by, n)
    held, half = lax.optimization_barrier((held, half))
    for by in range(3, a):
        nearest = by & -by
        if a & (a - 1) == 0 and nearest != by:
            held[by, 0] = moved(held[by - nearest, 0], 0, nearest, n)
        else:
            held[by, 0] = moved(held[0, 0], 0, by, n)
    for at in range(1, a):
        for by in range(1, b):
            held[at, by] = moved(held[at, 0], 1, by, n)
    if (1, 1) in held:
        held[1, 1], half = lax.optimization_barrier((held[1, 1], half))
    k = second_half(half, lengths)
    held[a - 1, b - 1], k = lax.optimization_barrier((held[a - 1, b - 1], k))
    blocks = [held[at, by] for by in range(b) for at in range(a)]
    blocks += [moved(block, 2, by, n) for by in range(1, c) for block in blocks]
    white = whitened_blocks(me, activations, out_grads, k, blocks)
    white = lax.all_to_all(white, "coord", split_axis=0, concat_axis=0, tiled=True)
    partials = partial_scores(me, seq_ids, white, bank)
    partials = lax.all_to_all(partials, "coord", split_axis=0, concat_axis=0, tiled=True)
    return place(partials, bank.shape[0] // n)


def solution(mesh):
    in_specs = (
        P(("groups", "coord"), None, None),
        P(("groups", "coord"), None, None),
        P("coord", None),
        P("coord", None),
        P(),
        P(),
        P(("groups", "coord")),
        P(("groups", "coord")),
        P(None, "coord"),
    )
    out_specs = P("groups", "coord")
    return jax.shard_map(
        functools.partial(body, mesh.shape["coord"]),
        mesh=mesh,
        in_specs=in_specs,
        out_specs=out_specs,
        check_vma=False,
    )
```

```python
import functools

import jax
import jax.numpy as jnp
from jax import lax
from jax.experimental import pallas as pl
from jax.experimental.pallas import tpu as pltpu
from jax.sharding import PartitionSpec as P

SUB = 8
LANES = 128
EXACT = lax.Precision.HIGHEST
VMEM = pl.BlockSpec(memory_space=pltpu.VMEM)
HBM = pl.BlockSpec(memory_space=pltpu.HBM)
SMEM = pl.BlockSpec(memory_space=pltpu.SMEM)


def factors(n):
    c = 2 if n % 2 == 0 else 1
    rest = n // c
    b = max(f for f in range(1, rest + 1) if rest % f == 0 and f * f <= rest)
    return rest // b, b, c


def partner(at, by, size, towards):
    if size & (size - 1) == 0:
        return at ^ by
    return (at + (by if towards else size - by)) % size


def sources(me, n):
    a, b, c = factors(n)
    ia, ib, ic = me // (b * c), (me // c) % b, me % c
    return [
        (partner(ia, da, a, False) * b + partner(ib, db, b, False)) * c + partner(ic, dc, c, False)
        for dc in range(c)
        for db in range(b)
        for da in range(a)
    ]


def moved(value, axis, by, n):
    sizes = factors(n)
    a, b, c = sizes
    pairs = []
    for me in range(n):
        at = [me // (b * c), (me // c) % b, me % c]
        at[axis] = partner(at[axis], by, sizes[axis], True)
        pairs.append((me, (at[0] * b + at[1]) * c + at[2]))
    return lax.ppermute(value, "coord", pairs)


def pack_kernel(first_hbm, second_hbm, out_ref, sems):
    rows = first_hbm.shape[0]
    copies = [
        pltpu.make_async_copy(source, out_ref.at[pl.ds(i * rows, rows)], sems.at[i])
        for i, source in enumerate((first_hbm, second_hbm))
    ]
    for copy in copies:
        copy.start()
    for copy in copies:
        copy.wait()


def pack(first, second):
    rows, columns = first.shape
    return pl.pallas_call(
        pack_kernel,
        out_shape=jax.ShapeDtypeStruct((2 * rows, columns), first.dtype),
        in_specs=[HBM, HBM],
        out_specs=VMEM,
        scratch_shapes=[pltpu.SemaphoreType.DMA((2,))],
        compiler_params=pltpu.CompilerParams(vmem_limit_bytes=8 << 20),
        name="pack",
    )(pinned(first), pinned(second))


def pinned(value):
    return pltpu.with_memory_space_constraint(value, pltpu.HBM)


def gauss_jordan(blocks):
    width = blocks[0].shape[1]
    half = width // 2
    lane = lax.broadcasted_iota(jnp.int32, (SUB, width), 1)
    sub = lax.broadcasted_iota(jnp.int32, (SUB, width), 0)
    start, within = lane // half * half, lane % half

    def column(block, at):
        return jnp.take_along_axis(block, start + at, axis=1, mode="promise_in_bounds")

    for k in range(len(blocks)):
        at = k * SUB
        head = within // SUB == k
        rows = [jnp.broadcast_to(blocks[k][i : i + 1, :], (SUB, width)) for i in range(SUB)]
        diag = {(i, j): column(rows[i], at + j) for i in range(SUB) for j in range(i, SUB)}
        rows = [jnp.where(head, (within == at + i).astype(jnp.float32), rows[i]) for i in range(SUB)]
        inverse, factor = [], {}
        for p in range(SUB):
            inverse.append(1.0 / diag[p, p])
            for i in range(p + 1, SUB):
                factor[p, i] = diag[p, i] * inverse[p]
                for j in range(i, SUB):
                    diag[i, j] = diag[i, j] - factor[p, i] * diag[p, j]
                rows[i] = rows[i] - factor[p, i] * rows[p]
        rows = [rows[p] * inverse[p] for p in range(SUB)]
        for p in reversed(range(SUB)):
            for i in range(p):
                rows[i] = rows[i] - factor[i, p] * rows[p]
        done = rows[0]
        for i in range(1, SUB):
            done = jnp.where(sub == i, rows[i], done)
        out = []
        for g, block in enumerate(blocks):
            if g == k:
                out.append(done)
                continue
            terms = [column(block, at + p) * rows[p] for p in range(SUB)]
            while len(terms) > 1:
                terms = [terms[i] + terms[i + 1] for i in range(0, len(terms), 2)]
            out.append(jnp.where(head, 0.0, block) - terms[0])
        blocks = out
    return blocks


def side_by_side_inverses(first, second):
    half = first.shape[0]
    both = jnp.concatenate([first, second], axis=1)
    blocks = gauss_jordan([both[g : g + SUB, :] for g in range(0, half, SUB)])
    both = jnp.concatenate(blocks, axis=0)
    return both[:, :half], both[:, half:]


def damped(cov):
    size = cov.shape[0]
    cov = 0.5 * (cov + cov.T)
    row = lax.broadcasted_iota(jnp.int32, (size, size), 0)
    col = lax.broadcasted_iota(jnp.int32, (size, size), 1)
    damping = 0.1 * jnp.sum(jnp.where(row == col, cov, 0.0)) / size
    return jnp.where(row == col, cov + damping, cov)


def product(left, right, dims=((1,), (0,))):
    return lax.dot_general(left, right, (dims, ((), ())), precision=EXACT, preferred_element_type=jnp.float32)


def inverse_kernel(len_hbm, cov_in_hbm, cov_out_hbm, k_ref, cov_ref, len_ref, sems):
    pairs = ((cov_in_hbm, cov_ref.at[0]), (cov_out_hbm, cov_ref.at[1]), (len_hbm, len_ref))
    copies = [pltpu.make_async_copy(source, target, sems.at[i]) for i, (source, target) in enumerate(pairs)]
    for copy in copies:
        copy.start()
    for copy in copies:
        copy.wait()
    size = cov_ref.shape[1]
    half = size // 2
    covs = [damped(cov_ref[0]), damped(cov_ref[1])]
    corner = [cov[:half, half:] for cov in covs]
    upper = side_by_side_inverses(*[cov[:half, :half] for cov in covs])
    solved = [product(u, c) for u, c in zip(upper, corner)]
    lower = side_by_side_inverses(
        *[cov[half:, half:] - product(c, t, ((0,), (0,))) for cov, c, t in zip(covs, corner, solved)]
    )
    for m, (u, t, low) in enumerate(zip(upper, solved, lower)):
        side = product(t, low)
        k_ref[m, :half, :half] = u + product(side, t, ((1,), (1,)))
        k_ref[m, :half, half:] = -side
        k_ref[m, half:, :half] = -side.T
        k_ref[m, half:, half:] = low
    token = lax.broadcasted_iota(jnp.int32, (size, size), 0)
    lane = lax.broadcasted_iota(jnp.int32, (size, size), 1)
    mask = jnp.zeros((size, size), jnp.float32)
    for s in range(len_ref.shape[0]):
        mask = jnp.where((lane == s) & (token < len_ref[s]), 1.0, mask)
    k_ref[2] = mask


def inverses(lengths, cov_in, cov_out):
    size = cov_in.shape[0]
    return pl.pallas_call(
        inverse_kernel,
        out_shape=jax.ShapeDtypeStruct((3, size, size), jnp.float32),
        in_specs=[HBM] * 3,
        out_specs=VMEM,
        scratch_shapes=[
            pltpu.VMEM((2, size, size), jnp.float32),
            pltpu.SMEM(lengths.shape, jnp.int32),
            pltpu.SemaphoreType.DMA((3,)),
        ],
        compiler_params=pltpu.CompilerParams(vmem_limit_bytes=8 << 20),
        cost_estimate=pl.CostEstimate(flops=size, bytes_accessed=size, transcendentals=0),
        name="inverses",
    )(pinned(lengths), pinned(cov_in), pinned(cov_out))


def project_kernel(n, early, late, me_ref, *rest):
    inputs, blocks, rest = rest[:2], rest[2 : 2 + len(early)], rest[2 + len(early) :]
    total_ref, rest = rest[0], rest[1:]
    later_ref, rest = (rest[0], rest[1:]) if late else (None, rest)
    held, sems = rest
    rows = blocks[0].shape[0] // 2
    source = sources(me_ref[0], n)
    copies = []
    for i, which in enumerate(early + late):
        columns = pl.ds(pl.multiple_of(source[which] * rows, rows), rows)
        for t in range(2):
            at = 2 * i + t
            target = held.at[at] if i < len(early) else later_ref.at[at - 2 * len(early)]
            copies.append(pltpu.make_async_copy(inputs[t].at[:, columns], target, sems.at[at]))
    for copy in copies:
        copy.start()
    sums = [None, None]
    for i, block in enumerate(blocks):
        for t in range(2):
            copies[2 * i + t].wait()
            term = jnp.dot(held[2 * i + t], block[t * rows : (t + 1) * rows, :], preferred_element_type=jnp.float32)
            sums[t] = term if sums[t] is None else sums[t] + term
    for t in range(2):
        total_ref[t] = sums[t]
    for copy in copies[2 * len(early) :]:
        copy.wait()


def project_whole_kernel(n, me_ref, act_ref, grad_ref, *rest):
    blocks, (total_ref, proj) = rest[:n], rest[n:]
    rows = blocks[0].shape[0] // 2
    for block, source in zip(blocks, sources(me_ref[0], n)):
        at = pl.ds(pl.multiple_of(source * rows, rows), rows)
        for t in range(2):
            proj[t, at, :] = block[t * rows : (t + 1) * rows, :]
    for t, ref in enumerate((act_ref, grad_ref)):
        total_ref[t] = jnp.dot(ref[...], proj[t], preferred_element_type=jnp.float32)


def project(me, activations, out_grads, blocks, early, late, n):
    tokens, width = activations.shape
    rank = blocks[0].shape[1]
    rows = blocks[0].shape[0] // 2
    total = jax.ShapeDtypeStruct((2, tokens, rank), jnp.float32)
    common = dict(
        compiler_params=pltpu.CompilerParams(vmem_limit_bytes=16 << 20),
        cost_estimate=pl.CostEstimate(
            flops=4 * tokens * width * rank, bytes_accessed=4 * tokens * width, transcendentals=0
        ),
        name="project",
    )
    if len(early) == n:
        result = pl.pallas_call(
            functools.partial(project_whole_kernel, n),
            out_shape=total,
            in_specs=[SMEM] + [VMEM] * (2 + n),
            out_specs=VMEM,
            scratch_shapes=[pltpu.VMEM((2, width, rank), jnp.bfloat16)],
            **common,
        )(me, activations, out_grads, *blocks)
        return result, None
    return pl.pallas_call(
        functools.partial(project_kernel, n, early, late),
        out_shape=(total, jax.ShapeDtypeStruct((2 * len(late), tokens, rows), activations.dtype)),
        in_specs=[SMEM, HBM, HBM] + [VMEM] * len(early),
        out_specs=(VMEM, VMEM),
        scratch_shapes=[
            pltpu.VMEM((2 * len(early), tokens, rows), activations.dtype),
            pltpu.SemaphoreType.DMA((2 * n,)),
        ],
        **common,
    )(me, pinned(activations), pinned(out_grads), *blocks)


def whiten_kernel(n, seqs, late, total_ref, k_ref, *rest):
    later, blocks, (out_ref, white) = rest[:1] if late else (), rest[1 : 1 + late], rest[-2:]
    rank = k_ref.shape[1]
    sums = [total_ref[0], total_ref[1]]
    for i, block in enumerate(blocks):
        rows = block.shape[0] // 2
        for t in range(2):
            sums[t] = sums[t] + jnp.dot(
                later[0][2 * i + t], block[t * rows : (t + 1) * rows, :], preferred_element_type=jnp.float32
            )
    length = total_ref.shape[1] // seqs
    share = rank // n
    for s in range(seqs):
        token = slice(s * length, (s + 1) * length)
        x_proj = (sums[0][token, :] * k_ref[2][:length, s : s + 1]).astype(jnp.bfloat16)
        d_proj = sums[1][token, :].astype(jnp.bfloat16)
        grads = lax.dot_general(d_proj, x_proj, (((0,), (0,)), ((), ())), preferred_element_type=jnp.float32)
        full = product(product(k_ref[1], grads), k_ref[0])
        for d in range(n):
            white[d, s * share : (s + 1) * share, :] = full[d * share : (d + 1) * share, :]
    out_ref[...] = white[...].astype(jnp.bfloat16)


def whitened_blocks(total, later, k, blocks, seqs, n):
    rank = k.shape[1]
    shape = (n, seqs * (rank // n), rank)
    operands = [total, k] + ([later] if blocks else []) + list(blocks)
    return pl.pallas_call(
        functools.partial(whiten_kernel, n, seqs, len(blocks)),
        out_shape=jax.ShapeDtypeStruct(shape, jnp.bfloat16),
        in_specs=[VMEM] * len(operands),
        out_specs=VMEM,
        scratch_shapes=[pltpu.VMEM(shape, jnp.float32)],
        compiler_params=pltpu.CompilerParams(vmem_limit_bytes=16 << 20),
        cost_estimate=pl.CostEstimate(flops=64 * rank**3, bytes_accessed=4 << 20, transcendentals=0),
        name="whiten",
    )(*operands)


def score_kernel(n, me_ref, ids_ref, white_ref, bank_ref, out_ref, spread):
    seqs = ids_ref.shape[0]
    chunk, rank = white_ref.shape[1:]
    share = chunk // seqs
    total = n * seqs
    spread[...] = white_ref[...].astype(jnp.float32).reshape(n * chunk, rank)
    columns = jnp.concatenate(
        [spread[pl.ds(j, total, stride=share), :].astype(jnp.bfloat16) for j in range(share)], axis=1
    )
    queries = bank_ref.shape[0] // n
    row = lax.broadcasted_iota(jnp.int32, (total, out_ref.shape[2] - queries), 0)
    tail = jnp.zeros(row.shape, jnp.float32)
    for s in range(seqs):
        tail = jnp.where(row == me_ref[0] * seqs + s, ids_ref[s].astype(jnp.float32), tail)
    partial = lax.dot_general(
        columns, bank_ref[...], (((1,), (1,)), ((), ())), preferred_element_type=jnp.float32
    )
    for d in range(n):
        out_ref[d, :, :queries] = partial[:, d * queries : (d + 1) * queries].astype(out_ref.dtype)
        out_ref[d, :, queries:] = tail.astype(out_ref.dtype)


def partial_scores(me, seq_ids, white, bank):
    n = white.shape[0]
    seqs = seq_ids.shape[0]
    queries = bank.shape[0] // n
    width = (queries // LANES + 1) * LANES
    return pl.pallas_call(
        functools.partial(score_kernel, n),
        out_shape=jax.ShapeDtypeStruct((n, n * seqs, width), jnp.bfloat16),
        in_specs=[SMEM, SMEM, VMEM, VMEM],
        out_specs=VMEM,
        scratch_shapes=[pltpu.VMEM((n * white.shape[1], white.shape[2]), jnp.float32)],
        compiler_params=pltpu.CompilerParams(vmem_limit_bytes=16 << 20),
        cost_estimate=pl.CostEstimate(
            flops=2 * n * seqs * bank.size, bytes_accessed=2 * bank.size, transcendentals=0
        ),
        name="score",
    )(me, seq_ids, white, bank)


def place_kernel(partial_ref, out_ref):
    rows, queries = out_ref.shape
    total = jnp.sum(partial_ref[...].astype(jnp.float32), axis=0)
    raw = total[:, :queries].astype(jnp.bfloat16)
    ids = total[:, queries : queries + 1].astype(jnp.int32)
    chosen = ids == lax.broadcasted_iota(jnp.int32, (rows, rows), 1)
    out_ref[...] = lax.dot_general(
        chosen.astype(jnp.bfloat16), raw, (((0,), (0,)), ((), ())), preferred_element_type=jnp.float32
    ).astype(jnp.bfloat16)


def place(partials, queries):
    return pl.pallas_call(
        lambda a, b: place_kernel(a, b),
        out_shape=jax.ShapeDtypeStruct((partials.shape[1], queries), jnp.bfloat16),
        in_specs=[VMEM],
        out_specs=VMEM,
        compiler_params=pltpu.CompilerParams(vmem_limit_bytes=16 << 20),
        name="place",
    )(partials)


def body(n, activations, out_grads, proj_in, proj_out, cov_in, cov_out, lengths, seq_ids, bank):
    me = lax.axis_index("coord").reshape(1)
    seqs, length, width = activations.shape
    activations, out_grads = activations.reshape(seqs * length, width), out_grads.reshape(seqs * length, width)
    a, b, c = factors(n)
    paired = a & (a - 1) == 0
    packed = pack(proj_in, proj_out)
    k = inverses(lengths, cov_in, cov_out)
    held = {(0, 0, 0): packed}
    for by in range(1, min(a, 3)):
        held[by, 0, 0] = moved(packed, 0, by, n)
    for by in range(1, b):
        held[0, by, 0] = moved(packed, 1, by, n)
    held, k = lax.optimization_barrier((held, k))
    for at in range(3, a):
        nearest = at & -at
        if paired and nearest != at:
            held[at, 0, 0] = moved(held[at - nearest, 0, 0], 0, nearest, n)
        else:
            held[at, 0, 0] = moved(held[0, 0, 0], 0, at, n)
    for at in range(1, a):
        for by in range(1, b):
            nearest = at & -at
            if paired and nearest != at and at == a - 1:
                held[at, by, 0] = moved(held[at - nearest, by, 0], 0, nearest, n)
            else:
                held[at, by, 0] = moved(held[at, 0, 0], 1, by, n)
    split = proj_in.shape[0] % LANES == 0 and a > 2 and b > 1 and c > 1
    after = [(1, b - 1, 0), (a - 1, b - 1, 0)] if split else []

    def to_other_cores(which):
        for at in which:
            for by in range(1, c):
                held[at[0], at[1], by] = moved(held[at], 2, by, n)

    to_other_cores([at for at in list(held) if at not in after])
    order = [(at, by, core) for core in range(c) for by in range(b) for at in range(a)]
    late = [at for at in order if at[0] and at[1] and (at[0] != 2 or at[2]) or at[0] > 2 and at[2]] if split else []
    early = [at for at in order if at not in late]
    total, later = project(
        me,
        activations,
        out_grads,
        [held[at] for at in early],
        [order.index(at) for at in early],
        [order.index(at) for at in late],
        n,
    )
    waiting, total = lax.optimization_barrier(({at: held[at] for at in after}, total))
    held.update(waiting)
    to_other_cores(after)
    white = whitened_blocks(total, later, k, [held[at] for at in late], seqs, n)
    white = lax.all_to_all(white, "coord", split_axis=0, concat_axis=0, tiled=True)
    partials = partial_scores(me, seq_ids, white, bank)
    partials = lax.all_to_all(partials, "coord", split_axis=0, concat_axis=0, tiled=True)
    return place(partials, bank.shape[0] // n)


def solution(mesh):
    in_specs = (
        P(("groups", "coord"), None, None),
        P(("groups", "coord"), None, None),
        P("coord", None),
        P("coord", None),
        P(),
        P(),
        P(("groups", "coord")),
        P(("groups", "coord")),
        P(None, "coord"),
    )
    out_specs = P("groups", "coord")
    return jax.shard_map(
        functools.partial(body, mesh.shape["coord"]),
        mesh=mesh,
        in_specs=in_specs,
        out_specs=out_specs,
        check_vma=False,
    )
```

```python
import functools

import jax
import jax.numpy as jnp
from jax import lax
from jax.experimental import pallas as pl
from jax.experimental.pallas import tpu as pltpu
from jax.sharding import PartitionSpec as P

SUB = 8
LANES = 128
EXACT = lax.Precision.HIGHEST
VMEM = pl.BlockSpec(memory_space=pltpu.VMEM)
HBM = pl.BlockSpec(memory_space=pltpu.HBM)
SMEM = pl.BlockSpec(memory_space=pltpu.SMEM)


def factors(n):
    c = 2 if n % 2 == 0 else 1
    rest = n // c
    b = max(f for f in range(1, rest + 1) if rest % f == 0 and f * f <= rest)
    return rest // b, b, c


def partner(at, by, size, towards):
    if size & (size - 1) == 0:
        return at ^ by
    return (at + (by if towards else size - by)) % size


def sources(me, n):
    a, b, c = factors(n)
    ia, ib, ic = me // (b * c), (me // c) % b, me % c
    return [
        (partner(ia, da, a, False) * b + partner(ib, db, b, False)) * c + partner(ic, dc, c, False)
        for dc in range(c)
        for db in range(b)
        for da in range(a)
    ]


def moved(value, axis, by, n):
    sizes = factors(n)
    a, b, c = sizes
    pairs = []
    for me in range(n):
        at = [me // (b * c), (me // c) % b, me % c]
        at[axis] = partner(at[axis], by, sizes[axis], True)
        pairs.append((me, (at[0] * b + at[1]) * c + at[2]))
    return lax.ppermute(value, "coord", pairs)


def pack_kernel(first_hbm, second_hbm, out_ref, sems):
    rows = first_hbm.shape[0]
    copies = [
        pltpu.make_async_copy(source, out_ref.at[pl.ds(i * rows, rows)], sems.at[i])
        for i, source in enumerate((first_hbm, second_hbm))
    ]
    for copy in copies:
        copy.start()
    for copy in copies:
        copy.wait()


def pack(first, second):
    rows, columns = first.shape
    return pl.pallas_call(
        pack_kernel,
        out_shape=jax.ShapeDtypeStruct((2 * rows, columns), first.dtype),
        in_specs=[HBM, HBM],
        out_specs=VMEM,
        scratch_shapes=[pltpu.SemaphoreType.DMA((2,))],
        compiler_params=pltpu.CompilerParams(vmem_limit_bytes=8 << 20),
        name="pack",
    )(pinned(first), pinned(second))


def pinned(value):
    return pltpu.with_memory_space_constraint(value, pltpu.HBM)


def gauss_jordan(blocks):
    width = blocks[0].shape[1]
    half = width // 2
    lane = lax.broadcasted_iota(jnp.int32, (SUB, width), 1)
    sub = lax.broadcasted_iota(jnp.int32, (SUB, width), 0)
    start, within = lane // half * half, lane % half

    def column(block, at):
        return jnp.take_along_axis(block, start + at, axis=1, mode="promise_in_bounds")

    for k in range(len(blocks)):
        at = k * SUB
        head = within // SUB == k
        rows = [jnp.broadcast_to(blocks[k][i : i + 1, :], (SUB, width)) for i in range(SUB)]
        diag = {(i, j): column(rows[i], at + j) for i in range(SUB) for j in range(i, SUB)}
        rows = [jnp.where(head, (within == at + i).astype(jnp.float32), rows[i]) for i in range(SUB)]
        inverse, factor = [], {}
        for p in range(SUB):
            inverse.append(1.0 / diag[p, p])
            for i in range(p + 1, SUB):
                factor[p, i] = diag[p, i] * inverse[p]
                for j in range(i, SUB):
                    diag[i, j] = diag[i, j] - factor[p, i] * diag[p, j]
                rows[i] = rows[i] - factor[p, i] * rows[p]
        rows = [rows[p] * inverse[p] for p in range(SUB)]
        for p in reversed(range(SUB)):
            for i in range(p):
                rows[i] = rows[i] - factor[i, p] * rows[p]
        done = rows[0]
        for i in range(1, SUB):
            done = jnp.where(sub == i, rows[i], done)
        out = []
        for g, block in enumerate(blocks):
            if g == k:
                out.append(done)
                continue
            terms = [column(block, at + p) * rows[p] for p in range(SUB)]
            while len(terms) > 1:
                terms = [terms[i] + terms[i + 1] for i in range(0, len(terms), 2)]
            out.append(jnp.where(head, 0.0, block) - terms[0])
        blocks = out
    return blocks


def side_by_side_inverses(first, second):
    half = first.shape[0]
    both = jnp.concatenate([first, second], axis=1)
    blocks = gauss_jordan([both[g : g + SUB, :] for g in range(0, half, SUB)])
    both = jnp.concatenate(blocks, axis=0)
    return both[:, :half], both[:, half:]


def damped(cov):
    size = cov.shape[0]
    cov = 0.5 * (cov + cov.T)
    row = lax.broadcasted_iota(jnp.int32, (size, size), 0)
    col = lax.broadcasted_iota(jnp.int32, (size, size), 1)
    damping = 0.1 * jnp.sum(jnp.where(row == col, cov, 0.0)) / size
    return jnp.where(row == col, cov + damping, cov)


def product(left, right, dims=((1,), (0,))):
    return lax.dot_general(left, right, (dims, ((), ())), precision=EXACT, preferred_element_type=jnp.float32)


def inverse_kernel(len_hbm, cov_in_hbm, cov_out_hbm, k_ref, cov_ref, len_ref, sems):
    pairs = ((cov_in_hbm, cov_ref.at[0]), (cov_out_hbm, cov_ref.at[1]), (len_hbm, len_ref))
    copies = [pltpu.make_async_copy(source, target, sems.at[i]) for i, (source, target) in enumerate(pairs)]
    for copy in copies:
        copy.start()
    for copy in copies:
        copy.wait()
    size = cov_ref.shape[1]
    half = size // 2
    covs = [damped(cov_ref[0]), damped(cov_ref[1])]
    corner = [cov[:half, half:] for cov in covs]
    upper = side_by_side_inverses(*[cov[:half, :half] for cov in covs])
    solved = [product(u, c) for u, c in zip(upper, corner)]
    lower = side_by_side_inverses(
        *[cov[half:, half:] - product(c, t, ((0,), (0,))) for cov, c, t in zip(covs, corner, solved)]
    )
    for m, (u, t, low) in enumerate(zip(upper, solved, lower)):
        side = product(t, low)
        k_ref[m, :half, :half] = u + product(side, t, ((1,), (1,)))
        k_ref[m, :half, half:] = -side
        k_ref[m, half:, :half] = -side.T
        k_ref[m, half:, half:] = low
    token = lax.broadcasted_iota(jnp.int32, (size, size), 0)
    lane = lax.broadcasted_iota(jnp.int32, (size, size), 1)
    mask = jnp.zeros((size, size), jnp.float32)
    for s in range(len_ref.shape[0]):
        mask = jnp.where((lane == s) & (token < len_ref[s]), 1.0, mask)
    k_ref[2] = mask


def inverses(lengths, cov_in, cov_out):
    size = cov_in.shape[0]
    return pl.pallas_call(
        inverse_kernel,
        out_shape=jax.ShapeDtypeStruct((3, size, size), jnp.float32),
        in_specs=[HBM] * 3,
        out_specs=VMEM,
        scratch_shapes=[
            pltpu.VMEM((2, size, size), jnp.float32),
            pltpu.SMEM(lengths.shape, jnp.int32),
            pltpu.SemaphoreType.DMA((3,)),
        ],
        compiler_params=pltpu.CompilerParams(vmem_limit_bytes=8 << 20),
        cost_estimate=pl.CostEstimate(flops=size, bytes_accessed=size, transcendentals=0),
        name="inverses",
    )(pinned(lengths), pinned(cov_in), pinned(cov_out))


def merge_kernel(*refs):
    rows = refs[0].shape[0]
    for i, ref in enumerate(refs[:-1]):
        refs[-1][i * rows : (i + 1) * rows, :] = ref[...]


def merge(blocks):
    rows, columns = blocks[0].shape
    return pl.pallas_call(
        merge_kernel,
        out_shape=jax.ShapeDtypeStruct((len(blocks) * rows, columns), blocks[0].dtype),
        in_specs=[VMEM] * len(blocks),
        out_specs=VMEM,
        compiler_params=pltpu.CompilerParams(vmem_limit_bytes=8 << 20),
        cost_estimate=pl.CostEstimate(flops=rows, bytes_accessed=rows, transcendentals=0),
        name="merge",
    )(*blocks)


def project_kernel(n, early, seqs, me_ref, *rest):
    inputs, blocks, (total_ref, held, sems) = rest[:2], rest[2 : 2 + len(early)], rest[2 + len(early) :]
    tokens = held.shape[1]
    part = tokens // sems.shape[1]
    copies = [
        [
            pltpu.make_async_copy(source.at[pl.ds(i * part, part)], held.at[t, pl.ds(i * part, part)], sems.at[t, i])
            for i in range(sems.shape[1])
        ]
        for t, source in enumerate(inputs)
    ]
    for copy in copies[0] + copies[1]:
        copy.start()
    rows = blocks[0].shape[0] // 2
    source = sources(me_ref[0], n)
    for t in range(2):
        for copy in copies[t]:
            copy.wait()
        total = None
        for which, block in zip(early, blocks):
            columns = pl.ds(pl.multiple_of(source[which] * rows, rows), rows)
            term = jnp.dot(
                held[t, :, columns], block[t * rows : (t + 1) * rows, :], preferred_element_type=jnp.float32
            )
            total = term if total is None else total + term
        total_ref[t] = total


def project_whole_kernel(n, me_ref, act_ref, grad_ref, *rest):
    blocks, (total_ref, proj) = rest[:n], rest[n:]
    rows = blocks[0].shape[0] // 2
    for block, source in zip(blocks, sources(me_ref[0], n)):
        at = pl.ds(pl.multiple_of(source * rows, rows), rows)
        for t in range(2):
            proj[t, at, :] = block[t * rows : (t + 1) * rows, :]
    for t, ref in enumerate((act_ref, grad_ref)):
        total_ref[t] = jnp.dot(ref[...], proj[t], preferred_element_type=jnp.float32)


def project(me, activations, out_grads, blocks, early, seqs, n):
    tokens, width = activations.shape
    rank = blocks[0].shape[1]
    total = jax.ShapeDtypeStruct((2, tokens, rank), jnp.float32)
    common = dict(
        compiler_params=pltpu.CompilerParams(vmem_limit_bytes=16 << 20),
        cost_estimate=pl.CostEstimate(
            flops=4 * tokens * width * rank, bytes_accessed=4 * tokens * width, transcendentals=0
        ),
        name="project",
    )
    if len(early) == n:
        result = pl.pallas_call(
            functools.partial(project_whole_kernel, n),
            out_shape=total,
            in_specs=[SMEM] + [VMEM] * (2 + n),
            out_specs=VMEM,
            scratch_shapes=[pltpu.VMEM((2, width, rank), jnp.bfloat16)],
            **common,
        )(me, activations, out_grads, *blocks)
        return result, None
    return pl.pallas_call(
        functools.partial(project_kernel, n, early, seqs),
        out_shape=(
            total,
            jax.ShapeDtypeStruct((2, tokens, width), activations.dtype),
        ),
        in_specs=[SMEM, HBM, HBM] + [VMEM] * len(early),
        out_specs=(VMEM, VMEM),
        scratch_shapes=[pltpu.SemaphoreType.DMA((2, 2 * seqs))],
        **common,
    )(me, pinned(activations), pinned(out_grads), *blocks)


def whiten_kernel(n, seqs, late, total_ref, k_ref, *rest):
    operands, (out_ref, white) = rest[:-2], rest[-2:]
    rank = k_ref.shape[1]
    sums = [total_ref[0], total_ref[1]]
    if late:
        me_ref, held, *blocks = operands
        source = sources(me_ref[0], n)
        rows = held.shape[2] // n
        for which, operand, at in late:
            columns = pl.ds(pl.multiple_of(source[which] * rows, rows), rows)
            for t in range(2):
                block = blocks[operand][(2 * at + t) * rows : (2 * at + t + 1) * rows, :]
                sums[t] = sums[t] + jnp.dot(held[t, :, columns], block, preferred_element_type=jnp.float32)
    length = total_ref.shape[1] // seqs
    share = rank // n
    for s in range(seqs):
        token = slice(s * length, (s + 1) * length)
        x_proj = (sums[0][token, :] * k_ref[2][:length, s : s + 1]).astype(jnp.bfloat16)
        d_proj = sums[1][token, :].astype(jnp.bfloat16)
        grads = lax.dot_general(d_proj, x_proj, (((0,), (0,)), ((), ())), preferred_element_type=jnp.float32)
        full = product(product(k_ref[1], grads), k_ref[0])
        for d in range(n):
            white[d, s * share : (s + 1) * share, :] = full[d * share : (d + 1) * share, :]
    out_ref[...] = white[...].astype(jnp.bfloat16)


def whitened_blocks(total, k, late, operands, seqs, n):
    rank = k.shape[1]
    shape = (n, seqs * (rank // n), rank)
    return pl.pallas_call(
        functools.partial(whiten_kernel, n, seqs, late),
        out_shape=jax.ShapeDtypeStruct(shape, jnp.bfloat16),
        in_specs=[VMEM, VMEM] + ([SMEM] + [VMEM] * (len(operands) - 1) if operands else []),
        out_specs=VMEM,
        scratch_shapes=[pltpu.VMEM(shape, jnp.float32)],
        compiler_params=pltpu.CompilerParams(vmem_limit_bytes=16 << 20),
        cost_estimate=pl.CostEstimate(flops=64 * rank**3, bytes_accessed=4 << 20, transcendentals=0),
        name="whiten",
    )(total, k, *operands)


def score_kernel(n, me_ref, ids_ref, white_ref, bank_ref, out_ref, spread):
    seqs = ids_ref.shape[0]
    chunk, rank = white_ref.shape[1:]
    share = chunk // seqs
    total = n * seqs
    spread[...] = white_ref[...].astype(jnp.float32).reshape(n * chunk, rank)
    columns = jnp.concatenate(
        [spread[pl.ds(j, total, stride=share), :].astype(jnp.bfloat16) for j in range(share)], axis=1
    )
    queries = bank_ref.shape[0] // n
    row = lax.broadcasted_iota(jnp.int32, (total, out_ref.shape[2] - queries), 0)
    tail = jnp.zeros(row.shape, jnp.float32)
    for s in range(seqs):
        tail = jnp.where(row == me_ref[0] * seqs + s, ids_ref[s].astype(jnp.float32), tail)
    partial = lax.dot_general(
        columns, bank_ref[...], (((1,), (1,)), ((), ())), preferred_element_type=jnp.float32
    )
    for d in range(n):
        out_ref[d, :, :queries] = partial[:, d * queries : (d + 1) * queries].astype(out_ref.dtype)
        out_ref[d, :, queries:] = tail.astype(out_ref.dtype)


def partial_scores(me, seq_ids, white, bank):
    n = white.shape[0]
    seqs = seq_ids.shape[0]
    queries = bank.shape[0] // n
    width = (queries // LANES + 1) * LANES
    return pl.pallas_call(
        functools.partial(score_kernel, n),
        out_shape=jax.ShapeDtypeStruct((n, n * seqs, width), jnp.bfloat16),
        in_specs=[SMEM, SMEM, VMEM, VMEM],
        out_specs=VMEM,
        scratch_shapes=[pltpu.VMEM((n * white.shape[1], white.shape[2]), jnp.float32)],
        compiler_params=pltpu.CompilerParams(vmem_limit_bytes=16 << 20),
        cost_estimate=pl.CostEstimate(
            flops=2 * n * seqs * bank.size, bytes_accessed=2 * bank.size, transcendentals=0
        ),
        name="score",
    )(me, seq_ids, white, bank)


def place_kernel(partial_ref, out_ref):
    rows, queries = out_ref.shape
    total = jnp.sum(partial_ref[...].astype(jnp.float32), axis=0)
    raw = total[:, :queries].astype(jnp.bfloat16)
    ids = total[:, queries : queries + 1].astype(jnp.int32)
    chosen = ids == lax.broadcasted_iota(jnp.int32, (rows, rows), 1)
    out_ref[...] = lax.dot_general(
        chosen.astype(jnp.bfloat16), raw, (((0,), (0,)), ((), ())), preferred_element_type=jnp.float32
    ).astype(jnp.bfloat16)


def place(partials, queries):
    return pl.pallas_call(
        lambda a, b: place_kernel(a, b),
        out_shape=jax.ShapeDtypeStruct((partials.shape[1], queries), jnp.bfloat16),
        in_specs=[VMEM],
        out_specs=VMEM,
        compiler_params=pltpu.CompilerParams(vmem_limit_bytes=16 << 20),
        name="place",
    )(partials)


def body(n, activations, out_grads, proj_in, proj_out, cov_in, cov_out, lengths, seq_ids, bank):
    me = lax.axis_index("coord").reshape(1)
    seqs, length, width = activations.shape
    activations, out_grads = activations.reshape(seqs * length, width), out_grads.reshape(seqs * length, width)
    a, b, c = factors(n)
    paired = a & (a - 1) == 0
    packed = pack(proj_in, proj_out)
    k = inverses(lengths, cov_in, cov_out)
    held = {(0, 0, 0): packed}
    for by in range(1, min(a, 3)):
        held[by, 0, 0] = moved(packed, 0, by, n)
    for by in range(1, b):
        held[0, by, 0] = moved(packed, 1, by, n)
    held, k = lax.optimization_barrier((held, k))
    for at in range(3, a):
        nearest = at & -at
        if paired and nearest != at:
            held[at, 0, 0] = moved(held[at - nearest, 0, 0], 0, nearest, n)
        else:
            held[at, 0, 0] = moved(held[0, 0, 0], 0, at, n)
    for at in range(1, a):
        for by in range(1, b):
            nearest = at & -at
            if paired and nearest != at and at == a - 1:
                held[at, by, 0] = moved(held[at - nearest, by, 0], 0, nearest, n)
            else:
                held[at, by, 0] = moved(held[at, 0, 0], 1, by, n)
    order = [(at, by, core) for core in range(c) for by in range(b) for at in range(a)]
    if proj_in.shape[0] % LANES == 0 and a > 2 and b > 1 and c == 2:
        after = [(1, b - 1, 0), (a - 1, b - 1, 0)]
        early = [at for at in order if at[2] == 0 and at not in after]
        across = moved(merge([held[at] for at in early]), 2, 1, n)
        total, inputs = project(
            me, activations, out_grads, [held[at] for at in early], [order.index(at) for at in early], seqs, n
        )
        waiting, total = lax.optimization_barrier(([held[at] for at in after], total))
        others = [moved(block, 2, 1, n) for block in waiting]
        operands = [me, inputs, across, *others, *waiting]
        late = [(order.index((*at[:2], 1)), 0, i) for i, at in enumerate(early)]
        late += [(order.index((*at[:2], 1)), 1 + i, 0) for i, at in enumerate(after)]
        late += [(order.index(at), 1 + len(others) + i, 0) for i, at in enumerate(after)]
    else:
        for at in list(held):
            for by in range(1, c):
                held[at[0], at[1], by] = moved(held[at], 2, by, n)
        total = project(me, activations, out_grads, [held[at] for at in order], list(range(n)), seqs, n)[0]
        operands, late = [], []
    white = whitened_blocks(total, k, late, operands, seqs, n)
    white = lax.all_to_all(white, "coord", split_axis=0, concat_axis=0, tiled=True)
    partials = partial_scores(me, seq_ids, white, bank)
    partials = lax.all_to_all(partials, "coord", split_axis=0, concat_axis=0, tiled=True)
    return place(partials, bank.shape[0] // n)


def solution(mesh):
    in_specs = (
        P(("groups", "coord"), None, None),
        P(("groups", "coord"), None, None),
        P("coord", None),
        P("coord", None),
        P(),
        P(),
        P(("groups", "coord")),
        P(("groups", "coord")),
        P(None, "coord"),
    )
    out_specs = P("groups", "coord")
    return jax.shard_map(
        functools.partial(body, mesh.shape["coord"]),
        mesh=mesh,
        in_specs=in_specs,
        out_specs=out_specs,
        check_vma=False,
    )
```

```python
import functools

import jax
import jax.numpy as jnp
from jax import lax
from jax.experimental import pallas as pl
from jax.experimental.pallas import tpu as pltpu
from jax.sharding import PartitionSpec as P

SUB = 8
LANES = 128
EXACT = lax.Precision.HIGHEST
VMEM = pl.BlockSpec(memory_space=pltpu.VMEM)
HBM = pl.BlockSpec(memory_space=pltpu.HBM)
SMEM = pl.BlockSpec(memory_space=pltpu.SMEM)


def factors(n):
    c = 2 if n % 2 == 0 else 1
    rest = n // c
    b = max(f for f in range(1, rest + 1) if rest % f == 0 and f * f <= rest)
    return rest // b, b, c


def partner(at, by, size, towards):
    if size & (size - 1) == 0:
        return at ^ by
    return (at + (by if towards else size - by)) % size


def sources(me, n):
    a, b, c = factors(n)
    ia, ib, ic = me // (b * c), (me // c) % b, me % c
    return [
        (partner(ia, da, a, False) * b + partner(ib, db, b, False)) * c + partner(ic, dc, c, False)
        for dc in range(c)
        for db in range(b)
        for da in range(a)
    ]


def moved(value, axis, by, n):
    sizes = factors(n)
    a, b, c = sizes
    pairs = []
    for me in range(n):
        at = [me // (b * c), (me // c) % b, me % c]
        at[axis] = partner(at[axis], by, sizes[axis], True)
        pairs.append((me, (at[0] * b + at[1]) * c + at[2]))
    return lax.ppermute(value, "coord", pairs)


def pack_kernel(first_hbm, second_hbm, out_ref, sems):
    rows = first_hbm.shape[0]
    copies = [
        pltpu.make_async_copy(source, out_ref.at[pl.ds(i * rows, rows)], sems.at[i])
        for i, source in enumerate((first_hbm, second_hbm))
    ]
    for copy in copies:
        copy.start()
    for copy in copies:
        copy.wait()


def pack(first, second):
    rows, columns = first.shape
    return pl.pallas_call(
        pack_kernel,
        out_shape=jax.ShapeDtypeStruct((2 * rows, columns), first.dtype),
        in_specs=[HBM, HBM],
        out_specs=VMEM,
        scratch_shapes=[pltpu.SemaphoreType.DMA((2,))],
        compiler_params=pltpu.CompilerParams(vmem_limit_bytes=8 << 20),
        name="pack",
    )(pinned(first), pinned(second))


def pinned(value):
    return pltpu.with_memory_space_constraint(value, pltpu.HBM)


def gauss_jordan(blocks):
    width = blocks[0].shape[1]
    half = width // 2
    lane = lax.broadcasted_iota(jnp.int32, (SUB, width), 1)
    sub = lax.broadcasted_iota(jnp.int32, (SUB, width), 0)
    start, within = lane // half * half, lane % half

    def column(block, at):
        return jnp.take_along_axis(block, start + at, axis=1, mode="promise_in_bounds")

    for k in range(len(blocks)):
        at = k * SUB
        head = within // SUB == k
        rows = [jnp.broadcast_to(blocks[k][i : i + 1, :], (SUB, width)) for i in range(SUB)]
        diag = {(i, j): column(rows[i], at + j) for i in range(SUB) for j in range(i, SUB)}
        rows = [jnp.where(head, (within == at + i).astype(jnp.float32), rows[i]) for i in range(SUB)]
        inverse, factor = [], {}
        for p in range(SUB):
            inverse.append(1.0 / diag[p, p])
            for i in range(p + 1, SUB):
                factor[p, i] = diag[p, i] * inverse[p]
                for j in range(i, SUB):
                    diag[i, j] = diag[i, j] - factor[p, i] * diag[p, j]
                rows[i] = rows[i] - factor[p, i] * rows[p]
        rows = [rows[p] * inverse[p] for p in range(SUB)]
        for p in reversed(range(SUB)):
            for i in range(p):
                rows[i] = rows[i] - factor[i, p] * rows[p]
        done = rows[0]
        for i in range(1, SUB):
            done = jnp.where(sub == i, rows[i], done)
        out = []
        for g, block in enumerate(blocks):
            if g == k:
                out.append(done)
                continue
            terms = [column(block, at + p) * rows[p] for p in range(SUB)]
            while len(terms) > 1:
                terms = [terms[i] + terms[i + 1] for i in range(0, len(terms), 2)]
            out.append(jnp.where(head, 0.0, block) - terms[0])
        blocks = out
    return blocks


def side_by_side_inverses(first, second):
    half = first.shape[0]
    both = jnp.concatenate([first, second], axis=1)
    blocks = gauss_jordan([both[g : g + SUB, :] for g in range(0, half, SUB)])
    both = jnp.concatenate(blocks, axis=0)
    return both[:, :half], both[:, half:]


def damped(cov):
    size = cov.shape[0]
    cov = 0.5 * (cov + cov.T)
    row = lax.broadcasted_iota(jnp.int32, (size, size), 0)
    col = lax.broadcasted_iota(jnp.int32, (size, size), 1)
    damping = 0.1 * jnp.sum(jnp.where(row == col, cov, 0.0)) / size
    return jnp.where(row == col, cov + damping, cov)


def product(left, right, dims=((1,), (0,))):
    return lax.dot_general(left, right, (dims, ((), ())), precision=EXACT, preferred_element_type=jnp.float32)


def first_half_kernel(cov_in_hbm, cov_out_hbm, out_ref, cov_ref, sems):
    copies = [
        pltpu.make_async_copy(source, cov_ref.at[i], sems.at[i]) for i, source in enumerate((cov_in_hbm, cov_out_hbm))
    ]
    for copy in copies:
        copy.start()
    for copy in copies:
        copy.wait()
    half = cov_ref.shape[1] // 2
    covs = [damped(cov_ref[0]), damped(cov_ref[1])]
    corner = [cov[:half, half:] for cov in covs]
    upper = side_by_side_inverses(*[cov[:half, :half] for cov in covs])
    solved = [product(u, c) for u, c in zip(upper, corner)]
    schur = [cov[half:, half:] - product(c, t, ((0,), (0,))) for cov, c, t in zip(covs, corner, solved)]
    for i, pair in enumerate((upper, solved, schur)):
        out_ref[i] = jnp.concatenate(pair, axis=1)


def second_half_kernel(first_ref, len_hbm, k_ref, len_ref, sem):
    copy = pltpu.make_async_copy(len_hbm, len_ref, sem)
    copy.start()
    size = k_ref.shape[1]
    half = size // 2
    upper, solved, schur = [(first_ref[i][:, :half], first_ref[i][:, half:]) for i in range(3)]
    lower = side_by_side_inverses(*schur)
    for m, (u, t, low) in enumerate(zip(upper, solved, lower)):
        side = product(t, low)
        k_ref[m, :half, :half] = u + product(side, t, ((1,), (1,)))
        k_ref[m, :half, half:] = -side
        k_ref[m, half:, :half] = -side.T
        k_ref[m, half:, half:] = low
    copy.wait()
    token = lax.broadcasted_iota(jnp.int32, (size, size), 0)
    lane = lax.broadcasted_iota(jnp.int32, (size, size), 1)
    mask = jnp.zeros((size, size), jnp.float32)
    for s in range(len_ref.shape[0]):
        mask = jnp.where((lane == s) & (token < len_ref[s]), 1.0, mask)
    k_ref[2] = mask


def first_half(cov_in, cov_out):
    size = cov_in.shape[0]
    return pl.pallas_call(
        first_half_kernel,
        out_shape=jax.ShapeDtypeStruct((3, size // 2, size), jnp.float32),
        in_specs=[HBM, HBM],
        out_specs=VMEM,
        scratch_shapes=[pltpu.VMEM((2, size, size), jnp.float32), pltpu.SemaphoreType.DMA((2,))],
        compiler_params=pltpu.CompilerParams(vmem_limit_bytes=8 << 20),
        cost_estimate=pl.CostEstimate(flops=size, bytes_accessed=size, transcendentals=0),
        name="first_half",
    )(pinned(cov_in), pinned(cov_out))


def second_half(first, lengths):
    size = first.shape[2]
    return pl.pallas_call(
        second_half_kernel,
        out_shape=jax.ShapeDtypeStruct((3, size, size), jnp.float32),
        in_specs=[VMEM, HBM],
        out_specs=VMEM,
        scratch_shapes=[pltpu.SMEM(lengths.shape, jnp.int32), pltpu.SemaphoreType.DMA],
        compiler_params=pltpu.CompilerParams(vmem_limit_bytes=8 << 20),
        cost_estimate=pl.CostEstimate(flops=2 * size**3, bytes_accessed=12 << 20, transcendentals=0),
        name="second_half",
    )(first, pinned(lengths))


def merge_kernel(*refs):
    rows = refs[0].shape[0]
    for i, ref in enumerate(refs[:-1]):
        refs[-1][i * rows : (i + 1) * rows, :] = ref[...]


def merge(blocks):
    rows, columns = blocks[0].shape
    return pl.pallas_call(
        merge_kernel,
        out_shape=jax.ShapeDtypeStruct((len(blocks) * rows, columns), blocks[0].dtype),
        in_specs=[VMEM] * len(blocks),
        out_specs=VMEM,
        compiler_params=pltpu.CompilerParams(vmem_limit_bytes=8 << 20),
        cost_estimate=pl.CostEstimate(flops=rows, bytes_accessed=rows, transcendentals=0),
        name="merge",
    )(*blocks)


def project_kernel(n, early, seqs, me_ref, *rest):
    inputs, blocks, (total_ref, held, sems) = rest[:2], rest[2 : 2 + len(early)], rest[2 + len(early) :]
    tokens = held.shape[1]
    part = tokens // sems.shape[1]
    copies = [
        [
            pltpu.make_async_copy(source.at[pl.ds(i * part, part)], held.at[t, pl.ds(i * part, part)], sems.at[t, i])
            for i in range(sems.shape[1])
        ]
        for t, source in enumerate(inputs)
    ]
    for copy in copies[0] + copies[1]:
        copy.start()
    rows = blocks[0].shape[0] // 2
    source = sources(me_ref[0], n)
    for t in range(2):
        for copy in copies[t]:
            copy.wait()
        total = None
        for which, block in zip(early, blocks):
            columns = pl.ds(pl.multiple_of(source[which] * rows, rows), rows)
            term = jnp.dot(
                held[t, :, columns], block[t * rows : (t + 1) * rows, :], preferred_element_type=jnp.float32
            )
            total = term if total is None else total + term
        total_ref[t] = total


def project_whole_kernel(n, me_ref, act_ref, grad_ref, *rest):
    blocks, (total_ref, proj) = rest[:n], rest[n:]
    rows = blocks[0].shape[0] // 2
    for block, source in zip(blocks, sources(me_ref[0], n)):
        at = pl.ds(pl.multiple_of(source * rows, rows), rows)
        for t in range(2):
            proj[t, at, :] = block[t * rows : (t + 1) * rows, :]
    for t, ref in enumerate((act_ref, grad_ref)):
        total_ref[t] = jnp.dot(ref[...], proj[t], preferred_element_type=jnp.float32)


def project(me, activations, out_grads, blocks, early, seqs, n):
    tokens, width = activations.shape
    rank = blocks[0].shape[1]
    total = jax.ShapeDtypeStruct((2, tokens, rank), jnp.float32)
    common = dict(
        compiler_params=pltpu.CompilerParams(vmem_limit_bytes=16 << 20),
        cost_estimate=pl.CostEstimate(flops=rank, bytes_accessed=rank, transcendentals=0),
        name="project",
    )
    if len(early) == n:
        result = pl.pallas_call(
            functools.partial(project_whole_kernel, n),
            out_shape=total,
            in_specs=[SMEM] + [VMEM] * (2 + n),
            out_specs=VMEM,
            scratch_shapes=[pltpu.VMEM((2, width, rank), jnp.bfloat16)],
            **common,
        )(me, activations, out_grads, *blocks)
        return result, None
    return pl.pallas_call(
        functools.partial(project_kernel, n, early, seqs),
        out_shape=(
            total,
            jax.ShapeDtypeStruct((2, tokens, width), activations.dtype),
        ),
        in_specs=[SMEM, HBM, HBM] + [VMEM] * len(early),
        out_specs=(VMEM, VMEM),
        scratch_shapes=[pltpu.SemaphoreType.DMA((2, 2 * seqs))],
        **common,
    )(me, pinned(activations), pinned(out_grads), *blocks)


def whiten_kernel(n, seqs, late, total_ref, k_ref, *rest):
    operands, (out_ref, white) = rest[:-2], rest[-2:]
    rank = k_ref.shape[1]
    sums = [total_ref[0], total_ref[1]]
    if late:
        me_ref, held, *blocks = operands
        source = sources(me_ref[0], n)
        rows = held.shape[2] // n
        for which, operand, at in late:
            columns = pl.ds(pl.multiple_of(source[which] * rows, rows), rows)
            for t in range(2):
                block = blocks[operand][(2 * at + t) * rows : (2 * at + t + 1) * rows, :]
                sums[t] = sums[t] + jnp.dot(held[t, :, columns], block, preferred_element_type=jnp.float32)
    length = total_ref.shape[1] // seqs
    share = rank // n
    for s in range(seqs):
        token = slice(s * length, (s + 1) * length)
        x_proj = (sums[0][token, :] * k_ref[2][:length, s : s + 1]).astype(jnp.bfloat16)
        d_proj = sums[1][token, :].astype(jnp.bfloat16)
        grads = lax.dot_general(d_proj, x_proj, (((0,), (0,)), ((), ())), preferred_element_type=jnp.float32)
        full = product(product(k_ref[1], grads), k_ref[0])
        for d in range(n):
            white[d, s * share : (s + 1) * share, :] = full[d * share : (d + 1) * share, :]
    out_ref[...] = white[...].astype(jnp.bfloat16)


def whitened_blocks(total, k, late, operands, seqs, n):
    rank = k.shape[1]
    shape = (n, seqs * (rank // n), rank)
    return pl.pallas_call(
        functools.partial(whiten_kernel, n, seqs, late),
        out_shape=jax.ShapeDtypeStruct(shape, jnp.bfloat16),
        in_specs=[VMEM, VMEM] + ([SMEM] + [VMEM] * (len(operands) - 1) if operands else []),
        out_specs=VMEM,
        scratch_shapes=[pltpu.VMEM(shape, jnp.float32)],
        compiler_params=pltpu.CompilerParams(vmem_limit_bytes=16 << 20),
        cost_estimate=pl.CostEstimate(flops=64 * rank**3, bytes_accessed=4 << 20, transcendentals=0),
        name="whiten",
    )(total, k, *operands)


def score_kernel(n, me_ref, ids_ref, white_ref, bank_ref, out_ref, spread):
    seqs = ids_ref.shape[0]
    chunk, rank = white_ref.shape[1:]
    share = chunk // seqs
    total = n * seqs
    spread[...] = white_ref[...].astype(jnp.float32).reshape(n * chunk, rank)
    columns = jnp.concatenate(
        [spread[pl.ds(j, total, stride=share), :].astype(jnp.bfloat16) for j in range(share)], axis=1
    )
    queries = bank_ref.shape[0] // n
    row = lax.broadcasted_iota(jnp.int32, (total, out_ref.shape[2] - queries), 0)
    tail = jnp.zeros(row.shape, jnp.float32)
    for s in range(seqs):
        tail = jnp.where(row == me_ref[0] * seqs + s, ids_ref[s].astype(jnp.float32), tail)
    partial = lax.dot_general(
        columns, bank_ref[...], (((1,), (1,)), ((), ())), preferred_element_type=jnp.float32
    )
    for d in range(n):
        out_ref[d, :, :queries] = partial[:, d * queries : (d + 1) * queries].astype(out_ref.dtype)
        out_ref[d, :, queries:] = tail.astype(out_ref.dtype)


def partial_scores(me, seq_ids, white, bank):
    n = white.shape[0]
    seqs = seq_ids.shape[0]
    queries = bank.shape[0] // n
    width = (queries // LANES + 1) * LANES
    return pl.pallas_call(
        functools.partial(score_kernel, n),
        out_shape=jax.ShapeDtypeStruct((n, n * seqs, width), jnp.bfloat16),
        in_specs=[SMEM, SMEM, VMEM, VMEM],
        out_specs=VMEM,
        scratch_shapes=[pltpu.VMEM((n * white.shape[1], white.shape[2]), jnp.float32)],
        compiler_params=pltpu.CompilerParams(vmem_limit_bytes=16 << 20),
        cost_estimate=pl.CostEstimate(
            flops=2 * n * seqs * bank.size, bytes_accessed=2 * bank.size, transcendentals=0
        ),
        name="score",
    )(me, seq_ids, white, bank)


def place_kernel(partial_ref, out_ref):
    rows, queries = out_ref.shape
    total = jnp.sum(partial_ref[...].astype(jnp.float32), axis=0)
    raw = total[:, :queries].astype(jnp.bfloat16)
    ids = total[:, queries : queries + 1].astype(jnp.int32)
    chosen = ids == lax.broadcasted_iota(jnp.int32, (rows, rows), 1)
    out_ref[...] = lax.dot_general(
        chosen.astype(jnp.bfloat16), raw, (((0,), (0,)), ((), ())), preferred_element_type=jnp.float32
    ).astype(jnp.bfloat16)


def place(partials, queries):
    return pl.pallas_call(
        lambda a, b: place_kernel(a, b),
        out_shape=jax.ShapeDtypeStruct((partials.shape[1], queries), jnp.bfloat16),
        in_specs=[VMEM],
        out_specs=VMEM,
        compiler_params=pltpu.CompilerParams(vmem_limit_bytes=16 << 20),
        name="place",
    )(partials)


def body(n, activations, out_grads, proj_in, proj_out, cov_in, cov_out, lengths, seq_ids, bank):
    me = lax.axis_index("coord").reshape(1)
    seqs, length, width = activations.shape
    activations, out_grads = activations.reshape(seqs * length, width), out_grads.reshape(seqs * length, width)
    a, b, c = factors(n)
    paired = a & (a - 1) == 0
    packed = pack(proj_in, proj_out)
    half = first_half(cov_in, cov_out)
    held = {(0, 0, 0): packed}
    for by in range(1, min(a, 3)):
        held[by, 0, 0] = moved(packed, 0, by, n)
    for by in range(1, b):
        held[0, by, 0] = moved(packed, 1, by, n)
    held, half = lax.optimization_barrier((held, half))
    for at in range(3, a):
        nearest = at & -at
        if paired and nearest != at:
            held[at, 0, 0] = moved(held[at - nearest, 0, 0], 0, nearest, n)
        else:
            held[at, 0, 0] = moved(held[0, 0, 0], 0, at, n)
    for at in range(2, a - 1):
        for by in range(1, b):
            held[at, by, 0] = moved(held[at, 0, 0], 1, by, n)
    held = lax.optimization_barrier(held)
    for at in sorted({1, a - 1} & set(range(1, a))):
        for by in range(1, b):
            nearest = at & -at
            if paired and nearest != at:
                held[at, by, 0] = moved(held[at - nearest, by, 0], 0, nearest, n)
            else:
                held[at, by, 0] = moved(held[at, 0, 0], 1, by, n)
    tied = (a - 1, b - 1, 0)
    k = second_half(half, lengths)
    held[tied], k = lax.optimization_barrier((held[tied], k))
    order = [(at, by, core) for core in range(c) for by in range(b) for at in range(a)]
    if proj_in.shape[0] % LANES == 0 and a > 2 and b > 1 and c == 2:
        own = [at for at in order if at[2] == 0]
        across = moved(merge([held[at] for at in own]), 2, 1, n)
        total, inputs = project(
            me, activations, out_grads, [held[at] for at in own], [order.index(at) for at in own], seqs, n
        )
        operands = [me, inputs, across]
        late = [(order.index((*at[:2], 1)), 0, i) for i, at in enumerate(own)]
    else:
        for at in list(held):
            for by in range(1, c):
                held[at[0], at[1], by] = moved(held[at], 2, by, n)
        total = project(me, activations, out_grads, [held[at] for at in order], list(range(n)), seqs, n)[0]
        operands, late = [], []
    white = whitened_blocks(total, k, late, operands, seqs, n)
    white = lax.all_to_all(white, "coord", split_axis=0, concat_axis=0, tiled=True)
    partials = partial_scores(me, seq_ids, white, bank)
    partials = lax.all_to_all(partials, "coord", split_axis=0, concat_axis=0, tiled=True)
    return place(partials, bank.shape[0] // n)


def solution(mesh):
    in_specs = (
        P(("groups", "coord"), None, None),
        P(("groups", "coord"), None, None),
        P("coord", None),
        P("coord", None),
        P(),
        P(),
        P(("groups", "coord")),
        P(("groups", "coord")),
        P(None, "coord"),
    )
    out_specs = P("groups", "coord")
    return jax.shard_map(
        functools.partial(body, mesh.shape["coord"]),
        mesh=mesh,
        in_specs=in_specs,
        out_specs=out_specs,
        check_vma=False,
    )
```

```python
import functools

import jax
import jax.numpy as jnp
from jax import lax
from jax.experimental import pallas as pl
from jax.experimental.pallas import tpu as pltpu
from jax.sharding import PartitionSpec as P

SUB = 8
LANES = 128
EXACT = lax.Precision.HIGHEST
VMEM = pl.BlockSpec(memory_space=pltpu.VMEM)
HBM = pl.BlockSpec(memory_space=pltpu.HBM)
SMEM = pl.BlockSpec(memory_space=pltpu.SMEM)


def factors(n):
    c = 2 if n % 2 == 0 else 1
    rest = n // c
    b = max(f for f in range(1, rest + 1) if rest % f == 0 and f * f <= rest)
    return rest // b, b, c


def partner(at, by, size, towards):
    if size & (size - 1) == 0:
        return at ^ by
    return (at + (by if towards else size - by)) % size


def sources(me, n):
    a, b, c = factors(n)
    ia, ib, ic = me // (b * c), (me // c) % b, me % c
    return [
        (partner(ia, da, a, False) * b + partner(ib, db, b, False)) * c + partner(ic, dc, c, False)
        for dc in range(c)
        for db in range(b)
        for da in range(a)
    ]


def moved(value, axis, by, n):
    sizes = factors(n)
    a, b, c = sizes
    pairs = []
    for me in range(n):
        at = [me // (b * c), (me // c) % b, me % c]
        at[axis] = partner(at[axis], by, sizes[axis], True)
        pairs.append((me, (at[0] * b + at[1]) * c + at[2]))
    return lax.ppermute(value, "coord", pairs)


def pack_kernel(first_hbm, second_hbm, out_ref, sems):
    rows = first_hbm.shape[0]
    copies = [
        pltpu.make_async_copy(source, out_ref.at[pl.ds(i * rows, rows)], sems.at[i])
        for i, source in enumerate((first_hbm, second_hbm))
    ]
    for copy in copies:
        copy.start()
    for copy in copies:
        copy.wait()


def pack(first, second):
    rows, columns = first.shape
    return pl.pallas_call(
        pack_kernel,
        out_shape=jax.ShapeDtypeStruct((2 * rows, columns), first.dtype),
        in_specs=[HBM, HBM],
        out_specs=VMEM,
        scratch_shapes=[pltpu.SemaphoreType.DMA((2,))],
        compiler_params=pltpu.CompilerParams(vmem_limit_bytes=8 << 20),
        name="pack",
    )(pinned(first), pinned(second))


def pinned(value):
    return pltpu.with_memory_space_constraint(value, pltpu.HBM)


def gauss_jordan(blocks):
    width = blocks[0].shape[1]
    half = width // 2
    lane = lax.broadcasted_iota(jnp.int32, (SUB, width), 1)
    sub = lax.broadcasted_iota(jnp.int32, (SUB, width), 0)
    start, within = lane // half * half, lane % half

    def column(block, at):
        return jnp.take_along_axis(block, start + at, axis=1, mode="promise_in_bounds")

    for k in range(len(blocks)):
        at = k * SUB
        head = within // SUB == k
        rows = [jnp.broadcast_to(blocks[k][i : i + 1, :], (SUB, width)) for i in range(SUB)]
        diag = {(i, j): column(rows[i], at + j) for i in range(SUB) for j in range(i, SUB)}
        rows = [jnp.where(head, (within == at + i).astype(jnp.float32), rows[i]) for i in range(SUB)]
        inverse, factor = [], {}
        for p in range(SUB):
            inverse.append(1.0 / diag[p, p])
            for i in range(p + 1, SUB):
                factor[p, i] = diag[p, i] * inverse[p]
                for j in range(i, SUB):
                    diag[i, j] = diag[i, j] - factor[p, i] * diag[p, j]
                rows[i] = rows[i] - factor[p, i] * rows[p]
        rows = [rows[p] * inverse[p] for p in range(SUB)]
        for p in reversed(range(SUB)):
            for i in range(p):
                rows[i] = rows[i] - factor[i, p] * rows[p]
        done = rows[0]
        for i in range(1, SUB):
            done = jnp.where(sub == i, rows[i], done)
        out = []
        for g, block in enumerate(blocks):
            if g == k:
                out.append(done)
                continue
            terms = [column(block, at + p) * rows[p] for p in range(SUB)]
            while len(terms) > 1:
                terms = [terms[i] + terms[i + 1] for i in range(0, len(terms), 2)]
            out.append(jnp.where(head, 0.0, block) - terms[0])
        blocks = out
    return blocks


def side_by_side_inverses(first, second):
    half = first.shape[0]
    both = jnp.concatenate([first, second], axis=1)
    blocks = gauss_jordan([both[g : g + SUB, :] for g in range(0, half, SUB)])
    both = jnp.concatenate(blocks, axis=0)
    return both[:, :half], both[:, half:]


def damped(cov):
    size = cov.shape[0]
    cov = 0.5 * (cov + cov.T)
    row = lax.broadcasted_iota(jnp.int32, (size, size), 0)
    col = lax.broadcasted_iota(jnp.int32, (size, size), 1)
    damping = 0.1 * jnp.sum(jnp.where(row == col, cov, 0.0)) / size
    return jnp.where(row == col, cov + damping, cov)


def product(left, right, dims=((1,), (0,))):
    return lax.dot_general(left, right, (dims, ((), ())), precision=EXACT, preferred_element_type=jnp.float32)


def first_half_kernel(cov_in_hbm, cov_out_hbm, out_ref, cov_ref, sems):
    copies = [
        pltpu.make_async_copy(source, cov_ref.at[i], sems.at[i]) for i, source in enumerate((cov_in_hbm, cov_out_hbm))
    ]
    for copy in copies:
        copy.start()
    for copy in copies:
        copy.wait()
    half = cov_ref.shape[1] // 2
    covs = [damped(cov_ref[0]), damped(cov_ref[1])]
    corner = [cov[:half, half:] for cov in covs]
    upper = side_by_side_inverses(*[cov[:half, :half] for cov in covs])
    solved = [product(u, c) for u, c in zip(upper, corner)]
    schur = [cov[half:, half:] - product(c, t, ((0,), (0,))) for cov, c, t in zip(covs, corner, solved)]
    for i, pair in enumerate((upper, solved, schur)):
        out_ref[i] = jnp.concatenate(pair, axis=1)


def second_half_kernel(first_ref, len_hbm, k_ref, len_ref, sem):
    copy = pltpu.make_async_copy(len_hbm, len_ref, sem)
    copy.start()
    size = k_ref.shape[1]
    half = size // 2
    upper, solved, schur = [(first_ref[i][:, :half], first_ref[i][:, half:]) for i in range(3)]
    lower = side_by_side_inverses(*schur)
    for m, (u, t, low) in enumerate(zip(upper, solved, lower)):
        side = product(t, low)
        k_ref[m, :half, :half] = u + product(side, t, ((1,), (1,)))
        k_ref[m, :half, half:] = -side
        k_ref[m, half:, :half] = -side.T
        k_ref[m, half:, half:] = low
    copy.wait()
    token = lax.broadcasted_iota(jnp.int32, (size, size), 0)
    lane = lax.broadcasted_iota(jnp.int32, (size, size), 1)
    mask = jnp.zeros((size, size), jnp.float32)
    for s in range(len_ref.shape[0]):
        mask = jnp.where((lane == s) & (token < len_ref[s]), 1.0, mask)
    k_ref[2] = mask


def first_half(cov_in, cov_out):
    size = cov_in.shape[0]
    return pl.pallas_call(
        first_half_kernel,
        out_shape=jax.ShapeDtypeStruct((3, size // 2, size), jnp.float32),
        in_specs=[HBM, HBM],
        out_specs=VMEM,
        scratch_shapes=[pltpu.VMEM((2, size, size), jnp.float32), pltpu.SemaphoreType.DMA((2,))],
        compiler_params=pltpu.CompilerParams(vmem_limit_bytes=8 << 20),
        cost_estimate=pl.CostEstimate(flops=size, bytes_accessed=size, transcendentals=0),
        name="first_half",
    )(pinned(cov_in), pinned(cov_out))


def second_half(first, lengths):
    size = first.shape[2]
    return pl.pallas_call(
        second_half_kernel,
        out_shape=jax.ShapeDtypeStruct((3, size, size), jnp.float32),
        in_specs=[VMEM, HBM],
        out_specs=VMEM,
        scratch_shapes=[pltpu.SMEM(lengths.shape, jnp.int32), pltpu.SemaphoreType.DMA],
        compiler_params=pltpu.CompilerParams(vmem_limit_bytes=8 << 20),
        cost_estimate=pl.CostEstimate(flops=2 * size**3, bytes_accessed=12 << 20, transcendentals=0),
        name="second_half",
    )(first, pinned(lengths))


def stages(n):
    a, b, c = factors(n)
    inner = [[high * b * c + low for low in range(b * c)] for high in range(a)]
    outer = [[high * b * c + low for high in range(a)] for low in range(b * c)]
    return inner, outer


def exchanged(value, groups):
    return lax.all_to_all(value, "coord", split_axis=0, concat_axis=0, axis_index_groups=groups, tiled=True)


def turn_kernel(in_ref, out_ref):
    for i in range(in_ref.shape[0]):
        for j in range(in_ref.shape[1]):
            out_ref[j, i] = in_ref[i, j]


def turn(value):
    return pl.pallas_call(
        turn_kernel,
        out_shape=jax.ShapeDtypeStruct((value.shape[1], value.shape[0], *value.shape[2:]), value.dtype),
        in_specs=[VMEM],
        out_specs=VMEM,
        compiler_params=pltpu.CompilerParams(vmem_limit_bytes=8 << 20),
        name="turn",
    )(value)


def add_kernel(in_ref, out_ref):
    total = in_ref[0].astype(jnp.float32)
    for i in range(1, in_ref.shape[0]):
        total = total + in_ref[i].astype(jnp.float32)
    out_ref[...] = total


def add(value):
    return pl.pallas_call(
        add_kernel,
        out_shape=jax.ShapeDtypeStruct(value.shape[1:], jnp.float32),
        in_specs=[VMEM],
        out_specs=VMEM,
        compiler_params=pltpu.CompilerParams(vmem_limit_bytes=16 << 20),
        name="add",
    )(value)


def merge_kernel(*refs):
    rows = refs[0].shape[0]
    for i, ref in enumerate(refs[:-1]):
        refs[-1][i * rows : (i + 1) * rows, :] = ref[...]


def merge(blocks):
    rows, columns = blocks[0].shape
    return pl.pallas_call(
        merge_kernel,
        out_shape=jax.ShapeDtypeStruct((len(blocks) * rows, columns), blocks[0].dtype),
        in_specs=[VMEM] * len(blocks),
        out_specs=VMEM,
        compiler_params=pltpu.CompilerParams(vmem_limit_bytes=8 << 20),
        cost_estimate=pl.CostEstimate(flops=rows, bytes_accessed=rows, transcendentals=0),
        name="merge",
    )(*blocks)


def project_kernel(n, early, seqs, me_ref, *rest):
    inputs, blocks, (total_ref, held, sems) = rest[:2], rest[2 : 2 + len(early)], rest[2 + len(early) :]
    tokens = held.shape[1]
    part = tokens // sems.shape[1]
    copies = [
        [
            pltpu.make_async_copy(source.at[pl.ds(i * part, part)], held.at[t, pl.ds(i * part, part)], sems.at[t, i])
            for i in range(sems.shape[1])
        ]
        for t, source in enumerate(inputs)
    ]
    for copy in copies[0] + copies[1]:
        copy.start()
    rows = blocks[0].shape[0] // 2
    source = sources(me_ref[0], n)
    for t in range(2):
        for copy in copies[t]:
            copy.wait()
        total = None
        for which, block in zip(early, blocks):
            columns = pl.ds(pl.multiple_of(source[which] * rows, rows), rows)
            term = jnp.dot(
                held[t, :, columns], block[t * rows : (t + 1) * rows, :], preferred_element_type=jnp.float32
            )
            total = term if total is None else total + term
        total_ref[t] = total


def project_whole_kernel(n, me_ref, act_ref, grad_ref, *rest):
    blocks, (total_ref, proj) = rest[:n], rest[n:]
    rows = blocks[0].shape[0] // 2
    for block, source in zip(blocks, sources(me_ref[0], n)):
        at = pl.ds(pl.multiple_of(source * rows, rows), rows)
        for t in range(2):
            proj[t, at, :] = block[t * rows : (t + 1) * rows, :]
    for t, ref in enumerate((act_ref, grad_ref)):
        total_ref[t] = jnp.dot(ref[...], proj[t], preferred_element_type=jnp.float32)


def project(me, activations, out_grads, blocks, early, seqs, n):
    tokens, width = activations.shape
    rank = blocks[0].shape[1]
    total = jax.ShapeDtypeStruct((2, tokens, rank), jnp.float32)
    common = dict(
        compiler_params=pltpu.CompilerParams(vmem_limit_bytes=16 << 20),
        cost_estimate=pl.CostEstimate(flops=rank, bytes_accessed=rank, transcendentals=0),
        name="project",
    )
    if len(early) == n:
        result = pl.pallas_call(
            functools.partial(project_whole_kernel, n),
            out_shape=total,
            in_specs=[SMEM] + [VMEM] * (2 + n),
            out_specs=VMEM,
            scratch_shapes=[pltpu.VMEM((2, width, rank), jnp.bfloat16)],
            **common,
        )(me, activations, out_grads, *blocks)
        return result, None
    return pl.pallas_call(
        functools.partial(project_kernel, n, early, seqs),
        out_shape=(
            total,
            jax.ShapeDtypeStruct((2, tokens, width), activations.dtype),
        ),
        in_specs=[SMEM, HBM, HBM] + [VMEM] * len(early),
        out_specs=(VMEM, VMEM),
        scratch_shapes=[pltpu.SemaphoreType.DMA((2, 2 * seqs))],
        **common,
    )(me, pinned(activations), pinned(out_grads), *blocks)


def whiten_kernel(n, seqs, late, total_ref, k_ref, *rest):
    operands, (out_ref, white) = rest[:-2], rest[-2:]
    rank = k_ref.shape[1]
    sums = [total_ref[0], total_ref[1]]
    if late:
        me_ref, held, *blocks = operands
        source = sources(me_ref[0], n)
        rows = held.shape[2] // n
        for which, operand, at in late:
            columns = pl.ds(pl.multiple_of(source[which] * rows, rows), rows)
            for t in range(2):
                block = blocks[operand][(2 * at + t) * rows : (2 * at + t + 1) * rows, :]
                sums[t] = sums[t] + jnp.dot(held[t, :, columns], block, preferred_element_type=jnp.float32)
    length = total_ref.shape[1] // seqs
    share = rank // n
    low = white.shape[0]
    for s in range(seqs):
        token = slice(s * length, (s + 1) * length)
        x_proj = (sums[0][token, :] * k_ref[2][:length, s : s + 1]).astype(jnp.bfloat16)
        d_proj = sums[1][token, :].astype(jnp.bfloat16)
        grads = lax.dot_general(d_proj, x_proj, (((0,), (0,)), ((), ())), preferred_element_type=jnp.float32)
        full = product(product(k_ref[1], grads), k_ref[0])
        for d in range(n):
            white[d % low, d // low, s * share : (s + 1) * share, :] = full[d * share : (d + 1) * share, :]
    out_ref[...] = white[...].astype(jnp.bfloat16)


def whitened_blocks(total, k, late, operands, seqs, n):
    rank = k.shape[1]
    a, b, c = factors(n)
    shape = (b * c, a, seqs * (rank // n), rank)
    return pl.pallas_call(
        functools.partial(whiten_kernel, n, seqs, late),
        out_shape=jax.ShapeDtypeStruct(shape, jnp.bfloat16),
        in_specs=[VMEM, VMEM] + ([SMEM] + [VMEM] * (len(operands) - 1) if operands else []),
        out_specs=VMEM,
        scratch_shapes=[pltpu.VMEM(shape, jnp.float32)],
        compiler_params=pltpu.CompilerParams(vmem_limit_bytes=16 << 20),
        cost_estimate=pl.CostEstimate(flops=64 * rank**3, bytes_accessed=4 << 20, transcendentals=0),
        name="whiten",
    )(total, k, *operands)


def score_kernel(n, me_ref, ids_ref, white_ref, bank_ref, out_ref, spread):
    seqs = ids_ref.shape[0]
    chunk, rank = white_ref.shape[1:]
    share = chunk // seqs
    total = n * seqs
    spread[...] = white_ref[...].astype(jnp.float32).reshape(n * chunk, rank)
    columns = jnp.concatenate(
        [spread[pl.ds(j, total, stride=share), :].astype(jnp.bfloat16) for j in range(share)], axis=1
    )
    queries = bank_ref.shape[0] // n
    low = out_ref.shape[0]
    row = lax.broadcasted_iota(jnp.int32, (total, out_ref.shape[3] - queries), 0)
    tail = jnp.zeros(row.shape, jnp.float32)
    for s in range(seqs):
        tail = jnp.where(row == me_ref[0] * seqs + s, ids_ref[s].astype(jnp.float32), tail)
    partial = lax.dot_general(
        columns, bank_ref[...], (((1,), (1,)), ((), ())), preferred_element_type=jnp.float32
    )
    for d in range(n):
        at = d % low, d // low
        out_ref[*at, :, :queries] = partial[:, d * queries : (d + 1) * queries].astype(out_ref.dtype)
        out_ref[*at, :, queries:] = tail.astype(out_ref.dtype)


def partial_scores(me, seq_ids, white, bank):
    n = white.shape[0]
    seqs = seq_ids.shape[0]
    queries = bank.shape[0] // n
    width = (queries // LANES + 1) * LANES
    a, b, c = factors(n)
    return pl.pallas_call(
        functools.partial(score_kernel, n),
        out_shape=jax.ShapeDtypeStruct((b * c, a, n * seqs, width), jnp.bfloat16),
        in_specs=[SMEM, SMEM, VMEM, VMEM],
        out_specs=VMEM,
        scratch_shapes=[pltpu.VMEM((n * white.shape[1], white.shape[2]), jnp.float32)],
        compiler_params=pltpu.CompilerParams(vmem_limit_bytes=16 << 20),
        cost_estimate=pl.CostEstimate(
            flops=2 * n * seqs * bank.size, bytes_accessed=2 * bank.size, transcendentals=0
        ),
        name="score",
    )(me, seq_ids, white, bank)


def place_kernel(partial_ref, out_ref):
    rows, queries = out_ref.shape
    total = jnp.sum(partial_ref[...].astype(jnp.float32), axis=0)
    raw = total[:, :queries].astype(jnp.bfloat16)
    ids = total[:, queries : queries + 1].astype(jnp.int32)
    chosen = ids == lax.broadcasted_iota(jnp.int32, (rows, rows), 1)
    out_ref[...] = lax.dot_general(
        chosen.astype(jnp.bfloat16), raw, (((0,), (0,)), ((), ())), preferred_element_type=jnp.float32
    ).astype(jnp.bfloat16)


def place(partials, queries):
    return pl.pallas_call(
        lambda a, b: place_kernel(a, b),
        out_shape=jax.ShapeDtypeStruct((partials.shape[1], queries), jnp.bfloat16),
        in_specs=[VMEM],
        out_specs=VMEM,
        compiler_params=pltpu.CompilerParams(vmem_limit_bytes=16 << 20),
        name="place",
    )(partials)


def body(n, activations, out_grads, proj_in, proj_out, cov_in, cov_out, lengths, seq_ids, bank):
    me = lax.axis_index("coord").reshape(1)
    seqs, length, width = activations.shape
    activations, out_grads = activations.reshape(seqs * length, width), out_grads.reshape(seqs * length, width)
    a, b, c = factors(n)
    paired = a & (a - 1) == 0
    packed = pack(proj_in, proj_out)
    half = first_half(cov_in, cov_out)
    held = {(0, 0, 0): packed}
    for by in range(1, min(a, 3)):
        held[by, 0, 0] = moved(packed, 0, by, n)
    for by in range(1, b):
        held[0, by, 0] = moved(packed, 1, by, n)
    held, half = lax.optimization_barrier((held, half))
    for at in range(3, a):
        nearest = at & -at
        if paired and nearest != at:
            held[at, 0, 0] = moved(held[at - nearest, 0, 0], 0, nearest, n)
        else:
            held[at, 0, 0] = moved(held[0, 0, 0], 0, at, n)
    for at in range(2, a - 1):
        for by in range(1, b):
            held[at, by, 0] = moved(held[at, 0, 0], 1, by, n)
    held = lax.optimization_barrier(held)
    for at in sorted({1, a - 1} & set(range(1, a))):
        for by in range(1, b):
            nearest = at & -at
            if paired and nearest != at:
                held[at, by, 0] = moved(held[at - nearest, by, 0], 0, nearest, n)
            else:
                held[at, by, 0] = moved(held[at, 0, 0], 1, by, n)
    tied = (a - 1, b - 1, 0)
    k = second_half(half, lengths)
    held[tied], k = lax.optimization_barrier((held[tied], k))
    order = [(at, by, core) for core in range(c) for by in range(b) for at in range(a)]
    if proj_in.shape[0] % LANES == 0 and a > 2 and b > 1 and c == 2:
        own = [at for at in order if at[2] == 0]
        across = moved(merge([held[at] for at in own]), 2, 1, n)
        total, inputs = project(
            me, activations, out_grads, [held[at] for at in own], [order.index(at) for at in own], seqs, n
        )
        operands = [me, inputs, across]
        late = [(order.index((*at[:2], 1)), 0, i) for i, at in enumerate(own)]
    else:
        for at in list(held):
            for by in range(1, c):
                held[at[0], at[1], by] = moved(held[at], 2, by, n)
        total = project(me, activations, out_grads, [held[at] for at in order], list(range(n)), seqs, n)[0]
        operands, late = [], []
    white = whitened_blocks(total, k, late, operands, seqs, n)
    inner, outer = stages(n)
    white = exchanged(turn(exchanged(white, inner)), outer)
    white = white.reshape(n, *white.shape[2:])
    partials = partial_scores(me, seq_ids, white, bank)
    partials = exchanged(add(exchanged(partials, inner)), outer)
    return place(partials, bank.shape[0] // n)


def solution(mesh):
    in_specs = (
        P(("groups", "coord"), None, None),
        P(("groups", "coord"), None, None),
        P("coord", None),
        P("coord", None),
        P(),
        P(),
        P(("groups", "coord")),
        P(("groups", "coord")),
        P(None, "coord"),
    )
    out_specs = P("groups", "coord")
    return jax.shard_map(
        functools.partial(body, mesh.shape["coord"]),
        mesh=mesh,
        in_specs=in_specs,
        out_specs=out_specs,
        check_vma=False,
    )
```

```python
import functools

import jax
import jax.numpy as jnp
from jax import lax
from jax.experimental import pallas as pl
from jax.experimental.pallas import tpu as pltpu
from jax.sharding import PartitionSpec as P

SUB = 8
LANES = 128
EXACT = lax.Precision.HIGHEST
VMEM = pl.BlockSpec(memory_space=pltpu.VMEM)
HBM = pl.BlockSpec(memory_space=pltpu.HBM)
SMEM = pl.BlockSpec(memory_space=pltpu.SMEM)


def factors(n):
    c = 2 if n % 2 == 0 else 1
    rest = n // c
    b = max(f for f in range(1, rest + 1) if rest % f == 0 and f * f <= rest)
    return rest // b, b, c


def partner(at, by, size, towards):
    if size & (size - 1) == 0:
        return at ^ by
    return (at + (by if towards else size - by)) % size


def sources(me, n):
    a, b, c = factors(n)
    ia, ib, ic = me // (b * c), (me // c) % b, me % c
    return [
        (partner(ia, da, a, False) * b + partner(ib, db, b, False)) * c + partner(ic, dc, c, False)
        for dc in range(c)
        for db in range(b)
        for da in range(a)
    ]


def moved(value, axis, by, n):
    sizes = factors(n)
    a, b, c = sizes
    pairs = []
    for me in range(n):
        at = [me // (b * c), (me // c) % b, me % c]
        at[axis] = partner(at[axis], by, sizes[axis], True)
        pairs.append((me, (at[0] * b + at[1]) * c + at[2]))
    return lax.ppermute(value, "coord", pairs)


def pack_kernel(first_hbm, second_hbm, out_ref, sems):
    rows = first_hbm.shape[0]
    copies = [
        pltpu.make_async_copy(source, out_ref.at[pl.ds(i * rows, rows)], sems.at[i])
        for i, source in enumerate((first_hbm, second_hbm))
    ]
    for copy in copies:
        copy.start()
    for copy in copies:
        copy.wait()


def pack(first, second):
    rows, columns = first.shape
    return pl.pallas_call(
        pack_kernel,
        out_shape=jax.ShapeDtypeStruct((2 * rows, columns), first.dtype),
        in_specs=[HBM, HBM],
        out_specs=VMEM,
        scratch_shapes=[pltpu.SemaphoreType.DMA((2,))],
        compiler_params=pltpu.CompilerParams(vmem_limit_bytes=8 << 20),
        name="pack",
    )(pinned(first), pinned(second))


def pinned(value):
    return pltpu.with_memory_space_constraint(value, pltpu.HBM)


def gauss_jordan(blocks):
    width = blocks[0].shape[1]
    half = width // 2
    lane = lax.broadcasted_iota(jnp.int32, (SUB, width), 1)
    sub = lax.broadcasted_iota(jnp.int32, (SUB, width), 0)
    start, within = lane // half * half, lane % half

    def column(block, at):
        return jnp.take_along_axis(block, start + at, axis=1, mode="promise_in_bounds")

    for k in range(len(blocks)):
        at = k * SUB
        head = within // SUB == k
        rows = [jnp.broadcast_to(blocks[k][i : i + 1, :], (SUB, width)) for i in range(SUB)]
        diag = {(i, j): column(rows[i], at + j) for i in range(SUB) for j in range(i, SUB)}
        rows = [jnp.where(head, (within == at + i).astype(jnp.float32), rows[i]) for i in range(SUB)]
        inverse, factor = [], {}
        for p in range(SUB):
            inverse.append(1.0 / diag[p, p])
            for i in range(p + 1, SUB):
                factor[p, i] = diag[p, i] * inverse[p]
                for j in range(i, SUB):
                    diag[i, j] = diag[i, j] - factor[p, i] * diag[p, j]
                rows[i] = rows[i] - factor[p, i] * rows[p]
        rows = [rows[p] * inverse[p] for p in range(SUB)]
        for p in reversed(range(SUB)):
            for i in range(p):
                rows[i] = rows[i] - factor[i, p] * rows[p]
        done = rows[0]
        for i in range(1, SUB):
            done = jnp.where(sub == i, rows[i], done)
        out = []
        for g, block in enumerate(blocks):
            if g == k:
                out.append(done)
                continue
            terms = [column(block, at + p) * rows[p] for p in range(SUB)]
            while len(terms) > 1:
                terms = [terms[i] + terms[i + 1] for i in range(0, len(terms), 2)]
            out.append(jnp.where(head, 0.0, block) - terms[0])
        blocks = out
    return blocks


def side_by_side_inverses(first, second):
    half = first.shape[0]
    both = jnp.concatenate([first, second], axis=1)
    blocks = gauss_jordan([both[g : g + SUB, :] for g in range(0, half, SUB)])
    both = jnp.concatenate(blocks, axis=0)
    return both[:, :half], both[:, half:]


def damped(cov):
    size = cov.shape[0]
    cov = 0.5 * (cov + cov.T)
    row = lax.broadcasted_iota(jnp.int32, (size, size), 0)
    col = lax.broadcasted_iota(jnp.int32, (size, size), 1)
    damping = 0.1 * jnp.sum(jnp.where(row == col, cov, 0.0)) / size
    return jnp.where(row == col, cov + damping, cov)


def product(left, right, dims=((1,), (0,))):
    return lax.dot_general(left, right, (dims, ((), ())), precision=EXACT, preferred_element_type=jnp.float32)


def first_half_kernel(cov_in_hbm, cov_out_hbm, out_ref, cov_ref, sems):
    copies = [
        pltpu.make_async_copy(source, cov_ref.at[i], sems.at[i]) for i, source in enumerate((cov_in_hbm, cov_out_hbm))
    ]
    for copy in copies:
        copy.start()
    for copy in copies:
        copy.wait()
    half = cov_ref.shape[1] // 2
    covs = [damped(cov_ref[0]), damped(cov_ref[1])]
    corner = [cov[:half, half:] for cov in covs]
    upper = side_by_side_inverses(*[cov[:half, :half] for cov in covs])
    solved = [product(u, c) for u, c in zip(upper, corner)]
    schur = [cov[half:, half:] - product(c, t, ((0,), (0,))) for cov, c, t in zip(covs, corner, solved)]
    for i, pair in enumerate((upper, solved, schur)):
        out_ref[i] = jnp.concatenate(pair, axis=1)


def second_half_kernel(first_ref, len_hbm, act_hbm, grad_hbm, k_ref, held, len_ref, sem, sems):
    copy = pltpu.make_async_copy(len_hbm, len_ref, sem)
    copy.start()
    part = held.shape[1] // sems.shape[1]
    copies = [
        pltpu.make_async_copy(source.at[pl.ds(i * part, part)], held.at[t, pl.ds(i * part, part)], sems.at[t, i])
        for t, source in enumerate((act_hbm, grad_hbm))
        for i in range(sems.shape[1])
    ]
    for held_copy in copies:
        held_copy.start()
    size = k_ref.shape[1]
    half = size // 2
    upper, solved, schur = [(first_ref[i][:, :half], first_ref[i][:, half:]) for i in range(3)]
    lower = side_by_side_inverses(*schur)
    for m, (u, t, low) in enumerate(zip(upper, solved, lower)):
        side = product(t, low)
        k_ref[m, :half, :half] = u + product(side, t, ((1,), (1,)))
        k_ref[m, :half, half:] = -side
        k_ref[m, half:, :half] = -side.T
        k_ref[m, half:, half:] = low
    copy.wait()
    token = lax.broadcasted_iota(jnp.int32, (size, size), 0)
    lane = lax.broadcasted_iota(jnp.int32, (size, size), 1)
    mask = jnp.zeros((size, size), jnp.float32)
    for s in range(len_ref.shape[0]):
        mask = jnp.where((lane == s) & (token < len_ref[s]), 1.0, mask)
    k_ref[2] = mask
    for held_copy in copies:
        held_copy.wait()


def first_half(cov_in, cov_out):
    size = cov_in.shape[0]
    return pl.pallas_call(
        first_half_kernel,
        out_shape=jax.ShapeDtypeStruct((3, size // 2, size), jnp.float32),
        in_specs=[HBM, HBM],
        out_specs=VMEM,
        scratch_shapes=[pltpu.VMEM((2, size, size), jnp.float32), pltpu.SemaphoreType.DMA((2,))],
        compiler_params=pltpu.CompilerParams(vmem_limit_bytes=8 << 20),
        cost_estimate=pl.CostEstimate(flops=size, bytes_accessed=size, transcendentals=0),
        name="first_half",
    )(pinned(cov_in), pinned(cov_out))


def second_half(first, lengths, activations, out_grads):
    size = first.shape[2]
    return pl.pallas_call(
        second_half_kernel,
        out_shape=(
            jax.ShapeDtypeStruct((3, size, size), jnp.float32),
            jax.ShapeDtypeStruct((2, *activations.shape), activations.dtype),
        ),
        in_specs=[VMEM, HBM, HBM, HBM],
        out_specs=(VMEM, VMEM),
        scratch_shapes=[
            pltpu.SMEM(lengths.shape, jnp.int32),
            pltpu.SemaphoreType.DMA,
            pltpu.SemaphoreType.DMA((2, 4)),
        ],
        compiler_params=pltpu.CompilerParams(vmem_limit_bytes=16 << 20),
        cost_estimate=pl.CostEstimate(flops=2 * size**3, bytes_accessed=12 << 20, transcendentals=0),
        name="second_half",
    )(first, pinned(lengths), pinned(activations), pinned(out_grads))


def merge_kernel(*refs):
    rows = refs[0].shape[0]
    for i, ref in enumerate(refs[:-1]):
        refs[-1][i * rows : (i + 1) * rows, :] = ref[...]


def merge(blocks):
    rows, columns = blocks[0].shape
    return pl.pallas_call(
        merge_kernel,
        out_shape=jax.ShapeDtypeStruct((len(blocks) * rows, columns), blocks[0].dtype),
        in_specs=[VMEM] * len(blocks),
        out_specs=VMEM,
        compiler_params=pltpu.CompilerParams(vmem_limit_bytes=8 << 20),
        cost_estimate=pl.CostEstimate(flops=rows, bytes_accessed=rows, transcendentals=0),
        name="merge",
    )(*blocks)


def project_kernel(n, own, me_ref, held, *rest):
    blocks, total_ref = rest[:-1], rest[-1]
    rows = blocks[0].shape[0] // 2
    source = sources(me_ref[0], n)
    for t in range(2):
        total = None
        for which, block in zip(own, blocks):
            columns = pl.ds(pl.multiple_of(source[which] * rows, rows), rows)
            term = jnp.dot(
                held[t, :, columns], block[t * rows : (t + 1) * rows, :], preferred_element_type=jnp.float32
            )
            total = term if total is None else total + term
        total_ref[t] = total


def project_whole_kernel(n, me_ref, held, *rest):
    blocks, (total_ref, proj) = rest[:n], rest[n:]
    rows = blocks[0].shape[0] // 2
    for block, source in zip(blocks, sources(me_ref[0], n)):
        at = pl.ds(pl.multiple_of(source * rows, rows), rows)
        for t in range(2):
            proj[t, at, :] = block[t * rows : (t + 1) * rows, :]
    for t in range(2):
        total_ref[t] = jnp.dot(held[t], proj[t], preferred_element_type=jnp.float32)


def project(me, inputs, blocks, own, n):
    _, tokens, width = inputs.shape
    rank = blocks[0].shape[1]
    whole = len(own) == n
    return pl.pallas_call(
        functools.partial(project_whole_kernel, n) if whole else functools.partial(project_kernel, n, own),
        out_shape=jax.ShapeDtypeStruct((2, tokens, rank), jnp.float32),
        in_specs=[SMEM] + [VMEM] * (1 + len(own)),
        out_specs=VMEM,
        scratch_shapes=[pltpu.VMEM((2, width, rank), jnp.bfloat16)] if whole else [],
        compiler_params=pltpu.CompilerParams(vmem_limit_bytes=16 << 20),
        cost_estimate=pl.CostEstimate(
            flops=4 * tokens * width * rank, bytes_accessed=4 * tokens * width, transcendentals=0
        ),
        name="project",
    )(me, inputs, *blocks)


def whiten_kernel(n, seqs, late, total_ref, k_ref, *rest):
    operands, (out_ref, white) = rest[:-2], rest[-2:]
    rank = k_ref.shape[1]
    sums = [total_ref[0], total_ref[1]]
    if late:
        me_ref, held, *blocks = operands
        source = sources(me_ref[0], n)
        rows = held.shape[2] // n
        for which, operand, at in late:
            columns = pl.ds(pl.multiple_of(source[which] * rows, rows), rows)
            for t in range(2):
                block = blocks[operand][(2 * at + t) * rows : (2 * at + t + 1) * rows, :]
                sums[t] = sums[t] + jnp.dot(held[t, :, columns], block, preferred_element_type=jnp.float32)
    length = total_ref.shape[1] // seqs
    share = rank // n
    grads = []
    for s in range(seqs):
        token = slice(s * length, (s + 1) * length)
        x_proj = (sums[0][token, :] * k_ref[2][:length, s : s + 1]).astype(jnp.bfloat16)
        d_proj = sums[1][token, :].astype(jnp.bfloat16)
        grads.append(
            lax.dot_general(d_proj, x_proj, (((0,), (0,)), ((), ())), preferred_element_type=jnp.float32)
        )
    left = product(k_ref[1], jnp.concatenate(grads, axis=1))
    left = jnp.concatenate([left[:, s * rank : (s + 1) * rank] for s in range(seqs)], axis=0)
    full = product(left, k_ref[0])
    for s in range(seqs):
        for d in range(n):
            at = s * rank + d * share
            white[d, s * share : (s + 1) * share, :] = full[at : at + share, :]
    out_ref[...] = white[...].astype(jnp.bfloat16)


def whitened_blocks(total, k, late, operands, seqs, n):
    rank = k.shape[1]
    shape = (n, seqs * (rank // n), rank)
    return pl.pallas_call(
        functools.partial(whiten_kernel, n, seqs, late),
        out_shape=jax.ShapeDtypeStruct(shape, jnp.bfloat16),
        in_specs=[VMEM, VMEM] + ([SMEM] + [VMEM] * (len(operands) - 1) if operands else []),
        out_specs=VMEM,
        scratch_shapes=[pltpu.VMEM(shape, jnp.float32)],
        compiler_params=pltpu.CompilerParams(vmem_limit_bytes=16 << 20),
        cost_estimate=pl.CostEstimate(flops=64 * rank**3, bytes_accessed=4 << 20, transcendentals=0),
        name="whiten",
    )(total, k, *operands)


def score_kernel(n, me_ref, ids_ref, white_ref, bank_ref, out_ref, spread):
    seqs = ids_ref.shape[0]
    chunk, rank = white_ref.shape[1:]
    share = chunk // seqs
    total = n * seqs
    spread[...] = white_ref[...].astype(jnp.float32).reshape(n * chunk, rank)
    columns = jnp.concatenate(
        [spread[pl.ds(j, total, stride=share), :].astype(jnp.bfloat16) for j in range(share)], axis=1
    )
    queries = bank_ref.shape[0] // n
    row = lax.broadcasted_iota(jnp.int32, (total, out_ref.shape[2] - queries), 0)
    tail = jnp.zeros(row.shape, jnp.float32)
    for s in range(seqs):
        tail = jnp.where(row == me_ref[0] * seqs + s, ids_ref[s].astype(jnp.float32), tail)
    partial = lax.dot_general(
        columns, bank_ref[...], (((1,), (1,)), ((), ())), preferred_element_type=jnp.float32
    )
    for d in range(n):
        out_ref[d, :, :queries] = partial[:, d * queries : (d + 1) * queries].astype(out_ref.dtype)
        out_ref[d, :, queries:] = tail.astype(out_ref.dtype)


def partial_scores(me, seq_ids, white, bank):
    n = white.shape[0]
    seqs = seq_ids.shape[0]
    queries = bank.shape[0] // n
    width = (queries // LANES + 1) * LANES
    return pl.pallas_call(
        functools.partial(score_kernel, n),
        out_shape=jax.ShapeDtypeStruct((n, n * seqs, width), jnp.bfloat16),
        in_specs=[SMEM, SMEM, VMEM, VMEM],
        out_specs=VMEM,
        scratch_shapes=[pltpu.VMEM((n * white.shape[1], white.shape[2]), jnp.float32)],
        compiler_params=pltpu.CompilerParams(vmem_limit_bytes=16 << 20),
        cost_estimate=pl.CostEstimate(
            flops=2 * n * seqs * bank.size, bytes_accessed=2 * bank.size, transcendentals=0
        ),
        name="score",
    )(me, seq_ids, white, bank)


def place_kernel(partial_ref, out_ref):
    rows, queries = out_ref.shape
    total = jnp.sum(partial_ref[...].astype(jnp.float32), axis=0)
    raw = total[:, :queries].astype(jnp.bfloat16)
    ids = total[:, queries : queries + 1].astype(jnp.int32)
    chosen = ids == lax.broadcasted_iota(jnp.int32, (rows, rows), 1)
    out_ref[...] = lax.dot_general(
        chosen.astype(jnp.bfloat16), raw, (((0,), (0,)), ((), ())), preferred_element_type=jnp.float32
    ).astype(jnp.bfloat16)


def place(partials, queries):
    return pl.pallas_call(
        lambda a, b: place_kernel(a, b),
        out_shape=jax.ShapeDtypeStruct((partials.shape[1], queries), jnp.bfloat16),
        in_specs=[VMEM],
        out_specs=VMEM,
        compiler_params=pltpu.CompilerParams(vmem_limit_bytes=16 << 20),
        name="place",
    )(partials)


def body(n, activations, out_grads, proj_in, proj_out, cov_in, cov_out, lengths, seq_ids, bank):
    me = lax.axis_index("coord").reshape(1)
    seqs, length, width = activations.shape
    activations, out_grads = activations.reshape(seqs * length, width), out_grads.reshape(seqs * length, width)
    a, b, c = factors(n)
    paired = a & (a - 1) == 0
    packed = pack(proj_in, proj_out)
    half = first_half(cov_in, cov_out)
    held = {(0, 0, 0): packed}
    middle = 2 if a > 2 else a - 1
    if middle:
        held[middle, 0, 0] = moved(packed, 0, middle, n)
    for by in range(1, b):
        held[0, by, 0] = moved(packed, 1, by, n)
    held, half = lax.optimization_barrier((held, half))
    far = {at: block for at, block in held.items() if at[0]}
    for at in list(far):
        for by in range(1, b):
            far[at[0], by, 0] = moved(far[at], 1, by, n)
    for at in range(3, a):
        nearest = at & -at
        if paired and nearest != at:
            far[at, 0, 0] = moved(far[at - nearest, 0, 0], 0, nearest, n)
        else:
            far[at, 0, 0] = moved(held[0, 0, 0], 0, at, n)
    if a > 2:
        far[1, 0, 0] = moved(held[0, 0, 0], 0, 1, n)
    far = lax.optimization_barrier(far)
    held.update(far)
    early = list(held)
    for at in range(1, a):
        for by in range(1, b):
            nearest = at & -at
            if (at, by, 0) not in held:
                if paired and nearest != at:
                    held[at, by, 0] = moved(held[at - nearest, by, 0], 0, nearest, n)
                else:
                    held[at, by, 0] = moved(held[at, 0, 0], 1, by, n)
    order = [(at, by, core) for core in range(c) for by in range(b) for at in range(a)]
    own = [at for at in order if at[2] == 0]
    last = [at for at in own if at not in early]
    k, inputs = second_half(half, lengths, activations, out_grads)
    if proj_in.shape[0] % LANES == 0 and last and c == 2:
        across = moved(merge([held[at] for at in early]), 2, 1, n)
        waiting, across, k = lax.optimization_barrier(([held[at] for at in last], across, k))
        held.update(zip(last, waiting))
        across = [across, moved(merge(waiting), 2, 1, n)]
        total = project(me, inputs, [held[at] for at in own], [order.index(at) for at in own], n)
        operands = [me, inputs, *across]
        late = [(order.index((*at[:2], 1)), t, i) for t, part in enumerate((early, last)) for i, at in enumerate(part)]
    else:
        for at in own:
            for by in range(1, c):
                held[at[0], at[1], by] = moved(held[at], 2, by, n)
        total = project(me, inputs, [held[at] for at in order], list(range(n)), n)
        operands, late = [], []
    white = whitened_blocks(total, k, late, operands, seqs, n)
    white = lax.all_to_all(white, "coord", split_axis=0, concat_axis=0, tiled=True)
    partials = partial_scores(me, seq_ids, white, bank)
    partials = lax.all_to_all(partials, "coord", split_axis=0, concat_axis=0, tiled=True)
    return place(partials, bank.shape[0] // n)


def solution(mesh):
    in_specs = (
        P(("groups", "coord"), None, None),
        P(("groups", "coord"), None, None),
        P("coord", None),
        P("coord", None),
        P(),
        P(),
        P(("groups", "coord")),
        P(("groups", "coord")),
        P(None, "coord"),
    )
    out_specs = P("groups", "coord")
    return jax.shard_map(
        functools.partial(body, mesh.shape["coord"]),
        mesh=mesh,
        in_specs=in_specs,
        out_specs=out_specs,
        check_vma=False,
    )
```

```python
import functools

import jax
import jax.numpy as jnp
from jax import lax
from jax.experimental import pallas as pl
from jax.experimental.pallas import tpu as pltpu
from jax.sharding import PartitionSpec as P

SUB = 8
LANES = 128
EXACT = lax.Precision.HIGHEST
VMEM = pl.BlockSpec(memory_space=pltpu.VMEM)
HBM = pl.BlockSpec(memory_space=pltpu.HBM)
SMEM = pl.BlockSpec(memory_space=pltpu.SMEM)


def factors(n):
    c = 2 if n % 2 == 0 else 1
    rest = n // c
    b = max(f for f in range(1, rest + 1) if rest % f == 0 and f * f <= rest)
    return rest // b, b, c


def partner(at, by, size, towards):
    if size & (size - 1) == 0:
        return at ^ by
    return (at + (by if towards else size - by)) % size


def sources(me, n):
    a, b, c = factors(n)
    ia, ib, ic = me // (b * c), (me // c) % b, me % c
    return [
        (partner(ia, da, a, False) * b + partner(ib, db, b, False)) * c + partner(ic, dc, c, False)
        for dc in range(c)
        for db in range(b)
        for da in range(a)
    ]


def moved(value, axis, by, n):
    sizes = factors(n)
    a, b, c = sizes
    pairs = []
    for me in range(n):
        at = [me // (b * c), (me // c) % b, me % c]
        at[axis] = partner(at[axis], by, sizes[axis], True)
        pairs.append((me, (at[0] * b + at[1]) * c + at[2]))
    return lax.ppermute(value, "coord", pairs)


def pack_kernel(first_hbm, second_hbm, out_ref, sems):
    rows = first_hbm.shape[0]
    copies = [
        pltpu.make_async_copy(source, out_ref.at[pl.ds(i * rows, rows)], sems.at[i])
        for i, source in enumerate((first_hbm, second_hbm))
    ]
    for copy in copies:
        copy.start()
    for copy in copies:
        copy.wait()


def pack(first, second):
    rows, columns = first.shape
    return pl.pallas_call(
        pack_kernel,
        out_shape=jax.ShapeDtypeStruct((2 * rows, columns), first.dtype),
        in_specs=[HBM, HBM],
        out_specs=VMEM,
        scratch_shapes=[pltpu.SemaphoreType.DMA((2,))],
        compiler_params=pltpu.CompilerParams(vmem_limit_bytes=8 << 20),
        name="pack",
    )(pinned(first), pinned(second))


def pinned(value):
    return pltpu.with_memory_space_constraint(value, pltpu.HBM)


def gauss_jordan(blocks):
    width = blocks[0].shape[1]
    half = width // 2
    lane = lax.broadcasted_iota(jnp.int32, (SUB, width), 1)
    sub = lax.broadcasted_iota(jnp.int32, (SUB, width), 0)
    start, within = lane // half * half, lane % half

    def column(block, at):
        return jnp.take_along_axis(block, start + at, axis=1, mode="promise_in_bounds")

    for k in range(len(blocks)):
        at = k * SUB
        head = within // SUB == k
        rows = [jnp.broadcast_to(blocks[k][i : i + 1, :], (SUB, width)) for i in range(SUB)]
        diag = {(i, j): column(rows[i], at + j) for i in range(SUB) for j in range(i, SUB)}
        rows = [jnp.where(head, (within == at + i).astype(jnp.float32), rows[i]) for i in range(SUB)]
        inverse, factor = [], {}
        for p in range(SUB):
            inverse.append(1.0 / diag[p, p])
            for i in range(p + 1, SUB):
                factor[p, i] = diag[p, i] * inverse[p]
                for j in range(i, SUB):
                    diag[i, j] = diag[i, j] - factor[p, i] * diag[p, j]
                rows[i] = rows[i] - factor[p, i] * rows[p]
        rows = [rows[p] * inverse[p] for p in range(SUB)]
        for p in reversed(range(SUB)):
            for i in range(p):
                rows[i] = rows[i] - factor[i, p] * rows[p]
        done = rows[0]
        for i in range(1, SUB):
            done = jnp.where(sub == i, rows[i], done)
        out = []
        for g, block in enumerate(blocks):
            if g == k:
                out.append(done)
                continue
            terms = [column(block, at + p) * rows[p] for p in range(SUB)]
            while len(terms) > 1:
                terms = [terms[i] + terms[i + 1] for i in range(0, len(terms), 2)]
            out.append(jnp.where(head, 0.0, block) - terms[0])
        blocks = out
    return blocks


def side_by_side_inverses(first, second):
    half = first.shape[0]
    both = jnp.concatenate([first, second], axis=1)
    blocks = gauss_jordan([both[g : g + SUB, :] for g in range(0, half, SUB)])
    both = jnp.concatenate(blocks, axis=0)
    return both[:, :half], both[:, half:]


def damped(cov):
    size = cov.shape[0]
    cov = 0.5 * (cov + cov.T)
    row = lax.broadcasted_iota(jnp.int32, (size, size), 0)
    col = lax.broadcasted_iota(jnp.int32, (size, size), 1)
    damping = 0.1 * jnp.sum(jnp.where(row == col, cov, 0.0)) / size
    return jnp.where(row == col, cov + damping, cov)


def product(left, right, dims=((1,), (0,))):
    return lax.dot_general(left, right, (dims, ((), ())), precision=EXACT, preferred_element_type=jnp.float32)


def first_half_kernel(cov_in_hbm, cov_out_hbm, out_ref, cov_ref, sems):
    copies = [
        pltpu.make_async_copy(source, cov_ref.at[i], sems.at[i]) for i, source in enumerate((cov_in_hbm, cov_out_hbm))
    ]
    for copy in copies:
        copy.start()
    for copy in copies:
        copy.wait()
    half = cov_ref.shape[1] // 2
    covs = [damped(cov_ref[0]), damped(cov_ref[1])]
    corner = [cov[:half, half:] for cov in covs]
    upper = side_by_side_inverses(*[cov[:half, :half] for cov in covs])
    solved = [product(u, c) for u, c in zip(upper, corner)]
    schur = [cov[half:, half:] - product(c, t, ((0,), (0,))) for cov, c, t in zip(covs, corner, solved)]
    for i, pair in enumerate((upper, solved, schur)):
        out_ref[i] = jnp.concatenate(pair, axis=1)


def second_half_kernel(first_ref, len_hbm, k_ref, len_ref, sem):
    copy = pltpu.make_async_copy(len_hbm, len_ref, sem)
    copy.start()
    size = k_ref.shape[1]
    half = size // 2
    upper, solved, schur = [(first_ref[i][:, :half], first_ref[i][:, half:]) for i in range(3)]
    lower = side_by_side_inverses(*schur)
    for m, (u, t, low) in enumerate(zip(upper, solved, lower)):
        side = product(t, low)
        k_ref[m, :half, :half] = u + product(side, t, ((1,), (1,)))
        k_ref[m, :half, half:] = -side
        k_ref[m, half:, :half] = -side.T
        k_ref[m, half:, half:] = low
    copy.wait()
    token = lax.broadcasted_iota(jnp.int32, (size, size), 0)
    lane = lax.broadcasted_iota(jnp.int32, (size, size), 1)
    mask = jnp.zeros((size, size), jnp.float32)
    for s in range(len_ref.shape[0]):
        mask = jnp.where((lane == s) & (token < len_ref[s]), 1.0, mask)
    k_ref[2] = mask


def first_half(cov_in, cov_out):
    size = cov_in.shape[0]
    return pl.pallas_call(
        first_half_kernel,
        out_shape=jax.ShapeDtypeStruct((3, size // 2, size), jnp.float32),
        in_specs=[HBM, HBM],
        out_specs=VMEM,
        scratch_shapes=[pltpu.VMEM((2, size, size), jnp.float32), pltpu.SemaphoreType.DMA((2,))],
        compiler_params=pltpu.CompilerParams(vmem_limit_bytes=8 << 20),
        cost_estimate=pl.CostEstimate(flops=size, bytes_accessed=size, transcendentals=0),
        name="first_half",
    )(pinned(cov_in), pinned(cov_out))


def second_half(first, lengths):
    size = first.shape[2]
    return pl.pallas_call(
        second_half_kernel,
        out_shape=jax.ShapeDtypeStruct((3, size, size), jnp.float32),
        in_specs=[VMEM, HBM],
        out_specs=VMEM,
        scratch_shapes=[pltpu.SMEM(lengths.shape, jnp.int32), pltpu.SemaphoreType.DMA],
        compiler_params=pltpu.CompilerParams(vmem_limit_bytes=8 << 20),
        cost_estimate=pl.CostEstimate(flops=2 * size**3, bytes_accessed=12 << 20, transcendentals=0),
        name="second_half",
    )(first, pinned(lengths))


def merge_kernel(*refs):
    rows = refs[0].shape[0]
    for i, ref in enumerate(refs[:-1]):
        refs[-1][i * rows : (i + 1) * rows, :] = ref[...]


def merge(blocks):
    rows, columns = blocks[0].shape
    return pl.pallas_call(
        merge_kernel,
        out_shape=jax.ShapeDtypeStruct((len(blocks) * rows, columns), blocks[0].dtype),
        in_specs=[VMEM] * len(blocks),
        out_specs=VMEM,
        compiler_params=pltpu.CompilerParams(vmem_limit_bytes=8 << 20),
        cost_estimate=pl.CostEstimate(flops=rows, bytes_accessed=rows, transcendentals=0),
        name="merge",
    )(*blocks)


def project_kernel(n, early, seqs, me_ref, *rest):
    inputs, blocks, (total_ref, held, sems) = rest[:2], rest[2 : 2 + len(early)], rest[2 + len(early) :]
    tokens = held.shape[1]
    part = tokens // sems.shape[1]
    copies = [
        [
            pltpu.make_async_copy(source.at[pl.ds(i * part, part)], held.at[t, pl.ds(i * part, part)], sems.at[t, i])
            for i in range(sems.shape[1])
        ]
        for t, source in enumerate(inputs)
    ]
    for copy in copies[0] + copies[1]:
        copy.start()
    rows = blocks[0].shape[0] // 2
    source = sources(me_ref[0], n)
    for t in range(2):
        for copy in copies[t]:
            copy.wait()
        total = None
        for which, block in zip(early, blocks):
            columns = pl.ds(pl.multiple_of(source[which] * rows, rows), rows)
            term = jnp.dot(
                held[t, :, columns], block[t * rows : (t + 1) * rows, :], preferred_element_type=jnp.float32
            )
            total = term if total is None else total + term
        total_ref[t] = total


def project_whole_kernel(n, me_ref, act_ref, grad_ref, *rest):
    blocks, (total_ref, proj) = rest[:n], rest[n:]
    rows = blocks[0].shape[0] // 2
    for block, source in zip(blocks, sources(me_ref[0], n)):
        at = pl.ds(pl.multiple_of(source * rows, rows), rows)
        for t in range(2):
            proj[t, at, :] = block[t * rows : (t + 1) * rows, :]
    for t, ref in enumerate((act_ref, grad_ref)):
        total_ref[t] = jnp.dot(ref[...], proj[t], preferred_element_type=jnp.float32)


def project(me, activations, out_grads, blocks, early, seqs, n):
    tokens, width = activations.shape
    rank = blocks[0].shape[1]
    total = jax.ShapeDtypeStruct((2, tokens, rank), jnp.float32)
    common = dict(
        compiler_params=pltpu.CompilerParams(vmem_limit_bytes=16 << 20),
        cost_estimate=pl.CostEstimate(flops=rank, bytes_accessed=rank, transcendentals=0),
        name="project",
    )
    if len(early) == n:
        result = pl.pallas_call(
            functools.partial(project_whole_kernel, n),
            out_shape=total,
            in_specs=[SMEM] + [VMEM] * (2 + n),
            out_specs=VMEM,
            scratch_shapes=[pltpu.VMEM((2, width, rank), jnp.bfloat16)],
            **common,
        )(me, activations, out_grads, *blocks)
        return result, None
    return pl.pallas_call(
        functools.partial(project_kernel, n, early, seqs),
        out_shape=(
            total,
            jax.ShapeDtypeStruct((2, tokens, width), activations.dtype),
        ),
        in_specs=[SMEM, HBM, HBM] + [VMEM] * len(early),
        out_specs=(VMEM, VMEM),
        scratch_shapes=[pltpu.SemaphoreType.DMA((2, 2 * seqs))],
        **common,
    )(me, pinned(activations), pinned(out_grads), *blocks)


def whiten_kernel(n, seqs, late, total_ref, k_ref, *rest):
    operands, (out_ref, white) = rest[:-2], rest[-2:]
    rank = k_ref.shape[1]
    sums = [total_ref[0], total_ref[1]]
    if late:
        me_ref, held, *blocks = operands
        source = sources(me_ref[0], n)
        rows = held.shape[2] // n
        for which, operand, at in late:
            columns = pl.ds(pl.multiple_of(source[which] * rows, rows), rows)
            for t in range(2):
                block = blocks[operand][(2 * at + t) * rows : (2 * at + t + 1) * rows, :]
                sums[t] = sums[t] + jnp.dot(held[t, :, columns], block, preferred_element_type=jnp.float32)
    length = total_ref.shape[1] // seqs
    share = rank // n
    grads = []
    for s in range(seqs):
        token = slice(s * length, (s + 1) * length)
        x_proj = (sums[0][token, :] * k_ref[2][:length, s : s + 1]).astype(jnp.bfloat16)
        d_proj = sums[1][token, :].astype(jnp.bfloat16)
        grads.append(
            lax.dot_general(d_proj, x_proj, (((0,), (0,)), ((), ())), preferred_element_type=jnp.float32)
        )
    left = product(k_ref[1], jnp.concatenate(grads, axis=1))
    left = jnp.concatenate([left[:, s * rank : (s + 1) * rank] for s in range(seqs)], axis=0)
    full = product(left, k_ref[0])
    for s in range(seqs):
        for d in range(n):
            at = s * rank + d * share
            white[d, s * share : (s + 1) * share, :] = full[at : at + share, :]
    out_ref[...] = white[...].astype(jnp.bfloat16)


def whitened_blocks(total, k, late, operands, seqs, n):
    rank = k.shape[1]
    shape = (n, seqs * (rank // n), rank)
    return pl.pallas_call(
        functools.partial(whiten_kernel, n, seqs, late),
        out_shape=jax.ShapeDtypeStruct(shape, jnp.bfloat16),
        in_specs=[VMEM, VMEM] + ([SMEM] + [VMEM] * (len(operands) - 1) if operands else []),
        out_specs=VMEM,
        scratch_shapes=[pltpu.VMEM(shape, jnp.float32)],
        compiler_params=pltpu.CompilerParams(vmem_limit_bytes=16 << 20),
        cost_estimate=pl.CostEstimate(flops=64 * rank**3, bytes_accessed=4 << 20, transcendentals=0),
        name="whiten",
    )(total, k, *operands)


def score_kernel(n, me_ref, ids_ref, white_ref, bank_ref, out_ref, spread):
    seqs = ids_ref.shape[0]
    chunk, rank = white_ref.shape[1:]
    share = chunk // seqs
    total = n * seqs
    spread[...] = white_ref[...].astype(jnp.float32).reshape(n * chunk, rank)
    columns = jnp.concatenate(
        [spread[pl.ds(j, total, stride=share), :].astype(jnp.bfloat16) for j in range(share)], axis=1
    )
    queries = bank_ref.shape[0] // n
    row = lax.broadcasted_iota(jnp.int32, (total, out_ref.shape[2] - queries), 0)
    tail = jnp.zeros(row.shape, jnp.float32)
    for s in range(seqs):
        tail = jnp.where(row == me_ref[0] * seqs + s, ids_ref[s].astype(jnp.float32), tail)
    partial = lax.dot_general(
        columns, bank_ref[...], (((1,), (1,)), ((), ())), preferred_element_type=jnp.float32
    )
    for d in range(n):
        out_ref[d, :, :queries] = partial[:, d * queries : (d + 1) * queries].astype(out_ref.dtype)
        out_ref[d, :, queries:] = tail.astype(out_ref.dtype)


def partial_scores(me, seq_ids, white, bank):
    n = white.shape[0]
    seqs = seq_ids.shape[0]
    queries = bank.shape[0] // n
    width = (queries // LANES + 1) * LANES
    return pl.pallas_call(
        functools.partial(score_kernel, n),
        out_shape=jax.ShapeDtypeStruct((n, n * seqs, width), jnp.bfloat16),
        in_specs=[SMEM, SMEM, VMEM, VMEM],
        out_specs=VMEM,
        scratch_shapes=[pltpu.VMEM((n * white.shape[1], white.shape[2]), jnp.float32)],
        compiler_params=pltpu.CompilerParams(vmem_limit_bytes=16 << 20),
        cost_estimate=pl.CostEstimate(
            flops=2 * n * seqs * bank.size, bytes_accessed=2 * bank.size, transcendentals=0
        ),
        name="score",
    )(me, seq_ids, white, bank)


def place_kernel(partial_ref, out_ref):
    rows, queries = out_ref.shape
    total = jnp.sum(partial_ref[...].astype(jnp.float32), axis=0)
    raw = total[:, :queries].astype(jnp.bfloat16)
    ids = total[:, queries : queries + 1].astype(jnp.int32)
    chosen = ids == lax.broadcasted_iota(jnp.int32, (rows, rows), 1)
    out_ref[...] = lax.dot_general(
        chosen.astype(jnp.bfloat16), raw, (((0,), (0,)), ((), ())), preferred_element_type=jnp.float32
    ).astype(jnp.bfloat16)


def place(partials, queries):
    return pl.pallas_call(
        lambda a, b: place_kernel(a, b),
        out_shape=jax.ShapeDtypeStruct((partials.shape[1], queries), jnp.bfloat16),
        in_specs=[VMEM],
        out_specs=VMEM,
        compiler_params=pltpu.CompilerParams(vmem_limit_bytes=16 << 20),
        name="place",
    )(partials)


def body(n, activations, out_grads, proj_in, proj_out, cov_in, cov_out, lengths, seq_ids, bank):
    me = lax.axis_index("coord").reshape(1)
    seqs, length, width = activations.shape
    activations, out_grads = activations.reshape(seqs * length, width), out_grads.reshape(seqs * length, width)
    a, b, c = factors(n)
    paired = a & (a - 1) == 0
    packed = pack(proj_in, proj_out)
    half = first_half(cov_in, cov_out)
    held = {(0, 0, 0): packed}
    for by in range(1, min(a, 3)):
        held[by, 0, 0] = moved(packed, 0, by, n)
    for by in range(1, b):
        held[0, by, 0] = moved(packed, 1, by, n)
    held, half = lax.optimization_barrier((held, half))
    for at in range(3, a):
        nearest = at & -at
        if paired and nearest != at:
            held[at, 0, 0] = moved(held[at - nearest, 0, 0], 0, nearest, n)
        else:
            held[at, 0, 0] = moved(held[0, 0, 0], 0, at, n)
    for at in range(2, a - 1):
        for by in range(1, b):
            held[at, by, 0] = moved(held[at, 0, 0], 1, by, n)
    held, k = lax.optimization_barrier((held, second_half(half, lengths)))
    early = list(held)
    for at in sorted({1, a - 1} & set(range(1, a))):
        for by in range(1, b):
            nearest = at & -at
            if paired and nearest != at:
                held[at, by, 0] = moved(held[at - nearest, by, 0], 0, nearest, n)
            else:
                held[at, by, 0] = moved(held[at, 0, 0], 1, by, n)
    order = [(at, by, core) for core in range(c) for by in range(b) for at in range(a)]
    last = [at for at in held if at not in early]
    if proj_in.shape[0] % LANES == 0 and last and c == 2:
        total, inputs = project(
            me, activations, out_grads, [held[at] for at in early], [order.index(at) for at in early], seqs, n
        )
        across = [moved(merge([held[at] for at in early]), 2, 1, n)]
        waiting, total = lax.optimization_barrier(([held[at] for at in last], total))
        across.append(moved(merge(waiting), 2, 1, n))
        operands = [me, inputs, *across, *waiting]
        late = [(order.index(at), 2 + i, 0) for i, at in enumerate(last)]
        late += [(order.index((*at[:2], 1)), t, i) for t, part in enumerate((early, last)) for i, at in enumerate(part)]
    else:
        for at in list(held):
            for by in range(1, c):
                held[at[0], at[1], by] = moved(held[at], 2, by, n)
        total = project(me, activations, out_grads, [held[at] for at in order], list(range(n)), seqs, n)[0]
        operands, late = [], []
    white = whitened_blocks(total, k, late, operands, seqs, n)
    white = lax.all_to_all(white, "coord", split_axis=0, concat_axis=0, tiled=True)
    partials = partial_scores(me, seq_ids, white, bank)
    partials = lax.all_to_all(partials, "coord", split_axis=0, concat_axis=0, tiled=True)
    return place(partials, bank.shape[0] // n)


def solution(mesh):
    in_specs = (
        P(("groups", "coord"), None, None),
        P(("groups", "coord"), None, None),
        P("coord", None),
        P("coord", None),
        P(),
        P(),
        P(("groups", "coord")),
        P(("groups", "coord")),
        P(None, "coord"),
    )
    out_specs = P("groups", "coord")
    return jax.shard_map(
        functools.partial(body, mesh.shape["coord"]),
        mesh=mesh,
        in_specs=in_specs,
        out_specs=out_specs,
        check_vma=False,
    )
```

```python
import functools

import jax
import jax.numpy as jnp
from jax import lax
from jax.experimental import pallas as pl
from jax.experimental.pallas import tpu as pltpu
from jax.sharding import PartitionSpec as P

SUB = 8
LANES = 128
EXACT = lax.Precision.HIGHEST
VMEM = pl.BlockSpec(memory_space=pltpu.VMEM)
HBM = pl.BlockSpec(memory_space=pltpu.HBM)
SMEM = pl.BlockSpec(memory_space=pltpu.SMEM)


def factors(n):
    c = 2 if n % 2 == 0 else 1
    rest = n // c
    b = max(f for f in range(1, rest + 1) if rest % f == 0 and f * f <= rest)
    return rest // b, b, c


def partner(at, by, size, towards):
    if size & (size - 1) == 0:
        return at ^ by
    return (at + (by if towards else size - by)) % size


def sources(me, n):
    a, b, c = factors(n)
    ia, ib, ic = me // (b * c), (me // c) % b, me % c
    return [
        (partner(ia, da, a, False) * b + partner(ib, db, b, False)) * c + partner(ic, dc, c, False)
        for dc in range(c)
        for db in range(b)
        for da in range(a)
    ]


def moved(value, by, n):
    sizes = factors(n)
    a, b, c = sizes
    pairs = []
    for me in range(n):
        at = (me // (b * c), (me // c) % b, me % c)
        to = [partner(place, step, size, True) for place, step, size in zip(at, by, sizes)]
        pairs.append((me, (to[0] * b + to[1]) * c + to[2]))
    return lax.ppermute(value, "coord", pairs)


def pack_kernel(first_hbm, second_hbm, out_ref, sems):
    rows = first_hbm.shape[0]
    copies = [
        pltpu.make_async_copy(source, out_ref.at[pl.ds(i * rows, rows)], sems.at[i])
        for i, source in enumerate((first_hbm, second_hbm))
    ]
    for copy in copies:
        copy.start()
    for copy in copies:
        copy.wait()


def pack(first, second):
    rows, columns = first.shape
    return pl.pallas_call(
        pack_kernel,
        out_shape=jax.ShapeDtypeStruct((2 * rows, columns), first.dtype),
        in_specs=[HBM, HBM],
        out_specs=VMEM,
        scratch_shapes=[pltpu.SemaphoreType.DMA((2,))],
        compiler_params=pltpu.CompilerParams(vmem_limit_bytes=8 << 20),
        name="pack",
    )(pinned(first), pinned(second))


def pinned(value):
    return pltpu.with_memory_space_constraint(value, pltpu.HBM)


def gauss_jordan(blocks):
    width = blocks[0].shape[1]
    half = width // 2
    lane = lax.broadcasted_iota(jnp.int32, (SUB, width), 1)
    sub = lax.broadcasted_iota(jnp.int32, (SUB, width), 0)
    start, within = lane // half * half, lane % half

    def column(block, at):
        return jnp.take_along_axis(block, start + at, axis=1, mode="promise_in_bounds")

    for k in range(len(blocks)):
        at = k * SUB
        head = within // SUB == k
        rows = [jnp.broadcast_to(blocks[k][i : i + 1, :], (SUB, width)) for i in range(SUB)]
        diag = {(i, j): column(rows[i], at + j) for i in range(SUB) for j in range(i, SUB)}
        rows = [jnp.where(head, (within == at + i).astype(jnp.float32), rows[i]) for i in range(SUB)]
        inverse, factor = [], {}
        for p in range(SUB):
            inverse.append(1.0 / diag[p, p])
            for i in range(p + 1, SUB):
                factor[p, i] = diag[p, i] * inverse[p]
                for j in range(i, SUB):
                    diag[i, j] = diag[i, j] - factor[p, i] * diag[p, j]
                rows[i] = rows[i] - factor[p, i] * rows[p]
        rows = [rows[p] * inverse[p] for p in range(SUB)]
        for p in reversed(range(SUB)):
            for i in range(p):
                rows[i] = rows[i] - factor[i, p] * rows[p]
        done = rows[0]
        for i in range(1, SUB):
            done = jnp.where(sub == i, rows[i], done)
        out = []
        for g, block in enumerate(blocks):
            if g == k:
                out.append(done)
                continue
            terms = [column(block, at + p) * rows[p] for p in range(SUB)]
            while len(terms) > 1:
                terms = [terms[i] + terms[i + 1] for i in range(0, len(terms), 2)]
            out.append(jnp.where(head, 0.0, block) - terms[0])
        blocks = out
    return blocks


def side_by_side_inverses(first, second):
    half = first.shape[0]
    both = jnp.concatenate([first, second], axis=1)
    blocks = gauss_jordan([both[g : g + SUB, :] for g in range(0, half, SUB)])
    both = jnp.concatenate(blocks, axis=0)
    return both[:, :half], both[:, half:]


def damped(cov):
    size = cov.shape[0]
    cov = 0.5 * (cov + cov.T)
    row = lax.broadcasted_iota(jnp.int32, (size, size), 0)
    col = lax.broadcasted_iota(jnp.int32, (size, size), 1)
    damping = 0.1 * jnp.sum(jnp.where(row == col, cov, 0.0)) / size
    return jnp.where(row == col, cov + damping, cov)


def product(left, right, dims=((1,), (0,))):
    return lax.dot_general(left, right, (dims, ((), ())), precision=EXACT, preferred_element_type=jnp.float32)


def first_half_kernel(cov_in_hbm, cov_out_hbm, out_ref, cov_ref, sems):
    copies = [
        pltpu.make_async_copy(source, cov_ref.at[i], sems.at[i]) for i, source in enumerate((cov_in_hbm, cov_out_hbm))
    ]
    for copy in copies:
        copy.start()
    for copy in copies:
        copy.wait()
    half = cov_ref.shape[1] // 2
    covs = [damped(cov_ref[0]), damped(cov_ref[1])]
    corner = [cov[:half, half:] for cov in covs]
    upper = side_by_side_inverses(*[cov[:half, :half] for cov in covs])
    solved = [product(u, c) for u, c in zip(upper, corner)]
    schur = [cov[half:, half:] - product(c, t, ((0,), (0,))) for cov, c, t in zip(covs, corner, solved)]
    for i, pair in enumerate((upper, solved, schur)):
        out_ref[i] = jnp.concatenate(pair, axis=1)


def second_half_kernel(first_ref, len_hbm, k_ref, len_ref, sem):
    copy = pltpu.make_async_copy(len_hbm, len_ref, sem)
    copy.start()
    size = k_ref.shape[1]
    half = size // 2
    upper, solved, schur = [(first_ref[i][:, :half], first_ref[i][:, half:]) for i in range(3)]
    lower = side_by_side_inverses(*schur)
    for m, (u, t, low) in enumerate(zip(upper, solved, lower)):
        side = product(t, low)
        k_ref[m, :half, :half] = u + product(side, t, ((1,), (1,)))
        k_ref[m, :half, half:] = -side
        k_ref[m, half:, :half] = -side.T
        k_ref[m, half:, half:] = low
    copy.wait()
    token = lax.broadcasted_iota(jnp.int32, (size, size), 0)
    lane = lax.broadcasted_iota(jnp.int32, (size, size), 1)
    mask = jnp.zeros((size, size), jnp.float32)
    for s in range(len_ref.shape[0]):
        mask = jnp.where((lane == s) & (token < len_ref[s]), 1.0, mask)
    k_ref[2] = mask


def first_half(cov_in, cov_out):
    size = cov_in.shape[0]
    return pl.pallas_call(
        first_half_kernel,
        out_shape=jax.ShapeDtypeStruct((3, size // 2, size), jnp.float32),
        in_specs=[HBM, HBM],
        out_specs=VMEM,
        scratch_shapes=[pltpu.VMEM((2, size, size), jnp.float32), pltpu.SemaphoreType.DMA((2,))],
        compiler_params=pltpu.CompilerParams(vmem_limit_bytes=8 << 20),
        cost_estimate=pl.CostEstimate(flops=size, bytes_accessed=size, transcendentals=0),
        name="first_half",
    )(pinned(cov_in), pinned(cov_out))


def second_half(first, lengths):
    size = first.shape[2]
    return pl.pallas_call(
        second_half_kernel,
        out_shape=jax.ShapeDtypeStruct((3, size, size), jnp.float32),
        in_specs=[VMEM, HBM],
        out_specs=VMEM,
        scratch_shapes=[pltpu.SMEM(lengths.shape, jnp.int32), pltpu.SemaphoreType.DMA],
        compiler_params=pltpu.CompilerParams(vmem_limit_bytes=8 << 20),
        cost_estimate=pl.CostEstimate(flops=size, bytes_accessed=size, transcendentals=0),
        name="second_half",
    )(first, pinned(lengths))


def merge_kernel(*refs):
    rows = refs[0].shape[0]
    for i, ref in enumerate(refs[:-1]):
        refs[-1][i * rows : (i + 1) * rows, :] = ref[...]


def merge(blocks):
    rows, columns = blocks[0].shape
    return pl.pallas_call(
        merge_kernel,
        out_shape=jax.ShapeDtypeStruct((len(blocks) * rows, columns), blocks[0].dtype),
        in_specs=[VMEM] * len(blocks),
        out_specs=VMEM,
        compiler_params=pltpu.CompilerParams(vmem_limit_bytes=8 << 20),
        cost_estimate=pl.CostEstimate(flops=rows, bytes_accessed=rows, transcendentals=0),
        name="merge",
    )(*blocks)


def project_kernel(n, early, seqs, me_ref, *rest):
    inputs, blocks, (total_ref, held, sems) = rest[:2], rest[2 : 2 + len(early)], rest[2 + len(early) :]
    tokens = held.shape[1]
    part = tokens // sems.shape[1]
    copies = [
        [
            pltpu.make_async_copy(source.at[pl.ds(i * part, part)], held.at[t, pl.ds(i * part, part)], sems.at[t, i])
            for i in range(sems.shape[1])
        ]
        for t, source in enumerate(inputs)
    ]
    for copy in copies[0] + copies[1]:
        copy.start()
    rows = blocks[0].shape[0] // 2
    source = sources(me_ref[0], n)
    for t in range(2):
        for copy in copies[t]:
            copy.wait()
        total = None
        for which, block in zip(early, blocks):
            columns = pl.ds(pl.multiple_of(source[which] * rows, rows), rows)
            term = jnp.dot(
                held[t, :, columns], block[t * rows : (t + 1) * rows, :], preferred_element_type=jnp.float32
            )
            total = term if total is None else total + term
        total_ref[t] = total


def project_whole_kernel(n, me_ref, act_ref, grad_ref, *rest):
    blocks, (total_ref, proj) = rest[:n], rest[n:]
    rows = blocks[0].shape[0] // 2
    for block, source in zip(blocks, sources(me_ref[0], n)):
        at = pl.ds(pl.multiple_of(source * rows, rows), rows)
        for t in range(2):
            proj[t, at, :] = block[t * rows : (t + 1) * rows, :]
    for t, ref in enumerate((act_ref, grad_ref)):
        total_ref[t] = jnp.dot(ref[...], proj[t], preferred_element_type=jnp.float32)


def project(me, activations, out_grads, blocks, early, seqs, n):
    tokens, width = activations.shape
    rank = blocks[0].shape[1]
    total = jax.ShapeDtypeStruct((2, tokens, rank), jnp.float32)
    common = dict(
        compiler_params=pltpu.CompilerParams(vmem_limit_bytes=16 << 20),
        cost_estimate=pl.CostEstimate(flops=rank, bytes_accessed=rank, transcendentals=0),
        name="project",
    )
    if len(early) == n:
        result = pl.pallas_call(
            functools.partial(project_whole_kernel, n),
            out_shape=total,
            in_specs=[SMEM] + [VMEM] * (2 + n),
            out_specs=VMEM,
            scratch_shapes=[pltpu.VMEM((2, width, rank), jnp.bfloat16)],
            **common,
        )(me, activations, out_grads, *blocks)
        return result, None
    return pl.pallas_call(
        functools.partial(project_kernel, n, early, seqs),
        out_shape=(
            total,
            jax.ShapeDtypeStruct((2, tokens, width), activations.dtype),
        ),
        in_specs=[SMEM, HBM, HBM] + [VMEM] * len(early),
        out_specs=(VMEM, VMEM),
        scratch_shapes=[pltpu.SemaphoreType.DMA((2, 2 * seqs))],
        **common,
    )(me, pinned(activations), pinned(out_grads), *blocks)


def whiten_kernel(n, seqs, late, total_ref, k_ref, *rest):
    operands, (out_ref, white) = rest[:-2], rest[-2:]
    rank = k_ref.shape[1]
    sums = [total_ref[0], total_ref[1]]
    if late:
        me_ref, held, *blocks = operands
        source = sources(me_ref[0], n)
        rows = held.shape[2] // n
        for which, operand, at in late:
            columns = pl.ds(pl.multiple_of(source[which] * rows, rows), rows)
            for t in range(2):
                block = blocks[operand][(2 * at + t) * rows : (2 * at + t + 1) * rows, :]
                sums[t] = sums[t] + jnp.dot(held[t, :, columns], block, preferred_element_type=jnp.float32)
    length = total_ref.shape[1] // seqs
    share = rank // n
    grads = []
    for s in range(seqs):
        token = slice(s * length, (s + 1) * length)
        x_proj = (sums[0][token, :] * k_ref[2][:length, s : s + 1]).astype(jnp.bfloat16)
        d_proj = sums[1][token, :].astype(jnp.bfloat16)
        grads.append(
            lax.dot_general(d_proj, x_proj, (((0,), (0,)), ((), ())), preferred_element_type=jnp.float32)
        )
    left = product(k_ref[1], jnp.concatenate(grads, axis=1))
    left = jnp.concatenate([left[:, s * rank : (s + 1) * rank] for s in range(seqs)], axis=0)
    full = product(left, k_ref[0])
    for s in range(seqs):
        for d in range(n):
            at = s * rank + d * share
            white[d, s * share : (s + 1) * share, :] = full[at : at + share, :]
    out_ref[...] = white[...].astype(jnp.bfloat16)


def whitened_blocks(total, k, late, operands, seqs, n):
    rank = k.shape[1]
    shape = (n, seqs * (rank // n), rank)
    return pl.pallas_call(
        functools.partial(whiten_kernel, n, seqs, late),
        out_shape=jax.ShapeDtypeStruct(shape, jnp.bfloat16),
        in_specs=[VMEM, VMEM] + ([SMEM] + [VMEM] * (len(operands) - 1) if operands else []),
        out_specs=VMEM,
        scratch_shapes=[pltpu.VMEM(shape, jnp.float32)],
        compiler_params=pltpu.CompilerParams(vmem_limit_bytes=16 << 20),
        cost_estimate=pl.CostEstimate(flops=64 * rank**3, bytes_accessed=4 << 20, transcendentals=0),
        name="whiten",
    )(total, k, *operands)


def score_kernel(n, me_ref, ids_ref, white_ref, bank_ref, out_ref, spread):
    seqs = ids_ref.shape[0]
    chunk, rank = white_ref.shape[1:]
    share = chunk // seqs
    total = n * seqs
    spread[...] = white_ref[...].astype(jnp.float32).reshape(n * chunk, rank)
    columns = jnp.concatenate(
        [spread[pl.ds(j, total, stride=share), :].astype(jnp.bfloat16) for j in range(share)], axis=1
    )
    queries = bank_ref.shape[0] // n
    row = lax.broadcasted_iota(jnp.int32, (total, out_ref.shape[2] - queries), 0)
    tail = jnp.zeros(row.shape, jnp.float32)
    for s in range(seqs):
        tail = jnp.where(row == me_ref[0] * seqs + s, ids_ref[s].astype(jnp.float32), tail)
    partial = lax.dot_general(
        columns, bank_ref[...], (((1,), (1,)), ((), ())), preferred_element_type=jnp.float32
    )
    for d in range(n):
        out_ref[d, :, :queries] = partial[:, d * queries : (d + 1) * queries].astype(out_ref.dtype)
        out_ref[d, :, queries:] = tail.astype(out_ref.dtype)


def partial_scores(me, seq_ids, white, bank):
    n = white.shape[0]
    seqs = seq_ids.shape[0]
    queries = bank.shape[0] // n
    width = (queries // LANES + 1) * LANES
    return pl.pallas_call(
        functools.partial(score_kernel, n),
        out_shape=jax.ShapeDtypeStruct((n, n * seqs, width), jnp.bfloat16),
        in_specs=[SMEM, SMEM, VMEM, VMEM],
        out_specs=VMEM,
        scratch_shapes=[pltpu.VMEM((n * white.shape[1], white.shape[2]), jnp.float32)],
        compiler_params=pltpu.CompilerParams(vmem_limit_bytes=16 << 20),
        cost_estimate=pl.CostEstimate(
            flops=2 * n * seqs * bank.size, bytes_accessed=2 * bank.size, transcendentals=0
        ),
        name="score",
    )(me, seq_ids, white, bank)


def place_kernel(partial_ref, out_ref):
    rows, queries = out_ref.shape
    total = jnp.sum(partial_ref[...].astype(jnp.float32), axis=0)
    raw = total[:, :queries].astype(jnp.bfloat16)
    ids = total[:, queries : queries + 1].astype(jnp.int32)
    chosen = ids == lax.broadcasted_iota(jnp.int32, (rows, rows), 1)
    out_ref[...] = lax.dot_general(
        chosen.astype(jnp.bfloat16), raw, (((0,), (0,)), ((), ())), preferred_element_type=jnp.float32
    ).astype(jnp.bfloat16)


def place(partials, queries):
    return pl.pallas_call(
        lambda a, b: place_kernel(a, b),
        out_shape=jax.ShapeDtypeStruct((partials.shape[1], queries), jnp.bfloat16),
        in_specs=[VMEM],
        out_specs=VMEM,
        compiler_params=pltpu.CompilerParams(vmem_limit_bytes=16 << 20),
        name="place",
    )(partials)


def body(n, activations, out_grads, proj_in, proj_out, cov_in, cov_out, lengths, seq_ids, bank):
    me = lax.axis_index("coord").reshape(1)
    seqs, length, width = activations.shape
    activations, out_grads = activations.reshape(seqs * length, width), out_grads.reshape(seqs * length, width)
    a, b, c = factors(n)
    paired = a & (a - 1) == 0
    packed = pack(proj_in, proj_out)
    half = first_half(cov_in, cov_out)
    held = {(0, 0, 0): packed}
    for at in range(1, min(a, 3)):
        held[at, 0, 0] = moved(packed, (at, 0, 0), n)
    for by in range(1, b):
        held[0, by, 0] = moved(packed, (0, by, 0), n)
    held, half = lax.optimization_barrier((held, half))
    early = list(held)
    for at in range(1, a):
        nearest = at & -at
        source = at - nearest if paired and nearest != at else 0
        if at > 2:
            held[at, 0, 0] = moved(held[source, 0, 0], (at - source, 0, 0), n)
        for by in range(1, b):
            if source or at > 2:
                held[at, by, 0] = moved(held[source, 0, 0], (at - source, by, 0), n)
            elif at == 1:
                held[at, by, 0] = moved(held[0, by, 0], (1, 0, 0), n)
            else:
                held[at, by, 0] = moved(held[at, 0, 0], (0, by, 0), n)
    k = second_half(half, lengths)
    order = [(at, by, core) for core in range(c) for by in range(b) for at in range(a)]
    last = [at for at in held if at not in early]
    if proj_in.shape[0] % LANES == 0 and last and c == 2:
        total, inputs = project(
            me, activations, out_grads, [held[at] for at in early], [order.index(at) for at in early], seqs, n
        )
        across = [moved(merge([held[at] for at in early]), (0, 0, 1), n)]
        waiting, total, k = lax.optimization_barrier(([held[at] for at in last], total, k))
        across.append(moved(merge(waiting), (0, 0, 1), n))
        operands = [me, inputs, *across, *waiting]
        late = [(order.index(at), 2 + i, 0) for i, at in enumerate(last)]
        late += [(order.index((*at[:2], 1)), t, i) for t, part in enumerate((early, last)) for i, at in enumerate(part)]
    else:
        for at in list(held):
            for by in range(1, c):
                held[at[0], at[1], by] = moved(held[at], (0, 0, by), n)
        total = project(me, activations, out_grads, [held[at] for at in order], list(range(n)), seqs, n)[0]
        operands, late = [], []
    white = whitened_blocks(total, k, late, operands, seqs, n)
    white = lax.all_to_all(white, "coord", split_axis=0, concat_axis=0, tiled=True)
    partials = partial_scores(me, seq_ids, white, bank)
    partials = lax.all_to_all(partials, "coord", split_axis=0, concat_axis=0, tiled=True)
    return place(partials, bank.shape[0] // n)


def solution(mesh):
    in_specs = (
        P(("groups", "coord"), None, None),
        P(("groups", "coord"), None, None),
        P("coord", None),
        P("coord", None),
        P(),
        P(),
        P(("groups", "coord")),
        P(("groups", "coord")),
        P(None, "coord"),
    )
    out_specs = P("groups", "coord")
    return jax.shard_map(
        functools.partial(body, mesh.shape["coord"]),
        mesh=mesh,
        in_specs=in_specs,
        out_specs=out_specs,
        check_vma=False,
    )
```

```python
import functools

import jax
import jax.numpy as jnp
from jax import lax
from jax.experimental import pallas as pl
from jax.experimental.pallas import tpu as pltpu
from jax.sharding import PartitionSpec as P

SUB = 8
LANES = 128
EXACT = lax.Precision.HIGHEST
VMEM = pl.BlockSpec(memory_space=pltpu.VMEM)
HBM = pl.BlockSpec(memory_space=pltpu.HBM)
SMEM = pl.BlockSpec(memory_space=pltpu.SMEM)


def factors(n):
    c = 2 if n % 2 == 0 else 1
    rest = n // c
    b = max(f for f in range(1, rest + 1) if rest % f == 0 and f * f <= rest)
    return rest // b, b, c


def partner(at, by, size, towards):
    if size & (size - 1) == 0:
        return at ^ by
    return (at + (by if towards else size - by)) % size


def sources(me, n):
    a, b, c = factors(n)
    ia, ib, ic = me // (b * c), (me // c) % b, me % c
    return [
        (partner(ia, da, a, False) * b + partner(ib, db, b, False)) * c + partner(ic, dc, c, False)
        for dc in range(c)
        for db in range(b)
        for da in range(a)
    ]


def moved(value, by, n):
    sizes = factors(n)
    a, b, c = sizes
    pairs = []
    for me in range(n):
        at = (me // (b * c), (me // c) % b, me % c)
        to = [partner(place, step, size, True) for place, step, size in zip(at, by, sizes)]
        pairs.append((me, (to[0] * b + to[1]) * c + to[2]))
    return lax.ppermute(value, "coord", pairs)


def pack_kernel(first_hbm, second_hbm, out_ref, sems):
    rows = first_hbm.shape[0]
    copies = [
        pltpu.make_async_copy(source, out_ref.at[pl.ds(i * rows, rows)], sems.at[i])
        for i, source in enumerate((first_hbm, second_hbm))
    ]
    for copy in copies:
        copy.start()
    for copy in copies:
        copy.wait()


def pack(first, second):
    rows, columns = first.shape
    return pl.pallas_call(
        pack_kernel,
        out_shape=jax.ShapeDtypeStruct((2 * rows, columns), first.dtype),
        in_specs=[HBM, HBM],
        out_specs=VMEM,
        scratch_shapes=[pltpu.SemaphoreType.DMA((2,))],
        compiler_params=pltpu.CompilerParams(vmem_limit_bytes=8 << 20),
        name="pack",
    )(pinned(first), pinned(second))


def pinned(value):
    return pltpu.with_memory_space_constraint(value, pltpu.HBM)


def gauss_jordan(blocks):
    width = blocks[0].shape[1]
    half = width // 2
    lane = lax.broadcasted_iota(jnp.int32, (SUB, width), 1)
    sub = lax.broadcasted_iota(jnp.int32, (SUB, width), 0)
    start, within = lane // half * half, lane % half

    def column(block, at):
        return jnp.take_along_axis(block, start + at, axis=1, mode="promise_in_bounds")

    for k in range(len(blocks)):
        at = k * SUB
        head = within // SUB == k
        rows = [jnp.broadcast_to(blocks[k][i : i + 1, :], (SUB, width)) for i in range(SUB)]
        diag = {(i, j): column(rows[i], at + j) for i in range(SUB) for j in range(i, SUB)}
        rows = [jnp.where(head, (within == at + i).astype(jnp.float32), rows[i]) for i in range(SUB)]
        inverse, factor = [], {}
        for p in range(SUB):
            inverse.append(1.0 / diag[p, p])
            for i in range(p + 1, SUB):
                factor[p, i] = diag[p, i] * inverse[p]
                for j in range(i, SUB):
                    diag[i, j] = diag[i, j] - factor[p, i] * diag[p, j]
                rows[i] = rows[i] - factor[p, i] * rows[p]
        rows = [rows[p] * inverse[p] for p in range(SUB)]
        for p in reversed(range(SUB)):
            for i in range(p):
                rows[i] = rows[i] - factor[i, p] * rows[p]
        done = rows[0]
        for i in range(1, SUB):
            done = jnp.where(sub == i, rows[i], done)
        out = []
        for g, block in enumerate(blocks):
            if g == k:
                out.append(done)
                continue
            terms = [column(block, at + p) * rows[p] for p in range(SUB)]
            while len(terms) > 1:
                terms = [terms[i] + terms[i + 1] for i in range(0, len(terms), 2)]
            out.append(jnp.where(head, 0.0, block) - terms[0])
        blocks = out
    return blocks


def side_by_side_inverses(first, second):
    half = first.shape[0]
    both = jnp.concatenate([first, second], axis=1)
    blocks = gauss_jordan([both[g : g + SUB, :] for g in range(0, half, SUB)])
    both = jnp.concatenate(blocks, axis=0)
    return both[:, :half], both[:, half:]


def damped(cov):
    size = cov.shape[0]
    cov = 0.5 * (cov + cov.T)
    row = lax.broadcasted_iota(jnp.int32, (size, size), 0)
    col = lax.broadcasted_iota(jnp.int32, (size, size), 1)
    damping = 0.1 * jnp.sum(jnp.where(row == col, cov, 0.0)) / size
    return jnp.where(row == col, cov + damping, cov)


def product(left, right, dims=((1,), (0,))):
    return lax.dot_general(left, right, (dims, ((), ())), precision=EXACT, preferred_element_type=jnp.float32)


def first_half_kernel(cov_in_hbm, cov_out_hbm, out_ref, cov_ref, sems):
    copies = [
        pltpu.make_async_copy(source, cov_ref.at[i], sems.at[i]) for i, source in enumerate((cov_in_hbm, cov_out_hbm))
    ]
    for copy in copies:
        copy.start()
    for copy in copies:
        copy.wait()
    half = cov_ref.shape[1] // 2
    covs = [damped(cov_ref[0]), damped(cov_ref[1])]
    corner = [cov[:half, half:] for cov in covs]
    upper = side_by_side_inverses(*[cov[:half, :half] for cov in covs])
    solved = [product(u, c) for u, c in zip(upper, corner)]
    schur = [cov[half:, half:] - product(c, t, ((0,), (0,))) for cov, c, t in zip(covs, corner, solved)]
    for i, pair in enumerate((upper, solved, schur)):
        out_ref[i] = jnp.concatenate(pair, axis=1)


def second_half_kernel(first_ref, len_hbm, k_ref, len_ref, sem):
    copy = pltpu.make_async_copy(len_hbm, len_ref, sem)
    copy.start()
    size = k_ref.shape[1]
    half = size // 2
    upper, solved, schur = [(first_ref[i][:, :half], first_ref[i][:, half:]) for i in range(3)]
    lower = side_by_side_inverses(*schur)
    for m, (u, t, low) in enumerate(zip(upper, solved, lower)):
        side = product(t, low)
        k_ref[m, :half, :half] = u + product(side, t, ((1,), (1,)))
        k_ref[m, :half, half:] = -side
        k_ref[m, half:, :half] = -side.T
        k_ref[m, half:, half:] = low
    copy.wait()
    token = lax.broadcasted_iota(jnp.int32, (size, size), 0)
    lane = lax.broadcasted_iota(jnp.int32, (size, size), 1)
    mask = jnp.zeros((size, size), jnp.float32)
    for s in range(len_ref.shape[0]):
        mask = jnp.where((lane == s) & (token < len_ref[s]), 1.0, mask)
    k_ref[2] = mask


def first_half(cov_in, cov_out):
    size = cov_in.shape[0]
    return pl.pallas_call(
        first_half_kernel,
        out_shape=jax.ShapeDtypeStruct((3, size // 2, size), jnp.float32),
        in_specs=[HBM, HBM],
        out_specs=VMEM,
        scratch_shapes=[pltpu.VMEM((2, size, size), jnp.float32), pltpu.SemaphoreType.DMA((2,))],
        compiler_params=pltpu.CompilerParams(vmem_limit_bytes=8 << 20),
        cost_estimate=pl.CostEstimate(flops=size, bytes_accessed=size, transcendentals=0),
        name="first_half",
    )(pinned(cov_in), pinned(cov_out))


def second_half(first, lengths):
    size = first.shape[2]
    return pl.pallas_call(
        second_half_kernel,
        out_shape=jax.ShapeDtypeStruct((3, size, size), jnp.float32),
        in_specs=[VMEM, HBM],
        out_specs=VMEM,
        scratch_shapes=[pltpu.SMEM(lengths.shape, jnp.int32), pltpu.SemaphoreType.DMA],
        compiler_params=pltpu.CompilerParams(vmem_limit_bytes=8 << 20),
        cost_estimate=pl.CostEstimate(flops=size, bytes_accessed=size, transcendentals=0),
        name="second_half",
    )(first, pinned(lengths))


def merge_kernel(*refs):
    at = 0
    for ref in refs[:-1]:
        refs[-1][at : at + ref.shape[0], :] = ref[...]
        at += ref.shape[0]


def merge(blocks):
    if len(blocks) == 1:
        return blocks[0]
    rows, columns = sum(block.shape[0] for block in blocks), blocks[0].shape[1]
    return pl.pallas_call(
        merge_kernel,
        out_shape=jax.ShapeDtypeStruct((rows, columns), blocks[0].dtype),
        in_specs=[VMEM] * len(blocks),
        out_specs=VMEM,
        compiler_params=pltpu.CompilerParams(vmem_limit_bytes=8 << 20),
        cost_estimate=pl.CostEstimate(flops=rows, bytes_accessed=rows, transcendentals=0),
        name="merge",
    )(*blocks)


def project_kernel(n, early, seqs, me_ref, *rest):
    inputs, blocks, (total_ref, held, sems) = rest[:2], rest[2 : 2 + len(early)], rest[2 + len(early) :]
    tokens = held.shape[1]
    part = tokens // sems.shape[1]
    copies = [
        [
            pltpu.make_async_copy(source.at[pl.ds(i * part, part)], held.at[t, pl.ds(i * part, part)], sems.at[t, i])
            for i in range(sems.shape[1])
        ]
        for t, source in enumerate(inputs)
    ]
    for copy in copies[0] + copies[1]:
        copy.start()
    rows = blocks[0].shape[0] // 2
    source = sources(me_ref[0], n)
    for t in range(2):
        for copy in copies[t]:
            copy.wait()
        total = None
        for which, block in zip(early, blocks):
            columns = pl.ds(pl.multiple_of(source[which] * rows, rows), rows)
            term = jnp.dot(
                held[t, :, columns], block[t * rows : (t + 1) * rows, :], preferred_element_type=jnp.float32
            )
            total = term if total is None else total + term
        total_ref[t] = total


def project_whole_kernel(n, me_ref, act_ref, grad_ref, *rest):
    blocks, (total_ref, proj) = rest[:n], rest[n:]
    rows = blocks[0].shape[0] // 2
    for block, source in zip(blocks, sources(me_ref[0], n)):
        at = pl.ds(pl.multiple_of(source * rows, rows), rows)
        for t in range(2):
            proj[t, at, :] = block[t * rows : (t + 1) * rows, :]
    for t, ref in enumerate((act_ref, grad_ref)):
        total_ref[t] = jnp.dot(ref[...], proj[t], preferred_element_type=jnp.float32)


def project(me, activations, out_grads, blocks, early, seqs, n):
    tokens, width = activations.shape
    rank = blocks[0].shape[1]
    total = jax.ShapeDtypeStruct((2, tokens, rank), jnp.float32)
    common = dict(
        compiler_params=pltpu.CompilerParams(vmem_limit_bytes=16 << 20),
        cost_estimate=pl.CostEstimate(flops=rank, bytes_accessed=rank, transcendentals=0),
        name="project",
    )
    if len(early) == n:
        result = pl.pallas_call(
            functools.partial(project_whole_kernel, n),
            out_shape=total,
            in_specs=[SMEM] + [VMEM] * (2 + n),
            out_specs=VMEM,
            scratch_shapes=[pltpu.VMEM((2, width, rank), jnp.bfloat16)],
            **common,
        )(me, activations, out_grads, *blocks)
        return result, None
    return pl.pallas_call(
        functools.partial(project_kernel, n, early, seqs),
        out_shape=(
            total,
            jax.ShapeDtypeStruct((2, tokens, width), activations.dtype),
        ),
        in_specs=[SMEM, HBM, HBM] + [VMEM] * len(early),
        out_specs=(VMEM, VMEM),
        scratch_shapes=[pltpu.SemaphoreType.DMA((2, 2 * seqs))],
        **common,
    )(me, pinned(activations), pinned(out_grads), *blocks)


def whiten_kernel(n, seqs, late, me_ref, total_ref, k_ref, *rest):
    operands, (keep_ref, send_ref, white) = rest[:-3], rest[-3:]
    rank = k_ref.shape[1]
    sums = [total_ref[0], total_ref[1]]
    if late:
        held, *blocks = operands
        source = sources(me_ref[0], n)
        rows = held.shape[2] // n
        for which, operand, at in late:
            columns = pl.ds(pl.multiple_of(source[which] * rows, rows), rows)
            for t in range(2):
                block = blocks[operand][(2 * at + t) * rows : (2 * at + t + 1) * rows, :]
                sums[t] = sums[t] + jnp.dot(held[t, :, columns], block, preferred_element_type=jnp.float32)
    length = total_ref.shape[1] // seqs
    share = rank // n
    grads = []
    for s in range(seqs):
        token = slice(s * length, (s + 1) * length)
        x_proj = (sums[0][token, :] * k_ref[2][:length, s : s + 1]).astype(jnp.bfloat16)
        d_proj = sums[1][token, :].astype(jnp.bfloat16)
        grads.append(
            lax.dot_general(d_proj, x_proj, (((0,), (0,)), ((), ())), preferred_element_type=jnp.float32)
        )
    left = product(k_ref[1], jnp.concatenate(grads, axis=1))
    left = jnp.concatenate([left[:, s * rank : (s + 1) * rank] for s in range(seqs)], axis=0)
    full = product(left, k_ref[0])
    for s in range(seqs):
        for d in range(n):
            at = s * rank + d * share
            white[d, s * share : (s + 1) * share, :] = full[at : at + share, :]
    bit = lax.rem(me_ref[0], 2)
    for j in range(n // 2):
        keep_ref[j, 0] = white[2 * j + bit].astype(jnp.bfloat16)
        send_ref[j, 0] = white[2 * j + 1 - bit].astype(jnp.bfloat16)


def whitened_blocks(me, total, k, late, operands, seqs, n):
    rank = k.shape[1]
    rows = seqs * (rank // n)
    half = jax.ShapeDtypeStruct((n // 2, 1, rows, rank), jnp.bfloat16)
    return pl.pallas_call(
        functools.partial(whiten_kernel, n, seqs, late),
        out_shape=(half, half),
        in_specs=[SMEM] + [VMEM] * (2 + len(operands)),
        out_specs=(VMEM, VMEM),
        scratch_shapes=[pltpu.VMEM((n, rows, rank), jnp.float32)],
        compiler_params=pltpu.CompilerParams(vmem_limit_bytes=16 << 20),
        cost_estimate=pl.CostEstimate(flops=64 * rank**3, bytes_accessed=4 << 20, transcendentals=0),
        name="whiten",
    )(me, total, k, *operands)


def regroup_kernel(step, me_ref, keep_ref, recv_ref, *out_refs):
    count = keep_ref.shape[1]
    bit = lax.rem(lax.div(me_ref[0], 1 << step), 2)
    following = lax.rem(lax.div(me_ref[0], 2 << step), 2)
    for j in range(out_refs[0].shape[0]):
        for out_ref, which in zip(out_refs, (following, 1 - following)):
            at = 2 * j + which if len(out_refs) > 1 else j
            out_ref[j, pl.ds(bit * count, count)] = keep_ref[at]
            out_ref[j, pl.ds((1 - bit) * count, count)] = recv_ref[at]


def regroup(me, keep, recv, step):
    left, count, *block = keep.shape
    outs = 2 if left > 1 else 1
    return pl.pallas_call(
        functools.partial(regroup_kernel, step),
        out_shape=(jax.ShapeDtypeStruct((max(left // 2, 1), 2 * count, *block), keep.dtype),) * outs,
        in_specs=[SMEM, VMEM, VMEM],
        out_specs=(VMEM,) * outs,
        compiler_params=pltpu.CompilerParams(vmem_limit_bytes=16 << 20),
        name="regroup",
    )(me, keep, recv)


def with_partner(value, step, n):
    return lax.ppermute(value, "coord", [(at, at ^ (1 << step)) for at in range(n)])


def exchange(me, keep, send, n):
    step = 0
    while True:
        parts = regroup(me, keep, with_partner(send, step, n), step)
        if len(parts) == 1:
            return parts[0][0]
        keep, send = parts
        step += 1


def score_type(step):
    return jnp.bfloat16 if step == 1 else jnp.float32


def add_kernel(step, me_ref, keep_ref, recv_ref, next_ref, send_ref):
    following = lax.rem(lax.div(me_ref[0], 2 << step), 2)
    for j in range(next_ref.shape[0]):
        for out_ref, which in ((next_ref, following), (send_ref, 1 - following)):
            at = 2 * j + which
            out_ref[j] = (keep_ref[at] + recv_ref[at].astype(jnp.float32)).astype(out_ref.dtype)


def add(me, keep, recv, step):
    left, *block = keep.shape
    return pl.pallas_call(
        functools.partial(add_kernel, step),
        out_shape=(
            jax.ShapeDtypeStruct((left // 2, *block), jnp.float32),
            jax.ShapeDtypeStruct((left // 2, *block), score_type(step + 1)),
        ),
        in_specs=[SMEM, VMEM, VMEM],
        out_specs=(VMEM, VMEM),
        compiler_params=pltpu.CompilerParams(vmem_limit_bytes=32 << 20),
        name="add",
    )(me, keep, recv)


def summed(me, keep, send, n):
    step = 0
    while True:
        recv = with_partner(send, step, n)
        if keep.shape[0] == 1:
            return keep[0], recv[0]
        keep, send = add(me, keep, recv, step)
        step += 1


def score_kernel(n, me_ref, ids_ref, white_ref, bank_ref, keep_ref, send_ref, spread):
    seqs = ids_ref.shape[0]
    chunk, rank = white_ref.shape[1:]
    share = chunk // seqs
    total = n * seqs
    spread[...] = white_ref[...].astype(jnp.float32).reshape(n * chunk, rank)
    columns = jnp.concatenate(
        [spread[pl.ds(j, total, stride=share), :].astype(jnp.bfloat16) for j in range(share)], axis=1
    )
    queries = bank_ref.shape[0] // n
    row = lax.broadcasted_iota(jnp.int32, (total, keep_ref.shape[2] - queries), 0)
    tail = jnp.zeros(row.shape, jnp.float32)
    for s in range(seqs):
        tail = jnp.where(row == me_ref[0] * seqs + s, ids_ref[s].astype(jnp.float32), tail)
    partial = lax.dot_general(
        columns, bank_ref[...], (((1,), (1,)), ((), ())), preferred_element_type=jnp.float32
    )
    odd = lax.rem(me_ref[0], 2) == 1
    for j in range(n // 2):
        even_part, odd_part = (partial[:, d * queries : (d + 1) * queries] for d in (2 * j, 2 * j + 1))
        for out_ref, flip in ((keep_ref, odd), (send_ref, jnp.logical_not(odd))):
            out_ref[j, :, :queries] = jnp.where(flip, odd_part, even_part).astype(out_ref.dtype)
            out_ref[j, :, queries:] = tail.astype(out_ref.dtype)


def partial_scores(me, seq_ids, white, bank):
    n = white.shape[0]
    seqs = seq_ids.shape[0]
    queries = bank.shape[0] // n
    width = (queries // LANES + 1) * LANES
    return pl.pallas_call(
        functools.partial(score_kernel, n),
        out_shape=(
            jax.ShapeDtypeStruct((n // 2, n * seqs, width), jnp.float32),
            jax.ShapeDtypeStruct((n // 2, n * seqs, width), score_type(0)),
        ),
        in_specs=[SMEM, SMEM, VMEM, VMEM],
        out_specs=(VMEM, VMEM),
        scratch_shapes=[pltpu.VMEM((n * white.shape[1], white.shape[2]), jnp.float32)],
        compiler_params=pltpu.CompilerParams(vmem_limit_bytes=16 << 20),
        cost_estimate=pl.CostEstimate(
            flops=2 * n * seqs * bank.size, bytes_accessed=2 * bank.size, transcendentals=0
        ),
        name="score",
    )(me, seq_ids, white, bank)


def place_kernel(first_ref, second_ref, out_ref):
    rows, queries = out_ref.shape
    total = first_ref[...] + second_ref[...].astype(jnp.float32)
    raw = total[:, :queries].astype(jnp.bfloat16)
    ids = total[:, queries : queries + 1].astype(jnp.int32)
    chosen = ids == lax.broadcasted_iota(jnp.int32, (rows, rows), 1)
    out_ref[...] = lax.dot_general(
        chosen.astype(jnp.bfloat16), raw, (((0,), (0,)), ((), ())), preferred_element_type=jnp.float32
    ).astype(jnp.bfloat16)


def place(first, second, queries):
    return pl.pallas_call(
        lambda a, b, c: place_kernel(a, b, c),
        out_shape=jax.ShapeDtypeStruct((first.shape[0], queries), jnp.bfloat16),
        in_specs=[VMEM, VMEM],
        out_specs=VMEM,
        compiler_params=pltpu.CompilerParams(vmem_limit_bytes=16 << 20),
        name="place",
    )(first, second)


def body(n, activations, out_grads, proj_in, proj_out, cov_in, cov_out, lengths, seq_ids, bank):
    me = lax.axis_index("coord").reshape(1)
    seqs, length, width = activations.shape
    activations, out_grads = activations.reshape(seqs * length, width), out_grads.reshape(seqs * length, width)
    a, b, c = factors(n)
    paired = a & (a - 1) == 0
    packed = pack(proj_in, proj_out)
    half = first_half(cov_in, cov_out)
    held = {(0, 0, 0): packed}
    for at in range(1, min(a, 3)):
        held[at, 0, 0] = moved(packed, (at, 0, 0), n)
    for by in range(1, b):
        held[0, by, 0] = moved(packed, (0, by, 0), n)
    held, half = lax.optimization_barrier((held, half))
    early = list(held)
    wanted = {}
    for at in range(1, a):
        nearest = at & -at
        source = at - nearest if paired and nearest != at else 0
        if at > 2:
            wanted[at, 0, 0] = (source, 0, 0), (at - source, 0, 0)
        for by in range(1, b):
            if source or at > 2:
                wanted[at, by, 0] = (source, 0, 0), (at - source, by, 0)
            elif at == 1:
                wanted[at, by, 0] = (0, by, 0), (1, 0, 0)
            else:
                wanted[at, by, 0] = (at, 0, 0), (0, by, 0)
    size = packed.shape[0]
    later = []
    while wanted:
        steps = {}
        for to, (source, step) in wanted.items():
            if source in held:
                steps.setdefault(step, []).append((to, source))
        for step, both in steps.items():
            arrived = moved(merge([held[source] for _, source in both]), step, n)
            later.append((arrived, [to for to, _ in both]))
            for i, (to, _) in enumerate(both):
                held[to] = arrived[i * size : (i + 1) * size] if len(both) > 1 else arrived
                del wanted[to]
    k = second_half(half, lengths)
    order = [(at, by, core) for core in range(c) for by in range(b) for at in range(a)]
    if proj_in.shape[0] % LANES == 0 and later and c == 2:
        total, inputs = project(
            me, activations, out_grads, [held[at] for at in early], [order.index(at) for at in early], seqs, n
        )
        across = [moved(merge([held[at] for at in early]), (0, 0, 1), n)]
        waiting, total, k = lax.optimization_barrier(([arrived for arrived, _ in later], total, k))
        across.append(moved(merge(waiting), (0, 0, 1), n))
        operands = [inputs, *across, *waiting]
        last = [at for _, group in later for at in group]
        late = [(order.index(at), 2 + t, i) for t, (_, group) in enumerate(later) for i, at in enumerate(group)]
        late += [(order.index((*at[:2], 1)), t, i) for t, part in enumerate((early, last)) for i, at in enumerate(part)]
    else:
        for at in list(held):
            for by in range(1, c):
                held[at[0], at[1], by] = moved(held[at], (0, 0, by), n)
        total = project(me, activations, out_grads, [held[at] for at in order], list(range(n)), seqs, n)[0]
        operands, late = [], []
    keep, send = whitened_blocks(me, total, k, late, operands, seqs, n)
    keep, send = partial_scores(me, seq_ids, exchange(me, keep, send, n), bank)
    return place(*summed(me, keep, send, n), bank.shape[0] // n)


def solution(mesh):
    in_specs = (
        P(("groups", "coord"), None, None),
        P(("groups", "coord"), None, None),
        P("coord", None),
        P("coord", None),
        P(),
        P(),
        P(("groups", "coord")),
        P(("groups", "coord")),
        P(None, "coord"),
    )
    out_specs = P("groups", "coord")
    return jax.shard_map(
        functools.partial(body, mesh.shape["coord"]),
        mesh=mesh,
        in_specs=in_specs,
        out_specs=out_specs,
        check_vma=False,
    )
```

```python
import functools

import jax
import jax.numpy as jnp
from jax import lax
from jax.experimental import pallas as pl
from jax.experimental.pallas import tpu as pltpu
from jax.sharding import PartitionSpec as P

SUB = 8
LANES = 128
EXACT = lax.Precision.HIGHEST
VMEM = pl.BlockSpec(memory_space=pltpu.VMEM)
HBM = pl.BlockSpec(memory_space=pltpu.HBM)
SMEM = pl.BlockSpec(memory_space=pltpu.SMEM)


def factors(n):
    c = 2 if n % 2 == 0 else 1
    rest = n // c
    b = max(f for f in range(1, rest + 1) if rest % f == 0 and f * f <= rest)
    return rest // b, b, c


def partner(at, by, size, towards):
    if size & (size - 1) == 0:
        return at ^ by
    return (at + (by if towards else size - by)) % size


def sources(me, n):
    a, b, c = factors(n)
    ia, ib, ic = me // (b * c), (me // c) % b, me % c
    return [
        (partner(ia, da, a, False) * b + partner(ib, db, b, False)) * c + partner(ic, dc, c, False)
        for dc in range(c)
        for db in range(b)
        for da in range(a)
    ]


def moved(value, by, n):
    sizes = factors(n)
    a, b, c = sizes
    pairs = []
    for me in range(n):
        at = (me // (b * c), (me // c) % b, me % c)
        to = [partner(place, step, size, True) for place, step, size in zip(at, by, sizes)]
        pairs.append((me, (to[0] * b + to[1]) * c + to[2]))
    return lax.ppermute(value, "coord", pairs)


def pack_kernel(first_hbm, second_hbm, out_ref, sems):
    rows = first_hbm.shape[0]
    copies = [
        pltpu.make_async_copy(source, out_ref.at[pl.ds(i * rows, rows)], sems.at[i])
        for i, source in enumerate((first_hbm, second_hbm))
    ]
    for copy in copies:
        copy.start()
    for copy in copies:
        copy.wait()


def pack(first, second):
    rows, columns = first.shape
    return pl.pallas_call(
        pack_kernel,
        out_shape=jax.ShapeDtypeStruct((2 * rows, columns), first.dtype),
        in_specs=[HBM, HBM],
        out_specs=VMEM,
        scratch_shapes=[pltpu.SemaphoreType.DMA((2,))],
        compiler_params=pltpu.CompilerParams(vmem_limit_bytes=8 << 20),
        name="pack",
    )(pinned(first), pinned(second))


def pinned(value):
    return pltpu.with_memory_space_constraint(value, pltpu.HBM)


def gauss_jordan(blocks):
    width = blocks[0].shape[1]
    half = width // 2
    lane = lax.broadcasted_iota(jnp.int32, (SUB, width), 1)
    sub = lax.broadcasted_iota(jnp.int32, (SUB, width), 0)
    start, within = lane // half * half, lane % half

    def column(block, at):
        return jnp.take_along_axis(block, start + at, axis=1, mode="promise_in_bounds")

    for k in range(len(blocks)):
        at = k * SUB
        head = within // SUB == k
        rows = [jnp.broadcast_to(blocks[k][i : i + 1, :], (SUB, width)) for i in range(SUB)]
        diag = {(i, j): column(rows[i], at + j) for i in range(SUB) for j in range(i, SUB)}
        rows = [jnp.where(head, (within == at + i).astype(jnp.float32), rows[i]) for i in range(SUB)]
        inverse, factor = [], {}
        for p in range(SUB):
            inverse.append(1.0 / diag[p, p])
            for i in range(p + 1, SUB):
                factor[p, i] = diag[p, i] * inverse[p]
                for j in range(i, SUB):
                    diag[i, j] = diag[i, j] - factor[p, i] * diag[p, j]
                rows[i] = rows[i] - factor[p, i] * rows[p]
        rows = [rows[p] * inverse[p] for p in range(SUB)]
        for p in reversed(range(SUB)):
            for i in range(p):
                rows[i] = rows[i] - factor[i, p] * rows[p]
        done = rows[0]
        for i in range(1, SUB):
            done = jnp.where(sub == i, rows[i], done)
        out = []
        for g, block in enumerate(blocks):
            if g == k:
                out.append(done)
                continue
            terms = [column(block, at + p) * rows[p] for p in range(SUB)]
            while len(terms) > 1:
                terms = [terms[i] + terms[i + 1] for i in range(0, len(terms), 2)]
            out.append(jnp.where(head, 0.0, block) - terms[0])
        blocks = out
    return blocks


def side_by_side_inverses(first, second):
    half = first.shape[0]
    both = jnp.concatenate([first, second], axis=1)
    blocks = gauss_jordan([both[g : g + SUB, :] for g in range(0, half, SUB)])
    both = jnp.concatenate(blocks, axis=0)
    return both[:, :half], both[:, half:]


def damped(cov):
    size = cov.shape[0]
    cov = 0.5 * (cov + cov.T)
    row = lax.broadcasted_iota(jnp.int32, (size, size), 0)
    col = lax.broadcasted_iota(jnp.int32, (size, size), 1)
    damping = 0.1 * jnp.sum(jnp.where(row == col, cov, 0.0)) / size
    return jnp.where(row == col, cov + damping, cov)


def product(left, right, dims=((1,), (0,))):
    return lax.dot_general(left, right, (dims, ((), ())), precision=EXACT, preferred_element_type=jnp.float32)


def first_half_kernel(cov_in_hbm, cov_out_hbm, out_ref, cov_ref, sems):
    copies = [
        pltpu.make_async_copy(source, cov_ref.at[i], sems.at[i]) for i, source in enumerate((cov_in_hbm, cov_out_hbm))
    ]
    for copy in copies:
        copy.start()
    for copy in copies:
        copy.wait()
    half = cov_ref.shape[1] // 2
    covs = [damped(cov_ref[0]), damped(cov_ref[1])]
    corner = [cov[:half, half:] for cov in covs]
    upper = side_by_side_inverses(*[cov[:half, :half] for cov in covs])
    solved = [product(u, c) for u, c in zip(upper, corner)]
    schur = [cov[half:, half:] - product(c, t, ((0,), (0,))) for cov, c, t in zip(covs, corner, solved)]
    for i, pair in enumerate((upper, solved, schur)):
        out_ref[i] = jnp.concatenate(pair, axis=1)


def second_half_kernel(first_ref, len_hbm, k_ref, len_ref, sem):
    copy = pltpu.make_async_copy(len_hbm, len_ref, sem)
    copy.start()
    size = k_ref.shape[1]
    half = size // 2
    upper, solved, schur = [(first_ref[i][:, :half], first_ref[i][:, half:]) for i in range(3)]
    lower = side_by_side_inverses(*schur)
    for m, (u, t, low) in enumerate(zip(upper, solved, lower)):
        side = product(t, low)
        k_ref[m, :half, :half] = u + product(side, t, ((1,), (1,)))
        k_ref[m, :half, half:] = -side
        k_ref[m, half:, :half] = -side.T
        k_ref[m, half:, half:] = low
    copy.wait()
    token = lax.broadcasted_iota(jnp.int32, (size, size), 0)
    lane = lax.broadcasted_iota(jnp.int32, (size, size), 1)
    mask = jnp.zeros((size, size), jnp.float32)
    for s in range(len_ref.shape[0]):
        mask = jnp.where((lane == s) & (token < len_ref[s]), 1.0, mask)
    k_ref[2] = mask


def first_half(cov_in, cov_out):
    size = cov_in.shape[0]
    return pl.pallas_call(
        first_half_kernel,
        out_shape=jax.ShapeDtypeStruct((3, size // 2, size), jnp.float32),
        in_specs=[HBM, HBM],
        out_specs=VMEM,
        scratch_shapes=[pltpu.VMEM((2, size, size), jnp.float32), pltpu.SemaphoreType.DMA((2,))],
        compiler_params=pltpu.CompilerParams(vmem_limit_bytes=8 << 20),
        cost_estimate=pl.CostEstimate(flops=size, bytes_accessed=size, transcendentals=0),
        name="first_half",
    )(pinned(cov_in), pinned(cov_out))


def second_half(first, lengths):
    size = first.shape[2]
    return pl.pallas_call(
        second_half_kernel,
        out_shape=jax.ShapeDtypeStruct((3, size, size), jnp.float32),
        in_specs=[VMEM, HBM],
        out_specs=VMEM,
        scratch_shapes=[pltpu.SMEM(lengths.shape, jnp.int32), pltpu.SemaphoreType.DMA],
        compiler_params=pltpu.CompilerParams(vmem_limit_bytes=8 << 20),
        cost_estimate=pl.CostEstimate(flops=size, bytes_accessed=size, transcendentals=0),
        name="second_half",
    )(first, pinned(lengths))


def merge_kernel(spans, *refs):
    at = 0
    for ref, (start, rows) in zip(refs[:-1], spans):
        refs[-1][at : at + rows, :] = ref[start : start + rows, :]
        at += rows


def merge(parts):
    array, start, rows = parts[0]
    if len(parts) == 1 and rows == array.shape[0]:
        return array
    total = sum(part[2] for part in parts)
    return pl.pallas_call(
        functools.partial(merge_kernel, [part[1:] for part in parts]),
        out_shape=jax.ShapeDtypeStruct((total, array.shape[1]), array.dtype),
        in_specs=[VMEM] * len(parts),
        out_specs=VMEM,
        compiler_params=pltpu.CompilerParams(vmem_limit_bytes=16 << 20),
        cost_estimate=pl.CostEstimate(flops=total, bytes_accessed=total, transcendentals=0),
        name="merge",
    )(*(part[0] for part in parts))


def joined(parts):
    out = []
    for array, start, rows in parts:
        if out and out[-1][0] is array and out[-1][1] + out[-1][2] == start:
            out[-1] = (array, out[-1][1], out[-1][2] + rows)
        else:
            out.append((array, start, rows))
    return out


def project_kernel(n, early, seqs, me_ref, *rest):
    inputs, blocks, (total_ref, held, sems) = rest[:2], rest[2 : 2 + len(early)], rest[2 + len(early) :]
    tokens = held.shape[1]
    part = tokens // sems.shape[1]
    copies = [
        [
            pltpu.make_async_copy(source.at[pl.ds(i * part, part)], held.at[t, pl.ds(i * part, part)], sems.at[t, i])
            for i in range(sems.shape[1])
        ]
        for t, source in enumerate(inputs)
    ]
    for copy in copies[0] + copies[1]:
        copy.start()
    rows = blocks[0].shape[0] // 2
    source = sources(me_ref[0], n)
    for t in range(2):
        for copy in copies[t]:
            copy.wait()
        total = None
        for which, block in zip(early, blocks):
            columns = pl.ds(pl.multiple_of(source[which] * rows, rows), rows)
            term = jnp.dot(
                held[t, :, columns], block[t * rows : (t + 1) * rows, :], preferred_element_type=jnp.float32
            )
            total = term if total is None else total + term
        total_ref[t] = total


def project_whole_kernel(n, me_ref, act_ref, grad_ref, *rest):
    blocks, (total_ref, proj) = rest[:n], rest[n:]
    rows = blocks[0].shape[0] // 2
    for block, source in zip(blocks, sources(me_ref[0], n)):
        at = pl.ds(pl.multiple_of(source * rows, rows), rows)
        for t in range(2):
            proj[t, at, :] = block[t * rows : (t + 1) * rows, :]
    for t, ref in enumerate((act_ref, grad_ref)):
        total_ref[t] = jnp.dot(ref[...], proj[t], preferred_element_type=jnp.float32)


def project(me, activations, out_grads, blocks, early, seqs, n):
    tokens, width = activations.shape
    rank = blocks[0].shape[1]
    total = jax.ShapeDtypeStruct((2, tokens, rank), jnp.float32)
    common = dict(
        compiler_params=pltpu.CompilerParams(vmem_limit_bytes=16 << 20),
        cost_estimate=pl.CostEstimate(flops=rank, bytes_accessed=rank, transcendentals=0),
        name="project",
    )
    if len(early) == n:
        result = pl.pallas_call(
            functools.partial(project_whole_kernel, n),
            out_shape=total,
            in_specs=[SMEM] + [VMEM] * (2 + n),
            out_specs=VMEM,
            scratch_shapes=[pltpu.VMEM((2, width, rank), jnp.bfloat16)],
            **common,
        )(me, activations, out_grads, *blocks)
        return result, None
    return pl.pallas_call(
        functools.partial(project_kernel, n, early, seqs),
        out_shape=(
            total,
            jax.ShapeDtypeStruct((2, tokens, width), activations.dtype),
        ),
        in_specs=[SMEM, HBM, HBM] + [VMEM] * len(early),
        out_specs=(VMEM, VMEM),
        scratch_shapes=[pltpu.SemaphoreType.DMA((2, 2 * seqs))],
        **common,
    )(me, pinned(activations), pinned(out_grads), *blocks)


def whiten_kernel(n, seqs, late, me_ref, total_ref, k_ref, *rest):
    operands, (out_ref, white) = rest[:-2], rest[-2:]
    rank = k_ref.shape[1]
    sums = [total_ref[0], total_ref[1]]
    if late:
        held, *blocks = operands
        source = sources(me_ref[0], n)
        rows = held.shape[2] // n
        for which, t, operand, at in late:
            columns = pl.ds(pl.multiple_of(source[which] * rows, rows), rows)
            block = blocks[operand][at : at + rows, :]
            sums[t] = sums[t] + jnp.dot(held[t, :, columns], block, preferred_element_type=jnp.float32)
    length = total_ref.shape[1] // seqs
    share = rank // n
    grads = []
    for s in range(seqs):
        token = slice(s * length, (s + 1) * length)
        x_proj = (sums[0][token, :] * k_ref[2][:length, s : s + 1]).astype(jnp.bfloat16)
        d_proj = sums[1][token, :].astype(jnp.bfloat16)
        grads.append(
            lax.dot_general(d_proj, x_proj, (((0,), (0,)), ((), ())), preferred_element_type=jnp.float32)
        )
    left = product(k_ref[1], jnp.concatenate(grads, axis=1))
    left = jnp.concatenate([left[:, s * rank : (s + 1) * rank] for s in range(seqs)], axis=0)
    full = product(left, k_ref[0])
    for s in range(seqs):
        for d in range(n):
            at = s * rank + d * share
            white[d, s * share : (s + 1) * share, :] = full[at : at + share, :]
    out_ref[...] = white[...].astype(jnp.bfloat16)


def whitened_blocks(me, total, k, late, operands, seqs, n):
    rank = k.shape[1]
    shape = (n, seqs * (rank // n), rank)
    return pl.pallas_call(
        functools.partial(whiten_kernel, n, seqs, late),
        out_shape=jax.ShapeDtypeStruct(shape, jnp.bfloat16),
        in_specs=[SMEM] + [VMEM] * (2 + len(operands)),
        out_specs=VMEM,
        scratch_shapes=[pltpu.VMEM(shape, jnp.float32)],
        compiler_params=pltpu.CompilerParams(vmem_limit_bytes=16 << 20),
        cost_estimate=pl.CostEstimate(flops=64 * rank**3, bytes_accessed=4 << 20, transcendentals=0),
        name="whiten",
    )(me, total, k, *operands)


def add_kernel(first_ref, second_ref, out_ref):
    out_ref[...] = (first_ref[...] + second_ref[...]).astype(out_ref.dtype)


def add(first, second):
    return pl.pallas_call(
        add_kernel,
        out_shape=jax.ShapeDtypeStruct(first.shape, jnp.bfloat16),
        in_specs=[VMEM, VMEM],
        out_specs=VMEM,
        compiler_params=pltpu.CompilerParams(vmem_limit_bytes=32 << 20),
        name="add",
    )(first, second)


def summed_pieces(keep, send, n):
    both = add(keep, moved(send, (0, 0, 1), n))
    groups = [list(range(core, n, 2)) for core in range(2)]
    return lax.all_to_all(both, "coord", split_axis=0, concat_axis=0, axis_index_groups=groups, tiled=True)


def score_kernel(n, me_ref, ids_ref, white_ref, bank_ref, keep_ref, send_ref, spread):
    seqs = ids_ref.shape[0]
    chunk, rank = white_ref.shape[1:]
    share = chunk // seqs
    total = n * seqs
    spread[...] = white_ref[...].astype(jnp.float32).reshape(n * chunk, rank)
    columns = jnp.concatenate(
        [spread[pl.ds(j, total, stride=share), :].astype(jnp.bfloat16) for j in range(share)], axis=1
    )
    queries = bank_ref.shape[0] // n
    row = lax.broadcasted_iota(jnp.int32, (total, keep_ref.shape[2] - queries), 0)
    tail = jnp.zeros(row.shape, jnp.float32)
    for s in range(seqs):
        tail = jnp.where(row == me_ref[0] * seqs + s, ids_ref[s].astype(jnp.float32), tail)
    partial = lax.dot_general(
        columns, bank_ref[...], (((1,), (1,)), ((), ())), preferred_element_type=jnp.float32
    )
    odd = lax.rem(me_ref[0], 2) == 1
    for j in range(n // 2):
        even_part, odd_part = (partial[:, d * queries : (d + 1) * queries] for d in (2 * j, 2 * j + 1))
        for out_ref, flip in ((keep_ref, odd), (send_ref, jnp.logical_not(odd))):
            out_ref[j, :, :queries] = jnp.where(flip, odd_part, even_part).astype(out_ref.dtype)
            out_ref[j, :, queries:] = tail.astype(out_ref.dtype)


def partial_scores(me, seq_ids, white, bank):
    n = white.shape[0]
    seqs = seq_ids.shape[0]
    queries = bank.shape[0] // n
    width = (queries // LANES + 1) * LANES
    return pl.pallas_call(
        functools.partial(score_kernel, n),
        out_shape=(
            jax.ShapeDtypeStruct((n // 2, n * seqs, width), jnp.float32),
            jax.ShapeDtypeStruct((n // 2, n * seqs, width), jnp.float32),
        ),
        in_specs=[SMEM, SMEM, VMEM, VMEM],
        out_specs=(VMEM, VMEM),
        scratch_shapes=[pltpu.VMEM((n * white.shape[1], white.shape[2]), jnp.float32)],
        compiler_params=pltpu.CompilerParams(vmem_limit_bytes=16 << 20),
        cost_estimate=pl.CostEstimate(
            flops=2 * n * seqs * bank.size, bytes_accessed=2 * bank.size, transcendentals=0
        ),
        name="score",
    )(me, seq_ids, white, bank)


def place_kernel(partial_ref, out_ref):
    rows, queries = out_ref.shape
    total = jnp.sum(partial_ref[...].astype(jnp.float32), axis=0)
    raw = total[:, :queries].astype(jnp.bfloat16)
    ids = total[:, queries : queries + 1].astype(jnp.int32)
    chosen = ids == lax.broadcasted_iota(jnp.int32, (rows, rows), 1)
    out_ref[...] = lax.dot_general(
        chosen.astype(jnp.bfloat16), raw, (((0,), (0,)), ((), ())), preferred_element_type=jnp.float32
    ).astype(jnp.bfloat16)


def place(partials, queries):
    return pl.pallas_call(
        lambda a, b: place_kernel(a, b),
        out_shape=jax.ShapeDtypeStruct((partials.shape[1], queries), jnp.bfloat16),
        in_specs=[VMEM],
        out_specs=VMEM,
        compiler_params=pltpu.CompilerParams(vmem_limit_bytes=16 << 20),
        name="place",
    )(partials)


def body(n, activations, out_grads, proj_in, proj_out, cov_in, cov_out, lengths, seq_ids, bank):
    me = lax.axis_index("coord").reshape(1)
    seqs, length, width = activations.shape
    activations, out_grads = activations.reshape(seqs * length, width), out_grads.reshape(seqs * length, width)
    a, b, c = factors(n)
    paired = a & (a - 1) == 0
    packed = pack(proj_in, proj_out)
    half = first_half(cov_in, cov_out)
    held = {(0, 0, 0): packed}
    for at in range(1, min(a, 3)):
        held[at, 0, 0] = moved(packed, (at, 0, 0), n)
    for by in range(1, b):
        held[0, by, 0] = moved(packed, (0, by, 0), n)
    held, half = lax.optimization_barrier((held, half))
    early = list(held)
    rows = proj_in.shape[0]
    halves = {(at, t): (held[at], t * rows, rows) for at in early for t in range(2)}
    wanted = {}
    for at in range(1, a):
        nearest = at & -at
        source = at - nearest if paired and nearest != at else 0
        for by in range(b):
            for t in range(2):
                if ((at, by, 0), t) in halves:
                    continue
                if source or at > 2:
                    wanted[(at, by, 0), t] = (source, 0, 0), (at - source, by, 0)
                elif at == 1 and t == 0:
                    wanted[(at, by, 0), t] = (0, by, 0), (1, 0, 0)
                else:
                    wanted[(at, by, 0), t] = (at, 0, 0), (0, by, 0)
    arrivals = []
    while wanted:
        steps = {}
        for to, (source, step) in wanted.items():
            if (source, to[1]) in halves:
                steps.setdefault(step, []).append((to, source))
        for step, both in steps.items():
            arrived = moved(merge(joined([halves[source, to[1]] for to, source in both])), step, n)
            arrivals.append((arrived, [to for to, _ in both]))
            for i, (to, _) in enumerate(both):
                halves[to] = arrived, i * rows, rows
                del wanted[to]
    k = second_half(half, lengths)
    order = [(at, by, core) for core in range(c) for by in range(b) for at in range(a)]
    if rows % LANES == 0 and arrivals and c == 2:
        total, inputs = project(
            me, activations, out_grads, [held[at] for at in early], [order.index(at) for at in early], seqs, n
        )
        across = [moved(merge([(held[at], 0, 2 * rows) for at in early]), (0, 0, 1), n)]
        waiting, total, k = lax.optimization_barrier(([arrived for arrived, _ in arrivals], total, k))
        across.append(moved(merge([(arrived, 0, arrived.shape[0]) for arrived in waiting]), (0, 0, 1), n))
        operands = [inputs, *across, *waiting]
        late = [
            (order.index(at), t, 2 + i, j * rows)
            for i, (_, group) in enumerate(arrivals)
            for j, (at, t) in enumerate(group)
        ]
        crossed = [[(at, t) for at in early for t in range(2)], [to for _, group in arrivals for to in group]]
        late += [
            (order.index((*at[:2], 1)), t, i, j * rows) for i, part in enumerate(crossed) for j, (at, t) in enumerate(part)
        ]
    else:
        for at in order:
            if at[2] == 0:
                held[at] = merge(joined([halves[at, 0], halves[at, 1]]))
                for by in range(1, c):
                    held[at[0], at[1], by] = moved(held[at], (0, 0, by), n)
        total = project(me, activations, out_grads, [held[at] for at in order], list(range(n)), seqs, n)[0]
        operands, late = [], []
    white = whitened_blocks(me, total, k, late, operands, seqs, n)
    white = lax.all_to_all(white, "coord", split_axis=0, concat_axis=0, tiled=True)
    keep, send = partial_scores(me, seq_ids, white, bank)
    return place(summed_pieces(keep, send, n), bank.shape[0] // n)


def solution(mesh):
    in_specs = (
        P(("groups", "coord"), None, None),
        P(("groups", "coord"), None, None),
        P("coord", None),
        P("coord", None),
        P(),
        P(),
        P(("groups", "coord")),
        P(("groups", "coord")),
        P(None, "coord"),
    )
    out_specs = P("groups", "coord")
    return jax.shard_map(
        functools.partial(body, mesh.shape["coord"]),
        mesh=mesh,
        in_specs=in_specs,
        out_specs=out_specs,
        check_vma=False,
    )
```

```python
import functools

import jax
import jax.numpy as jnp
from jax import lax
from jax.experimental import pallas as pl
from jax.experimental.pallas import tpu as pltpu
from jax.sharding import PartitionSpec as P

SUB = 8
LANES = 128
EXACT = lax.Precision.HIGHEST
VMEM = pl.BlockSpec(memory_space=pltpu.VMEM)
HBM = pl.BlockSpec(memory_space=pltpu.HBM)
SMEM = pl.BlockSpec(memory_space=pltpu.SMEM)


def factors(n):
    c = 2 if n % 2 == 0 else 1
    rest = n // c
    b = max(f for f in range(1, rest + 1) if rest % f == 0 and f * f <= rest)
    return rest // b, b, c


def partner(at, by, size, towards):
    if size & (size - 1) == 0:
        return at ^ by
    return (at + (by if towards else size - by)) % size


def sources(me, n):
    a, b, c = factors(n)
    ia, ib, ic = me // (b * c), (me // c) % b, me % c
    return [
        (partner(ia, da, a, False) * b + partner(ib, db, b, False)) * c + partner(ic, dc, c, False)
        for dc in range(c)
        for db in range(b)
        for da in range(a)
    ]


def moved(value, by, n):
    sizes = factors(n)
    a, b, c = sizes
    pairs = []
    for me in range(n):
        at = (me // (b * c), (me // c) % b, me % c)
        to = [partner(place, step, size, True) for place, step, size in zip(at, by, sizes)]
        pairs.append((me, (to[0] * b + to[1]) * c + to[2]))
    return lax.ppermute(value, "coord", pairs)


def pack_kernel(first_hbm, second_hbm, out_ref, sems):
    rows = first_hbm.shape[0]
    copies = [
        pltpu.make_async_copy(source, out_ref.at[pl.ds(i * rows, rows)], sems.at[i])
        for i, source in enumerate((first_hbm, second_hbm))
    ]
    for copy in copies:
        copy.start()
    for copy in copies:
        copy.wait()


def pack(first, second):
    rows, columns = first.shape
    return pl.pallas_call(
        pack_kernel,
        out_shape=jax.ShapeDtypeStruct((2 * rows, columns), first.dtype),
        in_specs=[HBM, HBM],
        out_specs=VMEM,
        scratch_shapes=[pltpu.SemaphoreType.DMA((2,))],
        compiler_params=pltpu.CompilerParams(vmem_limit_bytes=8 << 20),
        name="pack",
    )(pinned(first), pinned(second))


def pinned(value):
    return pltpu.with_memory_space_constraint(value, pltpu.HBM)


def gauss_jordan(blocks):
    width = blocks[0].shape[1]
    half = width // 2
    lane = lax.broadcasted_iota(jnp.int32, (SUB, width), 1)
    sub = lax.broadcasted_iota(jnp.int32, (SUB, width), 0)
    start, within = lane // half * half, lane % half

    def column(block, at):
        return jnp.take_along_axis(block, start + at, axis=1, mode="promise_in_bounds")

    for k in range(len(blocks)):
        at = k * SUB
        head = within // SUB == k
        rows = [jnp.broadcast_to(blocks[k][i : i + 1, :], (SUB, width)) for i in range(SUB)]
        diag = {(i, j): column(rows[i], at + j) for i in range(SUB) for j in range(i, SUB)}
        rows = [jnp.where(head, (within == at + i).astype(jnp.float32), rows[i]) for i in range(SUB)]
        inverse, factor = [], {}
        for p in range(SUB):
            inverse.append(1.0 / diag[p, p])
            for i in range(p + 1, SUB):
                factor[p, i] = diag[p, i] * inverse[p]
                for j in range(i, SUB):
                    diag[i, j] = diag[i, j] - factor[p, i] * diag[p, j]
                rows[i] = rows[i] - factor[p, i] * rows[p]
        rows = [rows[p] * inverse[p] for p in range(SUB)]
        for p in reversed(range(SUB)):
            for i in range(p):
                rows[i] = rows[i] - factor[i, p] * rows[p]
        done = rows[0]
        for i in range(1, SUB):
            done = jnp.where(sub == i, rows[i], done)
        out = []
        for g, block in enumerate(blocks):
            if g == k:
                out.append(done)
                continue
            terms = [column(block, at + p) * rows[p] for p in range(SUB)]
            while len(terms) > 1:
                terms = [terms[i] + terms[i + 1] for i in range(0, len(terms), 2)]
            out.append(jnp.where(head, 0.0, block) - terms[0])
        blocks = out
    return blocks


def side_by_side_inverses(first, second):
    half = first.shape[0]
    both = jnp.concatenate([first, second], axis=1)
    blocks = gauss_jordan([both[g : g + SUB, :] for g in range(0, half, SUB)])
    both = jnp.concatenate(blocks, axis=0)
    return both[:, :half], both[:, half:]


def damped(cov):
    size = cov.shape[0]
    cov = 0.5 * (cov + cov.T)
    row = lax.broadcasted_iota(jnp.int32, (size, size), 0)
    col = lax.broadcasted_iota(jnp.int32, (size, size), 1)
    damping = 0.1 * jnp.sum(jnp.where(row == col, cov, 0.0)) / size
    return jnp.where(row == col, cov + damping, cov)


def product(left, right, dims=((1,), (0,))):
    return lax.dot_general(left, right, (dims, ((), ())), precision=EXACT, preferred_element_type=jnp.float32)


def first_half_kernel(cov_in_hbm, cov_out_hbm, out_ref, cov_ref, sems):
    copies = [
        pltpu.make_async_copy(source, cov_ref.at[i], sems.at[i]) for i, source in enumerate((cov_in_hbm, cov_out_hbm))
    ]
    for copy in copies:
        copy.start()
    for copy in copies:
        copy.wait()
    half = cov_ref.shape[1] // 2
    covs = [damped(cov_ref[0]), damped(cov_ref[1])]
    corner = [cov[:half, half:] for cov in covs]
    upper = side_by_side_inverses(*[cov[:half, :half] for cov in covs])
    solved = [product(u, c) for u, c in zip(upper, corner)]
    schur = [cov[half:, half:] - product(c, t, ((0,), (0,))) for cov, c, t in zip(covs, corner, solved)]
    for i, pair in enumerate((upper, solved, schur)):
        out_ref[i] = jnp.concatenate(pair, axis=1)


def second_half_kernel(first_ref, len_hbm, k_ref, len_ref, sem):
    copy = pltpu.make_async_copy(len_hbm, len_ref, sem)
    copy.start()
    size = k_ref.shape[1]
    half = size // 2
    upper, solved, schur = [(first_ref[i][:, :half], first_ref[i][:, half:]) for i in range(3)]
    lower = side_by_side_inverses(*schur)
    for m, (u, t, low) in enumerate(zip(upper, solved, lower)):
        side = product(t, low)
        k_ref[m, :half, :half] = u + product(side, t, ((1,), (1,)))
        k_ref[m, :half, half:] = -side
        k_ref[m, half:, :half] = -side.T
        k_ref[m, half:, half:] = low
    copy.wait()
    token = lax.broadcasted_iota(jnp.int32, (size, size), 0)
    lane = lax.broadcasted_iota(jnp.int32, (size, size), 1)
    mask = jnp.zeros((size, size), jnp.float32)
    for s in range(len_ref.shape[0]):
        mask = jnp.where((lane == s) & (token < len_ref[s]), 1.0, mask)
    k_ref[2] = mask


def first_half(cov_in, cov_out):
    size = cov_in.shape[0]
    return pl.pallas_call(
        first_half_kernel,
        out_shape=jax.ShapeDtypeStruct((3, size // 2, size), jnp.float32),
        in_specs=[HBM, HBM],
        out_specs=VMEM,
        scratch_shapes=[pltpu.VMEM((2, size, size), jnp.float32), pltpu.SemaphoreType.DMA((2,))],
        compiler_params=pltpu.CompilerParams(vmem_limit_bytes=8 << 20),
        cost_estimate=pl.CostEstimate(flops=size, bytes_accessed=size, transcendentals=0),
        name="first_half",
    )(pinned(cov_in), pinned(cov_out))


def second_half(first, lengths):
    size = first.shape[2]
    return pl.pallas_call(
        second_half_kernel,
        out_shape=jax.ShapeDtypeStruct((3, size, size), jnp.float32),
        in_specs=[VMEM, HBM],
        out_specs=VMEM,
        scratch_shapes=[pltpu.SMEM(lengths.shape, jnp.int32), pltpu.SemaphoreType.DMA],
        compiler_params=pltpu.CompilerParams(vmem_limit_bytes=8 << 20),
        cost_estimate=pl.CostEstimate(flops=size, bytes_accessed=size, transcendentals=0),
        name="second_half",
    )(first, pinned(lengths))


def merge_kernel(spans, *refs):
    at = 0
    for ref, (start, rows) in zip(refs[:-1], spans):
        refs[-1][at : at + rows, :] = ref[start : start + rows, :]
        at += rows


def merge(parts):
    array, start, rows = parts[0]
    if len(parts) == 1 and rows == array.shape[0]:
        return array
    total = sum(part[2] for part in parts)
    return pl.pallas_call(
        functools.partial(merge_kernel, [part[1:] for part in parts]),
        out_shape=jax.ShapeDtypeStruct((total, array.shape[1]), array.dtype),
        in_specs=[VMEM] * len(parts),
        out_specs=VMEM,
        compiler_params=pltpu.CompilerParams(vmem_limit_bytes=16 << 20),
        cost_estimate=pl.CostEstimate(flops=total, bytes_accessed=total, transcendentals=0),
        name="merge",
    )(*(part[0] for part in parts))


def joined(parts):
    out = []
    for array, start, rows in parts:
        if out and out[-1][0] is array and out[-1][1] + out[-1][2] == start:
            out[-1] = (array, out[-1][1], out[-1][2] + rows)
        else:
            out.append((array, start, rows))
    return out


def project_kernel(n, early, seqs, me_ref, *rest):
    inputs, blocks, (total_ref, held, sems) = rest[:2], rest[2 : 2 + len(early)], rest[2 + len(early) :]
    tokens = held.shape[1]
    part = tokens // sems.shape[1]
    copies = [
        [
            pltpu.make_async_copy(source.at[pl.ds(i * part, part)], held.at[t, pl.ds(i * part, part)], sems.at[t, i])
            for i in range(sems.shape[1])
        ]
        for t, source in enumerate(inputs)
    ]
    for copy in copies[0] + copies[1]:
        copy.start()
    rows = blocks[0].shape[0] // 2
    source = sources(me_ref[0], n)
    for t in range(2):
        for copy in copies[t]:
            copy.wait()
        total = None
        for which, block in zip(early, blocks):
            columns = pl.ds(pl.multiple_of(source[which] * rows, rows), rows)
            term = jnp.dot(
                held[t, :, columns], block[t * rows : (t + 1) * rows, :], preferred_element_type=jnp.float32
            )
            total = term if total is None else total + term
        total_ref[t] = total


def project_whole_kernel(n, me_ref, act_ref, grad_ref, *rest):
    blocks, (total_ref, proj) = rest[:n], rest[n:]
    rows = blocks[0].shape[0] // 2
    for block, source in zip(blocks, sources(me_ref[0], n)):
        at = pl.ds(pl.multiple_of(source * rows, rows), rows)
        for t in range(2):
            proj[t, at, :] = block[t * rows : (t + 1) * rows, :]
    for t, ref in enumerate((act_ref, grad_ref)):
        total_ref[t] = jnp.dot(ref[...], proj[t], preferred_element_type=jnp.float32)


def project(me, activations, out_grads, blocks, early, seqs, n):
    tokens, width = activations.shape
    rank = blocks[0].shape[1]
    total = jax.ShapeDtypeStruct((2, tokens, rank), jnp.float32)
    common = dict(
        compiler_params=pltpu.CompilerParams(vmem_limit_bytes=16 << 20),
        cost_estimate=pl.CostEstimate(flops=rank, bytes_accessed=rank, transcendentals=0),
        name="project",
    )
    if len(early) == n:
        result = pl.pallas_call(
            functools.partial(project_whole_kernel, n),
            out_shape=total,
            in_specs=[SMEM] + [VMEM] * (2 + n),
            out_specs=VMEM,
            scratch_shapes=[pltpu.VMEM((2, width, rank), jnp.bfloat16)],
            **common,
        )(me, activations, out_grads, *blocks)
        return result, None
    return pl.pallas_call(
        functools.partial(project_kernel, n, early, seqs),
        out_shape=(
            total,
            jax.ShapeDtypeStruct((2, tokens, width), activations.dtype),
        ),
        in_specs=[SMEM, HBM, HBM] + [VMEM] * len(early),
        out_specs=(VMEM, VMEM),
        scratch_shapes=[pltpu.SemaphoreType.DMA((2, 2 * seqs))],
        **common,
    )(me, pinned(activations), pinned(out_grads), *blocks)


def whiten_kernel(n, seqs, late, me_ref, total_ref, k_ref, *rest):
    operands, (out_ref, white) = rest[:-2], rest[-2:]
    rank = k_ref.shape[1]
    sums = [total_ref[0], total_ref[1]]
    if late:
        held, *blocks = operands
        source = sources(me_ref[0], n)
        rows = held.shape[2] // n
        for which, t, operand, at in late:
            columns = pl.ds(pl.multiple_of(source[which] * rows, rows), rows)
            block = blocks[operand][at : at + rows, :]
            sums[t] = sums[t] + jnp.dot(held[t, :, columns], block, preferred_element_type=jnp.float32)
    length = total_ref.shape[1] // seqs
    share = rank // n
    grads = []
    for s in range(seqs):
        token = slice(s * length, (s + 1) * length)
        x_proj = (sums[0][token, :] * k_ref[2][:length, s : s + 1]).astype(jnp.bfloat16)
        d_proj = sums[1][token, :].astype(jnp.bfloat16)
        grads.append(
            lax.dot_general(d_proj, x_proj, (((0,), (0,)), ((), ())), preferred_element_type=jnp.float32)
        )
    left = product(k_ref[1], jnp.concatenate(grads, axis=1))
    left = jnp.concatenate([left[:, s * rank : (s + 1) * rank] for s in range(seqs)], axis=0)
    full = product(left, k_ref[0])
    for s in range(seqs):
        for d in range(n):
            at = s * rank + d * share
            white[d, s * share : (s + 1) * share, :] = full[at : at + share, :]
    out_ref[...] = white[...].astype(jnp.bfloat16)


def whitened_blocks(me, total, k, late, operands, seqs, n):
    rank = k.shape[1]
    shape = (n, seqs * (rank // n), rank)
    return pl.pallas_call(
        functools.partial(whiten_kernel, n, seqs, late),
        out_shape=jax.ShapeDtypeStruct(shape, jnp.bfloat16),
        in_specs=[SMEM] + [VMEM] * (2 + len(operands)),
        out_specs=VMEM,
        scratch_shapes=[pltpu.VMEM(shape, jnp.float32)],
        compiler_params=pltpu.CompilerParams(vmem_limit_bytes=16 << 20),
        cost_estimate=pl.CostEstimate(flops=64 * rank**3, bytes_accessed=4 << 20, transcendentals=0),
        name="whiten",
    )(me, total, k, *operands)


def add_kernel(first_ref, second_ref, out_ref):
    out_ref[...] = (first_ref[...] + second_ref[...]).astype(out_ref.dtype)


def add(first, second):
    return pl.pallas_call(
        add_kernel,
        out_shape=jax.ShapeDtypeStruct(first.shape, jnp.bfloat16),
        in_specs=[VMEM, VMEM],
        out_specs=VMEM,
        compiler_params=pltpu.CompilerParams(vmem_limit_bytes=32 << 20),
        name="add",
    )(first, second)


def summed_pieces(keep, send, n):
    both = add(keep, moved(send, (0, 0, 1), n))
    groups = [list(range(core, n, 2)) for core in range(2)]
    return lax.all_to_all(both, "coord", split_axis=0, concat_axis=0, axis_index_groups=groups, tiled=True)


def score_kernel(n, me_ref, ids_ref, white_ref, bank_ref, keep_ref, send_ref, spread):
    seqs = ids_ref.shape[0]
    chunk, rank = white_ref.shape[1:]
    share = chunk // seqs
    total = n * seqs
    spread[...] = white_ref[...].astype(jnp.float32).reshape(n * chunk, rank)
    columns = jnp.concatenate(
        [spread[pl.ds(j, total, stride=share), :].astype(jnp.bfloat16) for j in range(share)], axis=1
    )
    queries = bank_ref.shape[0] // n
    row = lax.broadcasted_iota(jnp.int32, (total, keep_ref.shape[2] - queries), 0)
    tail = jnp.zeros(row.shape, jnp.float32)
    for s in range(seqs):
        tail = jnp.where(row == me_ref[0] * seqs + s, ids_ref[s].astype(jnp.float32), tail)
    partial = lax.dot_general(
        columns, bank_ref[...], (((1,), (1,)), ((), ())), preferred_element_type=jnp.float32
    )
    odd = lax.rem(me_ref[0], 2) == 1
    for j in range(n // 2):
        even_part, odd_part = (partial[:, d * queries : (d + 1) * queries] for d in (2 * j, 2 * j + 1))
        for out_ref, flip in ((keep_ref, odd), (send_ref, jnp.logical_not(odd))):
            out_ref[j, :, :queries] = jnp.where(flip, odd_part, even_part).astype(out_ref.dtype)
            out_ref[j, :, queries:] = tail.astype(out_ref.dtype)


def partial_scores(me, seq_ids, white, bank):
    n = white.shape[0]
    seqs = seq_ids.shape[0]
    queries = bank.shape[0] // n
    width = (queries // LANES + 1) * LANES
    return pl.pallas_call(
        functools.partial(score_kernel, n),
        out_shape=(
            jax.ShapeDtypeStruct((n // 2, n * seqs, width), jnp.float32),
            jax.ShapeDtypeStruct((n // 2, n * seqs, width), jnp.float32),
        ),
        in_specs=[SMEM, SMEM, VMEM, VMEM],
        out_specs=(VMEM, VMEM),
        scratch_shapes=[pltpu.VMEM((n * white.shape[1], white.shape[2]), jnp.float32)],
        compiler_params=pltpu.CompilerParams(vmem_limit_bytes=16 << 20),
        cost_estimate=pl.CostEstimate(
            flops=2 * n * seqs * bank.size, bytes_accessed=2 * bank.size, transcendentals=0
        ),
        name="score",
    )(me, seq_ids, white, bank)


def place_kernel(partial_ref, out_ref):
    rows, queries = out_ref.shape
    total = jnp.sum(partial_ref[...].astype(jnp.float32), axis=0)
    raw = total[:, :queries].astype(jnp.bfloat16)
    ids = total[:, queries : queries + 1].astype(jnp.int32)
    chosen = ids == lax.broadcasted_iota(jnp.int32, (rows, rows), 1)
    out_ref[...] = lax.dot_general(
        chosen.astype(jnp.bfloat16), raw, (((0,), (0,)), ((), ())), preferred_element_type=jnp.float32
    ).astype(jnp.bfloat16)


def place(partials, queries):
    return pl.pallas_call(
        lambda a, b: place_kernel(a, b),
        out_shape=jax.ShapeDtypeStruct((partials.shape[1], queries), jnp.bfloat16),
        in_specs=[VMEM],
        out_specs=VMEM,
        compiler_params=pltpu.CompilerParams(vmem_limit_bytes=16 << 20),
        name="place",
    )(partials)


def body(n, activations, out_grads, proj_in, proj_out, cov_in, cov_out, lengths, seq_ids, bank):
    me = lax.axis_index("coord").reshape(1)
    seqs, length, width = activations.shape
    activations, out_grads = activations.reshape(seqs * length, width), out_grads.reshape(seqs * length, width)
    a, b, c = factors(n)
    paired = a & (a - 1) == 0
    packed = pack(proj_in, proj_out)
    half = first_half(cov_in, cov_out)
    held = {(0, 0, 0): packed}
    for at in range(1, min(a, 3)):
        held[at, 0, 0] = moved(packed, (at, 0, 0), n)
    for by in range(1, b):
        held[0, by, 0] = moved(packed, (0, by, 0), n)
    far = held.pop((2, 0, 0), None)
    held, half = lax.optimization_barrier((held, half))
    for by in range(1, b):
        if a > 1:
            held[1, by, 0] = moved(held[1, 0, 0], (0, by, 0), n)
    k = second_half(half, lengths)
    if far is not None:
        held[2, 0, 0] = far
    held, k = lax.optimization_barrier((held, k))
    early = list(held)
    rows = proj_in.shape[0]
    halves = {(at, t): (held[at], t * rows, rows) for at in early for t in range(2)}
    wanted = {}
    for at in range(2, a):
        nearest = at & -at
        source = at - nearest if paired and nearest != at else 0
        for by in range(b):
            for t in range(2):
                if ((at, by, 0), t) in halves:
                    continue
                if source or at > 2:
                    wanted[(at, by, 0), t] = (source, 0, 0), (at - source, by, 0)
                else:
                    wanted[(at, by, 0), t] = (at, 0, 0), (0, by, 0)
    arrivals = []
    while wanted:
        steps = {}
        for to, (source, step) in wanted.items():
            if (source, to[1]) in halves:
                steps.setdefault(step, []).append((to, source))
        for step, both in steps.items():
            arrived = moved(merge(joined([halves[source, to[1]] for to, source in both])), step, n)
            arrivals.append((arrived, [to for to, _ in both]))
            for i, (to, _) in enumerate(both):
                halves[to] = arrived, i * rows, rows
                del wanted[to]
    order = [(at, by, core) for core in range(c) for by in range(b) for at in range(a)]
    if rows % LANES == 0 and arrivals and c == 2:
        total, inputs = project(
            me, activations, out_grads, [held[at] for at in early], [order.index(at) for at in early], seqs, n
        )
        across = [moved(merge([(held[at], 0, 2 * rows) for at in early]), (0, 0, 1), n)]
        waiting, total = lax.optimization_barrier(([arrived for arrived, _ in arrivals], total))
        across.append(moved(merge([(arrived, 0, arrived.shape[0]) for arrived in waiting]), (0, 0, 1), n))
        operands = [inputs, *across, *waiting]
        late = [
            (order.index(at), t, 2 + i, j * rows)
            for i, (_, group) in enumerate(arrivals)
            for j, (at, t) in enumerate(group)
        ]
        crossed = [[(at, t) for at in early for t in range(2)], [to for _, group in arrivals for to in group]]
        late += [
            (order.index((*at[:2], 1)), t, i, j * rows) for i, part in enumerate(crossed) for j, (at, t) in enumerate(part)
        ]
    else:
        for at in order:
            if at[2] == 0:
                held[at] = merge(joined([halves[at, 0], halves[at, 1]]))
                for by in range(1, c):
                    held[at[0], at[1], by] = moved(held[at], (0, 0, by), n)
        total = project(me, activations, out_grads, [held[at] for at in order], list(range(n)), seqs, n)[0]
        operands, late = [], []
    white = whitened_blocks(me, total, k, late, operands, seqs, n)
    white = lax.all_to_all(white, "coord", split_axis=0, concat_axis=0, tiled=True)
    keep, send = partial_scores(me, seq_ids, white, bank)
    return place(summed_pieces(keep, send, n), bank.shape[0] // n)


def solution(mesh):
    in_specs = (
        P(("groups", "coord"), None, None),
        P(("groups", "coord"), None, None),
        P("coord", None),
        P("coord", None),
        P(),
        P(),
        P(("groups", "coord")),
        P(("groups", "coord")),
        P(None, "coord"),
    )
    out_specs = P("groups", "coord")
    return jax.shard_map(
        functools.partial(body, mesh.shape["coord"]),
        mesh=mesh,
        in_specs=in_specs,
        out_specs=out_specs,
        check_vma=False,
    )
```

```python
import functools

import jax
import jax.numpy as jnp
from jax import lax
from jax.experimental import pallas as pl
from jax.experimental.pallas import tpu as pltpu
from jax.sharding import PartitionSpec as P

SUB = 8
LANES = 128
EXACT = lax.Precision.HIGHEST
VMEM = pl.BlockSpec(memory_space=pltpu.VMEM)
HBM = pl.BlockSpec(memory_space=pltpu.HBM)
SMEM = pl.BlockSpec(memory_space=pltpu.SMEM)


def factors(n):
    c = 2 if n % 2 == 0 else 1
    rest = n // c
    b = max(f for f in range(1, rest + 1) if rest % f == 0 and f * f <= rest)
    return rest // b, b, c


def partner(at, by, size, towards):
    if size & (size - 1) == 0:
        return at ^ by
    return (at + (by if towards else size - by)) % size


def sources(me, n):
    a, b, c = factors(n)
    ia, ib, ic = me // (b * c), (me // c) % b, me % c
    return [
        (partner(ia, da, a, False) * b + partner(ib, db, b, False)) * c + partner(ic, dc, c, False)
        for dc in range(c)
        for db in range(b)
        for da in range(a)
    ]


def moved(value, by, n):
    sizes = factors(n)
    a, b, c = sizes
    pairs = []
    for me in range(n):
        at = (me // (b * c), (me // c) % b, me % c)
        to = [partner(place, step, size, True) for place, step, size in zip(at, by, sizes)]
        pairs.append((me, (to[0] * b + to[1]) * c + to[2]))
    return lax.ppermute(value, "coord", pairs)


def pack_kernel(first_hbm, second_hbm, out_ref, sems):
    rows = first_hbm.shape[0]
    copies = [
        pltpu.make_async_copy(source, out_ref.at[pl.ds(i * rows, rows)], sems.at[i])
        for i, source in enumerate((first_hbm, second_hbm))
    ]
    for copy in copies:
        copy.start()
    for copy in copies:
        copy.wait()


def pack(first, second):
    rows, columns = first.shape
    return pl.pallas_call(
        pack_kernel,
        out_shape=jax.ShapeDtypeStruct((2 * rows, columns), first.dtype),
        in_specs=[HBM, HBM],
        out_specs=VMEM,
        scratch_shapes=[pltpu.SemaphoreType.DMA((2,))],
        compiler_params=pltpu.CompilerParams(vmem_limit_bytes=8 << 20),
        name="pack",
    )(pinned(first), pinned(second))


def pinned(value):
    return pltpu.with_memory_space_constraint(value, pltpu.HBM)


def gauss_jordan(blocks):
    width = blocks[0].shape[1]
    half = width // 2
    lane = lax.broadcasted_iota(jnp.int32, (SUB, width), 1)
    sub = lax.broadcasted_iota(jnp.int32, (SUB, width), 0)
    start, within = lane // half * half, lane % half

    def column(block, at):
        return jnp.take_along_axis(block, start + at, axis=1, mode="promise_in_bounds")

    for k in range(len(blocks)):
        at = k * SUB
        head = within // SUB == k
        rows = [jnp.broadcast_to(blocks[k][i : i + 1, :], (SUB, width)) for i in range(SUB)]
        diag = {(i, j): column(rows[i], at + j) for i in range(SUB) for j in range(i, SUB)}
        rows = [jnp.where(head, (within == at + i).astype(jnp.float32), rows[i]) for i in range(SUB)]
        inverse, factor = [], {}
        for p in range(SUB):
            inverse.append(1.0 / diag[p, p])
            for i in range(p + 1, SUB):
                factor[p, i] = diag[p, i] * inverse[p]
                for j in range(i, SUB):
                    diag[i, j] = diag[i, j] - factor[p, i] * diag[p, j]
                rows[i] = rows[i] - factor[p, i] * rows[p]
        rows = [rows[p] * inverse[p] for p in range(SUB)]
        for p in reversed(range(SUB)):
            for i in range(p):
                rows[i] = rows[i] - factor[i, p] * rows[p]
        done = rows[0]
        for i in range(1, SUB):
            done = jnp.where(sub == i, rows[i], done)
        out = []
        for g, block in enumerate(blocks):
            if g == k:
                out.append(done)
                continue
            terms = [column(block, at + p) * rows[p] for p in range(SUB)]
            while len(terms) > 1:
                terms = [terms[i] + terms[i + 1] for i in range(0, len(terms), 2)]
            out.append(jnp.where(head, 0.0, block) - terms[0])
        blocks = out
    return blocks


def side_by_side_inverses(first, second):
    half = first.shape[0]
    both = jnp.concatenate([first, second], axis=1)
    blocks = gauss_jordan([both[g : g + SUB, :] for g in range(0, half, SUB)])
    both = jnp.concatenate(blocks, axis=0)
    return both[:, :half], both[:, half:]


def damped(cov):
    size = cov.shape[0]
    cov = 0.5 * (cov + cov.T)
    row = lax.broadcasted_iota(jnp.int32, (size, size), 0)
    col = lax.broadcasted_iota(jnp.int32, (size, size), 1)
    damping = 0.1 * jnp.sum(jnp.where(row == col, cov, 0.0)) / size
    return jnp.where(row == col, cov + damping, cov)


def product(left, right, dims=((1,), (0,))):
    return lax.dot_general(left, right, (dims, ((), ())), precision=EXACT, preferred_element_type=jnp.float32)


def first_half_kernel(cov_in_hbm, cov_out_hbm, out_ref, cov_ref, sems):
    copies = [
        pltpu.make_async_copy(source, cov_ref.at[i], sems.at[i]) for i, source in enumerate((cov_in_hbm, cov_out_hbm))
    ]
    for copy in copies:
        copy.start()
    for copy in copies:
        copy.wait()
    half = cov_ref.shape[1] // 2
    covs = [damped(cov_ref[0]), damped(cov_ref[1])]
    corner = [cov[:half, half:] for cov in covs]
    upper = side_by_side_inverses(*[cov[:half, :half] for cov in covs])
    solved = [product(u, c) for u, c in zip(upper, corner)]
    schur = [cov[half:, half:] - product(c, t, ((0,), (0,))) for cov, c, t in zip(covs, corner, solved)]
    for i, pair in enumerate((upper, solved, schur)):
        out_ref[i] = jnp.concatenate(pair, axis=1)


def second_half_kernel(first_ref, len_hbm, k_ref, len_ref, sem):
    copy = pltpu.make_async_copy(len_hbm, len_ref, sem)
    copy.start()
    size = k_ref.shape[1]
    half = size // 2
    upper, solved, schur = [(first_ref[i][:, :half], first_ref[i][:, half:]) for i in range(3)]
    lower = side_by_side_inverses(*schur)
    for m, (u, t, low) in enumerate(zip(upper, solved, lower)):
        side = product(t, low)
        k_ref[m, :half, :half] = u + product(side, t, ((1,), (1,)))
        k_ref[m, :half, half:] = -side
        k_ref[m, half:, :half] = -side.T
        k_ref[m, half:, half:] = low
    copy.wait()
    token = lax.broadcasted_iota(jnp.int32, (size, size), 0)
    lane = lax.broadcasted_iota(jnp.int32, (size, size), 1)
    mask = jnp.zeros((size, size), jnp.float32)
    for s in range(len_ref.shape[0]):
        mask = jnp.where((lane == s) & (token < len_ref[s]), 1.0, mask)
    k_ref[2] = mask


def first_half(cov_in, cov_out):
    size = cov_in.shape[0]
    return pl.pallas_call(
        first_half_kernel,
        out_shape=jax.ShapeDtypeStruct((3, size // 2, size), jnp.float32),
        in_specs=[HBM, HBM],
        out_specs=VMEM,
        scratch_shapes=[pltpu.VMEM((2, size, size), jnp.float32), pltpu.SemaphoreType.DMA((2,))],
        compiler_params=pltpu.CompilerParams(vmem_limit_bytes=8 << 20),
        cost_estimate=pl.CostEstimate(flops=size, bytes_accessed=size, transcendentals=0),
        name="first_half",
    )(pinned(cov_in), pinned(cov_out))


def second_half(first, lengths):
    size = first.shape[2]
    return pl.pallas_call(
        second_half_kernel,
        out_shape=jax.ShapeDtypeStruct((3, size, size), jnp.float32),
        in_specs=[VMEM, HBM],
        out_specs=VMEM,
        scratch_shapes=[pltpu.SMEM(lengths.shape, jnp.int32), pltpu.SemaphoreType.DMA],
        compiler_params=pltpu.CompilerParams(vmem_limit_bytes=8 << 20),
        cost_estimate=pl.CostEstimate(flops=size, bytes_accessed=size, transcendentals=0),
        name="second_half",
    )(first, pinned(lengths))


def merge_kernel(spans, *refs):
    at = 0
    for ref, (start, rows) in zip(refs[:-1], spans):
        refs[-1][at : at + rows, :] = ref[start : start + rows, :]
        at += rows


def merge(parts):
    array, start, rows = parts[0]
    if len(parts) == 1 and rows == array.shape[0]:
        return array
    total = sum(part[2] for part in parts)
    return pl.pallas_call(
        functools.partial(merge_kernel, [part[1:] for part in parts]),
        out_shape=jax.ShapeDtypeStruct((total, array.shape[1]), array.dtype),
        in_specs=[VMEM] * len(parts),
        out_specs=VMEM,
        compiler_params=pltpu.CompilerParams(vmem_limit_bytes=16 << 20),
        cost_estimate=pl.CostEstimate(flops=total, bytes_accessed=total, transcendentals=0),
        name="merge",
    )(*(part[0] for part in parts))


def joined(parts):
    out = []
    for array, start, rows in parts:
        if out and out[-1][0] is array and out[-1][1] + out[-1][2] == start:
            out[-1] = (array, out[-1][1], out[-1][2] + rows)
        else:
            out.append((array, start, rows))
    return out


def project_kernel(n, early, seqs, me_ref, *rest):
    inputs, blocks, (total_ref, held, sems) = rest[:2], rest[2 : 2 + len(early)], rest[2 + len(early) :]
    tokens = held.shape[1]
    part = tokens // sems.shape[1]
    copies = [
        [
            pltpu.make_async_copy(source.at[pl.ds(i * part, part)], held.at[t, pl.ds(i * part, part)], sems.at[t, i])
            for i in range(sems.shape[1])
        ]
        for t, source in enumerate(inputs)
    ]
    for copy in copies[0] + copies[1]:
        copy.start()
    rows = blocks[0].shape[0] // 2
    source = sources(me_ref[0], n)
    for t in range(2):
        for copy in copies[t]:
            copy.wait()
        total = None
        for which, block in zip(early, blocks):
            columns = pl.ds(pl.multiple_of(source[which] * rows, rows), rows)
            term = jnp.dot(
                held[t, :, columns], block[t * rows : (t + 1) * rows, :], preferred_element_type=jnp.float32
            )
            total = term if total is None else total + term
        total_ref[t] = total


def project_whole_kernel(n, me_ref, act_ref, grad_ref, *rest):
    blocks, (total_ref, proj) = rest[:n], rest[n:]
    rows = blocks[0].shape[0] // 2
    for block, source in zip(blocks, sources(me_ref[0], n)):
        at = pl.ds(pl.multiple_of(source * rows, rows), rows)
        for t in range(2):
            proj[t, at, :] = block[t * rows : (t + 1) * rows, :]
    for t, ref in enumerate((act_ref, grad_ref)):
        total_ref[t] = jnp.dot(ref[...], proj[t], preferred_element_type=jnp.float32)


def project(me, activations, out_grads, blocks, early, seqs, n):
    tokens, width = activations.shape
    rank = blocks[0].shape[1]
    total = jax.ShapeDtypeStruct((2, tokens, rank), jnp.float32)
    common = dict(
        compiler_params=pltpu.CompilerParams(vmem_limit_bytes=16 << 20),
        cost_estimate=pl.CostEstimate(flops=rank, bytes_accessed=rank, transcendentals=0),
        name="project",
    )
    if len(early) == n:
        result = pl.pallas_call(
            functools.partial(project_whole_kernel, n),
            out_shape=total,
            in_specs=[SMEM] + [VMEM] * (2 + n),
            out_specs=VMEM,
            scratch_shapes=[pltpu.VMEM((2, width, rank), jnp.bfloat16)],
            **common,
        )(me, activations, out_grads, *blocks)
        return result, None
    return pl.pallas_call(
        functools.partial(project_kernel, n, early, seqs),
        out_shape=(
            total,
            jax.ShapeDtypeStruct((2, tokens, width), activations.dtype),
        ),
        in_specs=[SMEM, HBM, HBM] + [VMEM] * len(early),
        out_specs=(VMEM, VMEM),
        scratch_shapes=[pltpu.SemaphoreType.DMA((2, 2 * seqs))],
        **common,
    )(me, pinned(activations), pinned(out_grads), *blocks)


def whiten_kernel(n, seqs, late, me_ref, total_ref, k_ref, *rest):
    operands, (out_ref, white) = rest[:-2], rest[-2:]
    rank = k_ref.shape[1]
    sums = [total_ref[0], total_ref[1]]
    if late:
        held, *blocks = operands
        source = sources(me_ref[0], n)
        rows = held.shape[2] // n
        for which, t, operand, at in late:
            columns = pl.ds(pl.multiple_of(source[which] * rows, rows), rows)
            block = blocks[operand][at : at + rows, :]
            sums[t] = sums[t] + jnp.dot(held[t, :, columns], block, preferred_element_type=jnp.float32)
    length = total_ref.shape[1] // seqs
    share = rank // n
    grads = []
    for s in range(seqs):
        token = slice(s * length, (s + 1) * length)
        x_proj = (sums[0][token, :] * k_ref[2][:length, s : s + 1]).astype(jnp.bfloat16)
        d_proj = sums[1][token, :].astype(jnp.bfloat16)
        grads.append(
            lax.dot_general(d_proj, x_proj, (((0,), (0,)), ((), ())), preferred_element_type=jnp.float32)
        )
    left = product(k_ref[1], jnp.concatenate(grads, axis=1))
    left = jnp.concatenate([left[:, s * rank : (s + 1) * rank] for s in range(seqs)], axis=0)
    full = product(left, k_ref[0])
    for s in range(seqs):
        for d in range(n):
            at = s * rank + d * share
            white[n - 1 - d, s * share : (s + 1) * share, :] = full[at : at + share, :]
    out_ref[...] = white[...].astype(jnp.bfloat16)


def whitened_blocks(me, total, k, late, operands, seqs, n):
    rank = k.shape[1]
    shape = (n, seqs * (rank // n), rank)
    return pl.pallas_call(
        functools.partial(whiten_kernel, n, seqs, late),
        out_shape=jax.ShapeDtypeStruct(shape, jnp.bfloat16),
        in_specs=[SMEM] + [VMEM] * (2 + len(operands)),
        out_specs=VMEM,
        scratch_shapes=[pltpu.VMEM(shape, jnp.float32)],
        compiler_params=pltpu.CompilerParams(vmem_limit_bytes=16 << 20),
        cost_estimate=pl.CostEstimate(flops=64 * rank**3, bytes_accessed=4 << 20, transcendentals=0),
        name="whiten",
    )(me, total, k, *operands)


def exchanged(value, n):
    order = [list(range(n))[::-1]]
    return lax.all_to_all(value, "coord", split_axis=0, concat_axis=0, axis_index_groups=order, tiled=True)


def score_kernel(n, me_ref, ids_ref, white_ref, bank_ref, out_ref, spread):
    seqs = ids_ref.shape[0]
    chunk, rank = white_ref.shape[1:]
    share = chunk // seqs
    total = n * seqs
    spread[...] = white_ref[...].astype(jnp.float32).reshape(n * chunk, rank)
    columns = jnp.concatenate(
        [spread[pl.ds(j, total, stride=share), :].astype(jnp.bfloat16) for j in range(share)], axis=1
    )
    queries = bank_ref.shape[0] // n
    row = lax.broadcasted_iota(jnp.int32, (total, out_ref.shape[2] - queries), 0)
    tail = jnp.zeros(row.shape, jnp.float32)
    for s in range(seqs):
        tail = jnp.where(row == (n - 1 - me_ref[0]) * seqs + s, ids_ref[s].astype(jnp.float32), tail)
    partial = lax.dot_general(
        columns, bank_ref[...], (((1,), (1,)), ((), ())), preferred_element_type=jnp.float32
    )
    for d in range(n):
        at = n - 1 - d
        out_ref[at, :, :queries] = partial[:, d * queries : (d + 1) * queries].astype(out_ref.dtype)
        out_ref[at, :, queries:] = tail.astype(out_ref.dtype)


def partial_scores(me, seq_ids, white, bank):
    n = white.shape[0]
    seqs = seq_ids.shape[0]
    queries = bank.shape[0] // n
    width = (queries // LANES + 1) * LANES
    return pl.pallas_call(
        functools.partial(score_kernel, n),
        out_shape=jax.ShapeDtypeStruct((n, n * seqs, width), jnp.bfloat16),
        in_specs=[SMEM, SMEM, VMEM, VMEM],
        out_specs=VMEM,
        scratch_shapes=[pltpu.VMEM((n * white.shape[1], white.shape[2]), jnp.float32)],
        compiler_params=pltpu.CompilerParams(vmem_limit_bytes=16 << 20),
        cost_estimate=pl.CostEstimate(
            flops=2 * n * seqs * bank.size, bytes_accessed=2 * bank.size, transcendentals=0
        ),
        name="score",
    )(me, seq_ids, white, bank)


def place_kernel(partial_ref, out_ref):
    rows, queries = out_ref.shape
    total = jnp.sum(partial_ref[...].astype(jnp.float32), axis=0)
    raw = total[:, :queries].astype(jnp.bfloat16)
    ids = total[:, queries : queries + 1].astype(jnp.int32)
    chosen = ids == lax.broadcasted_iota(jnp.int32, (rows, rows), 1)
    out_ref[...] = lax.dot_general(
        chosen.astype(jnp.bfloat16), raw, (((0,), (0,)), ((), ())), preferred_element_type=jnp.float32
    ).astype(jnp.bfloat16)


def place(partials, queries):
    return pl.pallas_call(
        lambda a, b: place_kernel(a, b),
        out_shape=jax.ShapeDtypeStruct((partials.shape[1], queries), jnp.bfloat16),
        in_specs=[VMEM],
        out_specs=VMEM,
        compiler_params=pltpu.CompilerParams(vmem_limit_bytes=16 << 20),
        name="place",
    )(partials)


def body(n, activations, out_grads, proj_in, proj_out, cov_in, cov_out, lengths, seq_ids, bank):
    me = lax.axis_index("coord").reshape(1)
    seqs, length, width = activations.shape
    activations, out_grads = activations.reshape(seqs * length, width), out_grads.reshape(seqs * length, width)
    a, b, c = factors(n)
    paired = a & (a - 1) == 0
    packed = pack(proj_in, proj_out)
    half = first_half(cov_in, cov_out)
    held = {(0, 0, 0): packed}
    for at in range(1, min(a, 3)):
        held[at, 0, 0] = moved(packed, (at, 0, 0), n)
    for by in range(1, b):
        held[0, by, 0] = moved(packed, (0, by, 0), n)
    held, half = lax.optimization_barrier((held, half))
    early = list(held)
    rows = proj_in.shape[0]
    halves = {(at, t): (held[at], t * rows, rows) for at in early for t in range(2)}
    wanted = {}
    for at in range(1, a):
        nearest = at & -at
        source = at - nearest if paired and nearest != at else 0
        for by in range(b):
            for t in range(2):
                if ((at, by, 0), t) in halves:
                    continue
                if source or at > 2:
                    wanted[(at, by, 0), t] = (source, 0, 0), (at - source, by, 0)
                elif at == 1 and t == 0:
                    wanted[(at, by, 0), t] = (0, by, 0), (1, 0, 0)
                else:
                    wanted[(at, by, 0), t] = (at, 0, 0), (0, by, 0)
    arrivals = []
    while wanted:
        steps = {}
        for to, (source, step) in wanted.items():
            if (source, to[1]) in halves:
                steps.setdefault(step, []).append((to, source))
        for step, both in steps.items():
            arrived = moved(merge(joined([halves[source, to[1]] for to, source in both])), step, n)
            arrivals.append((arrived, [to for to, _ in both]))
            for i, (to, _) in enumerate(both):
                halves[to] = arrived, i * rows, rows
                del wanted[to]
    k = second_half(half, lengths)
    order = [(at, by, core) for core in range(c) for by in range(b) for at in range(a)]
    if rows % LANES == 0 and arrivals and c == 2:
        total, inputs = project(
            me, activations, out_grads, [held[at] for at in early], [order.index(at) for at in early], seqs, n
        )
        across = [moved(merge([(held[at], 0, 2 * rows) for at in early]), (0, 0, 1), n)]
        waiting, total, k = lax.optimization_barrier(([arrived for arrived, _ in arrivals], total, k))
        across.append(moved(merge([(arrived, 0, arrived.shape[0]) for arrived in waiting]), (0, 0, 1), n))
        operands = [inputs, *across, *waiting]
        late = [
            (order.index(at), t, 2 + i, j * rows)
            for i, (_, group) in enumerate(arrivals)
            for j, (at, t) in enumerate(group)
        ]
        crossed = [[(at, t) for at in early for t in range(2)], [to for _, group in arrivals for to in group]]
        late += [
            (order.index((*at[:2], 1)), t, i, j * rows) for i, part in enumerate(crossed) for j, (at, t) in enumerate(part)
        ]
    else:
        for at in order:
            if at[2] == 0:
                held[at] = merge(joined([halves[at, 0], halves[at, 1]]))
                for by in range(1, c):
                    held[at[0], at[1], by] = moved(held[at], (0, 0, by), n)
        total = project(me, activations, out_grads, [held[at] for at in order], list(range(n)), seqs, n)[0]
        operands, late = [], []
    white = whitened_blocks(me, total, k, late, operands, seqs, n)
    partials = partial_scores(me, seq_ids, exchanged(white, n), bank)
    return place(exchanged(partials, n), bank.shape[0] // n)


def solution(mesh):
    in_specs = (
        P(("groups", "coord"), None, None),
        P(("groups", "coord"), None, None),
        P("coord", None),
        P("coord", None),
        P(),
        P(),
        P(("groups", "coord")),
        P(("groups", "coord")),
        P(None, "coord"),
    )
    out_specs = P("groups", "coord")
    return jax.shard_map(
        functools.partial(body, mesh.shape["coord"]),
        mesh=mesh,
        in_specs=in_specs,
        out_specs=out_specs,
        check_vma=False,
    )
```

```python
import functools

import jax
import jax.numpy as jnp
from jax import lax
from jax.experimental import pallas as pl
from jax.experimental.pallas import tpu as pltpu
from jax.sharding import PartitionSpec as P

SUB = 8
LANES = 128
EXACT = lax.Precision.HIGHEST
VMEM = pl.BlockSpec(memory_space=pltpu.VMEM)
HBM = pl.BlockSpec(memory_space=pltpu.HBM)
SMEM = pl.BlockSpec(memory_space=pltpu.SMEM)


def factors(n):
    c = 2 if n % 2 == 0 else 1
    rest = n // c
    b = max(f for f in range(1, rest + 1) if rest % f == 0 and f * f <= rest)
    return rest // b, b, c


def partner(at, by, size, towards):
    if size & (size - 1) == 0:
        return at ^ by
    return (at + (by if towards else size - by)) % size


def sources(me, n):
    a, b, c = factors(n)
    ia, ib, ic = me // (b * c), (me // c) % b, me % c
    return [
        (partner(ia, da, a, False) * b + partner(ib, db, b, False)) * c + partner(ic, dc, c, False)
        for dc in range(c)
        for db in range(b)
        for da in range(a)
    ]


def moved(value, by, n):
    sizes = factors(n)
    a, b, c = sizes
    pairs = []
    for me in range(n):
        at = (me // (b * c), (me // c) % b, me % c)
        to = [partner(place, step, size, True) for place, step, size in zip(at, by, sizes)]
        pairs.append((me, (to[0] * b + to[1]) * c + to[2]))
    return lax.ppermute(value, "coord", pairs)


def place_of(device, n):
    return (n - 1 - device) // 2 + (n // 2) * (1 - device % 2)


def pack_kernel(first_hbm, second_hbm, out_ref, sems):
    rows = first_hbm.shape[0]
    copies = [
        pltpu.make_async_copy(source, out_ref.at[pl.ds(i * rows, rows)], sems.at[i])
        for i, source in enumerate((first_hbm, second_hbm))
    ]
    for copy in copies:
        copy.start()
    for copy in copies:
        copy.wait()


def pack(first, second):
    rows, columns = first.shape
    return pl.pallas_call(
        pack_kernel,
        out_shape=jax.ShapeDtypeStruct((2 * rows, columns), first.dtype),
        in_specs=[HBM, HBM],
        out_specs=VMEM,
        scratch_shapes=[pltpu.SemaphoreType.DMA((2,))],
        compiler_params=pltpu.CompilerParams(vmem_limit_bytes=8 << 20),
        name="pack",
    )(pinned(first), pinned(second))


def pinned(value):
    return pltpu.with_memory_space_constraint(value, pltpu.HBM)


def gauss_jordan(blocks):
    width = blocks[0].shape[1]
    half = width // 2
    lane = lax.broadcasted_iota(jnp.int32, (SUB, width), 1)
    sub = lax.broadcasted_iota(jnp.int32, (SUB, width), 0)
    start, within = lane // half * half, lane % half

    def column(block, at):
        return jnp.take_along_axis(block, start + at, axis=1, mode="promise_in_bounds")

    for k in range(len(blocks)):
        at = k * SUB
        head = within // SUB == k
        rows = [jnp.broadcast_to(blocks[k][i : i + 1, :], (SUB, width)) for i in range(SUB)]
        diag = {(i, j): column(rows[i], at + j) for i in range(SUB) for j in range(i, SUB)}
        rows = [jnp.where(head, (within == at + i).astype(jnp.float32), rows[i]) for i in range(SUB)]
        inverse, factor = [], {}
        for p in range(SUB):
            inverse.append(1.0 / diag[p, p])
            for i in range(p + 1, SUB):
                factor[p, i] = diag[p, i] * inverse[p]
                for j in range(i, SUB):
                    diag[i, j] = diag[i, j] - factor[p, i] * diag[p, j]
                rows[i] = rows[i] - factor[p, i] * rows[p]
        rows = [rows[p] * inverse[p] for p in range(SUB)]
        for p in reversed(range(SUB)):
            for i in range(p):
                rows[i] = rows[i] - factor[i, p] * rows[p]
        done = rows[0]
        for i in range(1, SUB):
            done = jnp.where(sub == i, rows[i], done)
        out = []
        for g, block in enumerate(blocks):
            if g == k:
                out.append(done)
                continue
            terms = [column(block, at + p) * rows[p] for p in range(SUB)]
            while len(terms) > 1:
                terms = [terms[i] + terms[i + 1] for i in range(0, len(terms), 2)]
            out.append(jnp.where(head, 0.0, block) - terms[0])
        blocks = out
    return blocks


def side_by_side_inverses(first, second):
    half = first.shape[0]
    both = jnp.concatenate([first, second], axis=1)
    blocks = gauss_jordan([both[g : g + SUB, :] for g in range(0, half, SUB)])
    both = jnp.concatenate(blocks, axis=0)
    return both[:, :half], both[:, half:]


def damped(cov):
    size = cov.shape[0]
    cov = 0.5 * (cov + cov.T)
    row = lax.broadcasted_iota(jnp.int32, (size, size), 0)
    col = lax.broadcasted_iota(jnp.int32, (size, size), 1)
    damping = 0.1 * jnp.sum(jnp.where(row == col, cov, 0.0)) / size
    return jnp.where(row == col, cov + damping, cov)


def product(left, right, dims=((1,), (0,))):
    return lax.dot_general(left, right, (dims, ((), ())), precision=EXACT, preferred_element_type=jnp.float32)


def first_half_kernel(cov_in_hbm, cov_out_hbm, out_ref, cov_ref, sems):
    copies = [
        pltpu.make_async_copy(source, cov_ref.at[i], sems.at[i]) for i, source in enumerate((cov_in_hbm, cov_out_hbm))
    ]
    for copy in copies:
        copy.start()
    for copy in copies:
        copy.wait()
    half = cov_ref.shape[1] // 2
    covs = [damped(cov_ref[0]), damped(cov_ref[1])]
    corner = [cov[:half, half:] for cov in covs]
    upper = side_by_side_inverses(*[cov[:half, :half] for cov in covs])
    solved = [product(u, c) for u, c in zip(upper, corner)]
    schur = [cov[half:, half:] - product(c, t, ((0,), (0,))) for cov, c, t in zip(covs, corner, solved)]
    for i, pair in enumerate((upper, solved, schur)):
        out_ref[i] = jnp.concatenate(pair, axis=1)


def second_half_kernel(first_ref, len_hbm, k_ref, len_ref, sem):
    copy = pltpu.make_async_copy(len_hbm, len_ref, sem)
    copy.start()
    size = k_ref.shape[1]
    half = size // 2
    upper, solved, schur = [(first_ref[i][:, :half], first_ref[i][:, half:]) for i in range(3)]
    lower = side_by_side_inverses(*schur)
    for m, (u, t, low) in enumerate(zip(upper, solved, lower)):
        side = product(t, low)
        k_ref[m, :half, :half] = u + product(side, t, ((1,), (1,)))
        k_ref[m, :half, half:] = -side
        k_ref[m, half:, :half] = -side.T
        k_ref[m, half:, half:] = low
    copy.wait()
    token = lax.broadcasted_iota(jnp.int32, (size, size), 0)
    lane = lax.broadcasted_iota(jnp.int32, (size, size), 1)
    mask = jnp.zeros((size, size), jnp.float32)
    for s in range(len_ref.shape[0]):
        mask = jnp.where((lane == s) & (token < len_ref[s]), 1.0, mask)
    k_ref[2] = mask


def first_half(cov_in, cov_out):
    size = cov_in.shape[0]
    return pl.pallas_call(
        first_half_kernel,
        out_shape=jax.ShapeDtypeStruct((3, size // 2, size), jnp.float32),
        in_specs=[HBM, HBM],
        out_specs=VMEM,
        scratch_shapes=[pltpu.VMEM((2, size, size), jnp.float32), pltpu.SemaphoreType.DMA((2,))],
        compiler_params=pltpu.CompilerParams(vmem_limit_bytes=8 << 20),
        cost_estimate=pl.CostEstimate(flops=size, bytes_accessed=size, transcendentals=0),
        name="first_half",
    )(pinned(cov_in), pinned(cov_out))


def second_half(first, lengths):
    size = first.shape[2]
    return pl.pallas_call(
        second_half_kernel,
        out_shape=jax.ShapeDtypeStruct((3, size, size), jnp.float32),
        in_specs=[VMEM, HBM],
        out_specs=VMEM,
        scratch_shapes=[pltpu.SMEM(lengths.shape, jnp.int32), pltpu.SemaphoreType.DMA],
        compiler_params=pltpu.CompilerParams(vmem_limit_bytes=8 << 20),
        cost_estimate=pl.CostEstimate(flops=size, bytes_accessed=size, transcendentals=0),
        name="second_half",
    )(first, pinned(lengths))


def merge_kernel(spans, *refs):
    at = 0
    for ref, (start, rows) in zip(refs[:-1], spans):
        refs[-1][at : at + rows, :] = ref[start : start + rows, :]
        at += rows


def merge(parts):
    array, start, rows = parts[0]
    if len(parts) == 1 and rows == array.shape[0]:
        return array
    total = sum(part[2] for part in parts)
    return pl.pallas_call(
        functools.partial(merge_kernel, [part[1:] for part in parts]),
        out_shape=jax.ShapeDtypeStruct((total, array.shape[1]), array.dtype),
        in_specs=[VMEM] * len(parts),
        out_specs=VMEM,
        compiler_params=pltpu.CompilerParams(vmem_limit_bytes=16 << 20),
        cost_estimate=pl.CostEstimate(flops=total, bytes_accessed=total, transcendentals=0),
        name="merge",
    )(*(part[0] for part in parts))


def joined(parts):
    out = []
    for array, start, rows in parts:
        if out and out[-1][0] is array and out[-1][1] + out[-1][2] == start:
            out[-1] = (array, out[-1][1], out[-1][2] + rows)
        else:
            out.append((array, start, rows))
    return out


def project_kernel(n, early, seqs, me_ref, *rest):
    inputs, blocks, (total_ref, held, sems) = rest[:2], rest[2 : 2 + len(early)], rest[2 + len(early) :]
    tokens = held.shape[1]
    part = tokens // sems.shape[1]
    copies = [
        [
            pltpu.make_async_copy(source.at[pl.ds(i * part, part)], held.at[t, pl.ds(i * part, part)], sems.at[t, i])
            for i in range(sems.shape[1])
        ]
        for t, source in enumerate(inputs)
    ]
    for copy in copies[0] + copies[1]:
        copy.start()
    rows = blocks[0].shape[0] // 2
    source = sources(me_ref[0], n)
    for t in range(2):
        for copy in copies[t]:
            copy.wait()
        total = None
        for which, block in zip(early, blocks):
            columns = pl.ds(pl.multiple_of(source[which] * rows, rows), rows)
            term = jnp.dot(
                held[t, :, columns], block[t * rows : (t + 1) * rows, :], preferred_element_type=jnp.float32
            )
            total = term if total is None else total + term
        total_ref[t] = total


def project_whole_kernel(n, me_ref, act_ref, grad_ref, *rest):
    blocks, (total_ref, proj) = rest[:n], rest[n:]
    rows = blocks[0].shape[0] // 2
    for block, source in zip(blocks, sources(me_ref[0], n)):
        at = pl.ds(pl.multiple_of(source * rows, rows), rows)
        for t in range(2):
            proj[t, at, :] = block[t * rows : (t + 1) * rows, :]
    for t, ref in enumerate((act_ref, grad_ref)):
        total_ref[t] = jnp.dot(ref[...], proj[t], preferred_element_type=jnp.float32)


def project(me, activations, out_grads, blocks, early, seqs, n):
    tokens, width = activations.shape
    rank = blocks[0].shape[1]
    total = jax.ShapeDtypeStruct((2, tokens, rank), jnp.float32)
    common = dict(
        compiler_params=pltpu.CompilerParams(vmem_limit_bytes=16 << 20),
        cost_estimate=pl.CostEstimate(flops=rank, bytes_accessed=rank, transcendentals=0),
        name="project",
    )
    if len(early) == n:
        result = pl.pallas_call(
            functools.partial(project_whole_kernel, n),
            out_shape=total,
            in_specs=[SMEM] + [VMEM] * (2 + n),
            out_specs=VMEM,
            scratch_shapes=[pltpu.VMEM((2, width, rank), jnp.bfloat16)],
            **common,
        )(me, activations, out_grads, *blocks)
        return result, None
    return pl.pallas_call(
        functools.partial(project_kernel, n, early, seqs),
        out_shape=(
            total,
            jax.ShapeDtypeStruct((2, tokens, width), activations.dtype),
        ),
        in_specs=[SMEM, HBM, HBM] + [VMEM] * len(early),
        out_specs=(VMEM, VMEM),
        scratch_shapes=[pltpu.SemaphoreType.DMA((2, 2 * seqs))],
        **common,
    )(me, pinned(activations), pinned(out_grads), *blocks)


def whiten_kernel(n, seqs, late, me_ref, total_ref, k_ref, *rest):
    operands, (out_ref, white) = rest[:-2], rest[-2:]
    rank = k_ref.shape[1]
    sums = [total_ref[0], total_ref[1]]
    if late:
        held, *blocks = operands
        source = sources(me_ref[0], n)
        rows = held.shape[2] // n
        for which, t, operand, at in late:
            columns = pl.ds(pl.multiple_of(source[which] * rows, rows), rows)
            block = blocks[operand][at : at + rows, :]
            sums[t] = sums[t] + jnp.dot(held[t, :, columns], block, preferred_element_type=jnp.float32)
    length = total_ref.shape[1] // seqs
    share = rank // n
    grads = []
    for s in range(seqs):
        token = slice(s * length, (s + 1) * length)
        x_proj = (sums[0][token, :] * k_ref[2][:length, s : s + 1]).astype(jnp.bfloat16)
        d_proj = sums[1][token, :].astype(jnp.bfloat16)
        grads.append(
            lax.dot_general(d_proj, x_proj, (((0,), (0,)), ((), ())), preferred_element_type=jnp.float32)
        )
    left = product(k_ref[1], jnp.concatenate(grads, axis=1))
    left = jnp.concatenate([left[:, s * rank : (s + 1) * rank] for s in range(seqs)], axis=0)
    full = product(left, k_ref[0])
    for s in range(seqs):
        for d in range(n):
            at = s * rank + d * share
            white[place_of(d, n), s * share : (s + 1) * share, :] = full[at : at + share, :]
    out_ref[...] = white[...].astype(jnp.bfloat16)


def whitened_blocks(me, total, k, late, operands, seqs, n):
    rank = k.shape[1]
    shape = (n, seqs * (rank // n), rank)
    return pl.pallas_call(
        functools.partial(whiten_kernel, n, seqs, late),
        out_shape=jax.ShapeDtypeStruct(shape, jnp.bfloat16),
        in_specs=[SMEM] + [VMEM] * (2 + len(operands)),
        out_specs=VMEM,
        scratch_shapes=[pltpu.VMEM(shape, jnp.float32)],
        compiler_params=pltpu.CompilerParams(vmem_limit_bytes=16 << 20),
        cost_estimate=pl.CostEstimate(flops=64 * rank**3, bytes_accessed=4 << 20, transcendentals=0),
        name="whiten",
    )(me, total, k, *operands)


def exchanged(value, n):
    order = [sorted(range(n), key=lambda device: place_of(device, n))]
    return lax.all_to_all(value, "coord", split_axis=0, concat_axis=0, axis_index_groups=order, tiled=True)


def score_kernel(n, me_ref, ids_ref, white_ref, bank_ref, out_ref, spread):
    seqs = ids_ref.shape[0]
    chunk, rank = white_ref.shape[1:]
    share = chunk // seqs
    total = n * seqs
    spread[...] = white_ref[...].astype(jnp.float32).reshape(n * chunk, rank)
    columns = jnp.concatenate(
        [spread[pl.ds(j, total, stride=share), :].astype(jnp.bfloat16) for j in range(share)], axis=1
    )
    queries = bank_ref.shape[0] // n
    row = lax.broadcasted_iota(jnp.int32, (total, out_ref.shape[2] - queries), 0)
    tail = jnp.zeros(row.shape, jnp.float32)
    for s in range(seqs):
        tail = jnp.where(row == place_of(me_ref[0], n) * seqs + s, ids_ref[s].astype(jnp.float32), tail)
    partial = lax.dot_general(
        columns, bank_ref[...], (((1,), (1,)), ((), ())), preferred_element_type=jnp.float32
    )
    for d in range(n):
        at = place_of(d, n)
        out_ref[at, :, :queries] = partial[:, d * queries : (d + 1) * queries].astype(out_ref.dtype)
        out_ref[at, :, queries:] = tail.astype(out_ref.dtype)


def partial_scores(me, seq_ids, white, bank):
    n = white.shape[0]
    seqs = seq_ids.shape[0]
    queries = bank.shape[0] // n
    width = (queries // LANES + 1) * LANES
    return pl.pallas_call(
        functools.partial(score_kernel, n),
        out_shape=jax.ShapeDtypeStruct((n, n * seqs, width), jnp.bfloat16),
        in_specs=[SMEM, SMEM, VMEM, VMEM],
        out_specs=VMEM,
        scratch_shapes=[pltpu.VMEM((n * white.shape[1], white.shape[2]), jnp.float32)],
        compiler_params=pltpu.CompilerParams(vmem_limit_bytes=16 << 20),
        cost_estimate=pl.CostEstimate(
            flops=2 * n * seqs * bank.size, bytes_accessed=2 * bank.size, transcendentals=0
        ),
        name="score",
    )(me, seq_ids, white, bank)


def place_kernel(partial_ref, out_ref):
    rows, queries = out_ref.shape
    total = jnp.sum(partial_ref[...].astype(jnp.float32), axis=0)
    raw = total[:, :queries].astype(jnp.bfloat16)
    ids = total[:, queries : queries + 1].astype(jnp.int32)
    chosen = ids == lax.broadcasted_iota(jnp.int32, (rows, rows), 1)
    out_ref[...] = lax.dot_general(
        chosen.astype(jnp.bfloat16), raw, (((0,), (0,)), ((), ())), preferred_element_type=jnp.float32
    ).astype(jnp.bfloat16)


def place(partials, queries):
    return pl.pallas_call(
        lambda a, b: place_kernel(a, b),
        out_shape=jax.ShapeDtypeStruct((partials.shape[1], queries), jnp.bfloat16),
        in_specs=[VMEM],
        out_specs=VMEM,
        compiler_params=pltpu.CompilerParams(vmem_limit_bytes=16 << 20),
        name="place",
    )(partials)


def body(n, activations, out_grads, proj_in, proj_out, cov_in, cov_out, lengths, seq_ids, bank):
    me = lax.axis_index("coord").reshape(1)
    seqs, length, width = activations.shape
    activations, out_grads = activations.reshape(seqs * length, width), out_grads.reshape(seqs * length, width)
    a, b, c = factors(n)
    paired = a & (a - 1) == 0
    packed = pack(proj_in, proj_out)
    half = first_half(cov_in, cov_out)
    held = {(0, 0, 0): packed}
    for at in range(1, min(a, 3)):
        held[at, 0, 0] = moved(packed, (at, 0, 0), n)
    for by in range(1, b):
        held[0, by, 0] = moved(packed, (0, by, 0), n)
    held, half = lax.optimization_barrier((held, half))
    early = list(held)
    rows = proj_in.shape[0]
    halves = {(at, t): (held[at], t * rows, rows) for at in early for t in range(2)}
    wanted = {}
    for at in range(1, a):
        nearest = at & -at
        source = at - nearest if paired and nearest != at else 0
        for by in range(b):
            for t in range(2):
                if ((at, by, 0), t) in halves:
                    continue
                if source or at > 2:
                    wanted[(at, by, 0), t] = (source, 0, 0), (at - source, by, 0)
                elif at == 1 and t == 0:
                    wanted[(at, by, 0), t] = (0, by, 0), (1, 0, 0)
                else:
                    wanted[(at, by, 0), t] = (at, 0, 0), (0, by, 0)
    arrivals = []
    while wanted:
        steps = {}
        for to, (source, step) in wanted.items():
            if (source, to[1]) in halves:
                steps.setdefault(step, []).append((to, source))
        for step, both in steps.items():
            arrived = moved(merge(joined([halves[source, to[1]] for to, source in both])), step, n)
            arrivals.append((arrived, [to for to, _ in both]))
            for i, (to, _) in enumerate(both):
                halves[to] = arrived, i * rows, rows
                del wanted[to]
    k = second_half(half, lengths)
    order = [(at, by, core) for core in range(c) for by in range(b) for at in range(a)]
    if rows % LANES == 0 and arrivals and c == 2:
        total, inputs = project(
            me, activations, out_grads, [held[at] for at in early], [order.index(at) for at in early], seqs, n
        )
        across = [moved(merge([(held[at], 0, 2 * rows) for at in early]), (0, 0, 1), n)]
        waiting, total, k = lax.optimization_barrier(([arrived for arrived, _ in arrivals], total, k))
        across.append(moved(merge([(arrived, 0, arrived.shape[0]) for arrived in waiting]), (0, 0, 1), n))
        operands = [inputs, *across, *waiting]
        late = [
            (order.index(at), t, 2 + i, j * rows)
            for i, (_, group) in enumerate(arrivals)
            for j, (at, t) in enumerate(group)
        ]
        crossed = [[(at, t) for at in early for t in range(2)], [to for _, group in arrivals for to in group]]
        late += [
            (order.index((*at[:2], 1)), t, i, j * rows) for i, part in enumerate(crossed) for j, (at, t) in enumerate(part)
        ]
    else:
        for at in order:
            if at[2] == 0:
                held[at] = merge(joined([halves[at, 0], halves[at, 1]]))
                for by in range(1, c):
                    held[at[0], at[1], by] = moved(held[at], (0, 0, by), n)
        total = project(me, activations, out_grads, [held[at] for at in order], list(range(n)), seqs, n)[0]
        operands, late = [], []
    white = whitened_blocks(me, total, k, late, operands, seqs, n)
    partials = partial_scores(me, seq_ids, exchanged(white, n), bank)
    return place(exchanged(partials, n), bank.shape[0] // n)


def solution(mesh):
    in_specs = (
        P(("groups", "coord"), None, None),
        P(("groups", "coord"), None, None),
        P("coord", None),
        P("coord", None),
        P(),
        P(),
        P(("groups", "coord")),
        P(("groups", "coord")),
        P(None, "coord"),
    )
    out_specs = P("groups", "coord")
    return jax.shard_map(
        functools.partial(body, mesh.shape["coord"]),
        mesh=mesh,
        in_specs=in_specs,
        out_specs=out_specs,
        check_vma=False,
    )
```

```python
import functools

import jax
import jax.numpy as jnp
from jax import lax
from jax.experimental import pallas as pl
from jax.experimental.pallas import tpu as pltpu
from jax.sharding import PartitionSpec as P

SUB = 8
LANES = 128
EXACT = lax.Precision.HIGHEST
VMEM = pl.BlockSpec(memory_space=pltpu.VMEM)
HBM = pl.BlockSpec(memory_space=pltpu.HBM)
SMEM = pl.BlockSpec(memory_space=pltpu.SMEM)


def factors(n):
    c = 2 if n % 2 == 0 else 1
    rest = n // c
    b = max(f for f in range(1, rest + 1) if rest % f == 0 and f * f <= rest)
    return rest // b, b, c


def partner(at, by, size, towards):
    if size & (size - 1) == 0:
        return at ^ by
    return (at + (by if towards else size - by)) % size


def sources(me, n):
    a, b, c = factors(n)
    ia, ib, ic = me // (b * c), (me // c) % b, me % c
    return [
        (partner(ia, da, a, False) * b + partner(ib, db, b, False)) * c + partner(ic, dc, c, False)
        for dc in range(c)
        for db in range(b)
        for da in range(a)
    ]


def moved(value, by, n):
    sizes = factors(n)
    a, b, c = sizes
    pairs = []
    for me in range(n):
        at = (me // (b * c), (me // c) % b, me % c)
        to = [partner(place, step, size, True) for place, step, size in zip(at, by, sizes)]
        pairs.append((me, (to[0] * b + to[1]) * c + to[2]))
    return lax.ppermute(value, "coord", pairs)


def exchange_order(n):
    a, b, c = factors(n)
    return sorted(range(n), key=lambda device: (1 - device % 2, abs(2 * (device // (b * c)) - (a - 1)), -device))


def place_of(me, n):
    place = 0
    for i, device in enumerate(exchange_order(n)):
        place = jnp.where(me == device, i, place)
    return place


def pack_kernel(first_hbm, second_hbm, out_ref, sems):
    rows = first_hbm.shape[0]
    copies = [
        pltpu.make_async_copy(source, out_ref.at[pl.ds(i * rows, rows)], sems.at[i])
        for i, source in enumerate((first_hbm, second_hbm))
    ]
    for copy in copies:
        copy.start()
    for copy in copies:
        copy.wait()


def pack(first, second):
    rows, columns = first.shape
    return pl.pallas_call(
        pack_kernel,
        out_shape=jax.ShapeDtypeStruct((2 * rows, columns), first.dtype),
        in_specs=[HBM, HBM],
        out_specs=VMEM,
        scratch_shapes=[pltpu.SemaphoreType.DMA((2,))],
        compiler_params=pltpu.CompilerParams(vmem_limit_bytes=8 << 20),
        name="pack",
    )(pinned(first), pinned(second))


def pinned(value):
    return pltpu.with_memory_space_constraint(value, pltpu.HBM)


def gauss_jordan(blocks):
    width = blocks[0].shape[1]
    half = width // 2
    lane = lax.broadcasted_iota(jnp.int32, (SUB, width), 1)
    sub = lax.broadcasted_iota(jnp.int32, (SUB, width), 0)
    start, within = lane // half * half, lane % half

    def column(block, at):
        return jnp.take_along_axis(block, start + at, axis=1, mode="promise_in_bounds")

    for k in range(len(blocks)):
        at = k * SUB
        head = within // SUB == k
        rows = [jnp.broadcast_to(blocks[k][i : i + 1, :], (SUB, width)) for i in range(SUB)]
        diag = {(i, j): column(rows[i], at + j) for i in range(SUB) for j in range(i, SUB)}
        rows = [jnp.where(head, (within == at + i).astype(jnp.float32), rows[i]) for i in range(SUB)]
        inverse, factor = [], {}
        for p in range(SUB):
            inverse.append(1.0 / diag[p, p])
            for i in range(p + 1, SUB):
                factor[p, i] = diag[p, i] * inverse[p]
                for j in range(i, SUB):
                    diag[i, j] = diag[i, j] - factor[p, i] * diag[p, j]
                rows[i] = rows[i] - factor[p, i] * rows[p]
        rows = [rows[p] * inverse[p] for p in range(SUB)]
        for p in reversed(range(SUB)):
            for i in range(p):
                rows[i] = rows[i] - factor[i, p] * rows[p]
        done = rows[0]
        for i in range(1, SUB):
            done = jnp.where(sub == i, rows[i], done)
        out = []
        for g, block in enumerate(blocks):
            if g == k:
                out.append(done)
                continue
            terms = [column(block, at + p) * rows[p] for p in range(SUB)]
            while len(terms) > 1:
                terms = [terms[i] + terms[i + 1] for i in range(0, len(terms), 2)]
            out.append(jnp.where(head, 0.0, block) - terms[0])
        blocks = out
    return blocks


def side_by_side_inverses(first, second):
    half = first.shape[0]
    both = jnp.concatenate([first, second], axis=1)
    blocks = gauss_jordan([both[g : g + SUB, :] for g in range(0, half, SUB)])
    both = jnp.concatenate(blocks, axis=0)
    return both[:, :half], both[:, half:]


def damped(cov):
    size = cov.shape[0]
    cov = 0.5 * (cov + cov.T)
    row = lax.broadcasted_iota(jnp.int32, (size, size), 0)
    col = lax.broadcasted_iota(jnp.int32, (size, size), 1)
    damping = 0.1 * jnp.sum(jnp.where(row == col, cov, 0.0)) / size
    return jnp.where(row == col, cov + damping, cov)


def product(left, right, dims=((1,), (0,))):
    return lax.dot_general(left, right, (dims, ((), ())), precision=EXACT, preferred_element_type=jnp.float32)


def first_half_kernel(cov_in_hbm, cov_out_hbm, out_ref, cov_ref, sems):
    copies = [
        pltpu.make_async_copy(source, cov_ref.at[i], sems.at[i]) for i, source in enumerate((cov_in_hbm, cov_out_hbm))
    ]
    for copy in copies:
        copy.start()
    for copy in copies:
        copy.wait()
    half = cov_ref.shape[1] // 2
    covs = [damped(cov_ref[0]), damped(cov_ref[1])]
    corner = [cov[:half, half:] for cov in covs]
    upper = side_by_side_inverses(*[cov[:half, :half] for cov in covs])
    solved = [product(u, c) for u, c in zip(upper, corner)]
    schur = [cov[half:, half:] - product(c, t, ((0,), (0,))) for cov, c, t in zip(covs, corner, solved)]
    for i, pair in enumerate((upper, solved, schur)):
        out_ref[i] = jnp.concatenate(pair, axis=1)


def second_half_kernel(first_ref, len_hbm, k_ref, len_ref, sem):
    copy = pltpu.make_async_copy(len_hbm, len_ref, sem)
    copy.start()
    size = k_ref.shape[1]
    half = size // 2
    upper, solved, schur = [(first_ref[i][:, :half], first_ref[i][:, half:]) for i in range(3)]
    lower = side_by_side_inverses(*schur)
    for m, (u, t, low) in enumerate(zip(upper, solved, lower)):
        side = product(t, low)
        k_ref[m, :half, :half] = u + product(side, t, ((1,), (1,)))
        k_ref[m, :half, half:] = -side
        k_ref[m, half:, :half] = -side.T
        k_ref[m, half:, half:] = low
    copy.wait()
    token = lax.broadcasted_iota(jnp.int32, (size, size), 0)
    lane = lax.broadcasted_iota(jnp.int32, (size, size), 1)
    mask = jnp.zeros((size, size), jnp.float32)
    for s in range(len_ref.shape[0]):
        mask = jnp.where((lane == s) & (token < len_ref[s]), 1.0, mask)
    k_ref[2] = mask


def first_half(cov_in, cov_out):
    size = cov_in.shape[0]
    return pl.pallas_call(
        first_half_kernel,
        out_shape=jax.ShapeDtypeStruct((3, size // 2, size), jnp.float32),
        in_specs=[HBM, HBM],
        out_specs=VMEM,
        scratch_shapes=[pltpu.VMEM((2, size, size), jnp.float32), pltpu.SemaphoreType.DMA((2,))],
        compiler_params=pltpu.CompilerParams(vmem_limit_bytes=8 << 20),
        cost_estimate=pl.CostEstimate(flops=size, bytes_accessed=size, transcendentals=0),
        name="first_half",
    )(pinned(cov_in), pinned(cov_out))


def second_half(first, lengths):
    size = first.shape[2]
    return pl.pallas_call(
        second_half_kernel,
        out_shape=jax.ShapeDtypeStruct((3, size, size), jnp.float32),
        in_specs=[VMEM, HBM],
        out_specs=VMEM,
        scratch_shapes=[pltpu.SMEM(lengths.shape, jnp.int32), pltpu.SemaphoreType.DMA],
        compiler_params=pltpu.CompilerParams(vmem_limit_bytes=8 << 20),
        cost_estimate=pl.CostEstimate(flops=size, bytes_accessed=size, transcendentals=0),
        name="second_half",
    )(first, pinned(lengths))


def merge_kernel(spans, *refs):
    at = 0
    for ref, (start, rows) in zip(refs[:-1], spans):
        refs[-1][at : at + rows, :] = ref[start : start + rows, :]
        at += rows


def merge(parts):
    array, start, rows = parts[0]
    if len(parts) == 1 and rows == array.shape[0]:
        return array
    total = sum(part[2] for part in parts)
    return pl.pallas_call(
        functools.partial(merge_kernel, [part[1:] for part in parts]),
        out_shape=jax.ShapeDtypeStruct((total, array.shape[1]), array.dtype),
        in_specs=[VMEM] * len(parts),
        out_specs=VMEM,
        compiler_params=pltpu.CompilerParams(vmem_limit_bytes=16 << 20),
        cost_estimate=pl.CostEstimate(flops=total, bytes_accessed=total, transcendentals=0),
        name="merge",
    )(*(part[0] for part in parts))


def joined(parts):
    out = []
    for array, start, rows in parts:
        if out and out[-1][0] is array and out[-1][1] + out[-1][2] == start:
            out[-1] = (array, out[-1][1], out[-1][2] + rows)
        else:
            out.append((array, start, rows))
    return out


def project_kernel(n, early, seqs, me_ref, *rest):
    inputs, blocks, (total_ref, held, sems) = rest[:2], rest[2 : 2 + len(early)], rest[2 + len(early) :]
    tokens = held.shape[1]
    part = tokens // sems.shape[1]
    copies = [
        [
            pltpu.make_async_copy(source.at[pl.ds(i * part, part)], held.at[t, pl.ds(i * part, part)], sems.at[t, i])
            for i in range(sems.shape[1])
        ]
        for t, source in enumerate(inputs)
    ]
    for copy in copies[0] + copies[1]:
        copy.start()
    rows = blocks[0].shape[0] // 2
    source = sources(me_ref[0], n)
    for t in range(2):
        for copy in copies[t]:
            copy.wait()
        total = None
        for which, block in zip(early, blocks):
            columns = pl.ds(pl.multiple_of(source[which] * rows, rows), rows)
            term = jnp.dot(
                held[t, :, columns], block[t * rows : (t + 1) * rows, :], preferred_element_type=jnp.float32
            )
            total = term if total is None else total + term
        total_ref[t] = total


def project_whole_kernel(n, me_ref, act_ref, grad_ref, *rest):
    blocks, (total_ref, proj) = rest[:n], rest[n:]
    rows = blocks[0].shape[0] // 2
    for block, source in zip(blocks, sources(me_ref[0], n)):
        at = pl.ds(pl.multiple_of(source * rows, rows), rows)
        for t in range(2):
            proj[t, at, :] = block[t * rows : (t + 1) * rows, :]
    for t, ref in enumerate((act_ref, grad_ref)):
        total_ref[t] = jnp.dot(ref[...], proj[t], preferred_element_type=jnp.float32)


def project(me, activations, out_grads, blocks, early, seqs, n):
    tokens, width = activations.shape
    rank = blocks[0].shape[1]
    total = jax.ShapeDtypeStruct((2, tokens, rank), jnp.float32)
    common = dict(
        compiler_params=pltpu.CompilerParams(vmem_limit_bytes=16 << 20),
        cost_estimate=pl.CostEstimate(flops=rank, bytes_accessed=rank, transcendentals=0),
        name="project",
    )
    if len(early) == n:
        result = pl.pallas_call(
            functools.partial(project_whole_kernel, n),
            out_shape=total,
            in_specs=[SMEM] + [VMEM] * (2 + n),
            out_specs=VMEM,
            scratch_shapes=[pltpu.VMEM((2, width, rank), jnp.bfloat16)],
            **common,
        )(me, activations, out_grads, *blocks)
        return result, None
    return pl.pallas_call(
        functools.partial(project_kernel, n, early, seqs),
        out_shape=(
            total,
            jax.ShapeDtypeStruct((2, tokens, width), activations.dtype),
        ),
        in_specs=[SMEM, HBM, HBM] + [VMEM] * len(early),
        out_specs=(VMEM, VMEM),
        scratch_shapes=[pltpu.SemaphoreType.DMA((2, 2 * seqs))],
        **common,
    )(me, pinned(activations), pinned(out_grads), *blocks)


def whiten_kernel(n, seqs, late, me_ref, total_ref, k_ref, *rest):
    operands, (out_ref, white) = rest[:-2], rest[-2:]
    rank = k_ref.shape[1]
    sums = [total_ref[0], total_ref[1]]
    if late:
        held, *blocks = operands
        source = sources(me_ref[0], n)
        rows = held.shape[2] // n
        for which, t, operand, at in late:
            columns = pl.ds(pl.multiple_of(source[which] * rows, rows), rows)
            block = blocks[operand][at : at + rows, :]
            sums[t] = sums[t] + jnp.dot(held[t, :, columns], block, preferred_element_type=jnp.float32)
    length = total_ref.shape[1] // seqs
    share = rank // n
    grads = []
    for s in range(seqs):
        token = slice(s * length, (s + 1) * length)
        x_proj = (sums[0][token, :] * k_ref[2][:length, s : s + 1]).astype(jnp.bfloat16)
        d_proj = sums[1][token, :].astype(jnp.bfloat16)
        grads.append(
            lax.dot_general(d_proj, x_proj, (((0,), (0,)), ((), ())), preferred_element_type=jnp.float32)
        )
    left = product(k_ref[1], jnp.concatenate(grads, axis=1))
    left = jnp.concatenate([left[:, s * rank : (s + 1) * rank] for s in range(seqs)], axis=0)
    full = product(left, k_ref[0])
    places = [exchange_order(n).index(d) for d in range(n)]
    for s in range(seqs):
        for d in range(n):
            at = s * rank + d * share
            white[places[d], s * share : (s + 1) * share, :] = full[at : at + share, :]
    out_ref[...] = white[...].astype(jnp.bfloat16)


def whitened_blocks(me, total, k, late, operands, seqs, n):
    rank = k.shape[1]
    shape = (n, seqs * (rank // n), rank)
    return pl.pallas_call(
        functools.partial(whiten_kernel, n, seqs, late),
        out_shape=jax.ShapeDtypeStruct(shape, jnp.bfloat16),
        in_specs=[SMEM] + [VMEM] * (2 + len(operands)),
        out_specs=VMEM,
        scratch_shapes=[pltpu.VMEM(shape, jnp.float32)],
        compiler_params=pltpu.CompilerParams(vmem_limit_bytes=16 << 20),
        cost_estimate=pl.CostEstimate(flops=64 * rank**3, bytes_accessed=4 << 20, transcendentals=0),
        name="whiten",
    )(me, total, k, *operands)


def exchanged(value, n):
    order = [exchange_order(n)]
    return lax.all_to_all(value, "coord", split_axis=0, concat_axis=0, axis_index_groups=order, tiled=True)


def score_kernel(n, me_ref, ids_ref, white_ref, bank_ref, out_ref, spread):
    seqs = ids_ref.shape[0]
    chunk, rank = white_ref.shape[1:]
    share = chunk // seqs
    total = n * seqs
    spread[...] = white_ref[...].astype(jnp.float32).reshape(n * chunk, rank)
    columns = jnp.concatenate(
        [spread[pl.ds(j, total, stride=share), :].astype(jnp.bfloat16) for j in range(share)], axis=1
    )
    queries = bank_ref.shape[0] // n
    row = lax.broadcasted_iota(jnp.int32, (total, out_ref.shape[2] - queries), 0)
    tail = jnp.zeros(row.shape, jnp.float32)
    place = place_of(me_ref[0], n)
    for s in range(seqs):
        tail = jnp.where(row == place * seqs + s, ids_ref[s].astype(jnp.float32), tail)
    partial = lax.dot_general(
        columns, bank_ref[...], (((1,), (1,)), ((), ())), preferred_element_type=jnp.float32
    )
    for d in range(n):
        at = exchange_order(n).index(d)
        out_ref[at, :, :queries] = partial[:, d * queries : (d + 1) * queries].astype(out_ref.dtype)
        out_ref[at, :, queries:] = tail.astype(out_ref.dtype)


def partial_scores(me, seq_ids, white, bank):
    n = white.shape[0]
    seqs = seq_ids.shape[0]
    queries = bank.shape[0] // n
    width = (queries // LANES + 1) * LANES
    return pl.pallas_call(
        functools.partial(score_kernel, n),
        out_shape=jax.ShapeDtypeStruct((n, n * seqs, width), jnp.bfloat16),
        in_specs=[SMEM, SMEM, VMEM, VMEM],
        out_specs=VMEM,
        scratch_shapes=[pltpu.VMEM((n * white.shape[1], white.shape[2]), jnp.float32)],
        compiler_params=pltpu.CompilerParams(vmem_limit_bytes=16 << 20),
        cost_estimate=pl.CostEstimate(
            flops=2 * n * seqs * bank.size, bytes_accessed=2 * bank.size, transcendentals=0
        ),
        name="score",
    )(me, seq_ids, white, bank)


def place_kernel(partial_ref, out_ref):
    rows, queries = out_ref.shape
    total = jnp.sum(partial_ref[...].astype(jnp.float32), axis=0)
    raw = total[:, :queries].astype(jnp.bfloat16)
    ids = total[:, queries : queries + 1].astype(jnp.int32)
    chosen = ids == lax.broadcasted_iota(jnp.int32, (rows, rows), 1)
    out_ref[...] = lax.dot_general(
        chosen.astype(jnp.bfloat16), raw, (((0,), (0,)), ((), ())), preferred_element_type=jnp.float32
    ).astype(jnp.bfloat16)


def place(partials, queries):
    return pl.pallas_call(
        lambda a, b: place_kernel(a, b),
        out_shape=jax.ShapeDtypeStruct((partials.shape[1], queries), jnp.bfloat16),
        in_specs=[VMEM],
        out_specs=VMEM,
        compiler_params=pltpu.CompilerParams(vmem_limit_bytes=16 << 20),
        name="place",
    )(partials)


def body(n, activations, out_grads, proj_in, proj_out, cov_in, cov_out, lengths, seq_ids, bank):
    me = lax.axis_index("coord").reshape(1)
    seqs, length, width = activations.shape
    activations, out_grads = activations.reshape(seqs * length, width), out_grads.reshape(seqs * length, width)
    a, b, c = factors(n)
    paired = a & (a - 1) == 0
    packed = pack(proj_in, proj_out)
    half = first_half(cov_in, cov_out)
    held = {(0, 0, 0): packed}
    for at in range(1, min(a, 3)):
        held[at, 0, 0] = moved(packed, (at, 0, 0), n)
    for by in range(1, b):
        held[0, by, 0] = moved(packed, (0, by, 0), n)
    held, half = lax.optimization_barrier((held, half))
    early = list(held)
    rows = proj_in.shape[0]
    halves = {(at, t): (held[at], t * rows, rows) for at in early for t in range(2)}
    wanted = {}
    for at in range(1, a):
        nearest = at & -at
        source = at - nearest if paired and nearest != at else 0
        for by in range(b):
            for t in range(2):
                if ((at, by, 0), t) in halves:
                    continue
                if source or at > 2:
                    wanted[(at, by, 0), t] = (source, 0, 0), (at - source, by, 0)
                elif at == 1 and t == 0:
                    wanted[(at, by, 0), t] = (0, by, 0), (1, 0, 0)
                else:
                    wanted[(at, by, 0), t] = (at, 0, 0), (0, by, 0)
    arrivals = []
    while wanted:
        steps = {}
        for to, (source, step) in wanted.items():
            if (source, to[1]) in halves:
                steps.setdefault(step, []).append((to, source))
        for step, both in steps.items():
            arrived = moved(merge(joined([halves[source, to[1]] for to, source in both])), step, n)
            arrivals.append((arrived, [to for to, _ in both]))
            for i, (to, _) in enumerate(both):
                halves[to] = arrived, i * rows, rows
                del wanted[to]
    k = second_half(half, lengths)
    order = [(at, by, core) for core in range(c) for by in range(b) for at in range(a)]
    if rows % LANES == 0 and arrivals and c == 2:
        total, inputs = project(
            me, activations, out_grads, [held[at] for at in early], [order.index(at) for at in early], seqs, n
        )
        across = [moved(merge([(held[at], 0, 2 * rows) for at in early]), (0, 0, 1), n)]
        waiting, total, k = lax.optimization_barrier(([arrived for arrived, _ in arrivals], total, k))
        across.append(moved(merge([(arrived, 0, arrived.shape[0]) for arrived in waiting]), (0, 0, 1), n))
        operands = [inputs, *across, *waiting]
        late = [
            (order.index(at), t, 2 + i, j * rows)
            for i, (_, group) in enumerate(arrivals)
            for j, (at, t) in enumerate(group)
        ]
        crossed = [[(at, t) for at in early for t in range(2)], [to for _, group in arrivals for to in group]]
        late += [
            (order.index((*at[:2], 1)), t, i, j * rows) for i, part in enumerate(crossed) for j, (at, t) in enumerate(part)
        ]
    else:
        for at in order:
            if at[2] == 0:
                held[at] = merge(joined([halves[at, 0], halves[at, 1]]))
                for by in range(1, c):
                    held[at[0], at[1], by] = moved(held[at], (0, 0, by), n)
        total = project(me, activations, out_grads, [held[at] for at in order], list(range(n)), seqs, n)[0]
        operands, late = [], []
    white = whitened_blocks(me, total, k, late, operands, seqs, n)
    partials = partial_scores(me, seq_ids, exchanged(white, n), bank)
    return place(exchanged(partials, n), bank.shape[0] // n)


def solution(mesh):
    in_specs = (
        P(("groups", "coord"), None, None),
        P(("groups", "coord"), None, None),
        P("coord", None),
        P("coord", None),
        P(),
        P(),
        P(("groups", "coord")),
        P(("groups", "coord")),
        P(None, "coord"),
    )
    out_specs = P("groups", "coord")
    return jax.shard_map(
        functools.partial(body, mesh.shape["coord"]),
        mesh=mesh,
        in_specs=in_specs,
        out_specs=out_specs,
        check_vma=False,
    )
```

```python
import functools

import jax
import jax.numpy as jnp
from jax import lax
from jax.experimental import pallas as pl
from jax.experimental.pallas import tpu as pltpu
from jax.sharding import PartitionSpec as P

SUB = 8
LANES = 128
EXACT = lax.Precision.HIGHEST
VMEM = pl.BlockSpec(memory_space=pltpu.VMEM)
HBM = pl.BlockSpec(memory_space=pltpu.HBM)
SMEM = pl.BlockSpec(memory_space=pltpu.SMEM)


def factors(n):
    c = 2 if n % 2 == 0 else 1
    rest = n // c
    b = max(f for f in range(1, rest + 1) if rest % f == 0 and f * f <= rest)
    return rest // b, b, c


def partner(at, by, size, towards):
    if size & (size - 1) == 0:
        return at ^ by
    return (at + (by if towards else size - by)) % size


def sources(me, n):
    a, b, c = factors(n)
    ia, ib, ic = me // (b * c), (me // c) % b, me % c
    return [
        (partner(ia, da, a, False) * b + partner(ib, db, b, False)) * c + partner(ic, dc, c, False)
        for dc in range(c)
        for db in range(b)
        for da in range(a)
    ]


def moved(value, by, n):
    sizes = factors(n)
    a, b, c = sizes
    pairs = []
    for me in range(n):
        at = (me // (b * c), (me // c) % b, me % c)
        to = [partner(place, step, size, True) for place, step, size in zip(at, by, sizes)]
        pairs.append((me, (to[0] * b + to[1]) * c + to[2]))
    return lax.ppermute(value, "coord", pairs)


def exchange_order(n):
    a, b, c = factors(n)
    return sorted(range(n), key=lambda device: (1 - device % 2, abs(2 * (device // (b * c)) - (a - 1)), -device))


def place_of(me, n):
    place = 0
    for i, device in enumerate(exchange_order(n)):
        place = jnp.where(me == device, i, place)
    return place


def pack_kernel(first_hbm, second_hbm, out_ref, sems):
    rows = first_hbm.shape[0]
    copies = [
        pltpu.make_async_copy(source, out_ref.at[pl.ds(i * rows, rows)], sems.at[i])
        for i, source in enumerate((first_hbm, second_hbm))
    ]
    for copy in copies:
        copy.start()
    for copy in copies:
        copy.wait()


def pack(first, second):
    rows, columns = first.shape
    return pl.pallas_call(
        pack_kernel,
        out_shape=jax.ShapeDtypeStruct((2 * rows, columns), first.dtype),
        in_specs=[HBM, HBM],
        out_specs=VMEM,
        scratch_shapes=[pltpu.SemaphoreType.DMA((2,))],
        compiler_params=pltpu.CompilerParams(vmem_limit_bytes=8 << 20),
        name="pack",
    )(pinned(first), pinned(second))


def pinned(value):
    return pltpu.with_memory_space_constraint(value, pltpu.HBM)


def gauss_jordan(blocks):
    width = blocks[0].shape[1]
    half = width // 2
    lane = lax.broadcasted_iota(jnp.int32, (SUB, width), 1)
    sub = lax.broadcasted_iota(jnp.int32, (SUB, width), 0)
    start, within = lane // half * half, lane % half

    def column(block, at):
        return jnp.take_along_axis(block, start + at, axis=1, mode="promise_in_bounds")

    for k in range(len(blocks)):
        at = k * SUB
        head = within // SUB == k
        rows = [jnp.broadcast_to(blocks[k][i : i + 1, :], (SUB, width)) for i in range(SUB)]
        diag = {(i, j): column(rows[i], at + j) for i in range(SUB) for j in range(i, SUB)}
        rows = [jnp.where(head, (within == at + i).astype(jnp.float32), rows[i]) for i in range(SUB)]
        inverse, factor = [], {}
        for p in range(SUB):
            inverse.append(1.0 / diag[p, p])
            for i in range(p + 1, SUB):
                factor[p, i] = diag[p, i] * inverse[p]
                for j in range(i, SUB):
                    diag[i, j] = diag[i, j] - factor[p, i] * diag[p, j]
                rows[i] = rows[i] - factor[p, i] * rows[p]
        rows = [rows[p] * inverse[p] for p in range(SUB)]
        for p in reversed(range(SUB)):
            for i in range(p):
                rows[i] = rows[i] - factor[i, p] * rows[p]
        done = rows[0]
        for i in range(1, SUB):
            done = jnp.where(sub == i, rows[i], done)
        out = []
        for g, block in enumerate(blocks):
            if g == k:
                out.append(done)
                continue
            terms = [column(block, at + p) * rows[p] for p in range(SUB)]
            while len(terms) > 1:
                terms = [terms[i] + terms[i + 1] for i in range(0, len(terms), 2)]
            out.append(jnp.where(head, 0.0, block) - terms[0])
        blocks = out
    return blocks


def side_by_side_inverses(first, second):
    half = first.shape[0]
    both = jnp.concatenate([first, second], axis=1)
    blocks = gauss_jordan([both[g : g + SUB, :] for g in range(0, half, SUB)])
    both = jnp.concatenate(blocks, axis=0)
    return both[:, :half], both[:, half:]


def damped(cov):
    size = cov.shape[0]
    cov = 0.5 * (cov + cov.T)
    row = lax.broadcasted_iota(jnp.int32, (size, size), 0)
    col = lax.broadcasted_iota(jnp.int32, (size, size), 1)
    damping = 0.1 * jnp.sum(jnp.where(row == col, cov, 0.0)) / size
    return jnp.where(row == col, cov + damping, cov)


def product(left, right, dims=((1,), (0,))):
    return lax.dot_general(left, right, (dims, ((), ())), precision=EXACT, preferred_element_type=jnp.float32)


def first_half_kernel(cov_in_hbm, cov_out_hbm, out_ref, cov_ref, sems):
    copies = [
        pltpu.make_async_copy(source, cov_ref.at[i], sems.at[i]) for i, source in enumerate((cov_in_hbm, cov_out_hbm))
    ]
    for copy in copies:
        copy.start()
    for copy in copies:
        copy.wait()
    half = cov_ref.shape[1] // 2
    covs = [damped(cov_ref[0]), damped(cov_ref[1])]
    corner = [cov[:half, half:] for cov in covs]
    upper = side_by_side_inverses(*[cov[:half, :half] for cov in covs])
    solved = [product(u, c) for u, c in zip(upper, corner)]
    schur = [cov[half:, half:] - product(c, t, ((0,), (0,))) for cov, c, t in zip(covs, corner, solved)]
    for i, pair in enumerate((upper, solved, schur)):
        out_ref[i] = jnp.concatenate(pair, axis=1)


def second_half_kernel(first_ref, len_hbm, k_ref, len_ref, sem):
    copy = pltpu.make_async_copy(len_hbm, len_ref, sem)
    copy.start()
    size = k_ref.shape[1]
    half = size // 2
    upper, solved, schur = [(first_ref[i][:, :half], first_ref[i][:, half:]) for i in range(3)]
    lower = side_by_side_inverses(*schur)
    for m, (u, t, low) in enumerate(zip(upper, solved, lower)):
        side = product(t, low)
        k_ref[m, :half, :half] = u + product(side, t, ((1,), (1,)))
        k_ref[m, :half, half:] = -side
        k_ref[m, half:, :half] = -side.T
        k_ref[m, half:, half:] = low
    copy.wait()
    token = lax.broadcasted_iota(jnp.int32, (size, size), 0)
    lane = lax.broadcasted_iota(jnp.int32, (size, size), 1)
    mask = jnp.zeros((size, size), jnp.float32)
    for s in range(len_ref.shape[0]):
        mask = jnp.where((lane == s) & (token < len_ref[s]), 1.0, mask)
    k_ref[2] = mask


def first_half(cov_in, cov_out):
    size = cov_in.shape[0]
    return pl.pallas_call(
        first_half_kernel,
        out_shape=jax.ShapeDtypeStruct((3, size // 2, size), jnp.float32),
        in_specs=[HBM, HBM],
        out_specs=VMEM,
        scratch_shapes=[pltpu.VMEM((2, size, size), jnp.float32), pltpu.SemaphoreType.DMA((2,))],
        compiler_params=pltpu.CompilerParams(vmem_limit_bytes=8 << 20),
        cost_estimate=pl.CostEstimate(flops=size, bytes_accessed=size, transcendentals=0),
        name="first_half",
    )(pinned(cov_in), pinned(cov_out))


def second_half(first, lengths):
    size = first.shape[2]
    return pl.pallas_call(
        second_half_kernel,
        out_shape=jax.ShapeDtypeStruct((3, size, size), jnp.float32),
        in_specs=[VMEM, HBM],
        out_specs=VMEM,
        scratch_shapes=[pltpu.SMEM(lengths.shape, jnp.int32), pltpu.SemaphoreType.DMA],
        compiler_params=pltpu.CompilerParams(vmem_limit_bytes=8 << 20),
        cost_estimate=pl.CostEstimate(flops=size, bytes_accessed=size, transcendentals=0),
        name="second_half",
    )(first, pinned(lengths))


def merge_kernel(spans, *refs):
    at = 0
    for ref, (start, rows) in zip(refs[:-1], spans):
        refs[-1][at : at + rows, :] = ref[start : start + rows, :]
        at += rows


def merge(parts):
    array, start, rows = parts[0]
    if len(parts) == 1 and rows == array.shape[0]:
        return array
    total = sum(part[2] for part in parts)
    return pl.pallas_call(
        functools.partial(merge_kernel, [part[1:] for part in parts]),
        out_shape=jax.ShapeDtypeStruct((total, array.shape[1]), array.dtype),
        in_specs=[VMEM] * len(parts),
        out_specs=VMEM,
        compiler_params=pltpu.CompilerParams(vmem_limit_bytes=16 << 20),
        cost_estimate=pl.CostEstimate(flops=total, bytes_accessed=total, transcendentals=0),
        name="merge",
    )(*(part[0] for part in parts))


def joined(parts):
    out = []
    for array, start, rows in parts:
        if out and out[-1][0] is array and out[-1][1] + out[-1][2] == start:
            out[-1] = (array, out[-1][1], out[-1][2] + rows)
        else:
            out.append((array, start, rows))
    return out


def project_kernel(n, early, seqs, me_ref, *rest):
    inputs, blocks, (total_ref, held, sems) = rest[:2], rest[2 : 2 + len(early)], rest[2 + len(early) :]
    tokens = held.shape[1]
    part = tokens // sems.shape[1]
    copies = [
        [
            pltpu.make_async_copy(source.at[pl.ds(i * part, part)], held.at[t, pl.ds(i * part, part)], sems.at[t, i])
            for i in range(sems.shape[1])
        ]
        for t, source in enumerate(inputs)
    ]
    for copy in copies[0] + copies[1]:
        copy.start()
    rows = blocks[0].shape[0] // 2
    source = sources(me_ref[0], n)
    for t in range(2):
        for copy in copies[t]:
            copy.wait()
        total = None
        for which, block in zip(early, blocks):
            columns = pl.ds(pl.multiple_of(source[which] * rows, rows), rows)
            term = jnp.dot(
                held[t, :, columns], block[t * rows : (t + 1) * rows, :], preferred_element_type=jnp.float32
            )
            total = term if total is None else total + term
        total_ref[t] = total


def project_whole_kernel(n, me_ref, act_ref, grad_ref, *rest):
    blocks, (total_ref, proj) = rest[:n], rest[n:]
    rows = blocks[0].shape[0] // 2
    for block, source in zip(blocks, sources(me_ref[0], n)):
        at = pl.ds(pl.multiple_of(source * rows, rows), rows)
        for t in range(2):
            proj[t, at, :] = block[t * rows : (t + 1) * rows, :]
    for t, ref in enumerate((act_ref, grad_ref)):
        total_ref[t] = jnp.dot(ref[...], proj[t], preferred_element_type=jnp.float32)


def project(me, activations, out_grads, blocks, early, seqs, n):
    tokens, width = activations.shape
    rank = blocks[0].shape[1]
    total = jax.ShapeDtypeStruct((2, tokens, rank), jnp.float32)
    common = dict(
        compiler_params=pltpu.CompilerParams(vmem_limit_bytes=16 << 20),
        cost_estimate=pl.CostEstimate(flops=rank, bytes_accessed=rank, transcendentals=0),
        name="project",
    )
    if len(early) == n:
        result = pl.pallas_call(
            functools.partial(project_whole_kernel, n),
            out_shape=total,
            in_specs=[SMEM] + [VMEM] * (2 + n),
            out_specs=VMEM,
            scratch_shapes=[pltpu.VMEM((2, width, rank), jnp.bfloat16)],
            **common,
        )(me, activations, out_grads, *blocks)
        return result, None
    return pl.pallas_call(
        functools.partial(project_kernel, n, early, seqs),
        out_shape=(
            total,
            jax.ShapeDtypeStruct((2, tokens, width), activations.dtype),
        ),
        in_specs=[SMEM, HBM, HBM] + [VMEM] * len(early),
        out_specs=(VMEM, VMEM),
        scratch_shapes=[pltpu.SemaphoreType.DMA((2, 2 * seqs))],
        **common,
    )(me, pinned(activations), pinned(out_grads), *blocks)


def whiten_kernel(n, seqs, late, me_ref, total_ref, k_ref, *rest):
    operands, (out_ref, white) = rest[:-2], rest[-2:]
    rank = k_ref.shape[1]
    sums = [total_ref[0], total_ref[1]]
    if late:
        held, *blocks = operands
        source = sources(me_ref[0], n)
        rows = held.shape[2] // n
        for which, t, operand, at in late:
            columns = pl.ds(pl.multiple_of(source[which] * rows, rows), rows)
            block = blocks[operand][at : at + rows, :]
            sums[t] = sums[t] + jnp.dot(held[t, :, columns], block, preferred_element_type=jnp.float32)
    length = total_ref.shape[1] // seqs
    share = rank // n
    grads = []
    for s in range(seqs):
        token = slice(s * length, (s + 1) * length)
        x_proj = (sums[0][token, :] * k_ref[2][:length, s : s + 1]).astype(jnp.bfloat16)
        d_proj = sums[1][token, :].astype(jnp.bfloat16)
        grads.append(
            lax.dot_general(d_proj, x_proj, (((0,), (0,)), ((), ())), preferred_element_type=jnp.float32)
        )
    left = product(k_ref[1], jnp.concatenate(grads, axis=1))
    left = jnp.concatenate([left[:, s * rank : (s + 1) * rank] for s in range(seqs)], axis=0)
    full = product(left, k_ref[0])
    places = [exchange_order(n).index(d) for d in range(n)]
    for s in range(seqs):
        for d in range(n):
            at = s * rank + d * share
            white[places[d], s * share : (s + 1) * share, :] = full[at : at + share, :]
    out_ref[...] = white[...].astype(jnp.bfloat16)


def whitened_blocks(me, total, k, late, operands, seqs, n):
    rank = k.shape[1]
    shape = (n, seqs * (rank // n), rank)
    return pl.pallas_call(
        functools.partial(whiten_kernel, n, seqs, late),
        out_shape=jax.ShapeDtypeStruct(shape, jnp.bfloat16),
        in_specs=[SMEM] + [VMEM] * (2 + len(operands)),
        out_specs=VMEM,
        scratch_shapes=[pltpu.VMEM(shape, jnp.float32)],
        compiler_params=pltpu.CompilerParams(vmem_limit_bytes=16 << 20),
        cost_estimate=pl.CostEstimate(flops=64 * rank**3, bytes_accessed=4 << 20, transcendentals=0),
        name="whiten",
    )(me, total, k, *operands)


def exchanged(value, n):
    order = [exchange_order(n)]
    return lax.all_to_all(value, "coord", split_axis=0, concat_axis=0, axis_index_groups=order, tiled=True)


def score_kernel(n, me_ref, ids_ref, white_ref, bank_ref, out_ref, spread):
    seqs = ids_ref.shape[0]
    chunk, rank = white_ref.shape[1:]
    share = chunk // seqs
    total = n * seqs
    spread[...] = white_ref[...].astype(jnp.float32).reshape(n * chunk, rank)
    columns = jnp.concatenate(
        [spread[pl.ds(j, total, stride=share), :].astype(jnp.bfloat16) for j in range(share)], axis=1
    )
    queries = bank_ref.shape[0] // n
    row = lax.broadcasted_iota(jnp.int32, (total, out_ref.shape[2] - queries), 0)
    tail = jnp.zeros(row.shape, jnp.float32)
    place = place_of(me_ref[0], n)
    for s in range(seqs):
        tail = jnp.where(row == place * seqs + s, ids_ref[s].astype(jnp.float32), tail)
    partial = lax.dot_general(
        bank_ref[...], columns, (((1,), (1,)), ((), ())), preferred_element_type=jnp.float32
    ).T
    for d in range(n):
        at = exchange_order(n).index(d)
        out_ref[at, :, :queries] = partial[:, d * queries : (d + 1) * queries].astype(out_ref.dtype)
        out_ref[at, :, queries:] = tail.astype(out_ref.dtype)


def partial_scores(me, seq_ids, white, bank):
    n = white.shape[0]
    seqs = seq_ids.shape[0]
    queries = bank.shape[0] // n
    width = (queries // LANES + 1) * LANES
    return pl.pallas_call(
        functools.partial(score_kernel, n),
        out_shape=jax.ShapeDtypeStruct((n, n * seqs, width), jnp.bfloat16),
        in_specs=[SMEM, SMEM, VMEM, VMEM],
        out_specs=VMEM,
        scratch_shapes=[pltpu.VMEM((n * white.shape[1], white.shape[2]), jnp.float32)],
        compiler_params=pltpu.CompilerParams(vmem_limit_bytes=16 << 20),
        cost_estimate=pl.CostEstimate(
            flops=2 * n * seqs * bank.size, bytes_accessed=2 * bank.size, transcendentals=0
        ),
        name="score",
    )(me, seq_ids, white, bank)


def place_kernel(partial_ref, out_ref):
    rows, queries = out_ref.shape
    total = jnp.sum(partial_ref[...].astype(jnp.float32), axis=0)
    raw = total[:, :queries].astype(jnp.bfloat16)
    ids = total[:, queries : queries + 1].astype(jnp.int32)
    chosen = ids == lax.broadcasted_iota(jnp.int32, (rows, rows), 1)
    out_ref[...] = lax.dot_general(
        chosen.astype(jnp.bfloat16), raw, (((0,), (0,)), ((), ())), preferred_element_type=jnp.float32
    ).astype(jnp.bfloat16)


def place(partials, queries):
    return pl.pallas_call(
        lambda a, b: place_kernel(a, b),
        out_shape=jax.ShapeDtypeStruct((partials.shape[1], queries), jnp.bfloat16),
        in_specs=[VMEM],
        out_specs=VMEM,
        compiler_params=pltpu.CompilerParams(vmem_limit_bytes=16 << 20),
        name="place",
    )(partials)


def body(n, activations, out_grads, proj_in, proj_out, cov_in, cov_out, lengths, seq_ids, bank):
    me = lax.axis_index("coord").reshape(1)
    seqs, length, width = activations.shape
    activations, out_grads = activations.reshape(seqs * length, width), out_grads.reshape(seqs * length, width)
    a, b, c = factors(n)
    paired = a & (a - 1) == 0
    packed = pack(proj_in, proj_out)
    half = first_half(cov_in, cov_out)
    held = {(0, 0, 0): packed}
    for at in range(1, min(a, 3)):
        held[at, 0, 0] = moved(packed, (at, 0, 0), n)
    for by in range(1, b):
        held[0, by, 0] = moved(packed, (0, by, 0), n)
    held, half = lax.optimization_barrier((held, half))
    early = list(held)
    rows = proj_in.shape[0]
    halves = {(at, t): (held[at], t * rows, rows) for at in early for t in range(2)}
    wanted = {}
    for at in range(1, a):
        nearest = at & -at
        source = at - nearest if paired and nearest != at else 0
        for by in range(b):
            for t in range(2):
                if ((at, by, 0), t) in halves:
                    continue
                if source or at > 2:
                    wanted[(at, by, 0), t] = (source, 0, 0), (at - source, by, 0)
                elif at == 1 and t == 0:
                    wanted[(at, by, 0), t] = (0, by, 0), (1, 0, 0)
                else:
                    wanted[(at, by, 0), t] = (at, 0, 0), (0, by, 0)
    arrivals = []
    while wanted:
        steps = {}
        for to, (source, step) in wanted.items():
            if (source, to[1]) in halves:
                steps.setdefault(step, []).append((to, source))
        for step, both in steps.items():
            arrived = moved(merge(joined([halves[source, to[1]] for to, source in both])), step, n)
            arrivals.append((arrived, [to for to, _ in both]))
            for i, (to, _) in enumerate(both):
                halves[to] = arrived, i * rows, rows
                del wanted[to]
    k = second_half(half, lengths)
    order = [(at, by, core) for core in range(c) for by in range(b) for at in range(a)]
    if rows % LANES == 0 and arrivals and c == 2:
        total, inputs = project(
            me, activations, out_grads, [held[at] for at in early], [order.index(at) for at in early], seqs, n
        )
        across = [moved(merge([(held[at], 0, 2 * rows) for at in early]), (0, 0, 1), n)]
        waiting, total, k = lax.optimization_barrier(([arrived for arrived, _ in arrivals], total, k))
        across.append(moved(merge([(arrived, 0, arrived.shape[0]) for arrived in waiting]), (0, 0, 1), n))
        operands = [inputs, *across, *waiting]
        late = [
            (order.index(at), t, 2 + i, j * rows)
            for i, (_, group) in enumerate(arrivals)
            for j, (at, t) in enumerate(group)
        ]
        crossed = [[(at, t) for at in early for t in range(2)], [to for _, group in arrivals for to in group]]
        late += [
            (order.index((*at[:2], 1)), t, i, j * rows) for i, part in enumerate(crossed) for j, (at, t) in enumerate(part)
        ]
    else:
        for at in order:
            if at[2] == 0:
                held[at] = merge(joined([halves[at, 0], halves[at, 1]]))
                for by in range(1, c):
                    held[at[0], at[1], by] = moved(held[at], (0, 0, by), n)
        total = project(me, activations, out_grads, [held[at] for at in order], list(range(n)), seqs, n)[0]
        operands, late = [], []
    white = whitened_blocks(me, total, k, late, operands, seqs, n)
    partials = partial_scores(me, seq_ids, exchanged(white, n), bank)
    return place(exchanged(partials, n), bank.shape[0] // n)


def solution(mesh):
    in_specs = (
        P(("groups", "coord"), None, None),
        P(("groups", "coord"), None, None),
        P("coord", None),
        P("coord", None),
        P(),
        P(),
        P(("groups", "coord")),
        P(("groups", "coord")),
        P(None, "coord"),
    )
    out_specs = P("groups", "coord")
    return jax.shard_map(
        functools.partial(body, mesh.shape["coord"]),
        mesh=mesh,
        in_specs=in_specs,
        out_specs=out_specs,
        check_vma=False,
    )
```

```python
import functools

import jax
import jax.numpy as jnp
from jax import lax
from jax.experimental import pallas as pl
from jax.experimental.pallas import tpu as pltpu
from jax.sharding import PartitionSpec as P

SUB = 8
LANES = 128
EXACT = lax.Precision.HIGHEST
VMEM = pl.BlockSpec(memory_space=pltpu.VMEM)
HBM = pl.BlockSpec(memory_space=pltpu.HBM)
SMEM = pl.BlockSpec(memory_space=pltpu.SMEM)


def factors(n):
    c = 2 if n % 2 == 0 else 1
    rest = n // c
    b = max(f for f in range(1, rest + 1) if rest % f == 0 and f * f <= rest)
    return rest // b, b, c


def partner(at, by, size, towards):
    if size & (size - 1) == 0:
        return at ^ by
    return (at + (by if towards else size - by)) % size


def sources(me, n):
    a, b, c = factors(n)
    ia, ib, ic = me // (b * c), (me // c) % b, me % c
    return [
        (partner(ia, da, a, False) * b + partner(ib, db, b, False)) * c + partner(ic, dc, c, False)
        for dc in range(c)
        for db in range(b)
        for da in range(a)
    ]


def moved(value, by, n):
    sizes = factors(n)
    a, b, c = sizes
    pairs = []
    for me in range(n):
        at = (me // (b * c), (me // c) % b, me % c)
        to = [partner(place, step, size, True) for place, step, size in zip(at, by, sizes)]
        pairs.append((me, (to[0] * b + to[1]) * c + to[2]))
    return lax.ppermute(value, "coord", pairs)


def exchange_order(n):
    a, b, c = factors(n)
    return sorted(range(n), key=lambda device: (1 - device % 2, abs(2 * (device // (b * c)) - (a - 1)), -device))


def place_of(me, n):
    place = 0
    for i, device in enumerate(exchange_order(n)):
        place = jnp.where(me == device, i, place)
    return place


def pack_kernel(first_hbm, second_hbm, out_ref, sems):
    rows = first_hbm.shape[0]
    copies = [
        pltpu.make_async_copy(source, out_ref.at[pl.ds(i * rows, rows)], sems.at[i])
        for i, source in enumerate((first_hbm, second_hbm))
    ]
    for copy in copies:
        copy.start()
    for copy in copies:
        copy.wait()


def pack(first, second):
    rows, columns = first.shape
    return pl.pallas_call(
        pack_kernel,
        out_shape=jax.ShapeDtypeStruct((2 * rows, columns), first.dtype),
        in_specs=[HBM, HBM],
        out_specs=VMEM,
        scratch_shapes=[pltpu.SemaphoreType.DMA((2,))],
        compiler_params=pltpu.CompilerParams(vmem_limit_bytes=8 << 20),
        name="pack",
    )(pinned(first), pinned(second))


def pinned(value):
    return pltpu.with_memory_space_constraint(value, pltpu.HBM)


def gauss_jordan(blocks):
    width = blocks[0].shape[1]
    half = width // 2
    lane = lax.broadcasted_iota(jnp.int32, (SUB, width), 1)
    sub = lax.broadcasted_iota(jnp.int32, (SUB, width), 0)
    start, within = lane // half * half, lane % half

    def column(block, at):
        return jnp.take_along_axis(block, start + at, axis=1, mode="promise_in_bounds")

    for k in range(len(blocks)):
        at = k * SUB
        head = within // SUB == k
        rows = [jnp.broadcast_to(blocks[k][i : i + 1, :], (SUB, width)) for i in range(SUB)]
        diag = {(i, j): column(rows[i], at + j) for i in range(SUB) for j in range(i, SUB)}
        rows = [jnp.where(head, (within == at + i).astype(jnp.float32), rows[i]) for i in range(SUB)]
        inverse, factor = [], {}
        for p in range(SUB):
            inverse.append(1.0 / diag[p, p])
            for i in range(p + 1, SUB):
                factor[p, i] = diag[p, i] * inverse[p]
                for j in range(i, SUB):
                    diag[i, j] = diag[i, j] - factor[p, i] * diag[p, j]
                rows[i] = rows[i] - factor[p, i] * rows[p]
        rows = [rows[p] * inverse[p] for p in range(SUB)]
        for p in reversed(range(SUB)):
            for i in range(p):
                rows[i] = rows[i] - factor[i, p] * rows[p]
        done = rows[0]
        for i in range(1, SUB):
            done = jnp.where(sub == i, rows[i], done)
        out = []
        for g, block in enumerate(blocks):
            if g == k:
                out.append(done)
                continue
            terms = [column(block, at + p) * rows[p] for p in range(SUB)]
            while len(terms) > 1:
                terms = [terms[i] + terms[i + 1] for i in range(0, len(terms), 2)]
            out.append(jnp.where(head, 0.0, block) - terms[0])
        blocks = out
    return blocks


def side_by_side_inverses(first, second):
    half = first.shape[0]
    both = jnp.concatenate([first, second], axis=1)
    blocks = gauss_jordan([both[g : g + SUB, :] for g in range(0, half, SUB)])
    both = jnp.concatenate(blocks, axis=0)
    return both[:, :half], both[:, half:]


def damped(cov):
    size = cov.shape[0]
    cov = 0.5 * (cov + cov.T)
    row = lax.broadcasted_iota(jnp.int32, (size, size), 0)
    col = lax.broadcasted_iota(jnp.int32, (size, size), 1)
    damping = 0.1 * jnp.sum(jnp.where(row == col, cov, 0.0)) / size
    return jnp.where(row == col, cov + damping, cov)


def product(left, right, dims=((1,), (0,))):
    return lax.dot_general(left, right, (dims, ((), ())), precision=EXACT, preferred_element_type=jnp.float32)


def first_half_kernel(cov_in_hbm, cov_out_hbm, out_ref, cov_ref, sems):
    copies = [
        pltpu.make_async_copy(source, cov_ref.at[i], sems.at[i]) for i, source in enumerate((cov_in_hbm, cov_out_hbm))
    ]
    for copy in copies:
        copy.start()
    for copy in copies:
        copy.wait()
    half = cov_ref.shape[1] // 2
    covs = [damped(cov_ref[0]), damped(cov_ref[1])]
    corner = [cov[:half, half:] for cov in covs]
    upper = side_by_side_inverses(*[cov[:half, :half] for cov in covs])
    solved = [product(u, c) for u, c in zip(upper, corner)]
    schur = [cov[half:, half:] - product(c, t, ((0,), (0,))) for cov, c, t in zip(covs, corner, solved)]
    for i, pair in enumerate((upper, solved, schur)):
        out_ref[i] = jnp.concatenate(pair, axis=1)


def second_half_kernel(first_ref, len_hbm, k_ref, len_ref, sem):
    copy = pltpu.make_async_copy(len_hbm, len_ref, sem)
    copy.start()
    size = k_ref.shape[1]
    half = size // 2
    upper, solved, schur = [(first_ref[i][:, :half], first_ref[i][:, half:]) for i in range(3)]
    lower = side_by_side_inverses(*schur)
    for m, (u, t, low) in enumerate(zip(upper, solved, lower)):
        side = product(t, low)
        k_ref[m, :half, :half] = u + product(side, t, ((1,), (1,)))
        k_ref[m, :half, half:] = -side
        k_ref[m, half:, :half] = -side.T
        k_ref[m, half:, half:] = low
    copy.wait()
    token = lax.broadcasted_iota(jnp.int32, (size, size), 0)
    lane = lax.broadcasted_iota(jnp.int32, (size, size), 1)
    mask = jnp.zeros((size, size), jnp.float32)
    for s in range(len_ref.shape[0]):
        mask = jnp.where((lane == s) & (token < len_ref[s]), 1.0, mask)
    k_ref[2] = mask


def first_half(cov_in, cov_out):
    size = cov_in.shape[0]
    return pl.pallas_call(
        first_half_kernel,
        out_shape=jax.ShapeDtypeStruct((3, size // 2, size), jnp.float32),
        in_specs=[HBM, HBM],
        out_specs=VMEM,
        scratch_shapes=[pltpu.VMEM((2, size, size), jnp.float32), pltpu.SemaphoreType.DMA((2,))],
        compiler_params=pltpu.CompilerParams(vmem_limit_bytes=8 << 20),
        cost_estimate=pl.CostEstimate(flops=size, bytes_accessed=size, transcendentals=0),
        name="first_half",
    )(pinned(cov_in), pinned(cov_out))


def second_half(first, lengths):
    size = first.shape[2]
    return pl.pallas_call(
        second_half_kernel,
        out_shape=jax.ShapeDtypeStruct((3, size, size), jnp.float32),
        in_specs=[VMEM, HBM],
        out_specs=VMEM,
        scratch_shapes=[pltpu.SMEM(lengths.shape, jnp.int32), pltpu.SemaphoreType.DMA],
        compiler_params=pltpu.CompilerParams(vmem_limit_bytes=8 << 20),
        cost_estimate=pl.CostEstimate(flops=size, bytes_accessed=size, transcendentals=0),
        name="second_half",
    )(first, pinned(lengths))


def merge_kernel(spans, *refs):
    at = 0
    for ref, (start, rows) in zip(refs[:-1], spans):
        refs[-1][at : at + rows, :] = ref[start : start + rows, :]
        at += rows


def merge(parts):
    array, start, rows = parts[0]
    if len(parts) == 1 and rows == array.shape[0]:
        return array
    total = sum(part[2] for part in parts)
    return pl.pallas_call(
        functools.partial(merge_kernel, [part[1:] for part in parts]),
        out_shape=jax.ShapeDtypeStruct((total, array.shape[1]), array.dtype),
        in_specs=[VMEM] * len(parts),
        out_specs=VMEM,
        compiler_params=pltpu.CompilerParams(vmem_limit_bytes=16 << 20),
        cost_estimate=pl.CostEstimate(flops=total, bytes_accessed=total, transcendentals=0),
        name="merge",
    )(*(part[0] for part in parts))


def joined(parts):
    out = []
    for array, start, rows in parts:
        if out and out[-1][0] is array and out[-1][1] + out[-1][2] == start:
            out[-1] = (array, out[-1][1], out[-1][2] + rows)
        else:
            out.append((array, start, rows))
    return out


def project_kernel(n, early, seqs, me_ref, *rest):
    inputs, blocks, (total_ref, held, sems) = rest[:2], rest[2 : 2 + len(early)], rest[2 + len(early) :]
    tokens = held.shape[1]
    part = tokens // sems.shape[1]
    copies = [
        [
            pltpu.make_async_copy(source.at[pl.ds(i * part, part)], held.at[t, pl.ds(i * part, part)], sems.at[t, i])
            for i in range(sems.shape[1])
        ]
        for t, source in enumerate(inputs)
    ]
    for copy in copies[0] + copies[1]:
        copy.start()
    rows = blocks[0].shape[0] // 2
    source = sources(me_ref[0], n)
    for t in range(2):
        for copy in copies[t]:
            copy.wait()
        total = None
        for which, block in zip(early, blocks):
            columns = pl.ds(pl.multiple_of(source[which] * rows, rows), rows)
            term = jnp.dot(
                held[t, :, columns], block[t * rows : (t + 1) * rows, :], preferred_element_type=jnp.float32
            )
            total = term if total is None else total + term
        total_ref[t] = total


def project_whole_kernel(n, me_ref, act_ref, grad_ref, *rest):
    blocks, (total_ref, proj) = rest[:n], rest[n:]
    rows = blocks[0].shape[0] // 2
    for block, source in zip(blocks, sources(me_ref[0], n)):
        at = pl.ds(pl.multiple_of(source * rows, rows), rows)
        for t in range(2):
            proj[t, at, :] = block[t * rows : (t + 1) * rows, :]
    for t, ref in enumerate((act_ref, grad_ref)):
        total_ref[t] = jnp.dot(ref[...], proj[t], preferred_element_type=jnp.float32)


def project(me, activations, out_grads, blocks, early, seqs, n):
    tokens, width = activations.shape
    rank = blocks[0].shape[1]
    total = jax.ShapeDtypeStruct((2, tokens, rank), jnp.float32)
    common = dict(
        compiler_params=pltpu.CompilerParams(vmem_limit_bytes=16 << 20),
        cost_estimate=pl.CostEstimate(flops=rank, bytes_accessed=rank, transcendentals=0),
        name="project",
    )
    if len(early) == n:
        result = pl.pallas_call(
            functools.partial(project_whole_kernel, n),
            out_shape=total,
            in_specs=[SMEM] + [VMEM] * (2 + n),
            out_specs=VMEM,
            scratch_shapes=[pltpu.VMEM((2, width, rank), jnp.bfloat16)],
            **common,
        )(me, activations, out_grads, *blocks)
        return result, None
    return pl.pallas_call(
        functools.partial(project_kernel, n, early, seqs),
        out_shape=(
            total,
            jax.ShapeDtypeStruct((2, tokens, width), activations.dtype),
        ),
        in_specs=[SMEM, HBM, HBM] + [VMEM] * len(early),
        out_specs=(VMEM, VMEM),
        scratch_shapes=[pltpu.SemaphoreType.DMA((2, 2 * seqs))],
        **common,
    )(me, pinned(activations), pinned(out_grads), *blocks)


def add_products(n, late, me_ref, held, blocks, sums):
    source = sources(me_ref[0], n)
    rows = held.shape[2] // n
    for which, t, operand, at in late:
        columns = pl.ds(pl.multiple_of(source[which] * rows, rows), rows)
        block = blocks[operand][at : at + rows, :]
        sums[t] = sums[t] + jnp.dot(held[t, :, columns], block, preferred_element_type=jnp.float32)


def extend_kernel(n, late, me_ref, total_ref, held, *rest):
    blocks, out_ref = rest[:-1], rest[-1]
    sums = [total_ref[0], total_ref[1]]
    add_products(n, late, me_ref, held, blocks, sums)
    out_ref[0] = sums[0]
    out_ref[1] = sums[1]


def extended(me, total, inputs, late, blocks, n):
    return pl.pallas_call(
        functools.partial(extend_kernel, n, late),
        out_shape=jax.ShapeDtypeStruct(total.shape, total.dtype),
        in_specs=[SMEM] + [VMEM] * (2 + len(blocks)),
        out_specs=VMEM,
        compiler_params=pltpu.CompilerParams(vmem_limit_bytes=16 << 20),
        cost_estimate=pl.CostEstimate(flops=total.size, bytes_accessed=total.size, transcendentals=0),
        name="extend",
    )(me, total, inputs, *blocks)


def whiten_kernel(n, seqs, late, me_ref, total_ref, k_ref, *rest):
    operands, (out_ref, white) = rest[:-2], rest[-2:]
    rank = k_ref.shape[1]
    sums = [total_ref[0], total_ref[1]]
    if late:
        held, *blocks = operands
        add_products(n, late, me_ref, held, blocks, sums)
    length = total_ref.shape[1] // seqs
    share = rank // n
    grads = []
    for s in range(seqs):
        token = slice(s * length, (s + 1) * length)
        x_proj = (sums[0][token, :] * k_ref[2][:length, s : s + 1]).astype(jnp.bfloat16)
        d_proj = sums[1][token, :].astype(jnp.bfloat16)
        grads.append(
            lax.dot_general(d_proj, x_proj, (((0,), (0,)), ((), ())), preferred_element_type=jnp.float32)
        )
    left = product(k_ref[1], jnp.concatenate(grads, axis=1))
    left = jnp.concatenate([left[:, s * rank : (s + 1) * rank] for s in range(seqs)], axis=0)
    full = product(left, k_ref[0])
    places = [exchange_order(n).index(d) for d in range(n)]
    for s in range(seqs):
        for d in range(n):
            at = s * rank + d * share
            white[places[d], s * share : (s + 1) * share, :] = full[at : at + share, :]
    out_ref[...] = white[...].astype(jnp.bfloat16)


def whitened_blocks(me, total, k, late, operands, seqs, n):
    rank = k.shape[1]
    shape = (n, seqs * (rank // n), rank)
    return pl.pallas_call(
        functools.partial(whiten_kernel, n, seqs, late),
        out_shape=jax.ShapeDtypeStruct(shape, jnp.bfloat16),
        in_specs=[SMEM] + [VMEM] * (2 + len(operands)),
        out_specs=VMEM,
        scratch_shapes=[pltpu.VMEM(shape, jnp.float32)],
        compiler_params=pltpu.CompilerParams(vmem_limit_bytes=16 << 20),
        cost_estimate=pl.CostEstimate(flops=64 * rank**3, bytes_accessed=4 << 20, transcendentals=0),
        name="whiten",
    )(me, total, k, *operands)


def exchanged(value, n):
    order = [exchange_order(n)]
    return lax.all_to_all(value, "coord", split_axis=0, concat_axis=0, axis_index_groups=order, tiled=True)


def score_kernel(n, me_ref, ids_ref, white_ref, bank_ref, out_ref, spread):
    seqs = ids_ref.shape[0]
    chunk, rank = white_ref.shape[1:]
    share = chunk // seqs
    total = n * seqs
    spread[...] = white_ref[...].astype(jnp.float32).reshape(n * chunk, rank)
    columns = jnp.concatenate(
        [spread[pl.ds(j, total, stride=share), :].astype(jnp.bfloat16) for j in range(share)], axis=1
    )
    queries = bank_ref.shape[0] // n
    row = lax.broadcasted_iota(jnp.int32, (total, out_ref.shape[2] - queries), 0)
    tail = jnp.zeros(row.shape, jnp.float32)
    place = place_of(me_ref[0], n)
    for s in range(seqs):
        tail = jnp.where(row == place * seqs + s, ids_ref[s].astype(jnp.float32), tail)
    partial = lax.dot_general(
        columns, bank_ref[...], (((1,), (1,)), ((), ())), preferred_element_type=jnp.float32
    )
    for d in range(n):
        at = exchange_order(n).index(d)
        out_ref[at, :, :queries] = partial[:, d * queries : (d + 1) * queries].astype(out_ref.dtype)
        out_ref[at, :, queries:] = tail.astype(out_ref.dtype)


def partial_scores(me, seq_ids, white, bank):
    n = white.shape[0]
    seqs = seq_ids.shape[0]
    queries = bank.shape[0] // n
    width = (queries // LANES + 1) * LANES
    return pl.pallas_call(
        functools.partial(score_kernel, n),
        out_shape=jax.ShapeDtypeStruct((n, n * seqs, width), jnp.bfloat16),
        in_specs=[SMEM, SMEM, VMEM, VMEM],
        out_specs=VMEM,
        scratch_shapes=[pltpu.VMEM((n * white.shape[1], white.shape[2]), jnp.float32)],
        compiler_params=pltpu.CompilerParams(vmem_limit_bytes=16 << 20),
        cost_estimate=pl.CostEstimate(
            flops=2 * n * seqs * bank.size, bytes_accessed=2 * bank.size, transcendentals=0
        ),
        name="score",
    )(me, seq_ids, white, bank)


def place_kernel(partial_ref, out_ref):
    rows, queries = out_ref.shape
    total = jnp.sum(partial_ref[...].astype(jnp.float32), axis=0)
    raw = total[:, :queries].astype(jnp.bfloat16)
    ids = total[:, queries : queries + 1].astype(jnp.int32)
    chosen = ids == lax.broadcasted_iota(jnp.int32, (rows, rows), 1)
    out_ref[...] = lax.dot_general(
        chosen.astype(jnp.bfloat16), raw, (((0,), (0,)), ((), ())), preferred_element_type=jnp.float32
    ).astype(jnp.bfloat16)


def place(partials, queries):
    return pl.pallas_call(
        lambda a, b: place_kernel(a, b),
        out_shape=jax.ShapeDtypeStruct((partials.shape[1], queries), jnp.bfloat16),
        in_specs=[VMEM],
        out_specs=VMEM,
        compiler_params=pltpu.CompilerParams(vmem_limit_bytes=16 << 20),
        name="place",
    )(partials)


def body(n, activations, out_grads, proj_in, proj_out, cov_in, cov_out, lengths, seq_ids, bank):
    me = lax.axis_index("coord").reshape(1)
    seqs, length, width = activations.shape
    activations, out_grads = activations.reshape(seqs * length, width), out_grads.reshape(seqs * length, width)
    a, b, c = factors(n)
    paired = a & (a - 1) == 0
    packed = pack(proj_in, proj_out)
    half = first_half(cov_in, cov_out)
    held = {(0, 0, 0): packed}
    for at in range(1, min(a, 3)):
        held[at, 0, 0] = moved(packed, (at, 0, 0), n)
    for by in range(1, b):
        held[0, by, 0] = moved(packed, (0, by, 0), n)
    held, half = lax.optimization_barrier((held, half))
    early = list(held)
    rows = proj_in.shape[0]
    halves = {(at, t): (held[at], t * rows, rows) for at in early for t in range(2)}
    wanted = {}
    for at in range(1, a):
        nearest = at & -at
        source = at - nearest if paired and nearest != at else 0
        for by in range(b):
            for t in range(2):
                if ((at, by, 0), t) in halves:
                    continue
                if source or at > 2:
                    wanted[(at, by, 0), t] = (source, 0, 0), (at - source, by, 0)
                elif at == 1 and t == 0:
                    wanted[(at, by, 0), t] = (0, by, 0), (1, 0, 0)
                else:
                    wanted[(at, by, 0), t] = (at, 0, 0), (0, by, 0)
    arrivals = []
    while wanted:
        steps = {}
        for to, (source, step) in wanted.items():
            if (source, to[1]) in halves:
                steps.setdefault(step, []).append((to, source))
        for step, both in steps.items():
            arrived = moved(merge(joined([halves[source, to[1]] for to, source in both])), step, n)
            arrivals.append((arrived, [to for to, _ in both]))
            for i, (to, _) in enumerate(both):
                halves[to] = arrived, i * rows, rows
                del wanted[to]
    k = second_half(half, lengths)
    order = [(at, by, core) for core in range(c) for by in range(b) for at in range(a)]
    if rows % LANES == 0 and arrivals and c == 2:
        total, inputs = project(
            me, activations, out_grads, [held[at] for at in early], [order.index(at) for at in early], seqs, n
        )
        across = [moved(merge([(held[at], 0, 2 * rows) for at in early]), (0, 0, 1), n)]
        waiting, total, k = lax.optimization_barrier(([arrived for arrived, _ in arrivals], total, k))
        across.append(moved(merge([(arrived, 0, arrived.shape[0]) for arrived in waiting]), (0, 0, 1), n))
        operands = [inputs, across[1]]
        sooner = [
            (order.index(at), t, 1 + i, j * rows)
            for i, (_, group) in enumerate(arrivals)
            for j, (at, t) in enumerate(group)
        ]
        crossed = [[(at, t) for at in early for t in range(2)], [to for _, group in arrivals for to in group]]
        sooner += [(order.index((*at[:2], 1)), t, 0, j * rows) for j, (at, t) in enumerate(crossed[0])]
        late = [(order.index((*at[:2], 1)), t, 0, j * rows) for j, (at, t) in enumerate(crossed[1])]
        total = extended(me, total, inputs, sooner, [across[0], *waiting], n)
    else:
        for at in order:
            if at[2] == 0:
                held[at] = merge(joined([halves[at, 0], halves[at, 1]]))
                for by in range(1, c):
                    held[at[0], at[1], by] = moved(held[at], (0, 0, by), n)
        total = project(me, activations, out_grads, [held[at] for at in order], list(range(n)), seqs, n)[0]
        operands, late = [], []
    white = whitened_blocks(me, total, k, late, operands, seqs, n)
    partials = partial_scores(me, seq_ids, exchanged(white, n), bank)
    return place(exchanged(partials, n), bank.shape[0] // n)


def solution(mesh):
    in_specs = (
        P(("groups", "coord"), None, None),
        P(("groups", "coord"), None, None),
        P("coord", None),
        P("coord", None),
        P(),
        P(),
        P(("groups", "coord")),
        P(("groups", "coord")),
        P(None, "coord"),
    )
    out_specs = P("groups", "coord")
    return jax.shard_map(
        functools.partial(body, mesh.shape["coord"]),
        mesh=mesh,
        in_specs=in_specs,
        out_specs=out_specs,
        check_vma=False,
    )
```

```python
import functools

import jax
import jax.numpy as jnp
from jax import lax
from jax.experimental import pallas as pl
from jax.experimental.pallas import tpu as pltpu
from jax.sharding import PartitionSpec as P

SUB = 8
LANES = 128
EXACT = lax.Precision.HIGHEST
VMEM = pl.BlockSpec(memory_space=pltpu.VMEM)
HBM = pl.BlockSpec(memory_space=pltpu.HBM)
SMEM = pl.BlockSpec(memory_space=pltpu.SMEM)


def factors(n):
    c = 2 if n % 2 == 0 else 1
    rest = n // c
    b = max(f for f in range(1, rest + 1) if rest % f == 0 and f * f <= rest)
    return rest // b, b, c


def partner(at, by, size, towards):
    if size & (size - 1) == 0:
        return at ^ by
    return (at + (by if towards else size - by)) % size


def sources(me, n):
    a, b, c = factors(n)
    ia, ib, ic = me // (b * c), (me // c) % b, me % c
    return [
        (partner(ia, da, a, False) * b + partner(ib, db, b, False)) * c + partner(ic, dc, c, False)
        for dc in range(c)
        for db in range(b)
        for da in range(a)
    ]


def moved(value, by, n):
    sizes = factors(n)
    a, b, c = sizes
    pairs = []
    for me in range(n):
        at = (me // (b * c), (me // c) % b, me % c)
        to = [partner(place, step, size, True) for place, step, size in zip(at, by, sizes)]
        pairs.append((me, (to[0] * b + to[1]) * c + to[2]))
    return lax.ppermute(value, "coord", pairs)


def exchange_order(n):
    a, b, c = factors(n)
    return sorted(range(n), key=lambda device: (1 - device % 2, abs(2 * (device // (b * c)) - (a - 1)), -device))


def place_of(me, n):
    place = 0
    for i, device in enumerate(exchange_order(n)):
        place = jnp.where(me == device, i, place)
    return place


def pack_kernel(first_hbm, second_hbm, out_ref, sems):
    rows = first_hbm.shape[0]
    copies = [
        pltpu.make_async_copy(source, out_ref.at[pl.ds(i * rows, rows)], sems.at[i])
        for i, source in enumerate((first_hbm, second_hbm))
    ]
    for copy in copies:
        copy.start()
    for copy in copies:
        copy.wait()


def pack(first, second):
    rows, columns = first.shape
    return pl.pallas_call(
        pack_kernel,
        out_shape=jax.ShapeDtypeStruct((2 * rows, columns), first.dtype),
        in_specs=[HBM, HBM],
        out_specs=VMEM,
        scratch_shapes=[pltpu.SemaphoreType.DMA((2,))],
        compiler_params=pltpu.CompilerParams(vmem_limit_bytes=8 << 20),
        name="pack",
    )(pinned(first), pinned(second))


def pinned(value):
    return pltpu.with_memory_space_constraint(value, pltpu.HBM)


def gauss_jordan(blocks):
    width = blocks[0].shape[1]
    half = width // 2
    lane = lax.broadcasted_iota(jnp.int32, (SUB, width), 1)
    sub = lax.broadcasted_iota(jnp.int32, (SUB, width), 0)
    start, within = lane // half * half, lane % half

    def column(block, at):
        return jnp.take_along_axis(block, start + at, axis=1, mode="promise_in_bounds")

    for k in range(len(blocks)):
        at = k * SUB
        head = within // SUB == k
        rows = [jnp.broadcast_to(blocks[k][i : i + 1, :], (SUB, width)) for i in range(SUB)]
        diag = {(i, j): column(rows[i], at + j) for i in range(SUB) for j in range(i, SUB)}
        rows = [jnp.where(head, (within == at + i).astype(jnp.float32), rows[i]) for i in range(SUB)]
        inverse, factor = [], {}
        for p in range(SUB):
            inverse.append(1.0 / diag[p, p])
            for i in range(p + 1, SUB):
                factor[p, i] = diag[p, i] * inverse[p]
                for j in range(i, SUB):
                    diag[i, j] = diag[i, j] - factor[p, i] * diag[p, j]
                rows[i] = rows[i] - factor[p, i] * rows[p]
        rows = [rows[p] * inverse[p] for p in range(SUB)]
        for p in reversed(range(SUB)):
            for i in range(p):
                rows[i] = rows[i] - factor[i, p] * rows[p]
        done = rows[0]
        for i in range(1, SUB):
            done = jnp.where(sub == i, rows[i], done)
        out = []
        for g, block in enumerate(blocks):
            if g == k:
                out.append(done)
                continue
            terms = [column(block, at + p) * rows[p] for p in range(SUB)]
            while len(terms) > 1:
                terms = [terms[i] + terms[i + 1] for i in range(0, len(terms), 2)]
            out.append(jnp.where(head, 0.0, block) - terms[0])
        blocks = out
    return blocks


def side_by_side_inverses(first, second):
    half = first.shape[0]
    both = jnp.concatenate([first, second], axis=1)
    blocks = gauss_jordan([both[g : g + SUB, :] for g in range(0, half, SUB)])
    both = jnp.concatenate(blocks, axis=0)
    return both[:, :half], both[:, half:]


def damped(cov):
    size = cov.shape[0]
    cov = 0.5 * (cov + cov.T)
    row = lax.broadcasted_iota(jnp.int32, (size, size), 0)
    col = lax.broadcasted_iota(jnp.int32, (size, size), 1)
    damping = 0.1 * jnp.sum(jnp.where(row == col, cov, 0.0)) / size
    return jnp.where(row == col, cov + damping, cov)


def product(left, right, dims=((1,), (0,))):
    return lax.dot_general(left, right, (dims, ((), ())), precision=EXACT, preferred_element_type=jnp.float32)


def first_half_kernel(cov_in_hbm, cov_out_hbm, out_ref, cov_ref, sems):
    copies = [
        pltpu.make_async_copy(source, cov_ref.at[i], sems.at[i]) for i, source in enumerate((cov_in_hbm, cov_out_hbm))
    ]
    for copy in copies:
        copy.start()
    for copy in copies:
        copy.wait()
    half = cov_ref.shape[1] // 2
    covs = [damped(cov_ref[0]), damped(cov_ref[1])]
    corner = [cov[:half, half:] for cov in covs]
    upper = side_by_side_inverses(*[cov[:half, :half] for cov in covs])
    solved = [product(u, c) for u, c in zip(upper, corner)]
    schur = [cov[half:, half:] - product(c, t, ((0,), (0,))) for cov, c, t in zip(covs, corner, solved)]
    for i, pair in enumerate((upper, solved, schur)):
        out_ref[i] = jnp.concatenate(pair, axis=1)


def second_half_kernel(first_ref, len_hbm, k_ref, len_ref, sem):
    copy = pltpu.make_async_copy(len_hbm, len_ref, sem)
    copy.start()
    size = k_ref.shape[1]
    half = size // 2
    upper, solved, schur = [(first_ref[i][:, :half], first_ref[i][:, half:]) for i in range(3)]
    lower = side_by_side_inverses(*schur)
    for m, (u, t, low) in enumerate(zip(upper, solved, lower)):
        side = product(t, low)
        k_ref[m, :half, :half] = u + product(side, t, ((1,), (1,)))
        k_ref[m, :half, half:] = -side
        k_ref[m, half:, :half] = -side.T
        k_ref[m, half:, half:] = low
    copy.wait()
    token = lax.broadcasted_iota(jnp.int32, (size, size), 0)
    lane = lax.broadcasted_iota(jnp.int32, (size, size), 1)
    mask = jnp.zeros((size, size), jnp.float32)
    for s in range(len_ref.shape[0]):
        mask = jnp.where((lane == s) & (token < len_ref[s]), 1.0, mask)
    k_ref[2] = mask


def first_half(cov_in, cov_out):
    size = cov_in.shape[0]
    return pl.pallas_call(
        first_half_kernel,
        out_shape=jax.ShapeDtypeStruct((3, size // 2, size), jnp.float32),
        in_specs=[HBM, HBM],
        out_specs=VMEM,
        scratch_shapes=[pltpu.VMEM((2, size, size), jnp.float32), pltpu.SemaphoreType.DMA((2,))],
        compiler_params=pltpu.CompilerParams(vmem_limit_bytes=8 << 20),
        cost_estimate=pl.CostEstimate(flops=size, bytes_accessed=size, transcendentals=0),
        name="first_half",
    )(pinned(cov_in), pinned(cov_out))


def second_half(first, lengths):
    size = first.shape[2]
    return pl.pallas_call(
        second_half_kernel,
        out_shape=jax.ShapeDtypeStruct((3, size, size), jnp.float32),
        in_specs=[VMEM, HBM],
        out_specs=VMEM,
        scratch_shapes=[pltpu.SMEM(lengths.shape, jnp.int32), pltpu.SemaphoreType.DMA],
        compiler_params=pltpu.CompilerParams(vmem_limit_bytes=8 << 20),
        cost_estimate=pl.CostEstimate(flops=size, bytes_accessed=size, transcendentals=0),
        name="second_half",
    )(first, pinned(lengths))


def merge_kernel(spans, *refs):
    at = 0
    for ref, (start, rows) in zip(refs[:-1], spans):
        refs[-1][at : at + rows, :] = ref[start : start + rows, :]
        at += rows


def merge(parts):
    array, start, rows = parts[0]
    if len(parts) == 1 and rows == array.shape[0]:
        return array
    total = sum(part[2] for part in parts)
    return pl.pallas_call(
        functools.partial(merge_kernel, [part[1:] for part in parts]),
        out_shape=jax.ShapeDtypeStruct((total, array.shape[1]), array.dtype),
        in_specs=[VMEM] * len(parts),
        out_specs=VMEM,
        compiler_params=pltpu.CompilerParams(vmem_limit_bytes=16 << 20),
        cost_estimate=pl.CostEstimate(flops=total, bytes_accessed=total, transcendentals=0),
        name="merge",
    )(*(part[0] for part in parts))


def joined(parts):
    out = []
    for array, start, rows in parts:
        if out and out[-1][0] is array and out[-1][1] + out[-1][2] == start:
            out[-1] = (array, out[-1][1], out[-1][2] + rows)
        else:
            out.append((array, start, rows))
    return out


def project_kernel(n, early, seqs, me_ref, *rest):
    inputs, blocks, (total_ref, held, sems) = rest[:2], rest[2 : 2 + len(early)], rest[2 + len(early) :]
    tokens = held.shape[1]
    part = tokens // sems.shape[1]
    copies = [
        [
            pltpu.make_async_copy(source.at[pl.ds(i * part, part)], held.at[t, pl.ds(i * part, part)], sems.at[t, i])
            for i in range(sems.shape[1])
        ]
        for t, source in enumerate(inputs)
    ]
    for copy in copies[0] + copies[1]:
        copy.start()
    rows = blocks[0].shape[0] // 2
    source = sources(me_ref[0], n)
    for t in range(2):
        for copy in copies[t]:
            copy.wait()
        total = None
        for which, block in zip(early, blocks):
            columns = pl.ds(pl.multiple_of(source[which] * rows, rows), rows)
            term = jnp.dot(
                held[t, :, columns], block[t * rows : (t + 1) * rows, :], preferred_element_type=jnp.float32
            )
            total = term if total is None else total + term
        total_ref[t] = total


def project_whole_kernel(n, me_ref, act_ref, grad_ref, *rest):
    blocks, (total_ref, proj) = rest[:n], rest[n:]
    rows = blocks[0].shape[0] // 2
    for block, source in zip(blocks, sources(me_ref[0], n)):
        at = pl.ds(pl.multiple_of(source * rows, rows), rows)
        for t in range(2):
            proj[t, at, :] = block[t * rows : (t + 1) * rows, :]
    for t, ref in enumerate((act_ref, grad_ref)):
        total_ref[t] = jnp.dot(ref[...], proj[t], preferred_element_type=jnp.float32)


def project(me, activations, out_grads, blocks, early, seqs, n):
    tokens, width = activations.shape
    rank = blocks[0].shape[1]
    total = jax.ShapeDtypeStruct((2, tokens, rank), jnp.float32)
    common = dict(
        compiler_params=pltpu.CompilerParams(vmem_limit_bytes=16 << 20),
        cost_estimate=pl.CostEstimate(flops=rank, bytes_accessed=rank, transcendentals=0),
        name="project",
    )
    if len(early) == n:
        result = pl.pallas_call(
            functools.partial(project_whole_kernel, n),
            out_shape=total,
            in_specs=[SMEM] + [VMEM] * (2 + n),
            out_specs=VMEM,
            scratch_shapes=[pltpu.VMEM((2, width, rank), jnp.bfloat16)],
            **common,
        )(me, activations, out_grads, *blocks)
        return result, None
    return pl.pallas_call(
        functools.partial(project_kernel, n, early, seqs),
        out_shape=(
            total,
            jax.ShapeDtypeStruct((2, tokens, width), activations.dtype),
        ),
        in_specs=[SMEM, HBM, HBM] + [VMEM] * len(early),
        out_specs=(VMEM, VMEM),
        scratch_shapes=[pltpu.SemaphoreType.DMA((2, 2 * seqs))],
        **common,
    )(me, pinned(activations), pinned(out_grads), *blocks)


def add_products(n, late, me_ref, held, blocks, sums):
    source = sources(me_ref[0], n)
    rows = held.shape[2] // n
    for which, t, operand, at in late:
        columns = pl.ds(pl.multiple_of(source[which] * rows, rows), rows)
        block = blocks[operand][at : at + rows, :]
        sums[t] = sums[t] + jnp.dot(held[t, :, columns], block, preferred_element_type=jnp.float32)


def extend_kernel(n, late, me_ref, total_ref, held, *rest):
    blocks, out_ref = rest[:-1], rest[-1]
    sums = [total_ref[0], total_ref[1]]
    add_products(n, late, me_ref, held, blocks, sums)
    out_ref[0] = sums[0]
    out_ref[1] = sums[1]


def extended(me, total, inputs, late, blocks, n):
    return pl.pallas_call(
        functools.partial(extend_kernel, n, late),
        out_shape=jax.ShapeDtypeStruct(total.shape, total.dtype),
        in_specs=[SMEM] + [VMEM] * (2 + len(blocks)),
        out_specs=VMEM,
        compiler_params=pltpu.CompilerParams(vmem_limit_bytes=16 << 20),
        cost_estimate=pl.CostEstimate(flops=total.size, bytes_accessed=total.size, transcendentals=0),
        name="extend",
    )(me, total, inputs, *blocks)


def whiten_kernel(n, seqs, late, me_ref, total_ref, k_ref, *rest):
    operands, (out_ref, white) = rest[:-2], rest[-2:]
    rank = k_ref.shape[1]
    sums = [total_ref[0], total_ref[1]]
    if late:
        held, *blocks = operands
        add_products(n, late, me_ref, held, blocks, sums)
    length = total_ref.shape[1] // seqs
    share = rank // n
    grads = []
    for s in range(seqs):
        token = slice(s * length, (s + 1) * length)
        x_proj = (sums[0][token, :] * k_ref[2][:length, s : s + 1]).astype(jnp.bfloat16)
        d_proj = sums[1][token, :].astype(jnp.bfloat16)
        grads.append(
            lax.dot_general(d_proj, x_proj, (((0,), (0,)), ((), ())), preferred_element_type=jnp.float32)
        )
    left = product(k_ref[1], jnp.concatenate(grads, axis=1))
    left = jnp.concatenate([left[:, s * rank : (s + 1) * rank] for s in range(seqs)], axis=0)
    full = product(left, k_ref[0])
    places = [exchange_order(n).index(d) for d in range(n)]
    for s in range(seqs):
        for d in range(n):
            at = s * rank + d * share
            white[places[d], s * share : (s + 1) * share, :] = full[at : at + share, :]
    out_ref[...] = white[...].astype(jnp.bfloat16)


def whitened_blocks(me, total, k, late, operands, seqs, n):
    rank = k.shape[1]
    shape = (n, seqs * (rank // n), rank)
    return pl.pallas_call(
        functools.partial(whiten_kernel, n, seqs, late),
        out_shape=jax.ShapeDtypeStruct(shape, jnp.bfloat16),
        in_specs=[SMEM] + [VMEM] * (2 + len(operands)),
        out_specs=VMEM,
        scratch_shapes=[pltpu.VMEM(shape, jnp.float32)],
        compiler_params=pltpu.CompilerParams(vmem_limit_bytes=16 << 20),
        cost_estimate=pl.CostEstimate(flops=64 * rank**3, bytes_accessed=4 << 20, transcendentals=0),
        name="whiten",
    )(me, total, k, *operands)


def exchanged(value, n):
    order = [exchange_order(n)]
    return lax.all_to_all(value, "coord", split_axis=0, concat_axis=0, axis_index_groups=order, tiled=True)


def score_kernel(n, me_ref, ids_ref, white_ref, bank_ref, out_ref, spread):
    seqs = ids_ref.shape[0]
    chunk, rank = white_ref.shape[1:]
    share = chunk // seqs
    total = n * seqs
    spread[...] = white_ref[...].astype(jnp.float32).reshape(n * chunk, rank)
    columns = jnp.concatenate(
        [spread[pl.ds(j, total, stride=share), :].astype(jnp.bfloat16) for j in range(share)], axis=1
    )
    queries = bank_ref.shape[0] // n
    row = lax.broadcasted_iota(jnp.int32, (total, out_ref.shape[2] - queries), 0)
    tail = jnp.zeros(row.shape, jnp.float32)
    place = place_of(me_ref[0], n)
    for s in range(seqs):
        tail = jnp.where(row == place * seqs + s, ids_ref[s].astype(jnp.float32), tail)
    partial = lax.dot_general(
        columns, bank_ref[...], (((1,), (1,)), ((), ())), preferred_element_type=jnp.float32
    )
    for d in range(n):
        at = exchange_order(n).index(d)
        out_ref[at, :, :queries] = partial[:, d * queries : (d + 1) * queries].astype(out_ref.dtype)
        out_ref[at, :, queries:] = tail.astype(out_ref.dtype)


def partial_scores(me, seq_ids, white, bank):
    n = white.shape[0]
    seqs = seq_ids.shape[0]
    queries = bank.shape[0] // n
    width = (queries // LANES + 1) * LANES
    return pl.pallas_call(
        functools.partial(score_kernel, n),
        out_shape=jax.ShapeDtypeStruct((n, n * seqs, width), jnp.bfloat16),
        in_specs=[SMEM, SMEM, VMEM, VMEM],
        out_specs=VMEM,
        scratch_shapes=[pltpu.VMEM((n * white.shape[1], white.shape[2]), jnp.float32)],
        compiler_params=pltpu.CompilerParams(vmem_limit_bytes=16 << 20),
        cost_estimate=pl.CostEstimate(
            flops=2 * n * seqs * bank.size, bytes_accessed=2 * bank.size, transcendentals=0
        ),
        name="score",
    )(me, seq_ids, white, bank)


def place_kernel(partial_ref, out_ref):
    rows, queries = out_ref.shape
    total = jnp.sum(partial_ref[...].astype(jnp.float32), axis=0)
    raw = total[:, :queries].astype(jnp.bfloat16)
    ids = total[:, queries : queries + 1].astype(jnp.int32)
    chosen = ids == lax.broadcasted_iota(jnp.int32, (rows, rows), 1)
    out_ref[...] = lax.dot_general(
        chosen.astype(jnp.bfloat16), raw, (((0,), (0,)), ((), ())), preferred_element_type=jnp.float32
    ).astype(jnp.bfloat16)


def place(partials, queries):
    return pl.pallas_call(
        lambda a, b: place_kernel(a, b),
        out_shape=jax.ShapeDtypeStruct((partials.shape[1], queries), jnp.bfloat16),
        in_specs=[VMEM],
        out_specs=VMEM,
        compiler_params=pltpu.CompilerParams(vmem_limit_bytes=16 << 20),
        name="place",
    )(partials)


def body(n, activations, out_grads, proj_in, proj_out, cov_in, cov_out, lengths, seq_ids, bank):
    me = lax.axis_index("coord").reshape(1)
    seqs, length, width = activations.shape
    activations, out_grads = activations.reshape(seqs * length, width), out_grads.reshape(seqs * length, width)
    a, b, c = factors(n)
    paired = a & (a - 1) == 0
    packed = pack(proj_in, proj_out)
    half = first_half(cov_in, cov_out)
    held = {(0, 0, 0): packed}
    for at in range(1, min(a, 3)):
        held[at, 0, 0] = moved(packed, (at, 0, 0), n)
    for by in range(1, b):
        held[0, by, 0] = moved(packed, (0, by, 0), n)
    held, half = lax.optimization_barrier((held, half))
    early = list(held)
    rows = proj_in.shape[0]
    halves = {(at, t): (held[at], t * rows, rows) for at in early for t in range(2)}
    wanted = {}
    for at in range(1, a):
        nearest = at & -at
        source = at - nearest if paired and nearest != at else 0
        for by in range(b):
            for t in range(2):
                if ((at, by, 0), t) in halves:
                    continue
                if source or at > 2:
                    wanted[(at, by, 0), t] = (source, 0, 0), (at - source, by, 0)
                elif at == 1:
                    wanted[(at, by, 0), t] = (0, 0, 0), (1, by, 0)
                else:
                    wanted[(at, by, 0), t] = (at, 0, 0), (0, by, 0)
    arrivals = []
    while wanted:
        steps = {}
        for to, (source, step) in wanted.items():
            if (source, to[1]) in halves:
                steps.setdefault(step, []).append((to, source))
        for step, both in steps.items():
            arrived = moved(merge(joined([halves[source, to[1]] for to, source in both])), step, n)
            arrivals.append((arrived, [to for to, _ in both]))
            for i, (to, _) in enumerate(both):
                halves[to] = arrived, i * rows, rows
                del wanted[to]
    k = second_half(half, lengths)
    order = [(at, by, core) for core in range(c) for by in range(b) for at in range(a)]
    if rows % LANES == 0 and arrivals and c == 2:
        total, inputs = project(
            me, activations, out_grads, [held[at] for at in early], [order.index(at) for at in early], seqs, n
        )
        across = [moved(merge([(held[at], 0, 2 * rows) for at in early]), (0, 0, 1), n)]
        waiting, total, k = lax.optimization_barrier(([arrived for arrived, _ in arrivals], total, k))
        across.append(moved(merge([(arrived, 0, arrived.shape[0]) for arrived in waiting]), (0, 0, 1), n))
        operands = [inputs, across[1]]
        sooner = [
            (order.index(at), t, 1 + i, j * rows)
            for i, (_, group) in enumerate(arrivals)
            for j, (at, t) in enumerate(group)
        ]
        crossed = [[(at, t) for at in early for t in range(2)], [to for _, group in arrivals for to in group]]
        sooner += [(order.index((*at[:2], 1)), t, 0, j * rows) for j, (at, t) in enumerate(crossed[0])]
        late = [(order.index((*at[:2], 1)), t, 0, j * rows) for j, (at, t) in enumerate(crossed[1])]
        total = extended(me, total, inputs, sooner, [across[0], *waiting], n)
    else:
        for at in order:
            if at[2] == 0:
                held[at] = merge(joined([halves[at, 0], halves[at, 1]]))
                for by in range(1, c):
                    held[at[0], at[1], by] = moved(held[at], (0, 0, by), n)
        total = project(me, activations, out_grads, [held[at] for at in order], list(range(n)), seqs, n)[0]
        operands, late = [], []
    white = whitened_blocks(me, total, k, late, operands, seqs, n)
    partials = partial_scores(me, seq_ids, exchanged(white, n), bank)
    return place(exchanged(partials, n), bank.shape[0] // n)


def solution(mesh):
    in_specs = (
        P(("groups", "coord"), None, None),
        P(("groups", "coord"), None, None),
        P("coord", None),
        P("coord", None),
        P(),
        P(),
        P(("groups", "coord")),
        P(("groups", "coord")),
        P(None, "coord"),
    )
    out_specs = P("groups", "coord")
    return jax.shard_map(
        functools.partial(body, mesh.shape["coord"]),
        mesh=mesh,
        in_specs=in_specs,
        out_specs=out_specs,
        check_vma=False,
    )
```

```python
import functools

import jax
import jax.numpy as jnp
from jax import lax
from jax.experimental import pallas as pl
from jax.experimental.pallas import tpu as pltpu
from jax.sharding import PartitionSpec as P

SUB = 8
LANES = 128
EXACT = lax.Precision.HIGHEST
VMEM = pl.BlockSpec(memory_space=pltpu.VMEM)
HBM = pl.BlockSpec(memory_space=pltpu.HBM)
SMEM = pl.BlockSpec(memory_space=pltpu.SMEM)


def factors(n):
    c = 2 if n % 2 == 0 else 1
    rest = n // c
    b = max(f for f in range(1, rest + 1) if rest % f == 0 and f * f <= rest)
    return rest // b, b, c


def partner(at, by, size, towards):
    if size & (size - 1) == 0:
        return at ^ by
    return (at + (by if towards else size - by)) % size


def sources(me, n):
    a, b, c = factors(n)
    ia, ib, ic = me // (b * c), (me // c) % b, me % c
    return [
        (partner(ia, da, a, False) * b + partner(ib, db, b, False)) * c + partner(ic, dc, c, False)
        for dc in range(c)
        for db in range(b)
        for da in range(a)
    ]


def moved(value, by, n):
    sizes = factors(n)
    a, b, c = sizes
    pairs = []
    for me in range(n):
        at = (me // (b * c), (me // c) % b, me % c)
        to = [partner(place, step, size, True) for place, step, size in zip(at, by, sizes)]
        pairs.append((me, (to[0] * b + to[1]) * c + to[2]))
    return lax.ppermute(value, "coord", pairs)


def exchange_order(n):
    a, b, c = factors(n)
    return sorted(range(n), key=lambda device: (abs(2 * (device // (b * c)) - (a - 1)), 1 - device % 2, -device))


def place_of(me, n):
    place = 0
    for i, device in enumerate(exchange_order(n)):
        place = jnp.where(me == device, i, place)
    return place


def pack_kernel(first_hbm, second_hbm, out_ref, sems):
    rows = first_hbm.shape[0]
    copies = [
        pltpu.make_async_copy(source, out_ref.at[pl.ds(i * rows, rows)], sems.at[i])
        for i, source in enumerate((first_hbm, second_hbm))
    ]
    for copy in copies:
        copy.start()
    for copy in copies:
        copy.wait()


def pack(first, second):
    rows, columns = first.shape
    return pl.pallas_call(
        pack_kernel,
        out_shape=jax.ShapeDtypeStruct((2 * rows, columns), first.dtype),
        in_specs=[HBM, HBM],
        out_specs=VMEM,
        scratch_shapes=[pltpu.SemaphoreType.DMA((2,))],
        compiler_params=pltpu.CompilerParams(vmem_limit_bytes=8 << 20),
        name="pack",
    )(pinned(first), pinned(second))


def pinned(value):
    return pltpu.with_memory_space_constraint(value, pltpu.HBM)


def gauss_jordan(blocks):
    width = blocks[0].shape[1]
    half = width // 2
    lane = lax.broadcasted_iota(jnp.int32, (SUB, width), 1)
    sub = lax.broadcasted_iota(jnp.int32, (SUB, width), 0)
    start, within = lane // half * half, lane % half

    def column(block, at):
        return jnp.take_along_axis(block, start + at, axis=1, mode="promise_in_bounds")

    for k in range(len(blocks)):
        at = k * SUB
        head = within // SUB == k
        rows = [jnp.broadcast_to(blocks[k][i : i + 1, :], (SUB, width)) for i in range(SUB)]
        diag = {(i, j): column(rows[i], at + j) for i in range(SUB) for j in range(i, SUB)}
        rows = [jnp.where(head, (within == at + i).astype(jnp.float32), rows[i]) for i in range(SUB)]
        inverse, factor = [], {}
        for p in range(SUB):
            inverse.append(1.0 / diag[p, p])
            for i in range(p + 1, SUB):
                factor[p, i] = diag[p, i] * inverse[p]
                for j in range(i, SUB):
                    diag[i, j] = diag[i, j] - factor[p, i] * diag[p, j]
                rows[i] = rows[i] - factor[p, i] * rows[p]
        rows = [rows[p] * inverse[p] for p in range(SUB)]
        for p in reversed(range(SUB)):
            for i in range(p):
                rows[i] = rows[i] - factor[i, p] * rows[p]
        done = rows[0]
        for i in range(1, SUB):
            done = jnp.where(sub == i, rows[i], done)
        out = []
        for g, block in enumerate(blocks):
            if g == k:
                out.append(done)
                continue
            terms = [column(block, at + p) * rows[p] for p in range(SUB)]
            while len(terms) > 1:
                terms = [terms[i] + terms[i + 1] for i in range(0, len(terms), 2)]
            out.append(jnp.where(head, 0.0, block) - terms[0])
        blocks = out
    return blocks


def side_by_side_inverses(first, second):
    half = first.shape[0]
    both = jnp.concatenate([first, second], axis=1)
    blocks = gauss_jordan([both[g : g + SUB, :] for g in range(0, half, SUB)])
    both = jnp.concatenate(blocks, axis=0)
    return both[:, :half], both[:, half:]


def damped(cov):
    size = cov.shape[0]
    cov = 0.5 * (cov + cov.T)
    row = lax.broadcasted_iota(jnp.int32, (size, size), 0)
    col = lax.broadcasted_iota(jnp.int32, (size, size), 1)
    damping = 0.1 * jnp.sum(jnp.where(row == col, cov, 0.0)) / size
    return jnp.where(row == col, cov + damping, cov)


def product(left, right, dims=((1,), (0,))):
    return lax.dot_general(left, right, (dims, ((), ())), precision=EXACT, preferred_element_type=jnp.float32)


def first_half_kernel(cov_in_hbm, cov_out_hbm, out_ref, cov_ref, sems):
    copies = [
        pltpu.make_async_copy(source, cov_ref.at[i], sems.at[i]) for i, source in enumerate((cov_in_hbm, cov_out_hbm))
    ]
    for copy in copies:
        copy.start()
    for copy in copies:
        copy.wait()
    half = cov_ref.shape[1] // 2
    covs = [damped(cov_ref[0]), damped(cov_ref[1])]
    corner = [cov[:half, half:] for cov in covs]
    upper = side_by_side_inverses(*[cov[:half, :half] for cov in covs])
    solved = [product(u, c) for u, c in zip(upper, corner)]
    schur = [cov[half:, half:] - product(c, t, ((0,), (0,))) for cov, c, t in zip(covs, corner, solved)]
    for i, pair in enumerate((upper, solved, schur)):
        out_ref[i] = jnp.concatenate(pair, axis=1)


def second_half_kernel(first_ref, len_hbm, k_ref, len_ref, sem):
    copy = pltpu.make_async_copy(len_hbm, len_ref, sem)
    copy.start()
    size = k_ref.shape[1]
    half = size // 2
    upper, solved, schur = [(first_ref[i][:, :half], first_ref[i][:, half:]) for i in range(3)]
    lower = side_by_side_inverses(*schur)
    for m, (u, t, low) in enumerate(zip(upper, solved, lower)):
        side = product(t, low)
        k_ref[m, :half, :half] = u + product(side, t, ((1,), (1,)))
        k_ref[m, :half, half:] = -side
        k_ref[m, half:, :half] = -side.T
        k_ref[m, half:, half:] = low
    copy.wait()
    token = lax.broadcasted_iota(jnp.int32, (size, size), 0)
    lane = lax.broadcasted_iota(jnp.int32, (size, size), 1)
    mask = jnp.zeros((size, size), jnp.float32)
    for s in range(len_ref.shape[0]):
        mask = jnp.where((lane == s) & (token < len_ref[s]), 1.0, mask)
    k_ref[2] = mask


def first_half(cov_in, cov_out):
    size = cov_in.shape[0]
    return pl.pallas_call(
        first_half_kernel,
        out_shape=jax.ShapeDtypeStruct((3, size // 2, size), jnp.float32),
        in_specs=[HBM, HBM],
        out_specs=VMEM,
        scratch_shapes=[pltpu.VMEM((2, size, size), jnp.float32), pltpu.SemaphoreType.DMA((2,))],
        compiler_params=pltpu.CompilerParams(vmem_limit_bytes=8 << 20),
        cost_estimate=pl.CostEstimate(flops=size, bytes_accessed=size, transcendentals=0),
        name="first_half",
    )(pinned(cov_in), pinned(cov_out))


def second_half(first, lengths):
    size = first.shape[2]
    return pl.pallas_call(
        second_half_kernel,
        out_shape=jax.ShapeDtypeStruct((3, size, size), jnp.float32),
        in_specs=[VMEM, HBM],
        out_specs=VMEM,
        scratch_shapes=[pltpu.SMEM(lengths.shape, jnp.int32), pltpu.SemaphoreType.DMA],
        compiler_params=pltpu.CompilerParams(vmem_limit_bytes=8 << 20),
        cost_estimate=pl.CostEstimate(flops=size, bytes_accessed=size, transcendentals=0),
        name="second_half",
    )(first, pinned(lengths))


def merge_kernel(spans, *refs):
    at = 0
    for ref, (start, rows) in zip(refs[:-1], spans):
        refs[-1][at : at + rows, :] = ref[start : start + rows, :]
        at += rows


def merge(parts):
    array, start, rows = parts[0]
    if len(parts) == 1 and rows == array.shape[0]:
        return array
    total = sum(part[2] for part in parts)
    return pl.pallas_call(
        functools.partial(merge_kernel, [part[1:] for part in parts]),
        out_shape=jax.ShapeDtypeStruct((total, array.shape[1]), array.dtype),
        in_specs=[VMEM] * len(parts),
        out_specs=VMEM,
        compiler_params=pltpu.CompilerParams(vmem_limit_bytes=16 << 20),
        cost_estimate=pl.CostEstimate(flops=total, bytes_accessed=total, transcendentals=0),
        name="merge",
    )(*(part[0] for part in parts))


def joined(parts):
    out = []
    for array, start, rows in parts:
        if out and out[-1][0] is array and out[-1][1] + out[-1][2] == start:
            out[-1] = (array, out[-1][1], out[-1][2] + rows)
        else:
            out.append((array, start, rows))
    return out


def project_kernel(n, early, seqs, me_ref, *rest):
    inputs, blocks, (total_ref, held, sems) = rest[:2], rest[2 : 2 + len(early)], rest[2 + len(early) :]
    tokens = held.shape[1]
    part = tokens // sems.shape[1]
    copies = [
        [
            pltpu.make_async_copy(source.at[pl.ds(i * part, part)], held.at[t, pl.ds(i * part, part)], sems.at[t, i])
            for i in range(sems.shape[1])
        ]
        for t, source in enumerate(inputs)
    ]
    for copy in copies[0] + copies[1]:
        copy.start()
    rows = blocks[0].shape[0] // 2
    source = sources(me_ref[0], n)
    for t in range(2):
        for copy in copies[t]:
            copy.wait()
        total = None
        for which, block in zip(early, blocks):
            columns = pl.ds(pl.multiple_of(source[which] * rows, rows), rows)
            term = jnp.dot(
                held[t, :, columns], block[t * rows : (t + 1) * rows, :], preferred_element_type=jnp.float32
            )
            total = term if total is None else total + term
        total_ref[t] = total


def project_whole_kernel(n, me_ref, act_ref, grad_ref, *rest):
    blocks, (total_ref, proj) = rest[:n], rest[n:]
    rows = blocks[0].shape[0] // 2
    for block, source in zip(blocks, sources(me_ref[0], n)):
        at = pl.ds(pl.multiple_of(source * rows, rows), rows)
        for t in range(2):
            proj[t, at, :] = block[t * rows : (t + 1) * rows, :]
    for t, ref in enumerate((act_ref, grad_ref)):
        total_ref[t] = jnp.dot(ref[...], proj[t], preferred_element_type=jnp.float32)


def project(me, activations, out_grads, blocks, early, seqs, n):
    tokens, width = activations.shape
    rank = blocks[0].shape[1]
    total = jax.ShapeDtypeStruct((2, tokens, rank), jnp.float32)
    common = dict(
        compiler_params=pltpu.CompilerParams(vmem_limit_bytes=16 << 20),
        cost_estimate=pl.CostEstimate(flops=rank, bytes_accessed=rank, transcendentals=0),
        name="project",
    )
    if len(early) == n:
        result = pl.pallas_call(
            functools.partial(project_whole_kernel, n),
            out_shape=total,
            in_specs=[SMEM] + [VMEM] * (2 + n),
            out_specs=VMEM,
            scratch_shapes=[pltpu.VMEM((2, width, rank), jnp.bfloat16)],
            **common,
        )(me, activations, out_grads, *blocks)
        return result, None
    return pl.pallas_call(
        functools.partial(project_kernel, n, early, seqs),
        out_shape=(
            total,
            jax.ShapeDtypeStruct((2, tokens, width), activations.dtype),
        ),
        in_specs=[SMEM, HBM, HBM] + [VMEM] * len(early),
        out_specs=(VMEM, VMEM),
        scratch_shapes=[pltpu.SemaphoreType.DMA((2, 2 * seqs))],
        **common,
    )(me, pinned(activations), pinned(out_grads), *blocks)


def add_products(n, late, me_ref, held, blocks, sums):
    source = sources(me_ref[0], n)
    rows = held.shape[2] // n
    for which, t, operand, at in late:
        columns = pl.ds(pl.multiple_of(source[which] * rows, rows), rows)
        block = blocks[operand][at : at + rows, :]
        sums[t] = sums[t] + jnp.dot(held[t, :, columns], block, preferred_element_type=jnp.float32)


def extend_kernel(n, late, me_ref, total_ref, held, *rest):
    blocks, out_ref = rest[:-1], rest[-1]
    sums = [total_ref[0], total_ref[1]]
    add_products(n, late, me_ref, held, blocks, sums)
    out_ref[0] = sums[0]
    out_ref[1] = sums[1]


def extended(me, total, inputs, late, blocks, n):
    return pl.pallas_call(
        functools.partial(extend_kernel, n, late),
        out_shape=jax.ShapeDtypeStruct(total.shape, total.dtype),
        in_specs=[SMEM] + [VMEM] * (2 + len(blocks)),
        out_specs=VMEM,
        compiler_params=pltpu.CompilerParams(vmem_limit_bytes=16 << 20),
        cost_estimate=pl.CostEstimate(flops=total.size, bytes_accessed=total.size, transcendentals=0),
        name="extend",
    )(me, total, inputs, *blocks)


def whiten_kernel(n, seqs, late, me_ref, total_ref, k_ref, *rest):
    operands, (out_ref, white) = rest[:-2], rest[-2:]
    rank = k_ref.shape[1]
    sums = [total_ref[0], total_ref[1]]
    if late:
        held, *blocks = operands
        add_products(n, late, me_ref, held, blocks, sums)
    length = total_ref.shape[1] // seqs
    share = rank // n
    grads = []
    for s in range(seqs):
        token = slice(s * length, (s + 1) * length)
        x_proj = (sums[0][token, :] * k_ref[2][:length, s : s + 1]).astype(jnp.bfloat16)
        d_proj = sums[1][token, :].astype(jnp.bfloat16)
        grads.append(
            lax.dot_general(d_proj, x_proj, (((0,), (0,)), ((), ())), preferred_element_type=jnp.float32)
        )
    left = product(k_ref[1], jnp.concatenate(grads, axis=1))
    left = jnp.concatenate([left[:, s * rank : (s + 1) * rank] for s in range(seqs)], axis=0)
    full = product(left, k_ref[0])
    places = [exchange_order(n).index(d) for d in range(n)]
    for s in range(seqs):
        for d in range(n):
            at = s * rank + d * share
            white[places[d], s * share : (s + 1) * share, :] = full[at : at + share, :]
    out_ref[...] = white[...].astype(jnp.bfloat16)


def whitened_blocks(me, total, k, late, operands, seqs, n):
    rank = k.shape[1]
    shape = (n, seqs * (rank // n), rank)
    return pl.pallas_call(
        functools.partial(whiten_kernel, n, seqs, late),
        out_shape=jax.ShapeDtypeStruct(shape, jnp.bfloat16),
        in_specs=[SMEM] + [VMEM] * (2 + len(operands)),
        out_specs=VMEM,
        scratch_shapes=[pltpu.VMEM(shape, jnp.float32)],
        compiler_params=pltpu.CompilerParams(vmem_limit_bytes=16 << 20),
        cost_estimate=pl.CostEstimate(flops=64 * rank**3, bytes_accessed=4 << 20, transcendentals=0),
        name="whiten",
    )(me, total, k, *operands)


def exchanged(value, n):
    order = [exchange_order(n)]
    return lax.all_to_all(value, "coord", split_axis=0, concat_axis=0, axis_index_groups=order, tiled=True)


def score_kernel(n, me_ref, ids_ref, white_ref, bank_ref, out_ref, spread):
    seqs = ids_ref.shape[0]
    chunk, rank = white_ref.shape[1:]
    share = chunk // seqs
    total = n * seqs
    spread[...] = white_ref[...].astype(jnp.float32).reshape(n * chunk, rank)
    columns = jnp.concatenate(
        [spread[pl.ds(j, total, stride=share), :].astype(jnp.bfloat16) for j in range(share)], axis=1
    )
    queries = bank_ref.shape[0] // n
    row = lax.broadcasted_iota(jnp.int32, (total, out_ref.shape[2] - queries), 0)
    tail = jnp.zeros(row.shape, jnp.float32)
    place = place_of(me_ref[0], n)
    for s in range(seqs):
        tail = jnp.where(row == place * seqs + s, ids_ref[s].astype(jnp.float32), tail)
    partial = lax.dot_general(
        columns, bank_ref[...], (((1,), (1,)), ((), ())), preferred_element_type=jnp.float32
    )
    for d in range(n):
        at = exchange_order(n).index(d)
        out_ref[at, :, :queries] = partial[:, d * queries : (d + 1) * queries].astype(out_ref.dtype)
        out_ref[at, :, queries:] = tail.astype(out_ref.dtype)


def partial_scores(me, seq_ids, white, bank):
    n = white.shape[0]
    seqs = seq_ids.shape[0]
    queries = bank.shape[0] // n
    width = (queries // LANES + 1) * LANES
    return pl.pallas_call(
        functools.partial(score_kernel, n),
        out_shape=jax.ShapeDtypeStruct((n, n * seqs, width), jnp.bfloat16),
        in_specs=[SMEM, SMEM, VMEM, VMEM],
        out_specs=VMEM,
        scratch_shapes=[pltpu.VMEM((n * white.shape[1], white.shape[2]), jnp.float32)],
        compiler_params=pltpu.CompilerParams(vmem_limit_bytes=16 << 20),
        cost_estimate=pl.CostEstimate(
            flops=2 * n * seqs * bank.size, bytes_accessed=2 * bank.size, transcendentals=0
        ),
        name="score",
    )(me, seq_ids, white, bank)


def place_kernel(partial_ref, out_ref):
    rows, queries = out_ref.shape
    total = jnp.sum(partial_ref[...].astype(jnp.float32), axis=0)
    raw = total[:, :queries].astype(jnp.bfloat16)
    ids = total[:, queries : queries + 1].astype(jnp.int32)
    chosen = ids == lax.broadcasted_iota(jnp.int32, (rows, rows), 1)
    out_ref[...] = lax.dot_general(
        chosen.astype(jnp.bfloat16), raw, (((0,), (0,)), ((), ())), preferred_element_type=jnp.float32
    ).astype(jnp.bfloat16)


def place(partials, queries):
    return pl.pallas_call(
        lambda a, b: place_kernel(a, b),
        out_shape=jax.ShapeDtypeStruct((partials.shape[1], queries), jnp.bfloat16),
        in_specs=[VMEM],
        out_specs=VMEM,
        compiler_params=pltpu.CompilerParams(vmem_limit_bytes=16 << 20),
        name="place",
    )(partials)


def body(n, activations, out_grads, proj_in, proj_out, cov_in, cov_out, lengths, seq_ids, bank):
    me = lax.axis_index("coord").reshape(1)
    seqs, length, width = activations.shape
    activations, out_grads = activations.reshape(seqs * length, width), out_grads.reshape(seqs * length, width)
    a, b, c = factors(n)
    paired = a & (a - 1) == 0
    packed = pack(proj_in, proj_out)
    half = first_half(cov_in, cov_out)
    held = {(0, 0, 0): packed}
    for at in range(1, min(a, 3)):
        held[at, 0, 0] = moved(packed, (at, 0, 0), n)
    for by in range(1, b):
        held[0, by, 0] = moved(packed, (0, by, 0), n)
    held, half = lax.optimization_barrier((held, half))
    early = list(held)
    rows = proj_in.shape[0]
    halves = {(at, t): (held[at], t * rows, rows) for at in early for t in range(2)}
    wanted = {}
    for at in range(1, a):
        nearest = at & -at
        source = at - nearest if paired and nearest != at else 0
        for by in range(b):
            for t in range(2):
                if ((at, by, 0), t) in halves:
                    continue
                if source or at > 2:
                    wanted[(at, by, 0), t] = (source, 0, 0), (at - source, by, 0)
                elif at == 1 and t == 0:
                    wanted[(at, by, 0), t] = (0, by, 0), (1, 0, 0)
                else:
                    wanted[(at, by, 0), t] = (at, 0, 0), (0, by, 0)
    arrivals = []
    while wanted:
        steps = {}
        for to, (source, step) in wanted.items():
            if (source, to[1]) in halves:
                steps.setdefault(step, []).append((to, source))
        for step, both in steps.items():
            arrived = moved(merge(joined([halves[source, to[1]] for to, source in both])), step, n)
            arrivals.append((arrived, [to for to, _ in both]))
            for i, (to, _) in enumerate(both):
                halves[to] = arrived, i * rows, rows
                del wanted[to]
    k = second_half(half, lengths)
    order = [(at, by, core) for core in range(c) for by in range(b) for at in range(a)]
    if rows % LANES == 0 and arrivals and c == 2:
        total, inputs = project(
            me, activations, out_grads, [held[at] for at in early], [order.index(at) for at in early], seqs, n
        )
        across = [moved(merge([(held[at], 0, 2 * rows) for at in early]), (0, 0, 1), n)]
        waiting, total, k = lax.optimization_barrier(([arrived for arrived, _ in arrivals], total, k))
        across.append(moved(merge([(arrived, 0, arrived.shape[0]) for arrived in waiting]), (0, 0, 1), n))
        operands = [inputs, across[1]]
        sooner = [
            (order.index(at), t, 1 + i, j * rows)
            for i, (_, group) in enumerate(arrivals)
            for j, (at, t) in enumerate(group)
        ]
        crossed = [[(at, t) for at in early for t in range(2)], [to for _, group in arrivals for to in group]]
        sooner += [(order.index((*at[:2], 1)), t, 0, j * rows) for j, (at, t) in enumerate(crossed[0])]
        late = [(order.index((*at[:2], 1)), t, 0, j * rows) for j, (at, t) in enumerate(crossed[1])]
        total = extended(me, total, inputs, sooner, [across[0], *waiting], n)
    else:
        for at in order:
            if at[2] == 0:
                held[at] = merge(joined([halves[at, 0], halves[at, 1]]))
                for by in range(1, c):
                    held[at[0], at[1], by] = moved(held[at], (0, 0, by), n)
        total = project(me, activations, out_grads, [held[at] for at in order], list(range(n)), seqs, n)[0]
        operands, late = [], []
    white = whitened_blocks(me, total, k, late, operands, seqs, n)
    partials = partial_scores(me, seq_ids, exchanged(white, n), bank)
    return place(exchanged(partials, n), bank.shape[0] // n)


def solution(mesh):
    in_specs = (
        P(("groups", "coord"), None, None),
        P(("groups", "coord"), None, None),
        P("coord", None),
        P("coord", None),
        P(),
        P(),
        P(("groups", "coord")),
        P(("groups", "coord")),
        P(None, "coord"),
    )
    out_specs = P("groups", "coord")
    return jax.shard_map(
        functools.partial(body, mesh.shape["coord"]),
        mesh=mesh,
        in_specs=in_specs,
        out_specs=out_specs,
        check_vma=False,
    )
```
